32 devices in a mesh: dp: 2 (over core), ctx: 8 (over z, x), tp: 2 (over y).
Axes of the slice: x: 2, y: 2, z: 4, core: 2. Of those that a mesh axis runs over, the one named last changes fastest.
Arguments:
- queries: bfloat16 [2, 2048, 512], P('dp', 'ctx', 'tp'), may hold values from -32 to 32
- key_heads: bfloat16 [2, 2048, 512], P('dp', 'ctx', 'tp'), may hold values from -32 to 32
- value_heads: bfloat16 [2, 2048, 512], P('dp', 'ctx', 'tp'), may hold values from -6 to 6
- grad_output: bfloat16 [2, 2048, 4096], P('dp', 'ctx', 'tp'), may hold values from -6 to 6
- out_weight: bfloat16 [512, 4096], P('tp'), may hold values from -0.375 to 0.375
- block_pattern: int32 [8, 3], replicated, may hold values from 0 to 7, all different within a row; in each aligned block of 8 rows (0 to 7, 8 to 15, ...) at most 6 rows name the same one
- global_offsets: int32 [8, 8], replicated, may hold values from 0 to 255, as said below
Outputs:
- grad_queries: bfloat16 [2, 2048, 512], P('dp', 'ctx', 'tp')
- grad_keys: bfloat16 [2, 2048, 512], P('dp', 'ctx', 'tp')
- grad_values: bfloat16 [2, 2048, 512], P('dp', 'ctx', 'tp')
- grad_weight: bfloat16 [512, 4096], P('tp', ('dp', 'ctx'))
The draws below stay inside these ranges and needn't reach their ends.
Inputs may be any that keep to these rules, and one draw needn't show every extreme that they name: `block_pattern`: each row names 3 different blocks; no block is named by more than 6 rows in all, and one block is named by exactly 6 rows. A row may name its own block or a neighbour. `global_offsets`: row b holds the positions within block b of its 8 global tokens, all different.
All inputs are finite; a program needn't handle non-finite values.
Results may differ from the reference program's by a relative error of at most 0.017.
Values may be sent and summed in bfloat16 or wider, within the bound.
No kernel may reach another device: no remote copies, remote signals or barrier semaphores. Data moves between devices by JAX's collectives and lax.ppermute only.
A program may use at most 64 MiB of HBM per device.

```python
import math
import jax
import jax.numpy as jnp
import numpy as np
from jax import lax

D = 4096
HD = 128
BLK = 256
RAND = 3
GB = 8
MOST = 6
NBLK = 8
SEQ = 2048
BATCH = 2
FEATS = 512


def offset_table(key):
    table_key = jax.random.fold_in(key, 7)
    priority = jax.random.randint(table_key, (NBLK, BLK), 0, 1 << 20, dtype=jnp.int32) * BLK
    priority = priority + jnp.arange(BLK, dtype=jnp.int32)[None, :]
    return jnp.argsort(priority, axis=1)[:, :GB + 5].astype(jnp.int32)


def drawn_floats(key, stream_id):
    full_shape = (BATCH, SEQ, FEATS)
    return jnp.clip(jax.random.normal(jax.random.fold_in(key, stream_id), full_shape, dtype=jnp.float32), -4.0, 4.0)


def draw_queries(key, part):
    values = drawn_floats(key, 21)
    return values.astype(jnp.bfloat16)


def draw_key_heads(key, part):
    key_ramp = 0.6 + 1.2 * jnp.arange(SEQ, dtype=jnp.float32) / SEQ
    values = drawn_floats(key, 31) * key_ramp[None, :, None]
    return values.astype(jnp.bfloat16)


def draw_global_offsets(key, part):
    return offset_table(key)[:, :GB]


def with_spikes(result, stream_key, source, target, shards_of, factor):
    def block_of(axis_at):
        return (jnp.arange(result.shape[axis_at]) // (result.shape[axis_at] // shards_of)).reshape((-1,) + (1,) * (result.ndim - 1 - axis_at))

    first = jax.random.permutation(stream_key, shards_of)[block_of(target)]
    other_side = (block_of(target) + shards_of // 2) % shards_of
    return jnp.where((block_of(source) == first) | (block_of(source) == other_side), factor * result, result)


def steps_of(stream_key, extent, split, least, high):
    def one(position, shards_of):
        draws = jax.random.uniform(jax.random.fold_in(jax.random.fold_in(stream_key, 6), position), (shards_of,), jnp.float32, least / len(split), high / len(split))
        return jnp.repeat(jnp.exp(draws), extent[position] // shards_of).reshape((-1,) + (1,) * (len(extent) - position - 1))

    gain = one(*split[0])
    for cut in split[1:]:
        gain = gain * one(*cut)
    return gain


def shared_out(key, own, number, rows, number_of, top, limit, lean):
    order = jax.random.permutation(key, number_of)
    heavy_load, usual = load_shares(number_of, rows * top, limit, lean, True), load_shares(number_of, rows * top, limit, lean, False)
    places = jnp.arange(number_of)

    def named(lengths, turn):
        used = int((lengths > 0).sum())
        fixed = max(1, used // 4)
        moved = fixed + (places - fixed + turn * (used - fixed)) % max(1, number_of - fixed)
        return jnp.zeros((number_of,), jnp.int32).at[order[jnp.where(places < fixed, places, moved)]].set(jnp.asarray(lengths, jnp.int32))

    lengths = jnp.where(number % 4 == 0, named(heavy_load, number // 4), named(usual, number - number // 4 - 1))
    mixed = jax.random.permutation(jax.random.fold_in(own, 3), number_of)
    giver, taker = mixed[0:number_of // 2 * 2:2], mixed[1:number_of // 2 * 2:2]
    slack = jnp.minimum(lengths[giver] - 1, limit - lengths[taker]) // 2
    slack = jnp.where((giver == order[0]) | (taker == order[0]) | (lengths[taker] == 0), 0, jnp.maximum(slack, 0))
    moved = jax.random.randint(jax.random.fold_in(own, 4), (number_of // 2,), 0, 1 << 20) % (slack + 1)
    lengths = lengths.at[giver].add(-moved).at[taker].add(moved)
    labels = jnp.searchsorted(jnp.cumsum(lengths), jnp.arange(rows * top), side="right").astype(jnp.int32)
    table = labels.reshape(top, rows).T
    table = table[jax.random.permutation(jax.random.fold_in(own, 1), rows)]
    turn = jax.random.randint(jax.random.fold_in(own, 2), (rows, 1), 0, top)
    return jnp.take_along_axis(table, (jnp.arange(top)[None, :] + turn) % top, axis=1)


def load_shares(amount, total, most, skew, full):
    portions = [(1 << 20) // math.isqrt(standing ** skew) + 1 for standing in range(1, amount + 1)]
    largest = most if full else min(most, max(-(-total // amount), total * portions[0] // sum(portions)))
    least = 1 if total - largest >= amount - 1 else 0
    holding, rest = [largest] + [least] * (amount - 1), total - largest - least * (amount - 1)
    while rest > 0:
        movable = [i for i in range(1, amount) if holding[i] < largest] or [i for i in range(1, amount) if holding[i] < most]
        whole, remaining = sum([portions[i] for i in movable]), rest
        for i in movable:
            extra = min(most - holding[i], max(1, remaining * portions[i] // whole), rest)
            holding[i] = holding[i] + extra
            rest = rest - extra
    return np.array(holding)


def scatter_about(rng, shape, spread, reach, cuts=(), held_as=jnp.bfloat16):
    loudness = steps_of(rng, shape, cuts, -0.22, 0.18) if cuts else 1.0
    values = jax.random.normal(rng, shape, jnp.float32) * spread * loudness
    return jnp.minimum(jnp.maximum(values, -reach), reach).astype(held_as)


def gaussian_with(rng, extent, width, limit, cuts, heavy, kind=jnp.bfloat16):
    entries = width * jax.random.normal(rng, extent, jnp.float32)
    if cuts:
        entries = entries * steps_of(rng, extent, cuts, -0.22, 0.18)
    return jnp.clip(with_spikes(entries, jax.random.fold_in(rng, 3), *heavy), -limit, limit).astype(kind)


def setup_inputs(seed: int = 0) -> dict:
    keys = jax.random.split(jax.random.key(seed), 8)
    queries = draw_queries(jax.random.fold_in(keys[7], 71), 0)
    key_heads = draw_key_heads(jax.random.fold_in(keys[7], 71), 0)
    value_heads = scatter_about(keys[2], (BATCH, SEQ, FEATS), 1.0, 6.0, ((0, 2), (1, 8), (2, 2)))
    grad_output = gaussian_with(keys[3], (BATCH, SEQ, D), 1.0, 6.0, ((0, 2), (1, 8), (2, 2)), (1, 2, 8, 2.0))
    out_weight = scatter_about(keys[4], (FEATS, D), (D // 16) ** -0.5, 0.375, ((0, 2),))
    block_pattern_keys = jax.random.split(jax.random.fold_in(keys[5], 1), NBLK // NBLK)
    block_pattern_turns = jax.random.permutation(jax.random.fold_in(keys[5], 3), NBLK // NBLK)
    block_pattern = jax.vmap(lambda own, number: shared_out(jax.random.fold_in(keys[5], 2), own, number, NBLK, NBLK, RAND, MOST, 2))(block_pattern_keys, block_pattern_turns).reshape((NBLK, RAND))
    global_offsets = draw_global_offsets(jax.random.fold_in(keys[7], 71), 0)
    return {"queries": queries, "key_heads": key_heads, "value_heads": value_heads, "grad_output": grad_output, "out_weight": out_weight, "block_pattern": block_pattern, "global_offsets": global_offsets}


def rounded(values):
    return lax.optimization_barrier(values.astype(jnp.bfloat16)).astype(jnp.float32)


def softmax_last(scores):
    row_max = jnp.max(scores, axis=-1, keepdims=True)
    weights_f = jnp.exp(scores - row_max)
    row_total = jnp.sum(weights_f, axis=-1, keepdims=True)
    return weights_f / row_total


def document(query_doc, key_doc, value_doc, grad_doc, out_weight, block_pattern, global_offsets):
    token_count, feature_count = query_doc.shape
    block_count = block_pattern.shape[0]
    block_size = token_count // block_count
    head_count = feature_count // HD
    score_scale = HD ** -0.5
    grad_heads = jnp.dot(grad_doc, out_weight.T, preferred_element_type=jnp.float32).astype(jnp.bfloat16)
    query_all = query_doc.reshape(token_count, head_count, HD).astype(jnp.float32)
    key_all = key_doc.reshape(token_count, head_count, HD).astype(jnp.float32)
    value_all = value_doc.reshape(token_count, head_count, HD).astype(jnp.float32)
    grad_all = grad_heads.reshape(token_count, head_count, HD).astype(jnp.float32)
    positions = jnp.arange(block_size, dtype=jnp.int32)
    glob_flags = jnp.any(global_offsets[:, :, None] == positions[None, None, :], axis=1)
    glob_positions = (jnp.arange(block_count, dtype=jnp.int32)[:, None] * block_size + global_offsets).reshape(-1)

    def one_block(carry, own_block):
        row_keep = jnp.logical_not(glob_flags[own_block])
        own_offsets = global_offsets[own_block]
        neighbours = own_block + jnp.arange(-1, 2, dtype=jnp.int32)
        chosen = block_pattern[own_block]
        slot_ok = jnp.concatenate([(neighbours >= 0) & (neighbours < block_count), jnp.abs(chosen - own_block) > 1])
        slot_clip = jnp.clip(jnp.concatenate([neighbours, chosen]), 0, block_count - 1).astype(jnp.int32)
        slot_rows = (slot_clip[:, None] * block_size + positions[None, :]).reshape(-1)
        key_index = jnp.concatenate([slot_rows, glob_positions]).astype(jnp.int32)
        slot_valid = (slot_ok[:, None] & jnp.logical_not(glob_flags[slot_clip])).reshape(-1)
        key_valid = jnp.concatenate([slot_valid, glob_positions >= 0])
        block_start = (own_block * block_size).astype(jnp.int32)
        query_block = lax.dynamic_slice_in_dim(query_all, block_start, block_size, 0)
        grad_block = lax.dynamic_slice_in_dim(grad_all, block_start, block_size, 0)
        key_pick = jnp.take(key_all, key_index, axis=0)
        value_pick = jnp.take(value_all, key_index, axis=0)
        scores = score_scale * jnp.einsum('qhd,khd->hqk', query_block, key_pick)
        scores = jnp.where(key_valid[None, None, :], scores, -jnp.inf)
        attn_probs = jnp.where(row_keep[None, :, None], softmax_last(scores), 0.0)
        probs_low = rounded(attn_probs)
        glob_query = jnp.take(query_block, own_offsets, axis=0)
        glob_grad = jnp.take(grad_block, own_offsets, axis=0)
        glob_probs = softmax_last(score_scale * jnp.einsum('ghd,khd->hgk', glob_query, key_all))
        glob_low = rounded(glob_probs)
        attention = jnp.einsum('hqk,khd->qhd', probs_low, value_pick)
        attention = attention.at[own_offsets].set(jnp.einsum('hgk,khd->ghd', glob_low, value_all))
        attention = attention.astype(jnp.bfloat16)
        row_dot = jnp.sum(grad_block * attention.astype(jnp.float32), axis=2)
        glob_dot = jnp.take(row_dot, own_offsets, axis=0)
        grad_probs = jnp.einsum('qhd,khd->hqk', grad_block, value_pick)
        dscore_low = rounded(attn_probs * (grad_probs - row_dot.T[:, :, None]))
        glob_dscore = rounded(glob_probs * (jnp.einsum('ghd,khd->hgk', glob_grad, value_all) - glob_dot.T[:, :, None]))
        grad_query = jnp.einsum('hqk,khd->qhd', dscore_low, key_pick)
        grad_query = grad_query.at[own_offsets].set(jnp.einsum('hgk,khd->ghd', glob_dscore, key_all))
        grad_query = (score_scale * grad_query).astype(jnp.bfloat16)
        glob_term = jnp.stack([score_scale * jnp.einsum('hgk,ghd->khd', glob_dscore, glob_query),
                               jnp.einsum('hgk,ghd->khd', glob_low, glob_grad)], axis=1)
        pick_term = jnp.stack([score_scale * jnp.einsum('hqk,qhd->khd', dscore_low, query_block),
                               jnp.einsum('hqk,qhd->khd', probs_low, grad_block)], axis=1)
        key_term = glob_term.at[key_index].add(pick_term)
        return carry + rounded(key_term), (grad_query, attention)

    zeros = jnp.zeros((token_count, 2, head_count, HD), jnp.float32)
    summed, (grad_query, attention) = lax.scan(one_block, zeros, jnp.arange(block_count, dtype=jnp.int32))
    grad_queries = grad_query.reshape(token_count, feature_count)
    grad_keys = summed[:, 0].reshape(token_count, feature_count).astype(jnp.bfloat16)
    grad_values = summed[:, 1].reshape(token_count, feature_count).astype(jnp.bfloat16)
    weight_terms = jnp.dot(attention.reshape(token_count, feature_count).T, grad_doc, preferred_element_type=jnp.float32)
    return grad_queries, grad_keys, grad_values, weight_terms


def reference(queries, key_heads, value_heads, grad_output, out_weight, block_pattern, global_offsets):
    results = [document(queries[doc_index], key_heads[doc_index], value_heads[doc_index], grad_output[doc_index],
                        out_weight, block_pattern, global_offsets) for doc_index in range(queries.shape[0])]
    grad_queries = jnp.stack([entry[0] for entry in results])
    grad_keys = jnp.stack([entry[1] for entry in results])
    grad_values = jnp.stack([entry[2] for entry in results])
    weight_sum = results[0][3]
    for entry in results[1:]:
        weight_sum = weight_sum + entry[3]
    return grad_queries, grad_keys, grad_values, weight_sum.astype(jnp.bfloat16)
```

```python
import functools

import jax
import jax.numpy as jnp
from jax import lax
from jax.experimental import pallas as pl
from jax.experimental.pallas import tpu as pltpu
from jax.sharding import PartitionSpec as P

HD = 128
MASKED = -1e30


def against(left_op, right_op):
    return lax.dot_general(
        left_op, right_op, (((1,), (1,)), ((), ())), preferred_element_type=jnp.float32
    )


def across(left_op, right_op):
    return lax.dot_general(
        left_op, right_op, (((0,), (0,)), ((), ())), preferred_element_type=jnp.float32
    )


def product(left_op, right_op):
    return jnp.dot(left_op, right_op, preferred_element_type=jnp.float32)


def attention_kernel(block_count, *refs):
    query_ref, grad_ref, key_bias_ref, row_bias_ref = refs[:4]
    kv_refs = refs[4 : 4 + block_count]
    attn_ref, dquery_ref = refs[4 + block_count : 6 + block_count]
    part_refs = refs[6 + block_count : 6 + 2 * block_count]
    probs_ref, low_ref = refs[6 + 2 * block_count :]
    block_size, feat_count = query_ref.shape
    score_scale = HD ** (-0.5)
    row_bias = row_bias_ref[...]
    for head in range(feat_count // HD):
        cols = slice(head * HD, (head + 1) * HD)
        vcols = slice(feat_count + head * HD, feat_count + (head + 1) * HD)
        query = query_ref[:, cols]
        grad = grad_ref[:, cols]
        row_max = jnp.full((block_size, 1), MASKED, jnp.float32)
        for block in range(block_count):
            keys = slice(block * block_size, (block + 1) * block_size)
            scores = score_scale * against(query, kv_refs[block][:, cols])
            scores = scores + jnp.maximum(row_bias, key_bias_ref[:, keys])
            probs_ref[:, keys] = scores
            row_max = jnp.maximum(row_max, jnp.max(scores, axis=1, keepdims=True))
        row_total = jnp.zeros((block_size, 1), jnp.float32)
        for block in range(block_count):
            keys = slice(block * block_size, (block + 1) * block_size)
            weights = jnp.exp(probs_ref[:, keys] - row_max)
            probs_ref[:, keys] = weights
            row_total = row_total + jnp.sum(weights, axis=1, keepdims=True)
        inverse = 1.0 / row_total
        attn = jnp.zeros((block_size, HD), jnp.float32)
        for block in range(block_count):
            keys = slice(block * block_size, (block + 1) * block_size)
            probs = probs_ref[:, keys] * inverse
            probs_ref[:, keys] = probs
            low = probs.astype(jnp.bfloat16)
            low_ref[:, keys] = low
            attn = attn + product(low, kv_refs[block][:, vcols])
        attn_low = attn.astype(jnp.bfloat16)
        attn_ref[:, cols] = attn_low
        row_dot = jnp.sum(
            grad.astype(jnp.float32) * attn_low.astype(jnp.float32), axis=1, keepdims=True
        )
        dquery = jnp.zeros((block_size, HD), jnp.float32)
        for block in range(block_count):
            keys = slice(block * block_size, (block + 1) * block_size)
            dprobs = against(grad, kv_refs[block][:, vcols])
            dscore = (probs_ref[:, keys] * (dprobs - row_dot)).astype(jnp.bfloat16)
            dquery = dquery + product(dscore, kv_refs[block][:, cols])
            part_refs[block][:, cols] = (score_scale * across(dscore, query)).astype(jnp.bfloat16)
            part_refs[block][:, vcols] = across(low_ref[:, keys], grad).astype(jnp.bfloat16)
        dquery_ref[:, cols] = (score_scale * dquery).astype(jnp.bfloat16)


def attention_block(query, grad, key_bias, row_bias, kv_blocks):
    block_count = len(kv_blocks)
    block_size, feat_count = query.shape
    key_count = block_count * block_size
    small = jax.ShapeDtypeStruct(query.shape, jnp.bfloat16)
    part = jax.ShapeDtypeStruct((block_size, 2 * feat_count), jnp.bfloat16)
    vmem = pl.BlockSpec(memory_space=pltpu.VMEM)
    flops = 10 * block_size * key_count * feat_count
    out = pl.pallas_call(
        functools.partial(attention_kernel, block_count),
        out_shape=[small, small] + [part] * block_count,
        in_specs=[vmem] * (4 + block_count),
        out_specs=[vmem] * (2 + block_count),
        scratch_shapes=[
            pltpu.VMEM((block_size, key_count), jnp.float32),
            pltpu.VMEM((block_size, key_count), jnp.bfloat16),
        ],
        compiler_params=pltpu.CompilerParams(vmem_limit_bytes=48 * 1024 * 1024),
        cost_estimate=pl.CostEstimate(
            flops=flops,
            bytes_accessed=8 * key_count * feat_count,
            transcendentals=block_size * key_count * feat_count // HD,
        ),
        name="attention",
    )(query, grad, key_bias, row_bias, *kv_blocks)
    return out[0], out[1], out[2:]


def per_device(
    queries, key_heads, value_heads, grad_output, out_weight, block_pattern, global_offsets
):
    block_size = queries.shape[1]
    dp_count, ctx_count, tp_count = (lax.axis_size(name) for name in ("dp", "ctx", "tp"))
    dp_at, ctx_at, tp_at = (lax.axis_index(name) for name in ("dp", "ctx", "tp"))
    inner = 2 if ctx_count % 2 == 0 else 1
    outer = ctx_count // inner
    outer_at, inner_at = ctx_at // inner, ctx_at % inner

    def outer_pairs(step):
        return [
            (o * inner + i, ((o + step) % outer) * inner + i)
            for o in range(outer)
            for i in range(inner)
        ]

    def inner_pairs(step):
        return [
            (o * inner + i, o * inner + (i + step) % inner)
            for o in range(outer)
            for i in range(inner)
        ]

    def shift_pairs(count, step):
        return [(i, (i + step) % count) for i in range(count)]

    kv_own = jnp.concatenate([key_heads[0], value_heads[0]], axis=1)
    grad_own = grad_output[0]
    grad_parts = [grad_own] + [
        lax.ppermute(grad_own, "tp", shift_pairs(tp_count, -step)) for step in range(1, tp_count)
    ]
    kv_columns = [kv_own] + [
        lax.ppermute(kv_own, "ctx", outer_pairs(step)) for step in range(1, outer)
    ]
    kv_blocks, sources = [], []
    for o_step in range(outer):
        for i_step in range(inner):
            block = kv_columns[o_step]
            if i_step:
                block = lax.ppermute(block, "ctx", inner_pairs(i_step))
            kv_blocks.append(block)
            sources.append(
                ((outer_at - o_step) % outer) * inner + (inner_at - i_step) % inner
            )
    sources = jnp.stack(sources)

    positions = jnp.arange(block_size, dtype=jnp.int32)
    glob_flags = jnp.any(global_offsets[:, :, None] == positions[None, None, :], axis=1)
    chosen = block_pattern[ctx_at]
    seen = (jnp.abs(sources - ctx_at) <= 1) | jnp.any(sources[:, None] == chosen[None, :], axis=1)
    key_seen = seen[:, None] | glob_flags[sources]
    key_bias = jnp.where(key_seen, 0.0, MASKED).astype(jnp.float32).reshape(1, -1)
    row_bias = jnp.where(glob_flags[ctx_at], 0.0, MASKED).astype(jnp.float32)[:, None]

    col_count = grad_own.shape[1]
    grad_sum = 0.0
    for step in range(tp_count):
        start = ((tp_at + step) % tp_count) * col_count
        columns = lax.dynamic_slice_in_dim(out_weight, start, col_count, 1)
        grad_sum = grad_sum + against(grad_parts[step], columns)
    grad_heads = grad_sum.astype(jnp.bfloat16)

    attention, dquery, parts = attention_block(
        queries[0], grad_heads, key_bias, row_bias, kv_blocks
    )

    per_dp = tp_count // dp_count

    def dp_columns(which):
        picked = []
        for i in range(per_dp):
            step = (which * per_dp + i - tp_at) % tp_count
            piece = grad_parts[0]
            for k in range(1, tp_count):
                piece = jnp.where(step == k, grad_parts[k], piece)
            picked.append(piece)
        return picked[0] if per_dp == 1 else jnp.concatenate(picked, axis=1)

    weight_sum = across(attention, dp_columns(dp_at))
    for step in range(1, dp_count):
        send = across(attention, dp_columns((dp_at + step) % dp_count)).astype(jnp.bfloat16)
        weight_sum = weight_sum + lax.ppermute(send, "dp", shift_pairs(dp_count, step)).astype(
            jnp.float32
        )
    feat_count = weight_sum.shape[0]
    pieces = weight_sum.reshape(feat_count, outer, inner, -1).transpose(2, 1, 0, 3)
    inner_sum = lax.dynamic_index_in_dim(pieces, inner_at, 0, keepdims=False)
    for step in range(1, inner):
        send = lax.dynamic_index_in_dim(pieces, (inner_at + step) % inner, 0, keepdims=False)
        inner_sum = inner_sum + lax.ppermute(
            send.astype(jnp.bfloat16), "ctx", inner_pairs(step)
        ).astype(jnp.float32)
    grad_weight = lax.dynamic_index_in_dim(inner_sum, outer_at, 0, keepdims=False)
    for step in range(1, outer):
        send = lax.dynamic_index_in_dim(inner_sum, (outer_at + step) % outer, 0, keepdims=False)
        grad_weight = grad_weight + lax.ppermute(
            send.astype(jnp.bfloat16), "ctx", outer_pairs(step)
        ).astype(jnp.float32)

    summed = 0.0
    for o_step in range(outer):
        column = parts[o_step * inner].astype(jnp.float32)
        for i_step in range(1, inner):
            column = column + lax.ppermute(
                parts[o_step * inner + i_step], "ctx", inner_pairs(-i_step)
            ).astype(jnp.float32)
        if o_step:
            column = lax.ppermute(
                column.astype(jnp.bfloat16), "ctx", outer_pairs(-o_step)
            ).astype(jnp.float32)
        summed = summed + column
    grad_keys = summed[:, :feat_count].astype(jnp.bfloat16)
    grad_values = summed[:, feat_count:].astype(jnp.bfloat16)
    return dquery[None], grad_keys[None], grad_values[None], grad_weight.astype(jnp.bfloat16)


def solution(mesh):
    in_specs = (
        P("dp", "ctx", "tp"),
        P("dp", "ctx", "tp"),
        P("dp", "ctx", "tp"),
        P("dp", "ctx", "tp"),
        P("tp", None),
        P(),
        P(),
    )
    out_specs = (
        P("dp", "ctx", "tp"),
        P("dp", "ctx", "tp"),
        P("dp", "ctx", "tp"),
        P("tp", ("dp", "ctx")),
    )
    return jax.shard_map(
        per_device, mesh=mesh, in_specs=in_specs, out_specs=out_specs, check_vma=False
    )
```

```python
import functools

import jax
import jax.numpy as jnp
from jax import lax
from jax.experimental import pallas as pl
from jax.experimental.pallas import tpu as pltpu
from jax.sharding import PartitionSpec as P

HD = 128
MASKED = -1e30
INNER = 2
ANY = pl.BlockSpec(memory_space=pl.ANY)
VMEM = pl.BlockSpec(memory_space=pltpu.VMEM)
SMEM = pl.BlockSpec(memory_space=pltpu.SMEM)


def against(left_op, right_op):
    return lax.dot_general(
        left_op, right_op, (((1,), (1,)), ((), ())), preferred_element_type=jnp.float32
    )


def product(left_op, right_op):
    return jnp.dot(left_op, right_op, preferred_element_type=jnp.float32)


def begin(source, target, semaphore):
    copy = pltpu.make_async_copy(source, target, semaphore)
    copy.start()
    return copy


def call(kernel, out_shape, in_specs, out_specs, scratch, flops, moved, name):
    return pl.pallas_call(
        kernel,
        out_shape=out_shape,
        in_specs=in_specs,
        out_specs=out_specs,
        scratch_shapes=scratch,
        compiler_params=pltpu.CompilerParams(vmem_limit_bytes=40 * 1024 * 1024),
        cost_estimate=pl.CostEstimate(flops=flops, bytes_accessed=moved, transcendentals=0),
        name=name,
    )


def bf16(*shape):
    return jax.ShapeDtypeStruct(shape, jnp.bfloat16)


def part_kernel(at_ref, q_ref, k_ref, v_ref, kv_mine, kv_theirs, q_mine, q_theirs):
    width = q_mine.shape[1]
    mine = pl.ds(pl.multiple_of(at_ref[0] * width, width), width)
    theirs = pl.ds(pl.multiple_of((1 - at_ref[0]) * width, width), width)
    for cols, kv_out, q_out in ((mine, kv_mine, q_mine), (theirs, kv_theirs, q_theirs)):
        kv_out[:, :width] = k_ref[:, cols]
        kv_out[:, width:] = v_ref[:, cols]
        q_out[...] = q_ref[:, cols]


def part_heads(at, queries, keys, values):
    rows, feats = queries.shape
    half = feats // INNER
    return call(
        part_kernel,
        [bf16(rows, 2 * half), bf16(rows, 2 * half), bf16(rows, half), bf16(rows, half)],
        [SMEM] + [VMEM] * 3,
        [VMEM] * 4,
        [],
        0,
        12 * rows * feats,
        "part_heads",
    )(at, queries, keys, values)


def forward_kernel(block_count, head_count, *refs):
    q_mine, q_recv, key_bias, row_bias = refs[:4]
    kv_refs = refs[4 : 4 + block_count]
    e_out, inv_out, attn_mine, attn_theirs = refs[4 + block_count : 8 + block_count]
    kv_s, e_s, s_ref, kv_sem, e_sem = refs[8 + block_count :]
    rows = q_mine.shape[0]
    feats = head_count * HD
    score_scale = HD ** (-0.5)
    loads = [begin(kv_refs[j], kv_s.at[j], kv_sem.at[j]) for j in range(block_count)]
    stores = []
    for head in range(head_count):
        cols = slice(head * HD, (head + 1) * HD)
        vcols = slice(feats + head * HD, feats + (head + 1) * HD)
        q_t = jnp.concatenate(
            [jnp.transpose(q_mine[:, cols]), jnp.transpose(q_recv[:, cols])], axis=1
        )
        tops = [jnp.full((1, rows), MASKED, jnp.float32) for _ in range(2)]
        for j in range(block_count):
            if head == 0:
                loads[j].wait()
            scores = product(kv_s[j][:, cols], q_t)
            keys = slice(j * rows, (j + 1) * rows)
            for group in range(2):
                half = slice(group * rows, (group + 1) * rows)
                biased = scores[:, half] + jnp.maximum(
                    key_bias[keys, group : group + 1], row_bias[:, half]
                )
                s_ref[keys, half] = biased
                tops[group] = jnp.maximum(tops[group], jnp.max(biased, axis=0, keepdims=True))
        top = jnp.concatenate(tops, axis=1)
        total = jnp.zeros((1, 2 * rows), jnp.float32)
        attn_t = jnp.zeros((HD, 2 * rows), jnp.float32)
        for j in range(block_count):
            keys = slice(j * rows, (j + 1) * rows)
            weights = jnp.exp((s_ref[keys, :] - top) * score_scale)
            total = total + jnp.sum(weights, axis=0, keepdims=True)
            low = weights.astype(jnp.bfloat16)
            e_s[head, keys, :] = low
            stores.append(
                begin(e_s.at[head, keys], e_out.at[head, keys], e_sem.at[head * block_count + j])
            )
            attn_t = attn_t + product(jnp.transpose(kv_s[j][:, vcols]), low)
        inverse = 1.0 / total
        inv_out[head : head + 1, :] = inverse
        attn_low = (attn_t * inverse).astype(jnp.bfloat16)
        attn_mine[cols, :] = attn_low[:, :rows]
        attn_theirs[cols, :] = attn_low[:, rows:]
    for store in stores:
        store.wait()


def forward(q_mine, q_recv, key_bias, row_bias, kv_blocks):
    block_count = len(kv_blocks)
    rows, feats = q_mine.shape
    heads = feats // HD
    keys = block_count * rows
    return call(
        functools.partial(forward_kernel, block_count, heads),
        [
            bf16(heads, keys, 2 * rows),
            jax.ShapeDtypeStruct((heads, 2 * rows), jnp.float32),
            bf16(feats, rows),
            bf16(feats, rows),
        ],
        [VMEM] * 4 + [ANY] * block_count,
        [ANY] + [VMEM] * 3,
        [
            pltpu.VMEM((block_count, rows, 2 * feats), jnp.bfloat16),
            pltpu.VMEM((heads, keys, 2 * rows), jnp.bfloat16),
            pltpu.VMEM((keys, 2 * rows), jnp.float32),
            pltpu.SemaphoreType.DMA((block_count,)),
            pltpu.SemaphoreType.DMA((heads * block_count,)),
        ],
        8 * rows * keys * feats,
        8 * keys * feats + 4 * heads * keys * rows,
        "forward",
    )(q_mine, q_recv, key_bias, row_bias, *kv_blocks)


def backward_kernel(block_count, head_count, *refs):
    q_mine, q_recv, g_mine, g_recv, attn_mine, attn_theirs, inv_ref = refs[:7]
    e_ref = refs[7]
    kv_refs = refs[8 : 8 + block_count]
    outer = block_count // INNER
    dq_mine, dq_theirs = refs[8 + block_count : 10 + block_count]
    part_outs = refs[10 + block_count : 10 + block_count + outer]
    kv_s, e_s, part_s, kv_sem, e_sem, part_sem = refs[10 + block_count + outer :]
    rows = q_mine.shape[0]
    feats = head_count * HD
    score_scale = HD ** (-0.5)
    kv_loads, e_loads = [], {}
    for j in range(block_count):
        keys = slice(j * rows, (j + 1) * rows)
        kv_loads.append(begin(kv_refs[j], kv_s.at[j], kv_sem.at[j]))
        for head in range(head_count):
            e_loads[head, j] = begin(
                e_ref.at[head, keys], e_s.at[head, keys], e_sem.at[head * block_count + j]
            )
    for head in range(head_count):
        cols = slice(head * HD, (head + 1) * HD)
        vcols = slice(feats + head * HD, feats + (head + 1) * HD)
        inverse = inv_ref[head : head + 1, :]
        g_t = jnp.concatenate([g_mine[cols, :], g_recv[cols, :]], axis=1).astype(jnp.float32)
        attn_t = jnp.concatenate([attn_mine[cols, :], attn_theirs[cols, :]], axis=1)
        row_dot = jnp.sum(g_t * attn_t.astype(jnp.float32), axis=0, keepdims=True) * inverse
        g_t = (g_t * inverse).astype(jnp.bfloat16)
        grad = jnp.transpose(g_t)
        query = jnp.concatenate([q_mine[:, cols], q_recv[:, cols]], axis=0)
        dq_t = jnp.zeros((HD, 2 * rows), jnp.float32)
        for j in range(block_count):
            keys = slice(j * rows, (j + 1) * rows)
            if head == 0:
                kv_loads[j].wait()
            e_loads[head, j].wait()
            low = e_s[head, keys, :]
            dprobs = product(kv_s[j][:, vcols], g_t)
            dscore = (low.astype(jnp.float32) * (dprobs - row_dot)).astype(jnp.bfloat16)
            dq_t = dq_t + product(jnp.transpose(kv_s[j][:, cols]), dscore)
            part_s[j, :, cols] = (score_scale * product(dscore, query)).astype(jnp.bfloat16)
            part_s[j, :, vcols] = product(low, grad).astype(jnp.bfloat16)
        dquery = (score_scale * jnp.transpose(dq_t)).astype(jnp.bfloat16)
        dq_mine[:, cols] = dquery[:rows]
        dq_theirs[:, cols] = dquery[rows:]
    stores = []
    for j in range(block_count):
        target = part_outs[j // INNER].at[j % INNER]
        stores.append(begin(part_s.at[j], target, part_sem.at[j]))
    for store in stores:
        store.wait()


def backward(q_mine, q_recv, g_mine, g_recv, attn_mine, attn_theirs, inverse, weights, kv_blocks):
    block_count = len(kv_blocks)
    rows, feats = q_mine.shape
    heads = feats // HD
    keys = block_count * rows
    outer = block_count // INNER
    out = call(
        functools.partial(backward_kernel, block_count, heads),
        [bf16(rows, feats)] * 2 + [bf16(INNER, rows, 2 * feats)] * outer,
        [VMEM] * 7 + [ANY] * (1 + block_count),
        [VMEM] * 2 + [ANY] * outer,
        [
            pltpu.VMEM((block_count, rows, 2 * feats), jnp.bfloat16),
            pltpu.VMEM((heads, keys, 2 * rows), jnp.bfloat16),
            pltpu.VMEM((block_count, rows, 2 * feats), jnp.bfloat16),
            pltpu.SemaphoreType.DMA((block_count,)),
            pltpu.SemaphoreType.DMA((heads * block_count,)),
            pltpu.SemaphoreType.DMA((block_count,)),
        ],
        16 * rows * keys * feats,
        16 * keys * feats + 4 * heads * keys * rows,
        "backward",
    )(q_mine, q_recv, g_mine, g_recv, attn_mine, attn_theirs, inverse, weights, *kv_blocks)
    return out[0], out[1], out[2:]


def grad_heads_kernel(part_count, *refs):
    at_ref, first_ref = refs[:2]
    grads = refs[2 : 2 + part_count]
    columns = refs[2 + part_count : 2 + 2 * part_count]
    mine, theirs, total = refs[2 + 2 * part_count :]
    half = mine.shape[0]
    summed = first_ref[...]
    for k in range(part_count):
        summed = summed + against(columns[k][...], grads[k][...])
    total[...] = summed
    mine[...] = total[pl.ds(pl.multiple_of(at_ref[0] * half, half), half), :].astype(jnp.bfloat16)
    theirs[...] = total[pl.ds(pl.multiple_of((1 - at_ref[0]) * half, half), half), :].astype(
        jnp.bfloat16
    )


def grad_heads(at, first, grads, columns):
    feats, rows = first.shape
    half = feats // INNER
    count = len(grads)
    width = sum(grad.shape[1] for grad in grads)
    return call(
        functools.partial(grad_heads_kernel, count),
        [bf16(half, rows), bf16(half, rows)],
        [SMEM] + [VMEM] * (1 + 2 * count),
        [VMEM] * 2,
        [pltpu.VMEM((feats, rows), jnp.float32)],
        2 * feats * rows * width,
        2 * (feats + rows) * width,
        "grad_heads",
    )(at, first, *grads, *columns)


def weight_kernel(part_count, picked, doc_count, *refs):
    at_ref = refs[0]
    attn = refs[1 : 1 + INNER * doc_count]
    refs = refs[1 + INNER * doc_count :]
    grads, refs = refs[:part_count], refs[part_count:]
    swapped, refs = refs[: doc_count - 1], refs[doc_count - 1 :]
    keep_out, send_out, attn_s, grad_s, send_s, attn_sem, grad_sem, send_sem = refs
    inner_at, outer_at = at_ref[0], at_ref[1]
    outer, feats, width = send_out.shape
    half = feats // INNER
    rows = grads[0].shape[0]
    loads = []
    for doc in range(doc_count):
        for side in range(INNER):
            at = (1 - inner_at) if side else inner_at
            index = doc * INNER + side
            target = attn_s.at[doc, pl.ds(pl.multiple_of(at * half, half), half)]
            loads.append(begin(attn[index], target, attn_sem.at[index]))
    piece = grads[0].shape[1]
    for i in range(picked):
        cols = slice(i * piece, (i + 1) * piece)
        for k in range(part_count):

            @pl.when(at_ref[2 + i] == k)
            def _():
                begin(grads[k], grad_s.at[0, :, cols], grad_sem.at[i])

        loads.append(pltpu.make_async_copy(grads[0], grad_s.at[0, :, cols], grad_sem.at[i]))
    for doc in range(1, doc_count):
        loads.append(begin(swapped[doc - 1], grad_s.at[doc], grad_sem.at[picked + doc - 1]))
    for load in loads:
        load.wait()
    stores = []
    for side in (1, 0):
        at = (1 - inner_at) if side else inner_at
        for k in range(outer):
            place = lax.rem(outer_at + k, outer) * INNER + at
            cols = pl.ds(pl.multiple_of(place * width, width), width)
            term = product(attn_s[0], grad_s[0, :, cols])
            for doc in range(1, doc_count):
                term = term + product(attn_s[doc], grad_s[doc, :, cols])
            if side:
                send_s[k] = term.astype(jnp.bfloat16)
                stores.append(begin(send_s.at[k], send_out.at[k], send_sem.at[k]))
            else:
                keep_out[k] = term
    for store in stores:
        store.wait()


def weight_terms(at, attn, grads, swapped, outer, picked):
    half, rows = attn[0].shape
    feats = half * INNER
    doc_count = len(attn) // INNER
    columns = picked * grads[0].shape[1]
    width = columns // (outer * INNER)
    return call(
        functools.partial(weight_kernel, len(grads), picked, doc_count),
        [jax.ShapeDtypeStruct((outer, feats, width), jnp.float32), bf16(outer, feats, width)],
        [SMEM] + [ANY] * (len(attn) + len(grads) + len(swapped)),
        [VMEM, ANY],
        [
            pltpu.VMEM((doc_count, feats, rows), jnp.bfloat16),
            pltpu.VMEM((doc_count, rows, columns), jnp.bfloat16),
            pltpu.VMEM((outer, feats, width), jnp.bfloat16),
            pltpu.SemaphoreType.DMA((len(attn),)),
            pltpu.SemaphoreType.DMA((picked + doc_count - 1,)),
            pltpu.SemaphoreType.DMA((outer,)),
        ],
        2 * doc_count * feats * rows * columns,
        2 * doc_count * rows * columns + 6 * feats * columns // INNER,
        "weight_terms",
    )(at, *attn, *grads, *swapped)


def join_kernel(at_ref, mine, recv, dq_mine, dq_recv, grad_q, grad_k, grad_v):
    width = dq_mine.shape[1]
    here = pl.ds(pl.multiple_of(at_ref[0] * width, width), width)
    there = pl.ds(pl.multiple_of((1 - at_ref[0]) * width, width), width)
    for cols, terms, dquery in ((here, mine, dq_mine), (there, recv, dq_recv)):
        grad_k[:, cols] = terms[:, :width]
        grad_v[:, cols] = terms[:, width:]
        grad_q[:, cols] = dquery[...]


def join_heads(at, mine, recv, dq_mine, dq_recv):
    rows, half = dq_mine.shape
    return call(
        join_kernel,
        [bf16(rows, INNER * half)] * 3,
        [SMEM] + [VMEM] * 4,
        [VMEM] * 3,
        [],
        0,
        12 * rows * half * INNER,
        "join_heads",
    )(at, mine, recv, dq_mine, dq_recv)


def per_device(
    queries, key_heads, value_heads, grad_output, out_weight, block_pattern, global_offsets
):
    rows = queries.shape[1]
    dp_count, ctx_count, tp_count = (lax.axis_size(name) for name in ("dp", "ctx", "tp"))
    dp_at, ctx_at, tp_at = (lax.axis_index(name) for name in ("dp", "ctx", "tp"))
    outer = ctx_count // INNER
    outer_at, inner_at = ctx_at // INNER, ctx_at % INNER
    at = jnp.stack([inner_at, outer_at])

    swap = [(i, i ^ 1) for i in range(ctx_count)]

    def outer_pairs(step):
        return [(i, (i + step * INNER) % ctx_count) for i in range(ctx_count)]

    def shift_pairs(count, step):
        return [(i, (i + step) % count) for i in range(count)]

    grad_own = grad_output[0]
    grads = [grad_own] + [
        lax.ppermute(grad_own, "tp", shift_pairs(tp_count, -step)) for step in range(1, tp_count)
    ]

    kv_mine, kv_theirs, q_mine, q_theirs = part_heads(at, queries[0], key_heads[0], value_heads[0])
    kv_recv = lax.ppermute(kv_theirs, "ctx", swap)
    q_recv = lax.ppermute(q_theirs, "ctx", swap)
    kv_blocks, sources = [], []
    for step in range(outer):
        for side, held in enumerate((kv_mine, kv_recv)):
            kv_blocks.append(lax.ppermute(held, "ctx", outer_pairs(step)) if step else held)
            sources.append(((outer_at - step) % outer) * INNER + (inner_at + side) % INNER)
    sources = jnp.stack(sources)

    positions = jnp.arange(rows, dtype=jnp.int32)
    glob_flags = jnp.any(global_offsets[:, :, None] == positions[None, None, :], axis=1)
    both = jnp.stack([ctx_at, ctx_at ^ 1])
    chosen = block_pattern[both]
    seen = (jnp.abs(sources[:, None] - both[None, :]) <= 1) | jnp.any(
        sources[:, None, None] == chosen[None], axis=2
    )
    key_seen = seen[:, None, :] | glob_flags[sources][:, :, None]
    key_bias = jnp.where(key_seen, 0.0, MASKED).astype(jnp.float32).reshape(-1, 2)
    row_bias = jnp.where(glob_flags[both], 0.0, MASKED).astype(jnp.float32).reshape(1, -1)

    width = grad_own.shape[1]
    columns = [
        lax.dynamic_slice_in_dim(out_weight, ((tp_at + step) % tp_count) * width, width, 1)
        for step in range(tp_count)
    ]
    first = against(columns[0], grad_own)
    g_mine, g_theirs = grad_heads(at, first, grads[1:], columns[1:])
    g_recv = lax.ppermute(g_theirs, "ctx", swap)

    picked = tp_count // dp_count

    def dp_steps(which):
        return [(which * picked + i - tp_at) % tp_count for i in range(picked)]

    def dp_columns(which):
        pieces = []
        for step in dp_steps(which):
            piece = grads[0]
            for k in range(1, tp_count):
                piece = jnp.where(step == k, grads[k], piece)
            pieces.append(piece)
        return pieces[0] if picked == 1 else jnp.concatenate(pieces, axis=1)

    swapped = [
        lax.ppermute(dp_columns((dp_at + step) % dp_count), "dp", shift_pairs(dp_count, step))
        for step in range(1, dp_count)
    ]

    weights, inverse, attn_mine, attn_theirs = forward(
        q_mine, q_recv, key_bias, row_bias, kv_blocks
    )

    attn = []
    for step in range(dp_count):
        for held, side in ((attn_mine, 0), (attn_theirs, 1)):
            pairs = [
                (d * ctx_count + c, ((d + step) % dp_count) * ctx_count + (c ^ side))
                for d in range(dp_count)
                for c in range(ctx_count)
            ]
            attn.append(lax.ppermute(held, ("dp", "ctx"), pairs) if step or side else held)
    weight_at = jnp.stack([inner_at, outer_at] + dp_steps(dp_at))
    keep, send = weight_terms(weight_at, attn, grads, swapped, outer, picked)
    weight_sum = keep + lax.ppermute(send, "ctx", swap).astype(jnp.float32)
    grad_weight = weight_sum[0]
    for step in range(1, outer):
        grad_weight = grad_weight + lax.ppermute(
            weight_sum[step].astype(jnp.bfloat16), "ctx", outer_pairs(step)
        ).astype(jnp.float32)

    dq_mine, dq_theirs, parts = backward(
        q_mine, q_recv, g_mine, g_recv, attn_mine, attn_theirs, inverse, weights, kv_blocks
    )
    dq_recv = lax.ppermute(dq_theirs, "ctx", swap)
    summed = parts[0].astype(jnp.float32)
    for step in range(1, outer):
        summed = summed + lax.ppermute(parts[step], "ctx", outer_pairs(-step)).astype(jnp.float32)
    summed = summed.astype(jnp.bfloat16)
    terms_recv = lax.ppermute(summed[1], "ctx", swap)
    grad_q, grad_k, grad_v = join_heads(at, summed[0], terms_recv, dq_mine, dq_recv)
    return grad_q[None], grad_k[None], grad_v[None], grad_weight.astype(jnp.bfloat16)


def solution(mesh):
    in_specs = (
        P("dp", "ctx", "tp"),
        P("dp", "ctx", "tp"),
        P("dp", "ctx", "tp"),
        P("dp", "ctx", "tp"),
        P("tp", None),
        P(),
        P(),
    )
    out_specs = (
        P("dp", "ctx", "tp"),
        P("dp", "ctx", "tp"),
        P("dp", "ctx", "tp"),
        P("tp", ("dp", "ctx")),
    )
    return jax.shard_map(
        per_device, mesh=mesh, in_specs=in_specs, out_specs=out_specs, check_vma=False
    )
```

```python
import functools

import jax
import jax.numpy as jnp
from jax import lax
from jax.experimental import pallas as pl
from jax.experimental.pallas import tpu as pltpu
from jax.sharding import PartitionSpec as P

HD = 128
MASKED = -1e30
INNER = 2
ANY = pl.BlockSpec(memory_space=pl.ANY)
VMEM = pl.BlockSpec(memory_space=pltpu.VMEM)
SMEM = pl.BlockSpec(memory_space=pltpu.SMEM)


def against(left_op, right_op):
    return lax.dot_general(
        left_op, right_op, (((1,), (1,)), ((), ())), preferred_element_type=jnp.float32
    )


def product(left_op, right_op):
    return jnp.dot(left_op, right_op, preferred_element_type=jnp.float32)


def begin(source, target, semaphore):
    copy = pltpu.make_async_copy(source, target, semaphore)
    copy.start()
    return copy


def call(kernel, out_shape, in_specs, out_specs, scratch, flops, moved, name):
    return pl.pallas_call(
        kernel,
        out_shape=out_shape,
        in_specs=in_specs,
        out_specs=out_specs,
        scratch_shapes=scratch,
        compiler_params=pltpu.CompilerParams(vmem_limit_bytes=56 * 1024 * 1024),
        cost_estimate=pl.CostEstimate(flops=flops, bytes_accessed=moved, transcendentals=0),
        name=name,
    )


def bf16(*shape):
    return jax.ShapeDtypeStruct(shape, jnp.bfloat16)


def part_kernel(at_ref, q_ref, k_ref, v_ref, send_out, q_theirs, sem):
    half = q_theirs.shape[1]
    copies = []
    for place in range(send_out.shape[0]):
        side = place % INNER
        cols = slice(side * half, (side + 1) * half)
        for index, held in enumerate((k_ref, v_ref)):
            target = send_out.at[place, :, index * half : (index + 1) * half]
            copies.append(begin(held.at[:, cols], target, sem.at[2 * place + index]))
    theirs = pl.ds(pl.multiple_of((1 - at_ref[0]) * half, half), half)
    copies.append(begin(q_ref.at[:, theirs], q_theirs, sem.at[2 * send_out.shape[0]]))
    for copy in copies:
        copy.wait()


def part_heads(at, queries, keys, values, count):
    rows, feats = queries.shape
    half = feats // INNER
    return call(
        part_kernel,
        [bf16(count, rows, 2 * half), bf16(rows, half)],
        [SMEM] + [ANY] * 3,
        [ANY] * 2,
        [pltpu.SemaphoreType.DMA((2 * count + 1,))],
        0,
        8 * count * rows * half,
        "part_heads",
    )(at, queries, keys, values)


def prelude_kernel(at_ref, pattern, offsets, grad_ref, weight_ref, first, key_mask, row_mask, *rest):
    grad_s, weight_s, sem = rest
    rows, width = grad_s.shape
    block_count, glob_count = offsets.shape
    start = pl.multiple_of(at_ref[2] * width, width)
    loads = [
        begin(grad_ref, grad_s, sem.at[0]),
        begin(weight_ref.at[:, pl.ds(start, width)], weight_s, sem.at[1]),
    ]
    own = at_ref[1] * INNER + at_ref[0]
    partner = at_ref[1] * INNER + 1 - at_ref[0]
    lane = lax.broadcasted_iota(jnp.int32, (1, HD), 1)
    row_at = lax.broadcasted_iota(jnp.int32, (rows, HD), 0)
    col_at = lax.broadcasted_iota(jnp.int32, (8, rows), 1)
    group_at = lax.broadcasted_iota(jnp.int32, (8, rows), 0)
    for block in range(block_count):
        hidden = []
        for target in (own, partner):
            seen = jnp.abs(block - target) <= 1
            for r in range(pattern.shape[1]):
                seen = seen | (pattern[target, r] == block)
            hidden.append(jnp.where(seen, 0, 1))
        lane_hidden = jnp.where(lane == 0, hidden[0], jnp.where(lane == 1, hidden[1], 0))
        hidden_rows = jnp.broadcast_to(lane_hidden, (rows, HD))
        for r in range(glob_count):
            hidden_rows = jnp.where(row_at == offsets[block, r], 0, hidden_rows)
        key_mask[block * rows : (block + 1) * rows, :] = hidden_rows.astype(jnp.float32).astype(
            jnp.bfloat16
        )
    for group, target in enumerate((own, partner)):
        local = jnp.where(group_at == group, MASKED, 0.0)
        for r in range(glob_count):
            local = jnp.where(col_at == offsets[target, r], 0.0, local)
        row_mask[:, group * rows : (group + 1) * rows] = local
    for load in loads:
        load.wait()
    first[...] = against(weight_s[...], grad_s[...])


def prelude(at, pattern, offsets, grad_own, out_weight):
    rows, width = grad_own.shape
    feats = out_weight.shape[0]
    keys = offsets.shape[0] * rows
    return call(
        prelude_kernel,
        [
            jax.ShapeDtypeStruct((feats, rows), jnp.float32),
            bf16(keys, HD),
            jax.ShapeDtypeStruct((8, 2 * rows), jnp.float32),
        ],
        [SMEM] * 3 + [ANY] * 2,
        [VMEM] * 3,
        [
            pltpu.VMEM((rows, width), jnp.bfloat16),
            pltpu.VMEM((feats, width), jnp.bfloat16),
            pltpu.SemaphoreType.DMA((2,)),
        ],
        2 * feats * rows * width,
        2 * (feats + rows) * width,
        "prelude",
    )(at, pattern, offsets, grad_own, out_weight)


def forward_kernel(block_count, head_count, at_ref, q_ref, q_recv, key_mask, row_mask, kv_ref, *refs):
    e_out, inv_out, attn_mine, attn_theirs = refs[:4]
    q_s, mask_s, kv_s, e_s, s_ref, attn_s, inv_s, row_s, sem, kv_sem, e_sem, out_sem = refs[4:]
    rows = q_recv.shape[0]
    feats = head_count * HD
    score_scale = HD ** (-0.5)
    mine = pl.ds(pl.multiple_of(at_ref[0] * feats, feats), feats)
    loads = [
        begin(q_ref.at[:, mine], q_s.at[0], sem.at[0]),
        begin(q_recv, q_s.at[1], sem.at[1]),
        begin(key_mask, mask_s, sem.at[2]),
        begin(row_mask, row_s, sem.at[3]),
    ]
    kv_loads = [begin(kv_ref.at[j], kv_s.at[j], kv_sem.at[j]) for j in range(block_count)]
    for load in loads:
        load.wait()
    rows_low = row_s[...].astype(jnp.bfloat16)
    hidden = jnp.concatenate([rows_low, jnp.zeros((HD - 8, 2 * rows), jnp.bfloat16)], axis=0)
    stores = []
    for head in range(head_count):
        cols = slice(head * HD, (head + 1) * HD)
        vcols = slice(feats + head * HD, feats + (head + 1) * HD)
        q_t = jnp.concatenate(
            [jnp.transpose(q_s[0, :, cols]), jnp.transpose(q_s[1, :, cols])], axis=1
        )
        q_t = jnp.concatenate([q_t, hidden], axis=0)
        top = jnp.full((1, 2 * rows), MASKED, jnp.float32)
        for j in range(block_count):
            if head == 0:
                kv_loads[j].wait()
            keys = slice(j * rows, (j + 1) * rows)
            scores = product(jnp.concatenate([kv_s[j, :, cols], mask_s[keys, :]], axis=1), q_t)
            s_ref[keys, :] = scores
            top = jnp.maximum(top, jnp.max(scores, axis=0, keepdims=True))
        total = jnp.zeros((1, 2 * rows), jnp.float32)
        attn_t = jnp.zeros((HD, 2 * rows), jnp.float32)
        for j in range(block_count):
            keys = slice(j * rows, (j + 1) * rows)
            weights = jnp.exp((s_ref[keys, :] - top) * score_scale)
            total = total + jnp.sum(weights, axis=0, keepdims=True)
            low = weights.astype(jnp.bfloat16)
            e_s[head, keys, :] = low
            stores.append(
                begin(e_s.at[head, keys], e_out.at[head, keys], e_sem.at[head * block_count + j])
            )
            attn_t = attn_t + product(jnp.transpose(kv_s[j, :, vcols]), low)
        inverse = 1.0 / total
        inv_s[head : head + 1, :] = inverse
        attn_low = (attn_t * inverse).astype(jnp.bfloat16)
        attn_s[0, cols, :] = attn_low[:, :rows]
        attn_s[1, cols, :] = attn_low[:, rows:]
    stores.append(begin(attn_s.at[0], attn_mine, out_sem.at[0]))
    stores.append(begin(attn_s.at[1], attn_theirs, out_sem.at[1]))
    stores.append(begin(inv_s, inv_out, out_sem.at[2]))
    for store in stores:
        store.wait()


def forward(at, queries, q_recv, key_mask, row_mask, kv_all):
    block_count = kv_all.shape[0]
    rows, feats = q_recv.shape
    heads = feats // HD
    keys = block_count * rows
    return call(
        functools.partial(forward_kernel, block_count, heads),
        [
            bf16(heads, keys, 2 * rows),
            jax.ShapeDtypeStruct((max(heads, 8), 2 * rows), jnp.float32),
            bf16(feats, rows),
            bf16(feats, rows),
        ],
        [SMEM] + [ANY] * 5,
        [ANY] * 4,
        [
            pltpu.VMEM((2, rows, feats), jnp.bfloat16),
            pltpu.VMEM((keys, HD), jnp.bfloat16),
            pltpu.VMEM((block_count, rows, 2 * feats), jnp.bfloat16),
            pltpu.VMEM((heads, keys, 2 * rows), jnp.bfloat16),
            pltpu.VMEM((keys, 2 * rows), jnp.float32),
            pltpu.VMEM((2, feats, rows), jnp.bfloat16),
            pltpu.VMEM((max(heads, 8), 2 * rows), jnp.float32),
            pltpu.VMEM((8, 2 * rows), jnp.float32),
            pltpu.SemaphoreType.DMA((4,)),
            pltpu.SemaphoreType.DMA((block_count,)),
            pltpu.SemaphoreType.DMA((heads * block_count,)),
            pltpu.SemaphoreType.DMA((3,)),
        ],
        8 * rows * keys * feats,
        8 * keys * feats + 4 * heads * keys * rows,
        "forward",
    )(at, queries, q_recv, key_mask, row_mask, kv_all)


def backward_kernel(block_count, head_count, at_ref, *refs):
    q_ref, q_recv, g_mine, g_recv, attn_mine, attn_theirs, inv_ref, e_ref, kv_ref = refs[:9]
    dq_mine, dq_theirs, part_out = refs[9:12]
    q_s, t_s, inv_s, kv_s, e_s, part_s, dq_s, sem, kv_sem, e_sem, part_sem, dq_sem = refs[12:]
    rows = q_recv.shape[0]
    feats = head_count * HD
    score_scale = HD ** (-0.5)
    mine = pl.ds(pl.multiple_of(at_ref[0] * feats, feats), feats)
    loads = [begin(q_ref.at[:, mine], q_s.at[0], sem.at[0]), begin(q_recv, q_s.at[1], sem.at[1])]
    for index, held in enumerate((g_mine, g_recv, attn_mine, attn_theirs)):
        loads.append(begin(held, t_s.at[index], sem.at[2 + index]))
    loads.append(begin(inv_ref, inv_s, sem.at[6]))
    kv_loads, e_loads, stores = [], {}, []
    for j in range(block_count):
        keys = slice(j * rows, (j + 1) * rows)
        kv_loads.append(begin(kv_ref.at[j], kv_s.at[j], kv_sem.at[j]))
        for head in range(head_count):
            e_loads[head, j] = begin(
                e_ref.at[head, keys], e_s.at[head, keys], e_sem.at[head * block_count + j]
            )
    for load in loads:
        load.wait()
    for head in range(head_count):
        cols = slice(head * HD, (head + 1) * HD)
        vcols = slice(feats + head * HD, feats + (head + 1) * HD)
        inverse = inv_s[head : head + 1, :]
        g_t = jnp.concatenate([t_s[0, cols, :], t_s[1, cols, :]], axis=1).astype(jnp.float32)
        attn_t = jnp.concatenate([t_s[2, cols, :], t_s[3, cols, :]], axis=1)
        row_dot = jnp.sum(g_t * attn_t.astype(jnp.float32), axis=0, keepdims=True) * inverse
        g_t = (g_t * inverse).astype(jnp.bfloat16)
        grad = jnp.transpose(g_t)
        query = jnp.concatenate([q_s[0, :, cols], q_s[1, :, cols]], axis=0)
        dq_t = jnp.zeros((HD, 2 * rows), jnp.float32)
        for j in range(block_count):
            keys = slice(j * rows, (j + 1) * rows)
            if head == 0:
                kv_loads[j].wait()
            e_loads[head, j].wait()
            low = e_s[head, keys, :]
            dprobs = product(kv_s[j, :, vcols], g_t)
            dscore = (low.astype(jnp.float32) * (dprobs - row_dot)).astype(jnp.bfloat16)
            dq_t = dq_t + product(jnp.transpose(kv_s[j, :, cols]), dscore)
            part_s[j, :, cols] = (score_scale * product(dscore, query)).astype(jnp.bfloat16)
            part_s[j, :, vcols] = product(low, grad).astype(jnp.bfloat16)
            if head == head_count - 1:
                stores.append(begin(part_s.at[j], part_out.at[j], part_sem.at[j]))
        dquery = (score_scale * jnp.transpose(dq_t)).astype(jnp.bfloat16)
        dq_s[0, :, cols] = dquery[:rows]
        dq_s[1, :, cols] = dquery[rows:]
    stores.append(begin(dq_s.at[0], dq_mine, dq_sem.at[0]))
    stores.append(begin(dq_s.at[1], dq_theirs, dq_sem.at[1]))
    for store in stores:
        store.wait()


def backward(at, queries, q_recv, g_mine, g_recv, attn_mine, attn_theirs, inverse, weights, kv_all):
    block_count = kv_all.shape[0]
    rows, feats = q_recv.shape
    heads = feats // HD
    keys = block_count * rows
    return call(
        functools.partial(backward_kernel, block_count, heads),
        [bf16(rows, feats)] * 2 + [bf16(block_count, rows, 2 * feats)],
        [SMEM] + [ANY] * 9,
        [ANY] * 3,
        [
            pltpu.VMEM((2, rows, feats), jnp.bfloat16),
            pltpu.VMEM((4, feats, rows), jnp.bfloat16),
            pltpu.VMEM(inverse.shape, jnp.float32),
            pltpu.VMEM((block_count, rows, 2 * feats), jnp.bfloat16),
            pltpu.VMEM((heads, keys, 2 * rows), jnp.bfloat16),
            pltpu.VMEM((block_count, rows, 2 * feats), jnp.bfloat16),
            pltpu.VMEM((2, rows, feats), jnp.bfloat16),
            pltpu.SemaphoreType.DMA((7,)),
            pltpu.SemaphoreType.DMA((block_count,)),
            pltpu.SemaphoreType.DMA((heads * block_count,)),
            pltpu.SemaphoreType.DMA((block_count,)),
            pltpu.SemaphoreType.DMA((2,)),
        ],
        16 * rows * keys * feats,
        16 * keys * feats + 4 * heads * keys * rows,
        "backward",
    )(at, queries, q_recv, g_mine, g_recv, attn_mine, attn_theirs, inverse, weights, kv_all)


def grad_heads_kernel(part_count, sends, picked, at_ref, first_ref, weight_ref, *refs):
    grads, refs = refs[:part_count], refs[part_count:]
    outs, refs = refs[: 2 + sends], refs[2 + sends :]
    first_s, grad_s, weight_s, out_s, sem, send_sem, out_sem = refs
    half = out_s.shape[1]
    width = grads[0].shape[1]
    first_load = begin(first_ref, first_s, sem.at[0])
    loads = []
    for k in range(1, part_count):
        start = pl.multiple_of(at_ref[2 + k] * width, width)
        loads.append(
            (
                begin(grads[k], grad_s.at[k - 1], sem.at[2 * k - 1]),
                begin(weight_ref.at[:, pl.ds(start, width)], weight_s.at[k - 1], sem.at[2 * k]),
            )
        )
    copies = []
    for send in range(sends):
        for i in range(picked):
            place = send * picked + i
            target = outs[2 + send].at[:, i * width : (i + 1) * width]
            for k in range(part_count):

                @pl.when(at_ref[2 + part_count + place] == k)
                def _():
                    begin(grads[k], target, send_sem.at[place])

            copies.append(pltpu.make_async_copy(grads[0], target, send_sem.at[place]))
    first_load.wait()
    for k, pair in enumerate(loads):
        for load in pair:
            load.wait()
        first_s[...] = first_s[...] + against(weight_s[k], grad_s[k])
    for side, at in enumerate((at_ref[0], 1 - at_ref[0])):
        kept = first_s[pl.ds(pl.multiple_of(at * half, half), half), :]
        out_s[side] = kept.astype(jnp.bfloat16)
        copies.append(begin(out_s.at[side], outs[side], out_sem.at[side]))
    for copy in copies:
        copy.wait()


def grad_heads(at, first, out_weight, grads, sends, picked):
    feats, rows = first.shape
    half = feats // INNER
    count = len(grads)
    width = grads[0].shape[1]
    out = call(
        functools.partial(grad_heads_kernel, count, sends, picked),
        [bf16(half, rows), bf16(half, rows)] + [bf16(rows, picked * width)] * sends,
        [SMEM] + [ANY] * (2 + count),
        [ANY] * (2 + sends),
        [
            pltpu.VMEM((feats, rows), jnp.float32),
            pltpu.VMEM((count - 1, rows, width), jnp.bfloat16),
            pltpu.VMEM((count - 1, feats, width), jnp.bfloat16),
            pltpu.VMEM((INNER, half, rows), jnp.bfloat16),
            pltpu.SemaphoreType.DMA((2 * count - 1,)),
            pltpu.SemaphoreType.DMA((sends * picked,)),
            pltpu.SemaphoreType.DMA((INNER,)),
        ],
        2 * feats * rows * width * (count - 1),
        2 * (feats + rows) * width * (count - 1) + 4 * sends * rows * picked * width,
        "grad_heads",
    )(at, first, out_weight, *grads)
    return out[0], out[1], out[2:]


def weight_kernel(part_count, picked, doc_count, sent, at_ref, *refs):
    attn, refs = refs[: INNER * doc_count], refs[INNER * doc_count :]
    grads, refs = refs[:part_count], refs[part_count:]
    swapped, refs = refs[: doc_count - 1], refs[doc_count - 1 :]
    out, attn_s, grad_s, out_s, attn_sem, grad_sem, out_sem = refs
    outer, feats, width = out.shape
    half = feats // INNER
    loads = []
    for doc in range(doc_count):
        for side in range(INNER):
            at = (1 - at_ref[0]) if side else at_ref[0]
            index = doc * INNER + side
            target = attn_s.at[doc, pl.ds(pl.multiple_of(at * half, half), half)]
            loads.append(begin(attn[index], target, attn_sem.at[index]))
    piece = grads[0].shape[1]
    for i in range(picked):
        cols = slice(i * piece, (i + 1) * piece)
        for k in range(part_count):

            @pl.when(at_ref[1 + i] == k)
            def _():
                begin(grads[k], grad_s.at[0, :, cols], grad_sem.at[i])

        loads.append(pltpu.make_async_copy(grads[0], grad_s.at[0, :, cols], grad_sem.at[i]))
    for doc in range(1, doc_count):
        loads.append(begin(swapped[doc - 1], grad_s.at[doc], grad_sem.at[picked + doc - 1]))
    for load in loads:
        load.wait()
    stores = []
    at = (1 - at_ref[0]) if sent else at_ref[0]
    for k in range(outer):
        cols = pl.ds(pl.multiple_of((k * INNER + at) * width, width), width)
        term = product(attn_s[0], grad_s[0, :, cols])
        for doc in range(1, doc_count):
            term = term + product(attn_s[doc], grad_s[doc, :, cols])
        out_s[k] = term.astype(out_s.dtype)
        stores.append(begin(out_s.at[k], out.at[k], out_sem.at[k]))
    for store in stores:
        store.wait()


def weight_terms(at, attn, grads, swapped, outer, picked, sent):
    half, rows = attn[0].shape
    feats = half * INNER
    doc_count = len(attn) // INNER
    columns = picked * grads[0].shape[1]
    width = columns // (outer * INNER)
    dtype = jnp.bfloat16 if sent else jnp.float32
    return call(
        functools.partial(weight_kernel, len(grads), picked, doc_count, sent),
        jax.ShapeDtypeStruct((outer, feats, width), dtype),
        [SMEM] + [ANY] * (len(attn) + len(grads) + len(swapped)),
        ANY,
        [
            pltpu.VMEM((doc_count, feats, rows), jnp.bfloat16),
            pltpu.VMEM((doc_count, rows, columns), jnp.bfloat16),
            pltpu.VMEM((outer, feats, width), dtype),
            pltpu.SemaphoreType.DMA((len(attn),)),
            pltpu.SemaphoreType.DMA((picked + doc_count - 1,)),
            pltpu.SemaphoreType.DMA((outer,)),
        ],
        doc_count * feats * rows * columns,
        2 * doc_count * rows * columns + 4 * feats * columns // INNER,
        "weight_sent" if sent else "weight_kept",
    )(at, *attn, *grads, *swapped)


def collect_kernel(at_ref, terms, dq_mine, dq_recv, grad_q, grad_k, grad_v, terms_s, out_s, *sems):
    term_sem, q_sem, out_sem = sems
    count, rows, both = terms.shape
    half = both // 2
    loads = [begin(terms.at[c], terms_s.at[c], term_sem.at[c]) for c in range(count)]
    for side, held in enumerate((dq_mine, dq_recv)):
        at = (1 - at_ref[0]) if side else at_ref[0]
        cols = pl.ds(pl.multiple_of(at * half, half), half)
        loads.append(begin(held, grad_q.at[:, cols], q_sem.at[side]))
    for load in loads[:count]:
        load.wait()
    for side in range(INNER):
        summed = terms_s[side].astype(jnp.float32)
        for c in range(side + INNER, count, INNER):
            summed = summed + terms_s[c].astype(jnp.float32)
        summed = summed.astype(jnp.bfloat16)
        cols = slice(side * half, (side + 1) * half)
        out_s[0, :, cols] = summed[:, :half]
        out_s[1, :, cols] = summed[:, half:]
    stores = [begin(out_s.at[0], grad_k, out_sem.at[0]), begin(out_s.at[1], grad_v, out_sem.at[1])]
    for copy in loads[count:] + stores:
        copy.wait()


def collect(at, terms, dq_mine, dq_recv):
    count, rows, both = terms.shape
    feats = both // 2 * INNER
    return call(
        collect_kernel,
        [bf16(rows, feats)] * 3,
        [SMEM] + [ANY] * 3,
        [ANY] * 3,
        [
            pltpu.VMEM((count, rows, both), jnp.bfloat16),
            pltpu.VMEM((2, rows, feats), jnp.bfloat16),
            pltpu.SemaphoreType.DMA((count,)),
            pltpu.SemaphoreType.DMA((2,)),
            pltpu.SemaphoreType.DMA((2,)),
        ],
        count * rows * both,
        2 * count * rows * both + 6 * rows * feats,
        "collect",
    )(at, terms, dq_mine, dq_recv)


def per_device(
    queries, key_heads, value_heads, grad_output, out_weight, block_pattern, global_offsets
):
    dp_count, ctx_count, tp_count = (lax.axis_size(name) for name in ("dp", "ctx", "tp"))
    dp_at, ctx_at, tp_at = (lax.axis_index(name) for name in ("dp", "ctx", "tp"))
    outer = ctx_count // INNER
    outer_at, inner_at = ctx_at // INNER, ctx_at % INNER
    picked = tp_count // dp_count
    place = [inner_at, outer_at]

    swap = [(i, i ^ 1) for i in range(ctx_count)]
    columns = [[o * INNER + i for o in range(outer)] for i in range(INNER)]

    def shift_pairs(count, step):
        return [(i, (i + step) % count) for i in range(count)]

    def dp_steps(which):
        return [(which * picked + i - tp_at) % tp_count for i in range(picked)]

    kv_send, q_theirs = part_heads(
        jnp.stack(place), queries[0], key_heads[0], value_heads[0], ctx_count
    )
    kv_all = lax.all_to_all(kv_send, "ctx", split_axis=0, concat_axis=0, tiled=True)
    grad_own = grad_output[0]
    grads = [grad_own] + [
        lax.ppermute(grad_own, "tp", shift_pairs(tp_count, -step)) for step in range(1, tp_count)
    ]
    q_recv = lax.ppermute(q_theirs, "ctx", swap)

    first, key_mask, row_mask = prelude(
        jnp.stack(place + [tp_at]), block_pattern, global_offsets, grad_own, out_weight
    )
    g_at = place + [(tp_at + step) % tp_count for step in range(1, tp_count)]
    g_at = g_at[:2] + [tp_at] + g_at[2:]
    for step in range(1, dp_count):
        g_at = g_at + dp_steps((dp_at + step) % dp_count)
    g_mine, g_theirs, grad_sends = grad_heads(
        jnp.stack(g_at), first, out_weight, grads, dp_count - 1, picked
    )
    g_recv = lax.ppermute(g_theirs, "ctx", swap)
    swapped = [
        lax.ppermute(send, "dp", shift_pairs(dp_count, step + 1))
        for step, send in enumerate(grad_sends)
    ]

    at = jnp.stack(place)
    weights, inverse, attn_mine, attn_theirs = forward(
        at, queries[0], q_recv, key_mask, row_mask, kv_all
    )

    attn = []
    for step in range(dp_count):
        for held, side in ((attn_mine, 0), (attn_theirs, 1)):
            pairs = [
                (d * ctx_count + c, ((d + step) % dp_count) * ctx_count + (c ^ side))
                for d in range(dp_count)
                for c in range(ctx_count)
            ]
            attn.append(lax.ppermute(held, ("dp", "ctx"), pairs) if step or side else held)

    dq_mine, dq_theirs, parts = backward(
        at, queries[0], q_recv, g_mine, g_recv, attn_mine, attn_theirs, inverse, weights, kv_all
    )
    terms = lax.all_to_all(parts, "ctx", split_axis=0, concat_axis=0, tiled=True)
    dq_recv = lax.ppermute(dq_theirs, "ctx", swap)

    weight_at = jnp.stack([inner_at] + dp_steps(dp_at))
    send = weight_terms(weight_at, attn, grads, swapped, outer, picked, True)
    weight_recv = lax.ppermute(send, "ctx", swap)
    keep = weight_terms(weight_at, attn, grads, swapped, outer, picked, False)
    weight_sum = (keep + weight_recv.astype(jnp.float32)).astype(jnp.bfloat16)
    weight_all = lax.all_to_all(
        weight_sum, "ctx", split_axis=0, concat_axis=0, axis_index_groups=columns, tiled=True
    )
    grad_weight = jnp.sum(weight_all.astype(jnp.float32), axis=0).astype(jnp.bfloat16)

    grad_q, grad_k, grad_v = collect(at, terms, dq_mine, dq_recv)
    return grad_q[None], grad_k[None], grad_v[None], grad_weight


def solution(mesh):
    in_specs = (
        P("dp", "ctx", "tp"),
        P("dp", "ctx", "tp"),
        P("dp", "ctx", "tp"),
        P("dp", "ctx", "tp"),
        P("tp", None),
        P(),
        P(),
    )
    out_specs = (
        P("dp", "ctx", "tp"),
        P("dp", "ctx", "tp"),
        P("dp", "ctx", "tp"),
        P("tp", ("dp", "ctx")),
    )
    return jax.shard_map(
        per_device, mesh=mesh, in_specs=in_specs, out_specs=out_specs, check_vma=False
    )
```

```python
import functools

import jax
import jax.numpy as jnp
from jax import lax
from jax.experimental import pallas as pl
from jax.experimental.pallas import tpu as pltpu
from jax.sharding import PartitionSpec as P

HD = 128
MASKED = -1e30
INNER = 2
HBM = pl.BlockSpec(memory_space=pltpu.HBM)
VMEM = pl.BlockSpec(memory_space=pltpu.VMEM)
SMEM = pl.BlockSpec(memory_space=pltpu.SMEM)


def against(left_op, right_op):
    return lax.dot_general(
        left_op, right_op, (((1,), (1,)), ((), ())), preferred_element_type=jnp.float32
    )


def product(left_op, right_op):
    return jnp.dot(left_op, right_op, preferred_element_type=jnp.float32)


def begin(source, target, semaphore):
    copy = pltpu.make_async_copy(source, target, semaphore)
    copy.start()
    return copy


def call(kernel, out_shape, in_specs, out_specs, scratch, name, after=()):
    skipped = len(after)
    run = pl.pallas_call(
        lambda *refs: kernel(*refs[skipped:]),
        out_shape=out_shape,
        in_specs=[HBM] * skipped + in_specs,
        out_specs=out_specs,
        scratch_shapes=scratch,
        compiler_params=pltpu.CompilerParams(vmem_limit_bytes=32 * 1024 * 1024),
        cost_estimate=pl.CostEstimate(flops=1, bytes_accessed=1, transcendentals=0),
        name=name,
    )
    return functools.partial(run, *after)


def bf16(*shape):
    return jax.ShapeDtypeStruct(shape, jnp.bfloat16)


def part_kernel(at_ref, q_ref, k_ref, v_ref, k_send, v_send, q_theirs, held_s, in_sem, out_sem):
    half = q_theirs.shape[1]
    count = k_send.shape[0]
    loads = [begin(held, held_s.at[i], in_sem.at[i]) for i, held in enumerate((k_ref, v_ref, q_ref))]
    copies = []
    for index, send in enumerate((k_send, v_send)):
        loads[index].wait()
        for place in range(count):
            side = place % INNER
            source = held_s.at[index, :, side * half : (side + 1) * half]
            copies.append(begin(source, send.at[place], out_sem.at[index * count + place]))
    loads[2].wait()
    theirs = pl.ds(pl.multiple_of((1 - at_ref[0]) * half, half), half)
    copies.append(begin(held_s.at[2, :, theirs], q_theirs, out_sem.at[2 * count]))
    for copy in copies:
        copy.wait()


def part_heads(at, queries, keys, values, count):
    rows, feats = queries.shape
    half = feats // INNER
    return call(
        part_kernel,
        [bf16(count, rows, half), bf16(count, rows, half), bf16(rows, half)],
        [SMEM] + [HBM] * 3,
        [HBM] * 3,
        [
            pltpu.VMEM((3, rows, feats), jnp.bfloat16),
            pltpu.SemaphoreType.DMA((3,)),
            pltpu.SemaphoreType.DMA((2 * count + 1,)),
        ],
        "part_heads",
    )(at, queries, keys, values)


def prelude_kernel(at_ref, pattern, offsets, grad_ref, weight_ref, first, key_mask, row_mask, *rest):
    grad_s, weight_s, sem = rest
    rows, width = grad_s.shape
    block_count, glob_count = offsets.shape
    start = pl.multiple_of(at_ref[2] * width, width)
    loads = [
        begin(grad_ref, grad_s, sem.at[0]),
        begin(weight_ref.at[:, pl.ds(start, width)], weight_s, sem.at[1]),
    ]
    own = at_ref[1] * INNER + at_ref[0]
    partner = at_ref[1] * INNER + 1 - at_ref[0]
    lane = lax.broadcasted_iota(jnp.int32, (1, HD), 1)
    row_at = lax.broadcasted_iota(jnp.int32, (rows, HD), 0)
    col_at = lax.broadcasted_iota(jnp.int32, (8, rows), 1)
    group_at = lax.broadcasted_iota(jnp.int32, (8, rows), 0)
    for block in range(block_count):
        hidden = []
        for target in (own, partner):
            seen = jnp.abs(block - target) <= 1
            for r in range(pattern.shape[1]):
                seen = seen | (pattern[target, r] == block)
            hidden.append(jnp.where(seen, 0, 1))
        lane_hidden = jnp.where(lane == 0, hidden[0], jnp.where(lane == 1, hidden[1], 0))
        hidden_rows = jnp.broadcast_to(lane_hidden, (rows, HD))
        for r in range(glob_count):
            hidden_rows = jnp.where(row_at == offsets[block, r], 0, hidden_rows)
        key_mask[block * rows : (block + 1) * rows, :] = hidden_rows.astype(jnp.float32).astype(
            jnp.bfloat16
        )
    for group, target in enumerate((own, partner)):
        local = jnp.where(group_at == group, MASKED, 0.0)
        for r in range(glob_count):
            local = jnp.where(col_at == offsets[target, r], 0.0, local)
        row_mask[:, group * rows : (group + 1) * rows] = local
    for load in loads:
        load.wait()
    first[...] = against(weight_s[...], grad_s[...])


def prelude(at, pattern, offsets, grad_own, out_weight):
    rows, width = grad_own.shape
    feats = out_weight.shape[0]
    keys = offsets.shape[0] * rows
    return call(
        prelude_kernel,
        [
            jax.ShapeDtypeStruct((feats, rows), jnp.float32),
            bf16(keys, HD),
            jax.ShapeDtypeStruct((8, 2 * rows), jnp.float32),
        ],
        [SMEM] * 3 + [HBM] * 2,
        [VMEM] * 3,
        [
            pltpu.VMEM((rows, width), jnp.bfloat16),
            pltpu.VMEM((feats, width), jnp.bfloat16),
            pltpu.SemaphoreType.DMA((2,)),
        ],
        "prelude",
    )(at, pattern, offsets, grad_own, out_weight)


def softmax_kernel(at_ref, q_ref, q_recv, key_mask, row_mask, k_ref, e_out, inv_out, *scratch):
    q_s, k_s, s_ref, sem, k_sem = scratch
    rows, feats = q_recv.shape
    block_count = k_ref.shape[0]
    score_scale = HD ** (-0.5)
    mine = pl.ds(pl.multiple_of(at_ref[0] * feats, feats), feats)
    loads = [begin(q_ref.at[:, mine], q_s.at[0], sem.at[0]), begin(q_recv, q_s.at[1], sem.at[1])]
    k_loads = [begin(k_ref.at[j], k_s.at[j], k_sem.at[j]) for j in range(block_count)]
    for load in loads:
        load.wait()
    rows_low = row_mask[...].astype(jnp.bfloat16)
    hidden = jnp.concatenate([rows_low, jnp.zeros((HD - 8, 2 * rows), jnp.bfloat16)], axis=0)
    for head in range(feats // HD):
        cols = slice(head * HD, (head + 1) * HD)
        q_t = jnp.concatenate(
            [jnp.transpose(q_s[0, :, cols]), jnp.transpose(q_s[1, :, cols])], axis=1
        )
        q_t = jnp.concatenate([q_t, hidden], axis=0)
        top = jnp.full((1, 2 * rows), MASKED, jnp.float32)
        for j in range(block_count):
            if head == 0:
                k_loads[j].wait()
            keys = slice(j * rows, (j + 1) * rows)
            scores = product(jnp.concatenate([k_s[j, :, cols], key_mask[keys, :]], axis=1), q_t)
            s_ref[keys, :] = scores
            top = jnp.maximum(top, jnp.max(scores, axis=0, keepdims=True))
        total = jnp.zeros((1, 2 * rows), jnp.float32)
        for j in range(block_count):
            keys = slice(j * rows, (j + 1) * rows)
            weights = jnp.exp((s_ref[keys, :] - top) * score_scale)
            total = total + jnp.sum(weights, axis=0, keepdims=True)
            e_out[head, keys, :] = weights.astype(jnp.bfloat16)
        inv_out[head : head + 1, :] = 1.0 / total


def softmax(at, queries, q_recv, key_mask, row_mask, k_all):
    block_count, rows, feats = k_all.shape
    heads = feats // HD
    keys = block_count * rows
    return call(
        softmax_kernel,
        [
            bf16(heads, keys, 2 * rows),
            jax.ShapeDtypeStruct((max(heads, 8), 2 * rows), jnp.float32),
        ],
        [SMEM, HBM, HBM, VMEM, VMEM, HBM],
        [VMEM] * 2,
        [
            pltpu.VMEM((2, rows, feats), jnp.bfloat16),
            pltpu.VMEM((block_count, rows, feats), jnp.bfloat16),
            pltpu.VMEM((keys, 2 * rows), jnp.float32),
            pltpu.SemaphoreType.DMA((2,)),
            pltpu.SemaphoreType.DMA((block_count,)),
        ],
        "softmax",
    )(at, queries, q_recv, key_mask, row_mask, k_all)


def attend_kernel(e_ref, inv_ref, v_ref, attn_mine, attn_theirs, v_s, attn_s, v_sem, out_sem):
    block_count, rows, feats = v_ref.shape
    loads = [begin(v_ref.at[j], v_s.at[j], v_sem.at[j]) for j in range(block_count)]
    for head in range(feats // HD):
        cols = slice(head * HD, (head + 1) * HD)
        attn_t = jnp.zeros((HD, 2 * rows), jnp.float32)
        for j in range(block_count):
            keys = slice(j * rows, (j + 1) * rows)
            if head == 0:
                loads[j].wait()
            attn_t = attn_t + product(jnp.transpose(v_s[j, :, cols]), e_ref[head, keys, :])
        attn_low = (attn_t * inv_ref[head : head + 1, :]).astype(jnp.bfloat16)
        attn_s[0, cols, :] = attn_low[:, :rows]
        attn_s[1, cols, :] = attn_low[:, rows:]
    stores = [
        begin(attn_s.at[0], attn_mine, out_sem.at[0]),
        begin(attn_s.at[1], attn_theirs, out_sem.at[1]),
    ]
    for store in stores:
        store.wait()


def attend(e_all, inverse, v_all, after):
    block_count, rows, feats = v_all.shape
    return call(
        attend_kernel,
        [bf16(feats, rows)] * 2,
        [VMEM, VMEM, HBM],
        [HBM] * 2,
        [
            pltpu.VMEM((block_count, rows, feats), jnp.bfloat16),
            pltpu.VMEM((2, feats, rows), jnp.bfloat16),
            pltpu.SemaphoreType.DMA((block_count,)),
            pltpu.SemaphoreType.DMA((2,)),
        ],
        "attend",
        after,
    )(e_all, inverse, v_all)


def value_terms_kernel(g_mine, g_recv, inv_ref, e_ref, part_out, g_s, part_s, sem, part_sem):
    block_count, rows, feats = part_out.shape
    loads = [begin(g_mine, g_s.at[0], sem.at[0]), begin(g_recv, g_s.at[1], sem.at[1])]
    for load in loads:
        load.wait()
    stores = []
    for head in range(feats // HD):
        cols = slice(head * HD, (head + 1) * HD)
        g_t = jnp.concatenate([g_s[0, cols, :], g_s[1, cols, :]], axis=1).astype(jnp.float32)
        grad = jnp.transpose((g_t * inv_ref[head : head + 1, :]).astype(jnp.bfloat16))
        for j in range(block_count):
            keys = slice(j * rows, (j + 1) * rows)
            part_s[j, :, cols] = product(e_ref[head, keys, :], grad).astype(jnp.bfloat16)
            if (head + 1) * HD == feats:
                stores.append(begin(part_s.at[j], part_out.at[j], part_sem.at[j]))
    for store in stores:
        store.wait()


def value_terms(g_mine, g_recv, inverse, e_all, block_count, after):
    feats, rows = g_mine.shape
    return call(
        value_terms_kernel,
        bf16(block_count, rows, feats),
        [HBM, HBM, VMEM, VMEM],
        HBM,
        [
            pltpu.VMEM((2, feats, rows), jnp.bfloat16),
            pltpu.VMEM((block_count, rows, feats), jnp.bfloat16),
            pltpu.SemaphoreType.DMA((2,)),
            pltpu.SemaphoreType.DMA((block_count,)),
        ],
        "value_terms",
        after,
    )(g_mine, g_recv, inverse, e_all)


def key_terms_kernel(at_ref, q_ref, q_recv, g_mine, g_recv, attn_mine, attn_theirs, *refs):
    inv_ref, e_ref, k_ref, v_ref, dq_mine, dq_theirs, part_out = refs[:7]
    q_s, t_s, kv_s, part_s, dq_s, sem, kv_sem, part_sem, dq_sem = refs[7:]
    block_count, rows, feats = part_out.shape
    score_scale = HD ** (-0.5)
    mine = pl.ds(pl.multiple_of(at_ref[0] * feats, feats), feats)
    loads = [begin(q_ref.at[:, mine], q_s.at[0], sem.at[0]), begin(q_recv, q_s.at[1], sem.at[1])]
    for index, held in enumerate((g_mine, g_recv, attn_mine, attn_theirs)):
        loads.append(begin(held, t_s.at[index], sem.at[2 + index]))
    kv_loads, stores = [], []
    for j in range(block_count):
        for index, held in enumerate((v_ref, k_ref)):
            kv_loads.append(begin(held.at[j], kv_s.at[index, j], kv_sem.at[2 * j + index]))
    for load in loads:
        load.wait()
    for head in range(feats // HD):
        cols = slice(head * HD, (head + 1) * HD)
        inverse = inv_ref[head : head + 1, :]
        g_t = jnp.concatenate([t_s[0, cols, :], t_s[1, cols, :]], axis=1).astype(jnp.float32)
        attn_t = jnp.concatenate([t_s[2, cols, :], t_s[3, cols, :]], axis=1)
        row_dot = jnp.sum(g_t * attn_t.astype(jnp.float32), axis=0, keepdims=True) * inverse
        g_t = (g_t * inverse).astype(jnp.bfloat16)
        query = jnp.concatenate([q_s[0, :, cols], q_s[1, :, cols]], axis=0)
        dq_t = jnp.zeros((HD, 2 * rows), jnp.float32)
        for j in range(block_count):
            keys = slice(j * rows, (j + 1) * rows)
            if head == 0:
                kv_loads[2 * j].wait()
                kv_loads[2 * j + 1].wait()
            low = e_ref[head, keys, :].astype(jnp.float32)
            dprobs = product(kv_s[0, j, :, cols], g_t)
            dscore = (low * (dprobs - row_dot)).astype(jnp.bfloat16)
            dq_t = dq_t + product(jnp.transpose(kv_s[1, j, :, cols]), dscore)
            part_s[j, :, cols] = (score_scale * product(dscore, query)).astype(jnp.bfloat16)
            if (head + 1) * HD == feats:
                stores.append(begin(part_s.at[j], part_out.at[j], part_sem.at[j]))
        dquery = (score_scale * jnp.transpose(dq_t)).astype(jnp.bfloat16)
        dq_s[0, :, cols] = dquery[:rows]
        dq_s[1, :, cols] = dquery[rows:]
    stores.append(begin(dq_s.at[0], dq_mine, dq_sem.at[0]))
    stores.append(begin(dq_s.at[1], dq_theirs, dq_sem.at[1]))
    for store in stores:
        store.wait()


def key_terms(at, queries, q_recv, g_mine, g_recv, attn_mine, attn_theirs, inverse, e_all, k_all, v_all, after):
    block_count, rows, feats = v_all.shape
    return call(
        key_terms_kernel,
        [bf16(rows, feats)] * 2 + [bf16(block_count, rows, feats)],
        [SMEM] + [HBM] * 6 + [VMEM] * 2 + [HBM] * 2,
        [HBM] * 3,
        [
            pltpu.VMEM((2, rows, feats), jnp.bfloat16),
            pltpu.VMEM((4, feats, rows), jnp.bfloat16),
            pltpu.VMEM((2, block_count, rows, feats), jnp.bfloat16),
            pltpu.VMEM((block_count, rows, feats), jnp.bfloat16),
            pltpu.VMEM((2, rows, feats), jnp.bfloat16),
            pltpu.SemaphoreType.DMA((6,)),
            pltpu.SemaphoreType.DMA((2 * block_count,)),
            pltpu.SemaphoreType.DMA((block_count,)),
            pltpu.SemaphoreType.DMA((2,)),
        ],
        "key_terms",
        after,
    )(at, queries, q_recv, g_mine, g_recv, attn_mine, attn_theirs, inverse, e_all, k_all, v_all)


def grad_heads_kernel(part_count, sends, picked, at_ref, first_ref, weight_ref, *refs):
    grads, refs = refs[:part_count], refs[part_count:]
    outs, refs = refs[: 2 + sends], refs[2 + sends :]
    first_s, grad_s, weight_s, out_s, sem, send_sem, out_sem = refs
    half = out_s.shape[1]
    width = grads[0].shape[1]
    loads = []
    for k in range(1, part_count):
        start = pl.multiple_of(at_ref[2 + k] * width, width)
        columns = weight_ref.at[:, pl.ds(start, width)]
        loads.append(begin(columns, weight_s.at[k - 1], sem.at[2 * k]))
    grad_loads = [begin(grads[k], grad_s.at[k], sem.at[2 * k - 1 if k else 0]) for k in range(part_count)]
    for load in grad_loads:
        load.wait()
    copies = []
    for send in range(sends):
        for i in range(picked):
            place = send * picked + i
            target = outs[2 + send].at[:, i * width : (i + 1) * width]
            for k in range(part_count):

                @pl.when(at_ref[2 + part_count + place] == k)
                def _():
                    begin(grad_s.at[k], target, send_sem.at[place])

            copies.append(pltpu.make_async_copy(grad_s.at[0], target, send_sem.at[place]))
    summed = first_ref[...]
    for k in range(1, part_count):
        loads[k - 1].wait()
        summed = summed + against(weight_s[k - 1], grad_s[k])
    first_s[...] = summed
    for side, at in enumerate((at_ref[0], 1 - at_ref[0])):
        kept = first_s[pl.ds(pl.multiple_of(at * half, half), half), :]
        out_s[side] = kept.astype(jnp.bfloat16)
        copies.append(begin(out_s.at[side], outs[side], out_sem.at[side]))
    for copy in copies:
        copy.wait()


def grad_heads(at, first, out_weight, grads, sends, picked, after):
    feats, rows = first.shape
    half = feats // INNER
    count = len(grads)
    width = grads[0].shape[1]
    out = call(
        functools.partial(grad_heads_kernel, count, sends, picked),
        [bf16(half, rows), bf16(half, rows)] + [bf16(rows, picked * width)] * sends,
        [SMEM, VMEM] + [HBM] * (1 + count),
        [HBM] * (2 + sends),
        [
            pltpu.VMEM((feats, rows), jnp.float32),
            pltpu.VMEM((count, rows, width), jnp.bfloat16),
            pltpu.VMEM((count - 1, feats, width), jnp.bfloat16),
            pltpu.VMEM((INNER, half, rows), jnp.bfloat16),
            pltpu.SemaphoreType.DMA((2 * count - 1,)),
            pltpu.SemaphoreType.DMA((sends * picked,)),
            pltpu.SemaphoreType.DMA((INNER,)),
        ],
        "grad_heads",
        after,
    )(at, first, out_weight, *grads)
    return out[0], out[1], out[2:]


def weight_kernel(part_count, picked, doc_count, sent, at_ref, *refs):
    attn, refs = refs[: INNER * doc_count], refs[INNER * doc_count :]
    grads, refs = refs[:part_count], refs[part_count:]
    swapped, refs = refs[: doc_count - 1], refs[doc_count - 1 :]
    out, attn_s, grad_s, out_s, attn_sem, grad_sem, out_sem = refs
    outer, feats, width = out.shape
    half = feats // INNER
    loads = []
    for doc in range(doc_count):
        for side in range(INNER):
            at = (1 - at_ref[0]) if side else at_ref[0]
            index = doc * INNER + side
            target = attn_s.at[doc, pl.ds(pl.multiple_of(at * half, half), half)]
            loads.append(begin(attn[index], target, attn_sem.at[index]))
    piece = grads[0].shape[1]
    for i in range(picked):
        cols = slice(i * piece, (i + 1) * piece)
        for k in range(part_count):

            @pl.when(at_ref[1 + i] == k)
            def _():
                begin(grads[k], grad_s.at[0, :, cols], grad_sem.at[i])

        loads.append(pltpu.make_async_copy(grads[0], grad_s.at[0, :, cols], grad_sem.at[i]))
    for doc in range(1, doc_count):
        loads.append(begin(swapped[doc - 1], grad_s.at[doc], grad_sem.at[picked + doc - 1]))
    for load in loads:
        load.wait()
    stores = []
    at = (1 - at_ref[0]) if sent else at_ref[0]
    for k in range(outer):
        cols = pl.ds(pl.multiple_of((k * INNER + at) * width, width), width)
        term = product(attn_s[0], grad_s[0, :, cols])
        for doc in range(1, doc_count):
            term = term + product(attn_s[doc], grad_s[doc, :, cols])
        out_s[k] = term.astype(out_s.dtype)
        stores.append(begin(out_s.at[k], out.at[k], out_sem.at[k]))
    for store in stores:
        store.wait()


def weight_terms(at, attn, grads, swapped, outer, picked, sent, after=()):
    half, rows = attn[0].shape
    feats = half * INNER
    doc_count = len(attn) // INNER
    columns = picked * grads[0].shape[1]
    width = columns // (outer * INNER)
    dtype = jnp.bfloat16
    return call(
        functools.partial(weight_kernel, len(grads), picked, doc_count, sent),
        jax.ShapeDtypeStruct((outer, feats, width), dtype),
        [SMEM] + [HBM] * (len(attn) + len(grads) + len(swapped)),
        HBM,
        [
            pltpu.VMEM((doc_count, feats, rows), jnp.bfloat16),
            pltpu.VMEM((doc_count, rows, columns), jnp.bfloat16),
            pltpu.VMEM((outer, feats, width), dtype),
            pltpu.SemaphoreType.DMA((len(attn),)),
            pltpu.SemaphoreType.DMA((picked + doc_count - 1,)),
            pltpu.SemaphoreType.DMA((outer,)),
        ],
        "weight_sent" if sent else "weight_kept",
        after,
    )(at, *attn, *grads, *swapped)


def collect_kernel(terms, out, terms_s, out_s, sem, out_sem):
    count, rows, half = terms.shape
    loads = [begin(terms.at[c], terms_s.at[c], sem.at[c]) for c in range(count)]
    for load in loads:
        load.wait()
    for side in range(INNER):
        summed = terms_s[side].astype(jnp.float32)
        for c in range(side + INNER, count, INNER):
            summed = summed + terms_s[c].astype(jnp.float32)
        out_s[:, side * half : (side + 1) * half] = summed.astype(jnp.bfloat16)
    begin(out_s, out, out_sem).wait()


def collect(terms, name, after=()):
    count, rows, half = terms.shape
    return call(
        collect_kernel,
        bf16(rows, INNER * half),
        [HBM],
        HBM,
        [
            pltpu.VMEM((count, rows, half), jnp.bfloat16),
            pltpu.VMEM((rows, INNER * half), jnp.bfloat16),
            pltpu.SemaphoreType.DMA((count,)),
            pltpu.SemaphoreType.DMA,
        ],
        name,
        after,
    )(terms)


def join_kernel(at_ref, mine, recv, out, held_s, out_s, sem, out_sem):
    half = mine.shape[1]
    loads = [begin(held, held_s.at[i], sem.at[i]) for i, held in enumerate((mine, recv))]
    for side, at in enumerate((at_ref[0], 1 - at_ref[0])):
        loads[side].wait()
        out_s[:, pl.ds(pl.multiple_of(at * half, half), half)] = held_s[side]
    begin(out_s, out, out_sem).wait()


def join_heads(at, mine, recv):
    rows, half = mine.shape
    return call(
        join_kernel,
        bf16(rows, INNER * half),
        [SMEM, HBM, HBM],
        HBM,
        [
            pltpu.VMEM((2, rows, half), jnp.bfloat16),
            pltpu.VMEM((rows, INNER * half), jnp.bfloat16),
            pltpu.SemaphoreType.DMA((2,)),
            pltpu.SemaphoreType.DMA,
        ],
        "join_heads",
    )(at, mine, recv)


def per_device(
    queries, key_heads, value_heads, grad_output, out_weight, block_pattern, global_offsets
):
    dp_count, ctx_count, tp_count = (lax.axis_size(name) for name in ("dp", "ctx", "tp"))
    dp_at, ctx_at, tp_at = (lax.axis_index(name) for name in ("dp", "ctx", "tp"))
    outer = ctx_count // INNER
    outer_at, inner_at = ctx_at // INNER, ctx_at % INNER
    picked = tp_count // dp_count
    place = [inner_at, outer_at]

    swap = [(i, i ^ 1) for i in range(ctx_count)]
    columns = [[o * INNER + i for o in range(outer)] for i in range(INNER)]

    def shift_pairs(count, step):
        return [(i, (i + step) % count) for i in range(count)]

    def dp_steps(which):
        return [(which * picked + i - tp_at) % tp_count for i in range(picked)]

    def exchange(values, groups=None):
        return lax.all_to_all(
            values, "ctx", split_axis=0, concat_axis=0, axis_index_groups=groups, tiled=True
        )

    at = jnp.stack(place)
    grad_own = grad_output[0]
    grads = [grad_own] + [
        lax.ppermute(grad_own, "tp", shift_pairs(tp_count, -step)) for step in range(1, tp_count)
    ]
    k_send, v_send, q_theirs = part_heads(at, queries[0], key_heads[0], value_heads[0], ctx_count)
    k_all = exchange(k_send)
    q_recv = lax.ppermute(q_theirs, "ctx", swap)
    first, key_mask, row_mask = prelude(
        jnp.stack(place + [tp_at]), block_pattern, global_offsets, grad_own, out_weight
    )
    v_send, first = lax.optimization_barrier((v_send, first))
    v_all = exchange(v_send)

    e_all, inverse = softmax(at, queries[0], q_recv, key_mask, row_mask, k_all)

    g_at = place + [(tp_at + step) % tp_count for step in range(tp_count)]
    for step in range(1, dp_count):
        g_at = g_at + dp_steps((dp_at + step) % dp_count)
    g_mine, g_theirs, grad_sends = grad_heads(
        jnp.stack(g_at), first, out_weight, grads, dp_count - 1, picked, (inverse,)
    )
    g_recv = lax.ppermute(g_theirs, "ctx", swap)
    swapped = [
        lax.ppermute(send, "dp", shift_pairs(dp_count, step + 1))
        for step, send in enumerate(grad_sends)
    ]

    attn_mine, attn_theirs = attend(e_all, inverse, v_all, (g_theirs,))
    attn = []
    for step in range(dp_count):
        for held, side in ((attn_mine, 0), (attn_theirs, 1)):
            pairs = [
                (d * ctx_count + c, ((d + step) % dp_count) * ctx_count + (c ^ side))
                for d in range(dp_count)
                for c in range(ctx_count)
            ]
            attn.append(lax.ppermute(held, ("dp", "ctx"), pairs) if step or side else held)

    value_parts = value_terms(g_mine, g_recv, inverse, e_all, ctx_count, (attn_mine,))
    weight_at = jnp.stack([inner_at] + dp_steps(dp_at))
    send = weight_terms(weight_at, attn, grads, swapped, outer, picked, True, (value_parts,))
    weight_recv = lax.ppermute(send, "ctx", swap)
    terms_v = exchange(value_parts)

    dq_mine, dq_theirs, key_parts = key_terms(
        at, queries[0], q_recv, g_mine, g_recv, attn_mine, attn_theirs, inverse, e_all, k_all, v_all, (send,)
    )
    terms_k = exchange(key_parts)
    dq_recv = lax.ppermute(dq_theirs, "ctx", swap)

    keep = weight_terms(weight_at, attn, grads, swapped, outer, picked, False, (key_parts,))
    weight_sum = keep + weight_recv
    weight_all = exchange(weight_sum, columns)
    grad_weight = jnp.sum(weight_all.astype(jnp.float32), axis=0).astype(jnp.bfloat16)

    grad_q = join_heads(at, dq_mine, dq_recv)
    grad_v = collect(terms_v, "collect_values")
    grad_k = collect(terms_k, "collect_keys")
    return grad_q[None], grad_k[None], grad_v[None], grad_weight


def solution(mesh):
    in_specs = (
        P("dp", "ctx", "tp"),
        P("dp", "ctx", "tp"),
        P("dp", "ctx", "tp"),
        P("dp", "ctx", "tp"),
        P("tp", None),
        P(),
        P(),
    )
    out_specs = (
        P("dp", "ctx", "tp"),
        P("dp", "ctx", "tp"),
        P("dp", "ctx", "tp"),
        P("tp", ("dp", "ctx")),
    )
    return jax.shard_map(
        per_device, mesh=mesh, in_specs=in_specs, out_specs=out_specs, check_vma=False
    )
```

```python
import functools

import jax
import jax.numpy as jnp
from jax import lax
from jax.experimental import pallas as pl
from jax.experimental.pallas import tpu as pltpu
from jax.sharding import PartitionSpec as P

HD = 128
MASKED = -1e30
INNER = 2
SOURCES = 3
ANY = pl.BlockSpec(memory_space=pl.ANY)
VMEM = pl.BlockSpec(memory_space=pltpu.VMEM)
SMEM = pl.BlockSpec(memory_space=pltpu.SMEM)


def against(left_op, right_op):
    return lax.dot_general(
        left_op, right_op, (((1,), (1,)), ((), ())), preferred_element_type=jnp.float32
    )


def product(left_op, right_op):
    return jnp.dot(left_op, right_op, preferred_element_type=jnp.float32)


def begin(source, target, semaphore):
    copy = pltpu.make_async_copy(source, target, semaphore)
    copy.start()
    return copy


def call(kernel, out_shape, in_specs, out_specs, scratch, micros, name, after=()):
    skipped = len(after)
    in_specs = [ANY] * skipped + in_specs
    run = pl.pallas_call(
        lambda *refs: kernel(*refs[skipped:]),
        out_shape=out_shape,
        in_specs=in_specs,
        out_specs=out_specs,
        scratch_shapes=scratch,
        compiler_params=pltpu.CompilerParams(vmem_limit_bytes=60 * 1024 * 1024),
        cost_estimate=pl.CostEstimate(
            flops=int(micros * 1e9), bytes_accessed=int(micros * 3e6), transcendentals=0
        ),
        name=name,
    )

    def placed(*args):
        args = [
            pltpu.with_memory_space_constraint(arg, pltpu.HBM) if spec is ANY else arg
            for spec, arg in zip(in_specs, (*after, *args))
        ]
        return run(*args)

    return placed


def bf16(*shape):
    return pltpu.HBM(shape, jnp.bfloat16)


def f32(*shape):
    return pltpu.HBM(shape, jnp.float32)


def part_kernel(at_ref, q_ref, k_ref, v_ref, kv_mine, kv_theirs, q_theirs, held_s, in_sem, out_sem):
    half = q_theirs.shape[1]
    loads = [begin(held, held_s.at[i], in_sem.at[i]) for i, held in enumerate((k_ref, v_ref, q_ref))]
    mine = pl.ds(pl.multiple_of(at_ref[0] * half, half), half)
    theirs = pl.ds(pl.multiple_of((1 - at_ref[0]) * half, half), half)
    copies = []
    for index in range(2):
        loads[index].wait()
        place = slice(index * half, (index + 1) * half)
        for side, (cols, out) in enumerate(((mine, kv_mine), (theirs, kv_theirs))):
            sem = out_sem.at[2 * index + side]
            copies.append(begin(held_s.at[index, :, cols], out.at[:, place], sem))
    loads[2].wait()
    copies.append(begin(held_s.at[2, :, theirs], q_theirs, out_sem.at[4]))
    for copy in copies:
        copy.wait()


def part_heads(at, queries, keys, values):
    rows, feats = queries.shape
    half = feats // INNER
    return call(
        part_kernel,
        [bf16(rows, 2 * half), bf16(rows, 2 * half), bf16(rows, half)],
        [SMEM] + [ANY] * 3,
        [ANY] * 3,
        [
            pltpu.VMEM((3, rows, feats), jnp.bfloat16),
            pltpu.SemaphoreType.DMA((3,)),
            pltpu.SemaphoreType.DMA((5,)),
        ],
        2,
        "part_heads",
    )(at, queries, keys, values)


def prelude_kernel(at_ref, pattern, offsets, grad_ref, weight_ref, first, key_mask, row_mask, *rest):
    grad_s, weight_s, first_s, mask_s, row_s, sem, out_sem = rest
    rows, width = grad_s.shape
    block_count, glob_count = offsets.shape
    start = pl.multiple_of(at_ref[2] * width, width)
    loads = [
        begin(grad_ref, grad_s, sem.at[0]),
        begin(weight_ref.at[:, pl.ds(start, width)], weight_s, sem.at[1]),
    ]
    own = at_ref[1] * INNER + at_ref[0]
    partner = at_ref[1] * INNER + 1 - at_ref[0]
    lane = lax.broadcasted_iota(jnp.int32, (1, HD), 1)
    row_at = lax.broadcasted_iota(jnp.int32, (rows, HD), 0)
    col_at = lax.broadcasted_iota(jnp.int32, (8, rows), 1)
    group_at = lax.broadcasted_iota(jnp.int32, (8, rows), 0)
    for index in range(block_count):
        block = at_ref[SOURCES + index]
        hidden = []
        for target in (own, partner):
            seen = jnp.abs(block - target) <= 1
            for r in range(pattern.shape[1]):
                seen = seen | (pattern[target, r] == block)
            hidden.append(jnp.where(seen, 0, 1))
        lane_hidden = jnp.where(lane == 0, hidden[0], jnp.where(lane == 1, hidden[1], 0))
        hidden_rows = jnp.broadcast_to(lane_hidden, (rows, HD))
        for r in range(glob_count):
            hidden_rows = jnp.where(row_at == offsets[block, r], 0, hidden_rows)
        mask_s[index * rows : (index + 1) * rows, :] = hidden_rows.astype(jnp.float32).astype(
            jnp.bfloat16
        )
    for group, target in enumerate((own, partner)):
        local = jnp.where(group_at == group, MASKED, 0.0)
        for r in range(glob_count):
            local = jnp.where(col_at == offsets[target, r], 0.0, local)
        row_s[:, group * rows : (group + 1) * rows] = local
    stores = [begin(mask_s, key_mask, out_sem.at[0]), begin(row_s, row_mask, out_sem.at[1])]
    for load in loads:
        load.wait()
    first_s[...] = against(weight_s[...], grad_s[...])
    stores.append(begin(first_s, first, out_sem.at[2]))
    for store in stores:
        store.wait()


def prelude(at, pattern, offsets, grad_own, out_weight):
    rows, width = grad_own.shape
    feats = out_weight.shape[0]
    keys = offsets.shape[0] * rows
    return call(
        prelude_kernel,
        [
            f32(*(feats, rows)),
            bf16(keys, HD),
            f32(*(8, 2 * rows)),
        ],
        [SMEM] * 3 + [ANY] * 2,
        [ANY] * 3,
        [
            pltpu.VMEM((rows, width), jnp.bfloat16),
            pltpu.VMEM((feats, width), jnp.bfloat16),
            pltpu.VMEM((feats, rows), jnp.float32),
            pltpu.VMEM((keys, HD), jnp.bfloat16),
            pltpu.VMEM((8, 2 * rows), jnp.float32),
            pltpu.SemaphoreType.DMA((2,)),
            pltpu.SemaphoreType.DMA((3,)),
        ],
        3,
        "prelude",
    )(at, pattern, offsets, grad_own, out_weight)


def forward_kernel(block_count, head_count, at_ref, q_ref, q_recv, key_mask, row_mask, *refs):
    kv_refs, refs = refs[:block_count], refs[block_count:]
    e_out, inv_out, attn_mine, attn_theirs = refs[:4]
    q_s, mask_s, kv_s, e_s, s_ref, attn_s, inv_s, row_s, sem, kv_sem, e_sem, out_sem = refs[4:]
    rows = q_recv.shape[0]
    feats = head_count * HD
    score_scale = HD ** (-0.5)
    mine = pl.ds(pl.multiple_of(at_ref[0] * feats, feats), feats)
    loads = [
        begin(q_ref.at[:, mine], q_s.at[0], sem.at[0]),
        begin(q_recv, q_s.at[1], sem.at[1]),
        begin(key_mask, mask_s, sem.at[2]),
        begin(row_mask, row_s, sem.at[3]),
    ]
    kv_loads = [begin(kv_refs[j], kv_s.at[j], kv_sem.at[j]) for j in range(block_count)]
    for load in loads:
        load.wait()
    rows_low = row_s[...].astype(jnp.bfloat16)
    hidden = jnp.concatenate([rows_low, jnp.zeros((HD - 8, 2 * rows), jnp.bfloat16)], axis=0)
    stores = []
    for head in range(head_count):
        cols = slice(head * HD, (head + 1) * HD)
        vcols = slice(feats + head * HD, feats + (head + 1) * HD)
        q_t = jnp.concatenate(
            [jnp.transpose(q_s[0, :, cols]), jnp.transpose(q_s[1, :, cols])], axis=1
        )
        q_t = jnp.concatenate([q_t, hidden], axis=0)
        top = jnp.full((1, 2 * rows), MASKED, jnp.float32)
        for j in range(block_count):
            if head == 0:
                kv_loads[j].wait()
            keys = slice(j * rows, (j + 1) * rows)
            scores = product(jnp.concatenate([kv_s[j, :, cols], mask_s[keys, :]], axis=1), q_t)
            s_ref[keys, :] = scores
            top = jnp.maximum(top, jnp.max(scores, axis=0, keepdims=True))
        total = jnp.zeros((1, 2 * rows), jnp.float32)
        attn_t = jnp.zeros((HD, 2 * rows), jnp.float32)
        for j in range(block_count):
            keys = slice(j * rows, (j + 1) * rows)
            weights = jnp.exp((s_ref[keys, :] - top) * score_scale)
            total = total + jnp.sum(weights, axis=0, keepdims=True)
            low = weights.astype(jnp.bfloat16)
            e_s[head, keys, :] = low
            stores.append(
                begin(e_s.at[head, keys], e_out.at[head, keys], e_sem.at[head * block_count + j])
            )
            attn_t = attn_t + product(jnp.transpose(kv_s[j, :, vcols]), low)
        inverse = 1.0 / total
        inv_s[head : head + 1, :] = inverse
        attn_low = (attn_t * inverse).astype(jnp.bfloat16)
        attn_s[0, cols, :] = attn_low[:, :rows]
        attn_s[1, cols, :] = attn_low[:, rows:]
    stores.append(begin(attn_s.at[0], attn_mine, out_sem.at[0]))
    stores.append(begin(attn_s.at[1], attn_theirs, out_sem.at[1]))
    stores.append(begin(inv_s, inv_out, out_sem.at[2]))
    for store in stores:
        store.wait()


def forward(at, queries, q_recv, key_mask, row_mask, kv_blocks, after):
    block_count = len(kv_blocks)
    rows, feats = q_recv.shape
    heads = feats // HD
    keys = block_count * rows
    return call(
        functools.partial(forward_kernel, block_count, heads),
        [
            bf16(heads, keys, 2 * rows),
            f32(*(max(heads, 8), 2 * rows)),
            bf16(feats, rows),
            bf16(feats, rows),
        ],
        [SMEM] + [ANY] * (4 + block_count),
        [ANY] * 4,
        [
            pltpu.VMEM((2, rows, feats), jnp.bfloat16),
            pltpu.VMEM((keys, HD), jnp.bfloat16),
            pltpu.VMEM((block_count, rows, 2 * feats), jnp.bfloat16),
            pltpu.VMEM((heads, keys, 2 * rows), jnp.bfloat16),
            pltpu.VMEM((keys, 2 * rows), jnp.float32),
            pltpu.VMEM((2, feats, rows), jnp.bfloat16),
            pltpu.VMEM((max(heads, 8), 2 * rows), jnp.float32),
            pltpu.VMEM((8, 2 * rows), jnp.float32),
            pltpu.SemaphoreType.DMA((4,)),
            pltpu.SemaphoreType.DMA((block_count,)),
            pltpu.SemaphoreType.DMA((heads * block_count,)),
            pltpu.SemaphoreType.DMA((3,)),
        ],
        6,
        "forward",
        after,
    )(at, queries, q_recv, key_mask, row_mask, *kv_blocks)


def backward_kernel(block_count, head_count, at_ref, *refs):
    q_ref, q_recv, g_mine, g_recv, attn_mine, attn_theirs, inv_ref, e_ref = refs[:8]
    kv_refs, refs = refs[8 : 8 + block_count], refs[8 + block_count :]
    dq_mine, dq_theirs = refs[:2]
    part_outs, refs = refs[2 : 2 + block_count], refs[2 + block_count :]
    q_s, t_s, inv_s, kv_s, e_s, part_s, dq_s, sem, kv_sem, e_sem, part_sem, dq_sem = refs
    rows = q_recv.shape[0]
    feats = head_count * HD
    score_scale = HD ** (-0.5)
    mine = pl.ds(pl.multiple_of(at_ref[0] * feats, feats), feats)
    loads = [begin(q_ref.at[:, mine], q_s.at[0], sem.at[0]), begin(q_recv, q_s.at[1], sem.at[1])]
    for index, held in enumerate((g_mine, g_recv, attn_mine, attn_theirs)):
        loads.append(begin(held, t_s.at[index], sem.at[2 + index]))
    loads.append(begin(inv_ref, inv_s, sem.at[6]))
    kv_loads, e_loads, stores = [], {}, []
    for j in range(block_count):
        keys = slice(j * rows, (j + 1) * rows)
        kv_loads.append(begin(kv_refs[j], kv_s.at[j], kv_sem.at[j]))
        for head in range(head_count):
            e_loads[head, j] = begin(
                e_ref.at[head, keys], e_s.at[head, keys], e_sem.at[head * block_count + j]
            )
    for load in loads:
        load.wait()
    for head in range(head_count):
        cols = slice(head * HD, (head + 1) * HD)
        vcols = slice(feats + head * HD, feats + (head + 1) * HD)
        inverse = inv_s[head : head + 1, :]
        g_t = jnp.concatenate([t_s[0, cols, :], t_s[1, cols, :]], axis=1).astype(jnp.float32)
        attn_t = jnp.concatenate([t_s[2, cols, :], t_s[3, cols, :]], axis=1)
        row_dot = jnp.sum(g_t * attn_t.astype(jnp.float32), axis=0, keepdims=True) * inverse
        g_t = (g_t * inverse).astype(jnp.bfloat16)
        grad = jnp.transpose(g_t)
        query = jnp.concatenate([q_s[0, :, cols], q_s[1, :, cols]], axis=0)
        dq_t = jnp.zeros((HD, 2 * rows), jnp.float32)
        for j in range(block_count):
            keys = slice(j * rows, (j + 1) * rows)
            if head == 0:
                kv_loads[j].wait()
            e_loads[head, j].wait()
            low = e_s[head, keys, :]
            dprobs = product(kv_s[j, :, vcols], g_t)
            dscore = (low.astype(jnp.float32) * (dprobs - row_dot)).astype(jnp.bfloat16)
            dq_t = dq_t + product(jnp.transpose(kv_s[j, :, cols]), dscore)
            part_s[j, :, cols] = (score_scale * product(dscore, query)).astype(jnp.bfloat16)
            part_s[j, :, vcols] = product(low, grad).astype(jnp.bfloat16)
            if head == head_count - 1:
                stores.append(begin(part_s.at[j], part_outs[j], part_sem.at[j]))
        dquery = (score_scale * jnp.transpose(dq_t)).astype(jnp.bfloat16)
        dq_s[0, :, cols] = dquery[:rows]
        dq_s[1, :, cols] = dquery[rows:]
    stores.append(begin(dq_s.at[0], dq_mine, dq_sem.at[0]))
    stores.append(begin(dq_s.at[1], dq_theirs, dq_sem.at[1]))
    for store in stores:
        store.wait()


def backward(at, queries, q_recv, g_mine, g_recv, attn_mine, attn_theirs, inverse, weights, kv_blocks):
    block_count = len(kv_blocks)
    rows, feats = q_recv.shape
    heads = feats // HD
    keys = block_count * rows
    out = call(
        functools.partial(backward_kernel, block_count, heads),
        [bf16(rows, feats)] * 2 + [bf16(rows, 2 * feats)] * block_count,
        [SMEM] + [ANY] * (8 + block_count),
        [ANY] * (2 + block_count),
        [
            pltpu.VMEM((2, rows, feats), jnp.bfloat16),
            pltpu.VMEM((4, feats, rows), jnp.bfloat16),
            pltpu.VMEM(inverse.shape, jnp.float32),
            pltpu.VMEM((block_count, rows, 2 * feats), jnp.bfloat16),
            pltpu.VMEM((heads, keys, 2 * rows), jnp.bfloat16),
            pltpu.VMEM((block_count, rows, 2 * feats), jnp.bfloat16),
            pltpu.VMEM((2, rows, feats), jnp.bfloat16),
            pltpu.SemaphoreType.DMA((7,)),
            pltpu.SemaphoreType.DMA((block_count,)),
            pltpu.SemaphoreType.DMA((heads * block_count,)),
            pltpu.SemaphoreType.DMA((block_count,)),
            pltpu.SemaphoreType.DMA((2,)),
        ],
        8,
        "backward",
    )(at, queries, q_recv, g_mine, g_recv, attn_mine, attn_theirs, inverse, weights, *kv_blocks)
    return out[0], out[1], out[2:]


def grad_heads_kernel(part_count, sends, picked, at_ref, first_ref, weight_ref, *refs):
    grads, refs = refs[:part_count], refs[part_count:]
    outs, refs = refs[: 2 + sends], refs[2 + sends :]
    first_s, grad_s, weight_s, out_s, first_sem, weight_sem, grad_sem, send_sem, out_sem = refs
    half = out_s.shape[1]
    width = grads[0].shape[1]
    first_load = begin(first_ref, first_s, first_sem)
    weight_loads, grad_loads = [], []
    for k in range(part_count):
        grad_loads.append(begin(grads[k], grad_s.at[k], grad_sem.at[k]))
        if k:
            start = pl.multiple_of(at_ref[k] * width, width)
            columns = weight_ref.at[:, pl.ds(start, width)]
            weight_loads.append(begin(columns, weight_s.at[k - 1], weight_sem.at[k - 1]))
    for load in grad_loads:
        load.wait()
    copies = []
    for send in range(sends):
        for i in range(picked):
            place = send * picked + i
            target = outs[2 + send].at[:, i * width : (i + 1) * width]
            for k in range(part_count):

                @pl.when(at_ref[part_count + place] == k)
                def _():
                    begin(grad_s.at[k], target, send_sem.at[place])

            copies.append(pltpu.make_async_copy(grad_s.at[0], target, send_sem.at[place]))
    first_load.wait()
    summed = first_s[...]
    for k in range(1, part_count):
        weight_loads[k - 1].wait()
        summed = summed + against(weight_s[k - 1], grad_s[k])
    first_s[...] = summed
    for side, at in enumerate((at_ref[0], 1 - at_ref[0])):
        kept = first_s[pl.ds(pl.multiple_of(at * half, half), half), :]
        out_s[side] = kept.astype(jnp.bfloat16)
        copies.append(begin(out_s.at[side], outs[side], out_sem.at[side]))
    for copy in copies:
        copy.wait()


def grad_heads(at, first, out_weight, grads, sends, picked):
    feats, rows = first.shape
    half = feats // INNER
    count = len(grads)
    width = grads[0].shape[1]
    out = call(
        functools.partial(grad_heads_kernel, count, sends, picked),
        [bf16(half, rows), bf16(half, rows)] + [bf16(rows, picked * width)] * sends,
        [SMEM] + [ANY] * (2 + count),
        [ANY] * (2 + sends),
        [
            pltpu.VMEM((feats, rows), jnp.float32),
            pltpu.VMEM((count, rows, width), jnp.bfloat16),
            pltpu.VMEM((count - 1, feats, width), jnp.bfloat16),
            pltpu.VMEM((INNER, half, rows), jnp.bfloat16),
            pltpu.SemaphoreType.DMA,
            pltpu.SemaphoreType.DMA((count - 1,)),
            pltpu.SemaphoreType.DMA((count,)),
            pltpu.SemaphoreType.DMA((sends * picked,)),
            pltpu.SemaphoreType.DMA((INNER,)),
        ],
        3,
        "grad_heads",
    )(at, first, out_weight, *grads)
    return out[0], out[1], out[2:]


def weight_kernel(part_count, picked, doc_count, sent, at_ref, *refs):
    attn, refs = refs[: INNER * doc_count], refs[INNER * doc_count :]
    grads, refs = refs[:part_count], refs[part_count:]
    swapped, refs = refs[: doc_count - 1], refs[doc_count - 1 :]
    out, attn_s, grad_s, out_s, attn_sem, grad_sem, out_sem = refs
    outer, feats, width = out.shape
    half = feats // INNER
    piece = grads[0].shape[1]
    pieces = piece // width
    here = (1 - at_ref[0]) if sent else at_ref[0]
    attn_loads, grad_loads = [], []
    for doc in range(doc_count):
        for side in range(INNER):
            at = (1 - at_ref[0]) if side else at_ref[0]
            index = doc * INNER + side
            target = attn_s.at[doc, pl.ds(pl.multiple_of(at * half, half), half)]
            attn_loads.append(begin(attn[index], target, attn_sem.at[index]))
    for k in range(outer):
        place = lax.rem(at_ref[1] + k, outer) * INNER + here
        which = at_ref[2 + place // pieces]
        cols = pl.ds(pl.multiple_of(lax.rem(place, pieces) * width, width), width)
        for i in range(part_count):

            @pl.when(which == i)
            def _():
                begin(grads[i].at[:, cols], grad_s.at[0, k], grad_sem.at[k])

        loads = [pltpu.make_async_copy(grads[0].at[:, cols], grad_s.at[0, k], grad_sem.at[k])]
        cols = pl.ds(pl.multiple_of(place * width, width), width)
        for doc in range(1, doc_count):
            source = swapped[doc - 1].at[:, cols]
            loads.append(begin(source, grad_s.at[doc, k], grad_sem.at[doc * outer + k]))
        grad_loads.append(loads)
    for load in attn_loads:
        load.wait()
    stores = []
    for k in range(outer):
        term = 0.0
        for doc in range(doc_count):
            grad_loads[k][doc].wait()
            term = term + product(attn_s[doc], grad_s[doc, k])
        out_s[k] = term.astype(out_s.dtype)
        stores.append(begin(out_s.at[k], out.at[k], out_sem.at[k]))
    for store in stores:
        store.wait()


def weight_terms(at, attn, grads, swapped, outer, picked, sent, after=()):
    half, rows = attn[0].shape
    feats = half * INNER
    doc_count = len(attn) // INNER
    width = picked * grads[0].shape[1] // (outer * INNER)
    return call(
        functools.partial(weight_kernel, len(grads), picked, doc_count, sent),
        bf16(outer, feats, width),
        [SMEM] + [ANY] * (len(attn) + len(grads) + len(swapped)),
        ANY,
        [
            pltpu.VMEM((doc_count, feats, rows), jnp.bfloat16),
            pltpu.VMEM((doc_count, outer, rows, width), jnp.bfloat16),
            pltpu.VMEM((outer, feats, width), jnp.bfloat16),
            pltpu.SemaphoreType.DMA((len(attn),)),
            pltpu.SemaphoreType.DMA((doc_count * outer,)),
            pltpu.SemaphoreType.DMA((outer,)),
        ],
        3,
        "weight_sent" if sent else "weight_kept",
        after,
    )(at, *attn, *grads, *swapped)


def weight_add_kernel(keep, recv, *refs):
    outer = keep.shape[0]
    outs, (held_s, out_s, sem, out_sem) = refs[:outer], refs[outer:]
    loads = []
    for k in range(outer):
        for index, held in enumerate((keep, recv)):
            loads.append(begin(held.at[k], held_s.at[index, k], sem.at[2 * k + index]))
    stores = []
    for k in range(outer):
        loads[2 * k].wait()
        loads[2 * k + 1].wait()
        summed = held_s[0, k].astype(jnp.float32) + held_s[1, k].astype(jnp.float32)
        out_s[k] = summed.astype(jnp.bfloat16)
        stores.append(begin(out_s.at[k], outs[k], out_sem.at[k]))
    for store in stores:
        store.wait()


def weight_add(keep, recv):
    outer, feats, width = keep.shape
    return call(
        weight_add_kernel,
        [bf16(feats, width)] * outer,
        [ANY] * 2,
        [ANY] * outer,
        [
            pltpu.VMEM((2, outer, feats, width), jnp.bfloat16),
            pltpu.VMEM((outer, feats, width), jnp.bfloat16),
            pltpu.SemaphoreType.DMA((2 * outer,)),
            pltpu.SemaphoreType.DMA((outer,)),
        ],
        1.5,
        "weight_add",
    )(keep, recv)


def collect_kernel(count, at_ref, dq_mine, dq_recv, *refs):
    terms, (grad_q, grad_k, grad_v) = refs[:count], refs[count : count + 3]
    terms_s, dq_s, out_s, term_sem, dq_sem, out_sem = refs[count + 3 :]
    half = dq_mine.shape[1]
    dq_loads = [begin(held, dq_s.at[i], dq_sem.at[i]) for i, held in enumerate((dq_mine, dq_recv))]
    loads = [begin(terms[c], terms_s.at[c], term_sem.at[c]) for c in range(count)]
    for load in dq_loads + loads:
        load.wait()
    for side, at in enumerate((at_ref[0], 1 - at_ref[0])):
        cols = pl.ds(pl.multiple_of(at * half, half), half)
        summed = terms_s[side].astype(jnp.float32)
        for c in range(side + INNER, count, INNER):
            summed = summed + terms_s[c].astype(jnp.float32)
        summed = summed.astype(jnp.bfloat16)
        out_s[0, :, cols] = dq_s[side]
        out_s[1, :, cols] = summed[:, :half]
        out_s[2, :, cols] = summed[:, half:]
    stores = [
        begin(out_s.at[i], out, out_sem.at[i]) for i, out in enumerate((grad_q, grad_k, grad_v))
    ]
    for store in stores:
        store.wait()


def collect(at, dq_mine, dq_recv, terms):
    rows, half = dq_mine.shape
    count = len(terms)
    return call(
        functools.partial(collect_kernel, count),
        [bf16(rows, INNER * half)] * 3,
        [SMEM] + [ANY] * (2 + count),
        [ANY] * 3,
        [
            pltpu.VMEM((count, rows, 2 * half), jnp.bfloat16),
            pltpu.VMEM((2, rows, half), jnp.bfloat16),
            pltpu.VMEM((3, rows, INNER * half), jnp.bfloat16),
            pltpu.SemaphoreType.DMA((count,)),
            pltpu.SemaphoreType.DMA((2,)),
            pltpu.SemaphoreType.DMA((3,)),
        ],
        2,
        "collect",
    )(at, dq_mine, dq_recv, *terms)


def per_device(
    queries, key_heads, value_heads, grad_output, out_weight, block_pattern, global_offsets
):
    dp_count, ctx_count, tp_count = (lax.axis_size(name) for name in ("dp", "ctx", "tp"))
    dp_at, ctx_at, tp_at = (lax.axis_index(name) for name in ("dp", "ctx", "tp"))
    outer = ctx_count // INNER
    outer_at, inner_at = ctx_at // INNER, ctx_at % INNER
    picked = tp_count // dp_count

    def ctx_pairs(step, side, dp_step=0):
        moved = [(c + step * INNER) % ctx_count ^ side for c in range(ctx_count)]
        if not dp_step:
            return list(enumerate(moved))
        return [
            (d * ctx_count + c, (d + dp_step) % dp_count * ctx_count + moved[c])
            for d in range(dp_count)
            for c in range(ctx_count)
        ]

    def shift_pairs(count, step):
        return [(i, (i + step) % count) for i in range(count)]

    def dp_steps(which):
        return [(which * picked + i - tp_at) % tp_count for i in range(picked)]

    routes = [(step, side) for step in range(outer) for side in range(INNER)]
    sources = [
        ((outer_at - step) % outer) * INNER + (inner_at + side) % INNER for step, side in routes
    ]
    at = jnp.stack([inner_at, outer_at, tp_at] + sources)
    columns_at = [(tp_at + step) % tp_count for step in range(1, tp_count)]
    for step in range(1, dp_count):
        columns_at = columns_at + dp_steps((dp_at + step) % dp_count)
    columns_at = jnp.stack([inner_at] + columns_at)
    weight_at = jnp.stack([inner_at, outer_at] + dp_steps(dp_at))

    grad_own = grad_output[0]
    grads = [grad_own] + [
        lax.ppermute(grad_own, "tp", shift_pairs(tp_count, -step)) for step in range(1, tp_count)
    ]
    kv_mine, kv_theirs, q_theirs = part_heads(at, queries[0], key_heads[0], value_heads[0])
    kv_blocks = [
        lax.ppermute(kv_theirs if side else kv_mine, "ctx", ctx_pairs(step, side))
        if step or side
        else kv_mine
        for step, side in routes
    ]
    q_recv = lax.ppermute(q_theirs, "ctx", ctx_pairs(0, 1))

    first, key_mask, row_mask = prelude(at, block_pattern, global_offsets, grad_own, out_weight)
    g_mine, g_theirs, grad_sends = grad_heads(
        columns_at, first, out_weight, grads, dp_count - 1, picked
    )
    g_recv = lax.ppermute(g_theirs, "ctx", ctx_pairs(0, 1))
    swapped = [
        lax.ppermute(send, "dp", shift_pairs(dp_count, step + 1))
        for step, send in enumerate(grad_sends)
    ]

    weights, inverse, attn_mine, attn_theirs = forward(
        at, queries[0], q_recv, key_mask, row_mask, kv_blocks, (g_theirs,)
    )

    attn = []
    for step in range(dp_count):
        for held, side in ((attn_mine, 0), (attn_theirs, 1)):
            pairs = ctx_pairs(0, side, step)
            axes = ("dp", "ctx") if step else "ctx"
            attn.append(lax.ppermute(held, axes, pairs) if step or side else held)

    dq_mine, dq_theirs, parts = backward(
        at, queries[0], q_recv, g_mine, g_recv, attn_mine, attn_theirs, inverse, weights, kv_blocks
    )
    send = weight_terms(weight_at, attn, grads, swapped, outer, picked, True, (dq_mine,))
    weight_recv = lax.ppermute(send, "ctx", ctx_pairs(0, 1))
    terms = [
        lax.ppermute(part, "ctx", ctx_pairs(-step, side)) if step or side else part
        for (step, side), part in zip(routes, parts)
    ]
    dq_recv = lax.ppermute(dq_theirs, "ctx", ctx_pairs(0, 1))
    keep = weight_terms(weight_at, attn, grads, swapped, outer, picked, False, (send,))
    weight_sums = weight_add(keep, weight_recv)
    grad_weight = weight_sums[0].astype(jnp.float32)
    for step in range(1, outer):
        grad_weight = grad_weight + lax.ppermute(
            weight_sums[step], "ctx", ctx_pairs(step, 0)
        ).astype(jnp.float32)

    grad_q, grad_k, grad_v = collect(at, dq_mine, dq_recv, terms)
    return grad_q[None], grad_k[None], grad_v[None], grad_weight.astype(jnp.bfloat16)


def solution(mesh):
    in_specs = (
        P("dp", "ctx", "tp"),
        P("dp", "ctx", "tp"),
        P("dp", "ctx", "tp"),
        P("dp", "ctx", "tp"),
        P("tp", None),
        P(),
        P(),
    )
    out_specs = (
        P("dp", "ctx", "tp"),
        P("dp", "ctx", "tp"),
        P("dp", "ctx", "tp"),
        P("tp", ("dp", "ctx")),
    )
    return jax.shard_map(
        per_device, mesh=mesh, in_specs=in_specs, out_specs=out_specs, check_vma=False
    )
```

```python
import functools

import jax
import jax.numpy as jnp
from jax import lax
from jax.experimental import pallas as pl
from jax.experimental.pallas import tpu as pltpu
from jax.sharding import PartitionSpec as P

HD = 128
MASKED = -1e30
INNER = 2
SOURCES = 3
ANY = pl.BlockSpec(memory_space=pl.ANY)
VMEM = pl.BlockSpec(memory_space=pltpu.VMEM)
SMEM = pl.BlockSpec(memory_space=pltpu.SMEM)


def against(left_op, right_op):
    return lax.dot_general(
        left_op, right_op, (((1,), (1,)), ((), ())), preferred_element_type=jnp.float32
    )


def product(left_op, right_op):
    return jnp.dot(left_op, right_op, preferred_element_type=jnp.float32)


def begin(source, target, semaphore):
    copy = pltpu.make_async_copy(source, target, semaphore)
    copy.start()
    return copy


def call(kernel, out_shape, in_specs, out_specs, scratch, micros, name, after=()):
    skipped = len(after)
    in_specs = [ANY] * skipped + in_specs
    run = pl.pallas_call(
        lambda *refs: kernel(*refs[skipped:]),
        out_shape=out_shape,
        in_specs=in_specs,
        out_specs=out_specs,
        scratch_shapes=scratch,
        compiler_params=pltpu.CompilerParams(vmem_limit_bytes=60 * 1024 * 1024),
        cost_estimate=pl.CostEstimate(
            flops=int(micros * 1e9), bytes_accessed=int(micros * 3e6), transcendentals=0
        ),
        name=name,
    )

    def placed(*args):
        args = [
            pltpu.with_memory_space_constraint(arg, pltpu.HBM) if spec is ANY else arg
            for spec, arg in zip(in_specs, (*after, *args))
        ]
        return run(*args)

    return placed


def bf16(*shape):
    return pltpu.HBM(shape, jnp.bfloat16)


def f32(*shape):
    return pltpu.HBM(shape, jnp.float32)


def part_kernel(at_ref, k_ref, v_ref, kv_mine, kv_theirs, held_s, in_sem, out_sem):
    half = kv_mine.shape[1] // 2
    loads = [begin(held, held_s.at[i], in_sem.at[i]) for i, held in enumerate((k_ref, v_ref))]
    mine = pl.ds(pl.multiple_of(at_ref[0] * half, half), half)
    theirs = pl.ds(pl.multiple_of((1 - at_ref[0]) * half, half), half)
    copies = []
    for index in range(2):
        loads[index].wait()
        place = slice(index * half, (index + 1) * half)
        for side, (cols, out) in enumerate(((mine, kv_mine), (theirs, kv_theirs))):
            sem = out_sem.at[2 * index + side]
            copies.append(begin(held_s.at[index, :, cols], out.at[:, place], sem))
    for copy in copies:
        copy.wait()


def part_heads(at, keys, values):
    rows, feats = keys.shape
    return call(
        part_kernel,
        [bf16(rows, feats), bf16(rows, feats)],
        [SMEM] + [ANY] * 2,
        [ANY] * 2,
        [
            pltpu.VMEM((2, rows, feats), jnp.bfloat16),
            pltpu.SemaphoreType.DMA((2,)),
            pltpu.SemaphoreType.DMA((4,)),
        ],
        2,
        "part_heads",
    )(at, keys, values)


def prelude_kernel(at_ref, pattern, offsets, q_ref, grad_ref, weight_ref, *refs):
    first, key_mask, row_mask, q_theirs = refs[:4]
    grad_s, weight_s, first_s, mask_s, row_s, q_s, sem, out_sem = refs[4:]
    half = q_theirs.shape[1]
    theirs = pl.ds(pl.multiple_of((1 - at_ref[0]) * half, half), half)
    q_load = begin(q_ref.at[:, theirs], q_s, sem.at[2])
    rows, width = grad_s.shape
    block_count, glob_count = offsets.shape
    start = pl.multiple_of(at_ref[2] * width, width)
    loads = [
        begin(grad_ref, grad_s, sem.at[0]),
        begin(weight_ref.at[:, pl.ds(start, width)], weight_s, sem.at[1]),
    ]
    q_load.wait()
    stores = [begin(q_s, q_theirs, out_sem.at[3])]
    own = at_ref[1] * INNER + at_ref[0]
    partner = at_ref[1] * INNER + 1 - at_ref[0]
    lane = lax.broadcasted_iota(jnp.int32, (1, HD), 1)
    row_at = lax.broadcasted_iota(jnp.int32, (rows, HD), 0)
    col_at = lax.broadcasted_iota(jnp.int32, (8, rows), 1)
    group_at = lax.broadcasted_iota(jnp.int32, (8, rows), 0)
    for index in range(block_count):
        block = at_ref[SOURCES + index]
        hidden = []
        for target in (own, partner):
            seen = jnp.abs(block - target) <= 1
            for r in range(pattern.shape[1]):
                seen = seen | (pattern[target, r] == block)
            hidden.append(jnp.where(seen, 0, 1))
        lane_hidden = jnp.where(lane == 0, hidden[0], jnp.where(lane == 1, hidden[1], 0))
        hidden_rows = jnp.broadcast_to(lane_hidden, (rows, HD))
        for r in range(glob_count):
            hidden_rows = jnp.where(row_at == offsets[block, r], 0, hidden_rows)
        mask_s[index * rows : (index + 1) * rows, :] = hidden_rows.astype(jnp.float32).astype(
            jnp.bfloat16
        )
    for group, target in enumerate((own, partner)):
        local = jnp.where(group_at == group, MASKED, 0.0)
        for r in range(glob_count):
            local = jnp.where(col_at == offsets[target, r], 0.0, local)
        row_s[:, group * rows : (group + 1) * rows] = local
    stores.append(begin(mask_s, key_mask, out_sem.at[0]))
    stores.append(begin(row_s, row_mask, out_sem.at[1]))
    for load in loads:
        load.wait()
    first_s[...] = against(weight_s[...], grad_s[...])
    stores.append(begin(first_s, first, out_sem.at[2]))
    for store in stores:
        store.wait()


def prelude(at, pattern, offsets, queries, grad_own, out_weight, after):
    rows, width = grad_own.shape
    feats = out_weight.shape[0]
    keys = offsets.shape[0] * rows
    half = queries.shape[1] // INNER
    return call(
        prelude_kernel,
        [
            f32(feats, rows),
            bf16(keys, HD),
            f32(8, 2 * rows),
            bf16(rows, half),
        ],
        [SMEM] * 3 + [ANY] * 3,
        [ANY] * 4,
        [
            pltpu.VMEM((rows, width), jnp.bfloat16),
            pltpu.VMEM((feats, width), jnp.bfloat16),
            pltpu.VMEM((feats, rows), jnp.float32),
            pltpu.VMEM((keys, HD), jnp.bfloat16),
            pltpu.VMEM((8, 2 * rows), jnp.float32),
            pltpu.VMEM((rows, half), jnp.bfloat16),
            pltpu.SemaphoreType.DMA((3,)),
            pltpu.SemaphoreType.DMA((4,)),
        ],
        4,
        "prelude",
        after,
    )(at, pattern, offsets, queries, grad_own, out_weight)


def forward_kernel(block_count, head_count, at_ref, q_ref, q_recv, key_mask, row_mask, *refs):
    kv_refs, refs = refs[:block_count], refs[block_count:]
    e_out, inv_out, attn_mine, attn_theirs = refs[:4]
    q_s, mask_s, kv_s, e_s, s_ref, attn_s, inv_s, row_s, sem, kv_sem, e_sem, out_sem = refs[4:]
    rows = q_recv.shape[0]
    feats = head_count * HD
    score_scale = HD ** (-0.5)
    mine = pl.ds(pl.multiple_of(at_ref[0] * feats, feats), feats)
    loads = [
        begin(q_ref.at[:, mine], q_s.at[0], sem.at[0]),
        begin(q_recv, q_s.at[1], sem.at[1]),
        begin(key_mask, mask_s, sem.at[2]),
        begin(row_mask, row_s, sem.at[3]),
    ]
    kv_loads = [begin(kv_refs[j], kv_s.at[j], kv_sem.at[j]) for j in range(block_count)]
    for load in loads:
        load.wait()
    rows_low = row_s[...].astype(jnp.bfloat16)
    hidden = jnp.concatenate([rows_low, jnp.zeros((HD - 8, 2 * rows), jnp.bfloat16)], axis=0)
    stores = []
    for head in range(head_count):
        cols = slice(head * HD, (head + 1) * HD)
        vcols = slice(feats + head * HD, feats + (head + 1) * HD)
        q_t = jnp.concatenate(
            [jnp.transpose(q_s[0, :, cols]), jnp.transpose(q_s[1, :, cols])], axis=1
        )
        q_t = jnp.concatenate([q_t, hidden], axis=0)
        top = jnp.full((1, 2 * rows), MASKED, jnp.float32)
        for j in range(block_count):
            if head == 0:
                kv_loads[j].wait()
            keys = slice(j * rows, (j + 1) * rows)
            scores = product(jnp.concatenate([kv_s[j, :, cols], mask_s[keys, :]], axis=1), q_t)
            s_ref[keys, :] = scores
            top = jnp.maximum(top, jnp.max(scores, axis=0, keepdims=True))
        total = jnp.zeros((1, 2 * rows), jnp.float32)
        attn_t = jnp.zeros((HD, 2 * rows), jnp.float32)
        for j in range(block_count):
            keys = slice(j * rows, (j + 1) * rows)
            weights = jnp.exp((s_ref[keys, :] - top) * score_scale)
            total = total + jnp.sum(weights, axis=0, keepdims=True)
            low = weights.astype(jnp.bfloat16)
            e_s[head, keys, :] = low
            stores.append(
                begin(e_s.at[head, keys], e_out.at[head, keys], e_sem.at[head * block_count + j])
            )
            attn_t = attn_t + product(jnp.transpose(kv_s[j, :, vcols]), low)
        inverse = 1.0 / total
        inv_s[head : head + 1, :] = inverse
        attn_low = (attn_t * inverse).astype(jnp.bfloat16)
        attn_s[0, cols, :] = attn_low[:, :rows]
        attn_s[1, cols, :] = attn_low[:, rows:]
    stores.append(begin(attn_s.at[0], attn_mine, out_sem.at[0]))
    stores.append(begin(attn_s.at[1], attn_theirs, out_sem.at[1]))
    stores.append(begin(inv_s, inv_out, out_sem.at[2]))
    for store in stores:
        store.wait()


def forward(at, queries, q_recv, key_mask, row_mask, kv_blocks, after):
    block_count = len(kv_blocks)
    rows, feats = q_recv.shape
    heads = feats // HD
    keys = block_count * rows
    return call(
        functools.partial(forward_kernel, block_count, heads),
        [
            bf16(heads, keys, 2 * rows),
            f32(max(heads, 8), 2 * rows),
            bf16(feats, rows),
            bf16(feats, rows),
        ],
        [SMEM] + [ANY] * (4 + block_count),
        [ANY] * 4,
        [
            pltpu.VMEM((2, rows, feats), jnp.bfloat16),
            pltpu.VMEM((keys, HD), jnp.bfloat16),
            pltpu.VMEM((block_count, rows, 2 * feats), jnp.bfloat16),
            pltpu.VMEM((heads, keys, 2 * rows), jnp.bfloat16),
            pltpu.VMEM((keys, 2 * rows), jnp.float32),
            pltpu.VMEM((2, feats, rows), jnp.bfloat16),
            pltpu.VMEM((max(heads, 8), 2 * rows), jnp.float32),
            pltpu.VMEM((8, 2 * rows), jnp.float32),
            pltpu.SemaphoreType.DMA((4,)),
            pltpu.SemaphoreType.DMA((block_count,)),
            pltpu.SemaphoreType.DMA((heads * block_count,)),
            pltpu.SemaphoreType.DMA((3,)),
        ],
        6,
        "forward",
        after,
    )(at, queries, q_recv, key_mask, row_mask, *kv_blocks)


def backward_kernel(block_count, head_count, at_ref, *refs):
    q_ref, q_recv, g_mine, g_recv, attn_mine, attn_theirs, inv_ref, e_ref = refs[:8]
    kv_refs, refs = refs[8 : 8 + block_count], refs[8 + block_count :]
    dq_mine, dq_theirs = refs[:2]
    outer = block_count // INNER
    part_outs, refs = refs[2 : 2 + outer], refs[2 + outer :]
    q_s, t_s, inv_s, kv_s, e_s, part_s, dq_s, sem, kv_sem, e_sem, part_sem, dq_sem = refs
    rows = q_recv.shape[0]
    feats = head_count * HD
    score_scale = HD ** (-0.5)
    mine = pl.ds(pl.multiple_of(at_ref[0] * feats, feats), feats)
    loads = [begin(q_ref.at[:, mine], q_s.at[0], sem.at[0]), begin(q_recv, q_s.at[1], sem.at[1])]
    for index, held in enumerate((g_mine, g_recv, attn_mine, attn_theirs)):
        loads.append(begin(held, t_s.at[index], sem.at[2 + index]))
    loads.append(begin(inv_ref, inv_s, sem.at[6]))
    kv_loads, e_loads, stores = [], {}, []
    for j in range(block_count):
        keys = slice(j * rows, (j + 1) * rows)
        kv_loads.append(begin(kv_refs[j], kv_s.at[j], kv_sem.at[j]))
        for head in range(head_count):
            e_loads[head, j] = begin(
                e_ref.at[head, keys], e_s.at[head, keys], e_sem.at[head * block_count + j]
            )
    for load in loads:
        load.wait()
    for head in range(head_count):
        cols = slice(head * HD, (head + 1) * HD)
        vcols = slice(feats + head * HD, feats + (head + 1) * HD)
        inverse = inv_s[head : head + 1, :]
        g_t = jnp.concatenate([t_s[0, cols, :], t_s[1, cols, :]], axis=1).astype(jnp.float32)
        attn_t = jnp.concatenate([t_s[2, cols, :], t_s[3, cols, :]], axis=1)
        row_dot = jnp.sum(g_t * attn_t.astype(jnp.float32), axis=0, keepdims=True) * inverse
        g_t = (g_t * inverse).astype(jnp.bfloat16)
        grad = jnp.transpose(g_t)
        query = jnp.concatenate([q_s[0, :, cols], q_s[1, :, cols]], axis=0)
        dq_t = jnp.zeros((HD, 2 * rows), jnp.float32)
        for j in range(block_count):
            keys = slice(j * rows, (j + 1) * rows)
            if head == 0:
                kv_loads[j].wait()
            e_loads[head, j].wait()
            low = e_s[head, keys, :]
            dprobs = product(kv_s[j, :, vcols], g_t)
            dscore = (low.astype(jnp.float32) * (dprobs - row_dot)).astype(jnp.bfloat16)
            dq_t = dq_t + product(jnp.transpose(kv_s[j, :, cols]), dscore)
            part_s[j, :, cols] = (score_scale * product(dscore, query)).astype(jnp.bfloat16)
            part_s[j, :, vcols] = product(low, grad).astype(jnp.bfloat16)
            if head == head_count - 1:
                stores.append(begin(part_s.at[j], part_outs[j // INNER].at[j % INNER], part_sem.at[j]))
        dquery = (score_scale * jnp.transpose(dq_t)).astype(jnp.bfloat16)
        dq_s[0, :, cols] = dquery[:rows]
        dq_s[1, :, cols] = dquery[rows:]
    stores.append(begin(dq_s.at[0], dq_mine, dq_sem.at[0]))
    stores.append(begin(dq_s.at[1], dq_theirs, dq_sem.at[1]))
    for store in stores:
        store.wait()


def backward(at, queries, q_recv, g_mine, g_recv, attn_mine, attn_theirs, inverse, weights, kv_blocks):
    block_count = len(kv_blocks)
    rows, feats = q_recv.shape
    heads = feats // HD
    keys = block_count * rows
    out = call(
        functools.partial(backward_kernel, block_count, heads),
        [bf16(rows, feats)] * 2 + [bf16(INNER, rows, 2 * feats)] * (block_count // INNER),
        [SMEM] + [ANY] * (8 + block_count),
        [ANY] * (2 + block_count // INNER),
        [
            pltpu.VMEM((2, rows, feats), jnp.bfloat16),
            pltpu.VMEM((4, feats, rows), jnp.bfloat16),
            pltpu.VMEM(inverse.shape, jnp.float32),
            pltpu.VMEM((block_count, rows, 2 * feats), jnp.bfloat16),
            pltpu.VMEM((heads, keys, 2 * rows), jnp.bfloat16),
            pltpu.VMEM((block_count, rows, 2 * feats), jnp.bfloat16),
            pltpu.VMEM((2, rows, feats), jnp.bfloat16),
            pltpu.SemaphoreType.DMA((7,)),
            pltpu.SemaphoreType.DMA((block_count,)),
            pltpu.SemaphoreType.DMA((heads * block_count,)),
            pltpu.SemaphoreType.DMA((block_count,)),
            pltpu.SemaphoreType.DMA((2,)),
        ],
        8,
        "backward",
    )(at, queries, q_recv, g_mine, g_recv, attn_mine, attn_theirs, inverse, weights, *kv_blocks)
    return out[0], out[1], out[2:]


def grad_heads_kernel(part_count, sends, picked, at_ref, first_ref, weight_ref, *refs):
    grads, refs = refs[:part_count], refs[part_count:]
    outs, refs = refs[: 2 + sends], refs[2 + sends :]
    first_s, grad_s, weight_s, out_s, first_sem, weight_sem, grad_sem, send_sem, out_sem = refs
    half = out_s.shape[1]
    width = grads[0].shape[1]
    first_load = begin(first_ref, first_s, first_sem)
    weight_loads, grad_loads = [], []
    for k in range(part_count):
        grad_loads.append(begin(grads[k], grad_s.at[k], grad_sem.at[k]))
        if k:
            start = pl.multiple_of(at_ref[k] * width, width)
            columns = weight_ref.at[:, pl.ds(start, width)]
            weight_loads.append(begin(columns, weight_s.at[k - 1], weight_sem.at[k - 1]))
    for load in grad_loads:
        load.wait()
    copies = []
    for send in range(sends):
        for i in range(picked):
            place = send * picked + i
            target = outs[2 + send].at[:, i * width : (i + 1) * width]
            for k in range(part_count):

                @pl.when(at_ref[part_count + place] == k)
                def _():
                    begin(grad_s.at[k], target, send_sem.at[place])

            copies.append(pltpu.make_async_copy(grad_s.at[0], target, send_sem.at[place]))
    first_load.wait()
    summed = first_s[...]
    for k in range(1, part_count):
        weight_loads[k - 1].wait()
        summed = summed + against(weight_s[k - 1], grad_s[k])
    first_s[...] = summed
    for side, at in enumerate((at_ref[0], 1 - at_ref[0])):
        kept = first_s[pl.ds(pl.multiple_of(at * half, half), half), :]
        out_s[side] = kept.astype(jnp.bfloat16)
        copies.append(begin(out_s.at[side], outs[side], out_sem.at[side]))
    for copy in copies:
        copy.wait()


def grad_heads(at, first, out_weight, grads, sends, picked):
    feats, rows = first.shape
    half = feats // INNER
    count = len(grads)
    width = grads[0].shape[1]
    out = call(
        functools.partial(grad_heads_kernel, count, sends, picked),
        [bf16(half, rows), bf16(half, rows)] + [bf16(rows, picked * width)] * sends,
        [SMEM] + [ANY] * (2 + count),
        [ANY] * (2 + sends),
        [
            pltpu.VMEM((feats, rows), jnp.float32),
            pltpu.VMEM((count, rows, width), jnp.bfloat16),
            pltpu.VMEM((count - 1, feats, width), jnp.bfloat16),
            pltpu.VMEM((INNER, half, rows), jnp.bfloat16),
            pltpu.SemaphoreType.DMA,
            pltpu.SemaphoreType.DMA((count - 1,)),
            pltpu.SemaphoreType.DMA((count,)),
            pltpu.SemaphoreType.DMA((sends * picked,)),
            pltpu.SemaphoreType.DMA((INNER,)),
        ],
        3,
        "grad_heads",
    )(at, first, out_weight, *grads)
    return out[0], out[1], out[2:]


def weight_kernel(part_count, picked, doc_count, sent, at_ref, *refs):
    attn, refs = refs[: INNER * doc_count], refs[INNER * doc_count :]
    grads, refs = refs[:part_count], refs[part_count:]
    swapped, refs = refs[: doc_count - 1], refs[doc_count - 1 :]
    out, attn_s, grad_s, out_s, attn_sem, grad_sem, out_sem = refs
    outer, feats, width = out.shape
    half = feats // INNER
    piece = grads[0].shape[1]
    pieces = piece // width
    here = (1 - at_ref[0]) if sent else at_ref[0]
    attn_loads, grad_loads = [], []
    for doc in range(doc_count):
        for side in range(INNER):
            at = (1 - at_ref[0]) if side else at_ref[0]
            index = doc * INNER + side
            target = attn_s.at[doc, pl.ds(pl.multiple_of(at * half, half), half)]
            attn_loads.append(begin(attn[index], target, attn_sem.at[index]))
    for k in range(outer):
        place = lax.rem(at_ref[1] + k, outer) * INNER + here
        which = at_ref[2 + place // pieces]
        cols = pl.ds(pl.multiple_of(lax.rem(place, pieces) * width, width), width)
        for i in range(part_count):

            @pl.when(which == i)
            def _():
                begin(grads[i].at[:, cols], grad_s.at[0, k], grad_sem.at[k])

        loads = [pltpu.make_async_copy(grads[0].at[:, cols], grad_s.at[0, k], grad_sem.at[k])]
        cols = pl.ds(pl.multiple_of(place * width, width), width)
        for doc in range(1, doc_count):
            source = swapped[doc - 1].at[:, cols]
            loads.append(begin(source, grad_s.at[doc, k], grad_sem.at[doc * outer + k]))
        grad_loads.append(loads)
    for load in attn_loads:
        load.wait()
    stores = []
    for k in range(outer):
        term = 0.0
        for doc in range(doc_count):
            grad_loads[k][doc].wait()
            term = term + product(attn_s[doc], grad_s[doc, k])
        out_s[k] = term.astype(out_s.dtype)
        stores.append(begin(out_s.at[k], out.at[k], out_sem.at[k]))
    for store in stores:
        store.wait()


def weight_terms(at, attn, grads, swapped, outer, picked, sent, after=()):
    half, rows = attn[0].shape
    feats = half * INNER
    doc_count = len(attn) // INNER
    width = picked * grads[0].shape[1] // (outer * INNER)
    return call(
        functools.partial(weight_kernel, len(grads), picked, doc_count, sent),
        bf16(outer, feats, width),
        [SMEM] + [ANY] * (len(attn) + len(grads) + len(swapped)),
        ANY,
        [
            pltpu.VMEM((doc_count, feats, rows), jnp.bfloat16),
            pltpu.VMEM((doc_count, outer, rows, width), jnp.bfloat16),
            pltpu.VMEM((outer, feats, width), jnp.bfloat16),
            pltpu.SemaphoreType.DMA((len(attn),)),
            pltpu.SemaphoreType.DMA((doc_count * outer,)),
            pltpu.SemaphoreType.DMA((outer,)),
        ],
        3,
        "weight_sent" if sent else "weight_kept",
        after,
    )(at, *attn, *grads, *swapped)


def weight_add_kernel(keep, recv, *refs):
    outer = keep.shape[0]
    outs, (held_s, out_s, sem, out_sem) = refs[:outer], refs[outer:]
    loads = []
    for k in range(outer):
        for index, held in enumerate((keep, recv)):
            loads.append(begin(held.at[k], held_s.at[index, k], sem.at[2 * k + index]))
    stores = []
    for k in range(outer):
        loads[2 * k].wait()
        loads[2 * k + 1].wait()
        summed = held_s[0, k].astype(jnp.float32) + held_s[1, k].astype(jnp.float32)
        out_s[k] = summed.astype(jnp.bfloat16)
        stores.append(begin(out_s.at[k], outs[k], out_sem.at[k]))
    for store in stores:
        store.wait()


def weight_add(keep, recv):
    outer, feats, width = keep.shape
    return call(
        weight_add_kernel,
        [bf16(feats, width)] * outer,
        [ANY] * 2,
        [ANY] * outer,
        [
            pltpu.VMEM((2, outer, feats, width), jnp.bfloat16),
            pltpu.VMEM((outer, feats, width), jnp.bfloat16),
            pltpu.SemaphoreType.DMA((2 * outer,)),
            pltpu.SemaphoreType.DMA((outer,)),
        ],
        1.5,
        "weight_add",
    )(keep, recv)


def add_kernel(count, *refs):
    terms, (mine, theirs) = refs[:count], refs[count : count + 2]
    terms_s, out_s, term_sem, out_sem = refs[count + 2 :]
    loads = [
        begin(terms[c].at[side], terms_s.at[c, side], term_sem.at[c * INNER + side])
        for side in (1, 0)
        for c in range(count)
    ]
    stores = []
    for index, (side, out) in enumerate(((1, theirs), (0, mine))):
        for load in loads[index * count : (index + 1) * count]:
            load.wait()
        summed = terms_s[0, side].astype(jnp.float32)
        for c in range(1, count):
            summed = summed + terms_s[c, side].astype(jnp.float32)
        out_s[side] = summed.astype(jnp.bfloat16)
        stores.append(begin(out_s.at[side], out, out_sem.at[side]))
    for store in stores:
        store.wait()


def add_terms(terms, after):
    _, rows, width = terms[0].shape
    count = len(terms)
    return call(
        functools.partial(add_kernel, count),
        [bf16(rows, width)] * 2,
        [ANY] * count,
        [ANY] * 2,
        [
            pltpu.VMEM((count, INNER, rows, width), jnp.bfloat16),
            pltpu.VMEM((INNER, rows, width), jnp.bfloat16),
            pltpu.SemaphoreType.DMA((count * INNER,)),
            pltpu.SemaphoreType.DMA((INNER,)),
        ],
        2,
        "add_terms",
        after,
    )(*terms)


def join_kernel(at_ref, dq_mine, dq_recv, mine, recv, *refs):
    outs, (held_s, out_s, sem, out_sem) = refs[:3], refs[3:]
    half = dq_mine.shape[1]
    loads = [
        begin(dq_mine, held_s.at[0, 0], sem.at[0]),
        begin(dq_recv, held_s.at[1, 0], sem.at[1]),
    ]
    for side, held in enumerate((mine, recv)):
        for index in range(2):
            source = held.at[:, index * half : (index + 1) * half]
            loads.append(begin(source, held_s.at[side, 1 + index], sem.at[2 + 2 * side + index]))
    for load in loads:
        load.wait()
    stores = []
    for index, out in enumerate(outs):
        for side, at in enumerate((at_ref[0], 1 - at_ref[0])):
            cols = pl.ds(pl.multiple_of(at * half, half), half)
            out_s[index, :, cols] = held_s[side, index]
        stores.append(begin(out_s.at[index], out, out_sem.at[index]))
    for store in stores:
        store.wait()


def join_heads(at, dq_mine, dq_recv, mine, recv):
    rows, half = dq_mine.shape
    return call(
        join_kernel,
        [bf16(rows, INNER * half)] * 3,
        [SMEM] + [ANY] * 4,
        [ANY] * 3,
        [
            pltpu.VMEM((INNER, 3, rows, half), jnp.bfloat16),
            pltpu.VMEM((3, rows, INNER * half), jnp.bfloat16),
            pltpu.SemaphoreType.DMA((6,)),
            pltpu.SemaphoreType.DMA((3,)),
        ],
        2,
        "join_heads",
    )(at, dq_mine, dq_recv, mine, recv)


def per_device(
    queries, key_heads, value_heads, grad_output, out_weight, block_pattern, global_offsets
):
    dp_count, ctx_count, tp_count = (lax.axis_size(name) for name in ("dp", "ctx", "tp"))
    dp_at, ctx_at, tp_at = (lax.axis_index(name) for name in ("dp", "ctx", "tp"))
    outer = ctx_count // INNER
    outer_at, inner_at = ctx_at // INNER, ctx_at % INNER
    picked = tp_count // dp_count

    def ctx_pairs(step, side, dp_step=0):
        moved = [(c + step * INNER) % ctx_count ^ side for c in range(ctx_count)]
        if not dp_step:
            return list(enumerate(moved))
        return [
            (d * ctx_count + c, (d + dp_step) % dp_count * ctx_count + moved[c])
            for d in range(dp_count)
            for c in range(ctx_count)
        ]

    def shift_pairs(count, step):
        return [(i, (i + step) % count) for i in range(count)]

    def dp_steps(which):
        return [(which * picked + i - tp_at) % tp_count for i in range(picked)]

    routes = [(step, side) for step in range(outer) for side in range(INNER)]
    sources = [
        ((outer_at - step) % outer) * INNER + (inner_at + side) % INNER for step, side in routes
    ]
    at = jnp.stack([inner_at, outer_at, tp_at] + sources)
    columns_at = [(tp_at + step) % tp_count for step in range(1, tp_count)]
    for step in range(1, dp_count):
        columns_at = columns_at + dp_steps((dp_at + step) % dp_count)
    columns_at = jnp.stack([inner_at] + columns_at)
    weight_at = jnp.stack([inner_at, outer_at] + dp_steps(dp_at))

    grad_own = grad_output[0]
    grads = [grad_own] + [
        lax.ppermute(grad_own, "tp", shift_pairs(tp_count, -step)) for step in range(1, tp_count)
    ]
    kv_mine, kv_theirs = part_heads(at, key_heads[0], value_heads[0])
    kv_recv = lax.ppermute(kv_theirs, "ctx", ctx_pairs(0, 1))
    kv_blocks = [
        lax.ppermute(kv_recv if side else kv_mine, "ctx", ctx_pairs(step, 0))
        if step
        else (kv_recv if side else kv_mine)
        for step, side in routes
    ]
    first, key_mask, row_mask, q_theirs = prelude(
        at, block_pattern, global_offsets, queries[0], grad_own, out_weight, (kv_recv,)
    )
    q_recv = lax.ppermute(q_theirs, "ctx", ctx_pairs(0, 1))
    g_mine, g_theirs, grad_sends = grad_heads(
        columns_at, first, out_weight, grads, dp_count - 1, picked
    )
    g_recv = lax.ppermute(g_theirs, "ctx", ctx_pairs(0, 1))
    swapped = [
        lax.ppermute(send, "dp", shift_pairs(dp_count, step + 1))
        for step, send in enumerate(grad_sends)
    ]

    weights, inverse, attn_mine, attn_theirs = forward(
        at, queries[0], q_recv, key_mask, row_mask, kv_blocks, (g_theirs,)
    )

    attn = []
    for step in range(dp_count):
        for held, side in ((attn_mine, 0), (attn_theirs, 1)):
            pairs = ctx_pairs(0, side, step)
            axes = ("dp", "ctx") if step else "ctx"
            attn.append(lax.ppermute(held, axes, pairs) if step or side else held)

    dq_mine, dq_theirs, parts = backward(
        at, queries[0], q_recv, g_mine, g_recv, attn_mine, attn_theirs, inverse, weights, kv_blocks
    )
    send = weight_terms(weight_at, attn, grads, swapped, outer, picked, True, (dq_mine,))
    weight_recv = lax.ppermute(send, "ctx", ctx_pairs(0, 1))
    terms = [
        lax.ppermute(part, "ctx", ctx_pairs(-step, 0)) if step else part
        for step, part in enumerate(parts)
    ]
    dq_recv = lax.ppermute(dq_theirs, "ctx", ctx_pairs(0, 1))
    keep = weight_terms(weight_at, attn, grads, swapped, outer, picked, False, (send,))
    weight_sums = weight_add(keep, weight_recv)
    grad_weight = weight_sums[0].astype(jnp.float32)
    for step in range(1, outer):
        grad_weight = grad_weight + lax.ppermute(
            weight_sums[step], "ctx", ctx_pairs(step, 0)
        ).astype(jnp.float32)

    terms_mine, terms_theirs = add_terms(terms, (weight_sums[0],))
    terms_recv = lax.ppermute(terms_theirs, "ctx", ctx_pairs(0, 1))
    grad_q, grad_k, grad_v = join_heads(at, dq_mine, dq_recv, terms_mine, terms_recv)
    return grad_q[None], grad_k[None], grad_v[None], grad_weight.astype(jnp.bfloat16)


def solution(mesh):
    in_specs = (
        P("dp", "ctx", "tp"),
        P("dp", "ctx", "tp"),
        P("dp", "ctx", "tp"),
        P("dp", "ctx", "tp"),
        P("tp", None),
        P(),
        P(),
    )
    out_specs = (
        P("dp", "ctx", "tp"),
        P("dp", "ctx", "tp"),
        P("dp", "ctx", "tp"),
        P("tp", ("dp", "ctx")),
    )
    return jax.shard_map(
        per_device, mesh=mesh, in_specs=in_specs, out_specs=out_specs, check_vma=False
    )
```

```python
import functools

import jax
import jax.numpy as jnp
from jax import lax
from jax.experimental import pallas as pl
from jax.experimental.pallas import tpu as pltpu
from jax.sharding import PartitionSpec as P

HD = 128
MASKED = -1e30
INNER = 2
SOURCES = 3
ANY = pl.BlockSpec(memory_space=pl.ANY)
VMEM = pl.BlockSpec(memory_space=pltpu.VMEM)
SMEM = pl.BlockSpec(memory_space=pltpu.SMEM)


def against(left_op, right_op):
    return lax.dot_general(
        left_op, right_op, (((1,), (1,)), ((), ())), preferred_element_type=jnp.float32
    )


def product(left_op, right_op):
    return jnp.dot(left_op, right_op, preferred_element_type=jnp.float32)


def begin(source, target, semaphore):
    copy = pltpu.make_async_copy(source, target, semaphore)
    copy.start()
    return copy


def call(kernel, out_shape, in_specs, out_specs, scratch, micros, name, after=()):
    skipped = len(after)
    in_specs = [ANY] * skipped + in_specs
    run = pl.pallas_call(
        lambda *refs: kernel(*refs[skipped:]),
        out_shape=out_shape,
        in_specs=in_specs,
        out_specs=out_specs,
        scratch_shapes=scratch,
        compiler_params=pltpu.CompilerParams(vmem_limit_bytes=60 * 1024 * 1024),
        cost_estimate=pl.CostEstimate(
            flops=int(micros * 1e9), bytes_accessed=int(micros * 3e6), transcendentals=0
        ),
        name=name,
    )

    def placed(*args):
        args = [
            pltpu.with_memory_space_constraint(arg, pltpu.HBM) if spec is ANY else arg
            for spec, arg in zip(in_specs, (*after, *args))
        ]
        return run(*args)

    return placed


def bf16(*shape):
    return pltpu.HBM(shape, jnp.bfloat16)


def f32(*shape):
    return pltpu.HBM(shape, jnp.float32)


def part_kernel(at_ref, q_ref, k_ref, v_ref, send, q_theirs, held_s, in_sem, out_sem):
    count, rows, both = send.shape
    half = both // 2
    loads = [begin(held, held_s.at[i], in_sem.at[i]) for i, held in enumerate((k_ref, v_ref, q_ref))]
    copies = []
    for index in range(2):
        loads[index].wait()
        for place in range(count):
            side = place % INNER
            source = held_s.at[index, :, side * half : (side + 1) * half]
            target = send.at[place, :, index * half : (index + 1) * half]
            copies.append(begin(source, target, out_sem.at[index * count + place]))
    loads[2].wait()
    theirs = pl.ds(pl.multiple_of((1 - at_ref[0]) * half, half), half)
    copies.append(begin(held_s.at[2, :, theirs], q_theirs, out_sem.at[2 * count]))
    for copy in copies:
        copy.wait()


def part_heads(at, queries, keys, values, count):
    rows, feats = queries.shape
    half = feats // INNER
    return call(
        part_kernel,
        [bf16(count, rows, 2 * half), bf16(rows, half)],
        [SMEM] + [ANY] * 3,
        [ANY] * 2,
        [
            pltpu.VMEM((3, rows, feats), jnp.bfloat16),
            pltpu.SemaphoreType.DMA((3,)),
            pltpu.SemaphoreType.DMA((2 * count + 1,)),
        ],
        2,
        "part_heads",
    )(at, queries, keys, values)


def prelude_kernel(at_ref, pattern, offsets, grad_ref, weight_ref, *refs):
    first, key_mask, row_mask = refs[:3]
    grad_s, weight_s, first_s, mask_s, row_s, sem, out_sem = refs[3:]
    rows, width = grad_s.shape
    block_count, glob_count = offsets.shape
    start = pl.multiple_of(at_ref[2] * width, width)
    loads = [
        begin(grad_ref, grad_s, sem.at[0]),
        begin(weight_ref.at[:, pl.ds(start, width)], weight_s, sem.at[1]),
    ]
    stores = []
    own = at_ref[1] * INNER + at_ref[0]
    partner = at_ref[1] * INNER + 1 - at_ref[0]
    lane = lax.broadcasted_iota(jnp.int32, (1, HD), 1)
    row_at = lax.broadcasted_iota(jnp.int32, (rows, HD), 0)
    col_at = lax.broadcasted_iota(jnp.int32, (8, rows), 1)
    group_at = lax.broadcasted_iota(jnp.int32, (8, rows), 0)
    for index in range(block_count):
        block = at_ref[SOURCES + index]
        hidden = []
        for target in (own, partner):
            seen = jnp.abs(block - target) <= 1
            for r in range(pattern.shape[1]):
                seen = seen | (pattern[target, r] == block)
            hidden.append(jnp.where(seen, 0, 1))
        lane_hidden = jnp.where(lane == 0, hidden[0], jnp.where(lane == 1, hidden[1], 0))
        hidden_rows = jnp.broadcast_to(lane_hidden, (rows, HD))
        for r in range(glob_count):
            hidden_rows = jnp.where(row_at == offsets[block, r], 0, hidden_rows)
        mask_s[index * rows : (index + 1) * rows, :] = hidden_rows.astype(jnp.float32).astype(
            jnp.bfloat16
        )
    for group, target in enumerate((own, partner)):
        local = jnp.where(group_at == group, MASKED, 0.0)
        for r in range(glob_count):
            local = jnp.where(col_at == offsets[target, r], 0.0, local)
        row_s[:, group * rows : (group + 1) * rows] = local
    stores.append(begin(mask_s, key_mask, out_sem.at[0]))
    stores.append(begin(row_s, row_mask, out_sem.at[1]))
    for load in loads:
        load.wait()
    first_s[...] = against(weight_s[...], grad_s[...])
    stores.append(begin(first_s, first, out_sem.at[2]))
    for store in stores:
        store.wait()


def prelude(at, pattern, offsets, grad_own, out_weight, after):
    rows, width = grad_own.shape
    feats = out_weight.shape[0]
    keys = offsets.shape[0] * rows
    return call(
        prelude_kernel,
        [
            f32(feats, rows),
            bf16(keys, HD),
            f32(8, 2 * rows),
        ],
        [SMEM] * 3 + [ANY] * 2,
        [ANY] * 3,
        [
            pltpu.VMEM((rows, width), jnp.bfloat16),
            pltpu.VMEM((feats, width), jnp.bfloat16),
            pltpu.VMEM((feats, rows), jnp.float32),
            pltpu.VMEM((keys, HD), jnp.bfloat16),
            pltpu.VMEM((8, 2 * rows), jnp.float32),
            pltpu.SemaphoreType.DMA((2,)),
            pltpu.SemaphoreType.DMA((3,)),
        ],
        4,
        "prelude",
        after,
    )(at, pattern, offsets, grad_own, out_weight)


def forward_kernel(block_count, head_count, at_ref, q_ref, q_recv, key_mask, row_mask, *refs):
    g_mine, g_recv = refs[:2]
    kv_ref, refs = refs[2], refs[3:]
    outer = block_count // INNER
    e_out, inv_out, attn_mine, attn_theirs = refs[:4]
    part_outs, refs = refs[4 : 4 + outer], refs[4 + outer :]
    q_s, g_s, mask_s, kv_s, e_s, s_ref, attn_s, inv_s, row_s, part_s = refs[:10]
    sem, kv_sem, e_sem, out_sem, part_sem = refs[10:]
    rows = q_recv.shape[0]
    feats = head_count * HD
    score_scale = HD ** (-0.5)
    mine = pl.ds(pl.multiple_of(at_ref[0] * feats, feats), feats)
    loads = [
        begin(q_ref.at[:, mine], q_s.at[0], sem.at[0]),
        begin(q_recv, q_s.at[1], sem.at[1]),
        begin(key_mask, mask_s, sem.at[2]),
        begin(row_mask, row_s, sem.at[3]),
    ]
    kv_loads = [begin(kv_ref.at[at_ref[SOURCES + j]], kv_s.at[j], kv_sem.at[j]) for j in range(block_count)]
    g_loads = [begin(g_mine, g_s.at[0], sem.at[4]), begin(g_recv, g_s.at[1], sem.at[5])]
    for load in loads:
        load.wait()
    rows_low = row_s[...].astype(jnp.bfloat16)
    hidden = jnp.concatenate([rows_low, jnp.zeros((HD - 8, 2 * rows), jnp.bfloat16)], axis=0)
    stores = []
    for head in range(head_count):
        cols = slice(head * HD, (head + 1) * HD)
        vcols = slice(feats + head * HD, feats + (head + 1) * HD)
        q_t = jnp.concatenate(
            [jnp.transpose(q_s[0, :, cols]), jnp.transpose(q_s[1, :, cols])], axis=1
        )
        q_t = jnp.concatenate([q_t, hidden], axis=0)
        top = jnp.full((1, 2 * rows), MASKED, jnp.float32)
        for j in range(block_count):
            if head == 0:
                kv_loads[j].wait()
            keys = slice(j * rows, (j + 1) * rows)
            scores = product(jnp.concatenate([kv_s[j, :, cols], mask_s[keys, :]], axis=1), q_t)
            s_ref[keys, :] = scores
            top = jnp.maximum(top, jnp.max(scores, axis=0, keepdims=True))
        total = jnp.zeros((1, 2 * rows), jnp.float32)
        attn_t = jnp.zeros((HD, 2 * rows), jnp.float32)
        for j in range(block_count):
            keys = slice(j * rows, (j + 1) * rows)
            weights = jnp.exp((s_ref[keys, :] - top) * score_scale)
            total = total + jnp.sum(weights, axis=0, keepdims=True)
            low = weights.astype(jnp.bfloat16)
            e_s[head, keys, :] = low
            stores.append(
                begin(e_s.at[head, keys], e_out.at[head, keys], e_sem.at[head * block_count + j])
            )
            attn_t = attn_t + product(jnp.transpose(kv_s[j, :, vcols]), low)
        inverse = 1.0 / total
        inv_s[head : head + 1, :] = inverse
        attn_low = (attn_t * inverse).astype(jnp.bfloat16)
        attn_s[0, cols, :] = attn_low[:, :rows]
        attn_s[1, cols, :] = attn_low[:, rows:]
        if head == 0:
            for load in g_loads:
                load.wait()
        if head == head_count - 1:
            stores.append(begin(attn_s.at[0], attn_mine, out_sem.at[0]))
            stores.append(begin(attn_s.at[1], attn_theirs, out_sem.at[1]))
            stores.append(begin(inv_s, inv_out, out_sem.at[2]))
        g_t = jnp.concatenate([g_s[0, cols, :], g_s[1, cols, :]], axis=1).astype(jnp.float32)
        grad = jnp.transpose((g_t * inverse).astype(jnp.bfloat16))
        for j in range(block_count):
            keys = slice(j * rows, (j + 1) * rows)
            part_s[j, :, cols] = product(e_s[head, keys, :], grad).astype(jnp.bfloat16)
            if head == head_count - 1:
                target = part_outs[j // INNER].at[j % INNER]
                stores.append(begin(part_s.at[j], target, part_sem.at[j]))
    for store in stores:
        store.wait()


def forward(at, queries, q_recv, key_mask, row_mask, g_mine, g_recv, kv_all, after=()):
    block_count = kv_all.shape[0]
    rows, feats = q_recv.shape
    heads = feats // HD
    keys = block_count * rows
    outer = block_count // INNER
    out = call(
        functools.partial(forward_kernel, block_count, heads),
        [
            bf16(heads, keys, 2 * rows),
            f32(max(heads, 8), 2 * rows),
            bf16(feats, rows),
            bf16(feats, rows),
        ]
        + [bf16(INNER, rows, feats)] * outer,
        [SMEM] + [ANY] * 7,
        [ANY] * (4 + outer),
        [
            pltpu.VMEM((2, rows, feats), jnp.bfloat16),
            pltpu.VMEM((2, feats, rows), jnp.bfloat16),
            pltpu.VMEM((keys, HD), jnp.bfloat16),
            pltpu.VMEM((block_count, rows, 2 * feats), jnp.bfloat16),
            pltpu.VMEM((heads, keys, 2 * rows), jnp.bfloat16),
            pltpu.VMEM((keys, 2 * rows), jnp.float32),
            pltpu.VMEM((2, feats, rows), jnp.bfloat16),
            pltpu.VMEM((max(heads, 8), 2 * rows), jnp.float32),
            pltpu.VMEM((8, 2 * rows), jnp.float32),
            pltpu.VMEM((block_count, rows, feats), jnp.bfloat16),
            pltpu.SemaphoreType.DMA((6,)),
            pltpu.SemaphoreType.DMA((block_count,)),
            pltpu.SemaphoreType.DMA((heads * block_count,)),
            pltpu.SemaphoreType.DMA((3,)),
            pltpu.SemaphoreType.DMA((block_count,)),
        ],
        8,
        "forward",
        after,
    )(at, queries, q_recv, key_mask, row_mask, g_mine, g_recv, kv_all)
    return out[0], out[1], out[2], out[3], out[4:]


def key_terms_kernel(block_count, at_ref, q_ref, q_recv, g_mine, g_recv, attn_mine, attn_theirs, *refs):
    inv_ref, e_ref = refs[:2]
    kv_ref, refs = refs[2], refs[3:]
    outer = block_count // INNER
    dq_mine, dq_theirs = refs[:2]
    part_outs, refs = refs[2 : 2 + outer], refs[2 + outer :]
    q_s, t_s, inv_s, kv_s, e_s, part_s, dq_s, sem, kv_sem, e_sem, part_sem, dq_sem = refs
    rows, feats = q_recv.shape
    head_count = feats // HD
    score_scale = HD ** (-0.5)
    mine = pl.ds(pl.multiple_of(at_ref[0] * feats, feats), feats)
    loads = [begin(q_ref.at[:, mine], q_s.at[0], sem.at[0]), begin(q_recv, q_s.at[1], sem.at[1])]
    for index, held in enumerate((g_mine, g_recv, attn_mine, attn_theirs)):
        loads.append(begin(held, t_s.at[index], sem.at[2 + index]))
    loads.append(begin(inv_ref, inv_s, sem.at[6]))
    kv_loads, e_loads, stores = [], {}, []
    for j in range(block_count):
        keys = slice(j * rows, (j + 1) * rows)
        kv_loads.append(begin(kv_ref.at[at_ref[SOURCES + j]], kv_s.at[j], kv_sem.at[j]))
        for head in range(head_count):
            e_loads[head, j] = begin(
                e_ref.at[head, keys], e_s.at[head, keys], e_sem.at[head * block_count + j]
            )
    for load in loads:
        load.wait()
    for head in range(head_count):
        cols = slice(head * HD, (head + 1) * HD)
        vcols = slice(feats + head * HD, feats + (head + 1) * HD)
        inverse = inv_s[head : head + 1, :]
        g_t = jnp.concatenate([t_s[0, cols, :], t_s[1, cols, :]], axis=1).astype(jnp.float32)
        attn_t = jnp.concatenate([t_s[2, cols, :], t_s[3, cols, :]], axis=1)
        row_dot = jnp.sum(g_t * attn_t.astype(jnp.float32), axis=0, keepdims=True) * inverse
        g_t = (g_t * inverse).astype(jnp.bfloat16)
        query = jnp.concatenate([q_s[0, :, cols], q_s[1, :, cols]], axis=0)
        dq_t = jnp.zeros((HD, 2 * rows), jnp.float32)
        for j in range(block_count):
            keys = slice(j * rows, (j + 1) * rows)
            if head == 0:
                kv_loads[j].wait()
            e_loads[head, j].wait()
            dprobs = product(kv_s[j, :, vcols], g_t)
            dscore = (e_s[head, keys, :].astype(jnp.float32) * (dprobs - row_dot)).astype(
                jnp.bfloat16
            )
            dq_t = dq_t + product(jnp.transpose(kv_s[j, :, cols]), dscore)
            part_s[j, :, cols] = (score_scale * product(dscore, query)).astype(jnp.bfloat16)
            if head == head_count - 1:
                target = part_outs[j // INNER].at[j % INNER]
                stores.append(begin(part_s.at[j], target, part_sem.at[j]))
        dquery = (score_scale * jnp.transpose(dq_t)).astype(jnp.bfloat16)
        dq_s[0, :, cols] = dquery[:rows]
        dq_s[1, :, cols] = dquery[rows:]
    stores.append(begin(dq_s.at[0], dq_mine, dq_sem.at[0]))
    stores.append(begin(dq_s.at[1], dq_theirs, dq_sem.at[1]))
    for store in stores:
        store.wait()


def key_terms(at, queries, q_recv, g_mine, g_recv, attn_mine, attn_theirs, inverse, weights, kv_all, after):
    block_count = kv_all.shape[0]
    rows, feats = q_recv.shape
    heads = feats // HD
    keys = block_count * rows
    outer = block_count // INNER
    out = call(
        functools.partial(key_terms_kernel, block_count),
        [bf16(rows, feats)] * 2 + [bf16(INNER, rows, feats)] * outer,
        [SMEM] + [ANY] * 9,
        [ANY] * (2 + outer),
        [
            pltpu.VMEM((2, rows, feats), jnp.bfloat16),
            pltpu.VMEM((4, feats, rows), jnp.bfloat16),
            pltpu.VMEM(inverse.shape, jnp.float32),
            pltpu.VMEM((block_count, rows, 2 * feats), jnp.bfloat16),
            pltpu.VMEM((heads, keys, 2 * rows), jnp.bfloat16),
            pltpu.VMEM((block_count, rows, feats), jnp.bfloat16),
            pltpu.VMEM((2, rows, feats), jnp.bfloat16),
            pltpu.SemaphoreType.DMA((7,)),
            pltpu.SemaphoreType.DMA((block_count,)),
            pltpu.SemaphoreType.DMA((heads * block_count,)),
            pltpu.SemaphoreType.DMA((block_count,)),
            pltpu.SemaphoreType.DMA((2,)),
        ],
        7,
        "key_terms",
        after,
    )(at, queries, q_recv, g_mine, g_recv, attn_mine, attn_theirs, inverse, weights, kv_all)
    return out[0], out[1], out[2:]


def grad_heads_kernel(part_count, sends, picked, columns_at, send_at, at_ref, first_ref, weight_ref, *refs):
    grads, refs = refs[:part_count], refs[part_count:]
    outs, refs = refs[: 2 + sends], refs[2 + sends :]
    first_s, grad_s, weight_s, out_s, first_sem, weight_sem, grad_sem, send_sem, out_sem = refs
    half = out_s.shape[1]
    width = grads[0].shape[1]
    first_load = begin(first_ref, first_s, first_sem)
    weight_loads, grad_loads = [], []
    for k in range(part_count):
        grad_loads.append(begin(grads[k], grad_s.at[k], grad_sem.at[k]))
        if k:
            start = pl.multiple_of(at_ref[columns_at + k - 1] * width, width)
            columns = weight_ref.at[:, pl.ds(start, width)]
            weight_loads.append(begin(columns, weight_s.at[k - 1], weight_sem.at[k - 1]))
    for load in grad_loads:
        load.wait()
    copies = []
    for send in range(sends):
        for i in range(picked):
            place = send * picked + i
            target = outs[2 + send].at[:, i * width : (i + 1) * width]
            for k in range(part_count):

                @pl.when(at_ref[send_at + place] == k)
                def _():
                    begin(grad_s.at[k], target, send_sem.at[place])

            copies.append(pltpu.make_async_copy(grad_s.at[0], target, send_sem.at[place]))
    first_load.wait()
    summed = first_s[...]
    for k in range(1, part_count):
        weight_loads[k - 1].wait()
        summed = summed + against(weight_s[k - 1], grad_s[k])
    first_s[...] = summed
    for side, at in enumerate((at_ref[0], 1 - at_ref[0])):
        kept = first_s[pl.ds(pl.multiple_of(at * half, half), half), :]
        out_s[side] = kept.astype(jnp.bfloat16)
        copies.append(begin(out_s.at[side], outs[side], out_sem.at[side]))
    for copy in copies:
        copy.wait()


def grad_heads(at, columns_at, send_at, first, out_weight, grads, sends, picked):
    feats, rows = first.shape
    half = feats // INNER
    count = len(grads)
    width = grads[0].shape[1]
    out = call(
        functools.partial(grad_heads_kernel, count, sends, picked, columns_at, send_at),
        [bf16(half, rows), bf16(half, rows)] + [bf16(rows, picked * width)] * sends,
        [SMEM] + [ANY] * (2 + count),
        [ANY] * (2 + sends),
        [
            pltpu.VMEM((feats, rows), jnp.float32),
            pltpu.VMEM((count, rows, width), jnp.bfloat16),
            pltpu.VMEM((count - 1, feats, width), jnp.bfloat16),
            pltpu.VMEM((INNER, half, rows), jnp.bfloat16),
            pltpu.SemaphoreType.DMA,
            pltpu.SemaphoreType.DMA((count - 1,)),
            pltpu.SemaphoreType.DMA((count,)),
            pltpu.SemaphoreType.DMA((sends * picked,)),
            pltpu.SemaphoreType.DMA((INNER,)),
        ],
        3,
        "grad_heads",
    )(at, first, out_weight, *grads)
    return out[0], out[1], out[2:]


def weight_kernel(part_count, doc_count, sent, step_at, at_ref, *refs):
    attn, refs = refs[: INNER * doc_count], refs[INNER * doc_count :]
    grads, refs = refs[:part_count], refs[part_count:]
    swapped, refs = refs[: doc_count - 1], refs[doc_count - 1 :]
    out, attn_s, grad_s, out_s, attn_sem, grad_sem, out_sem = refs
    outer, feats, width = out.shape
    half = feats // INNER
    piece = grads[0].shape[1]
    pieces = piece // width
    here = (1 - at_ref[0]) if sent else at_ref[0]
    attn_loads, grad_loads = [], []
    for doc in range(doc_count):
        for side in range(INNER):
            at = (1 - at_ref[0]) if side else at_ref[0]
            index = doc * INNER + side
            target = attn_s.at[doc, pl.ds(pl.multiple_of(at * half, half), half)]
            attn_loads.append(begin(attn[index], target, attn_sem.at[index]))
    for k in range(outer):
        place = lax.rem(at_ref[1] + k, outer) * INNER + here
        which = at_ref[step_at + place // pieces]
        cols = pl.ds(pl.multiple_of(lax.rem(place, pieces) * width, width), width)
        for i in range(part_count):

            @pl.when(which == i)
            def _():
                begin(grads[i].at[:, cols], grad_s.at[0, k], grad_sem.at[k])

        loads = [pltpu.make_async_copy(grads[0].at[:, cols], grad_s.at[0, k], grad_sem.at[k])]
        cols = pl.ds(pl.multiple_of(place * width, width), width)
        for doc in range(1, doc_count):
            source = swapped[doc - 1].at[:, cols]
            loads.append(begin(source, grad_s.at[doc, k], grad_sem.at[doc * outer + k]))
        grad_loads.append(loads)
    for load in attn_loads:
        load.wait()
    stores = []
    for k in range(outer):
        term = 0.0
        for doc in range(doc_count):
            grad_loads[k][doc].wait()
            term = term + product(attn_s[doc], grad_s[doc, k])
        out_s[k] = term.astype(out_s.dtype)
        stores.append(begin(out_s.at[k], out.at[k], out_sem.at[k]))
    for store in stores:
        store.wait()


def weight_terms(at, step_at, attn, grads, swapped, outer, picked, sent, after=()):
    half, rows = attn[0].shape
    feats = half * INNER
    doc_count = len(attn) // INNER
    width = picked * grads[0].shape[1] // (outer * INNER)
    return call(
        functools.partial(weight_kernel, len(grads), doc_count, sent, step_at),
        bf16(outer, feats, width),
        [SMEM] + [ANY] * (len(attn) + len(grads) + len(swapped)),
        ANY,
        [
            pltpu.VMEM((doc_count, feats, rows), jnp.bfloat16),
            pltpu.VMEM((doc_count, outer, rows, width), jnp.bfloat16),
            pltpu.VMEM((outer, feats, width), jnp.bfloat16),
            pltpu.SemaphoreType.DMA((len(attn),)),
            pltpu.SemaphoreType.DMA((doc_count * outer,)),
            pltpu.SemaphoreType.DMA((outer,)),
        ],
        3,
        "weight_sent" if sent else "weight_kept",
        after,
    )(at, *attn, *grads, *swapped)


def weight_add_kernel(keep, recv, *refs):
    outer = keep.shape[0]
    outs, (held_s, out_s, sem, out_sem) = refs[:outer], refs[outer:]
    loads = []
    for k in range(outer):
        for index, held in enumerate((keep, recv)):
            loads.append(begin(held.at[k], held_s.at[index, k], sem.at[2 * k + index]))
    stores = []
    for k in range(outer):
        loads[2 * k].wait()
        loads[2 * k + 1].wait()
        summed = held_s[0, k].astype(jnp.float32) + held_s[1, k].astype(jnp.float32)
        out_s[k] = summed.astype(jnp.bfloat16)
        stores.append(begin(out_s.at[k], outs[k], out_sem.at[k]))
    for store in stores:
        store.wait()


def weight_add(keep, recv):
    outer, feats, width = keep.shape
    return call(
        weight_add_kernel,
        [bf16(feats, width)] * outer,
        [ANY] * 2,
        [ANY] * outer,
        [
            pltpu.VMEM((2, outer, feats, width), jnp.bfloat16),
            pltpu.VMEM((outer, feats, width), jnp.bfloat16),
            pltpu.SemaphoreType.DMA((2 * outer,)),
            pltpu.SemaphoreType.DMA((outer,)),
        ],
        1.5,
        "weight_add",
    )(keep, recv)


def add_kernel(count, *refs):
    terms, (mine, theirs) = refs[: 2 * count], refs[2 * count : 2 * count + 2]
    terms_s, out_s, term_sem, out_sem = refs[2 * count + 2 :]
    half = terms[0].shape[2]
    loads = {}
    for side in (1, 0):
        for c, held in enumerate(terms):
            sem = term_sem.at[c * INNER + side]
            loads[side, c] = begin(held.at[side], terms_s.at[c, side], sem)
    stores = []
    for side, out in ((1, theirs), (0, mine)):
        for kind in range(2):
            summed = 0.0
            for c in range(kind * count, (kind + 1) * count):
                loads[side, c].wait()
                summed = summed + terms_s[c, side].astype(jnp.float32)
            out_s[side, :, kind * half : (kind + 1) * half] = summed.astype(jnp.bfloat16)
        stores.append(begin(out_s.at[side], out, out_sem.at[side]))
    for store in stores:
        store.wait()


def add_terms(key_parts, value_parts, after):
    _, rows, half = key_parts[0].shape
    count = len(key_parts)
    return call(
        functools.partial(add_kernel, count),
        [bf16(rows, 2 * half)] * 2,
        [ANY] * (2 * count),
        [ANY] * 2,
        [
            pltpu.VMEM((2 * count, INNER, rows, half), jnp.bfloat16),
            pltpu.VMEM((INNER, rows, 2 * half), jnp.bfloat16),
            pltpu.SemaphoreType.DMA((2 * count * INNER,)),
            pltpu.SemaphoreType.DMA((INNER,)),
        ],
        2,
        "add_terms",
        after,
    )(*key_parts, *value_parts)


def join_kernel(at_ref, dq_mine, dq_recv, mine, recv, *refs):
    outs, (held_s, out_s, sem, out_sem) = refs[:3], refs[3:]
    half = dq_mine.shape[1]
    loads = [
        begin(dq_mine, held_s.at[0, 0], sem.at[0]),
        begin(dq_recv, held_s.at[1, 0], sem.at[1]),
    ]
    for side, held in enumerate((mine, recv)):
        for index in range(2):
            source = held.at[:, index * half : (index + 1) * half]
            loads.append(begin(source, held_s.at[side, 1 + index], sem.at[2 + 2 * side + index]))
    for load in loads:
        load.wait()
    stores = []
    for index, out in enumerate(outs):
        for side, at in enumerate((at_ref[0], 1 - at_ref[0])):
            cols = pl.ds(pl.multiple_of(at * half, half), half)
            out_s[index, :, cols] = held_s[side, index]
        stores.append(begin(out_s.at[index], out, out_sem.at[index]))
    for store in stores:
        store.wait()


def join_heads(at, dq_mine, dq_recv, mine, recv):
    rows, half = dq_mine.shape
    return call(
        join_kernel,
        [bf16(rows, INNER * half)] * 3,
        [SMEM] + [ANY] * 4,
        [ANY] * 3,
        [
            pltpu.VMEM((INNER, 3, rows, half), jnp.bfloat16),
            pltpu.VMEM((3, rows, INNER * half), jnp.bfloat16),
            pltpu.SemaphoreType.DMA((6,)),
            pltpu.SemaphoreType.DMA((3,)),
        ],
        2,
        "join_heads",
    )(at, dq_mine, dq_recv, mine, recv)


def per_device(
    queries, key_heads, value_heads, grad_output, out_weight, block_pattern, global_offsets
):
    dp_count, ctx_count, tp_count = (lax.axis_size(name) for name in ("dp", "ctx", "tp"))
    dp_at, ctx_at, tp_at = (lax.axis_index(name) for name in ("dp", "ctx", "tp"))
    outer = ctx_count // INNER
    outer_at, inner_at = ctx_at // INNER, ctx_at % INNER
    picked = tp_count // dp_count

    def ctx_pairs(step, side, dp_step=0):
        moved = [(c + step * INNER) % ctx_count ^ side for c in range(ctx_count)]
        if not dp_step:
            return list(enumerate(moved))
        return [
            (d * ctx_count + c, (d + dp_step) % dp_count * ctx_count + moved[c])
            for d in range(dp_count)
            for c in range(ctx_count)
        ]

    def shift_pairs(count, step):
        return [(i, (i + step) % count) for i in range(count)]

    def dp_steps(which):
        return [(which * picked + i - tp_at) % tp_count for i in range(picked)]

    routes = [(step, side) for step in range(outer) for side in range(INNER)]
    sources = [
        ((outer_at - step) % outer) * INNER + (inner_at + side) % INNER for step, side in routes
    ]
    scalars = [inner_at, outer_at, tp_at] + sources
    columns_at = len(scalars)
    scalars = scalars + [(tp_at + step) % tp_count for step in range(1, tp_count)]
    send_at = len(scalars)
    for step in range(1, dp_count):
        scalars = scalars + dp_steps((dp_at + step) % dp_count)
    keep_at = len(scalars)
    at = jnp.stack(scalars + dp_steps(dp_at))

    grad_own = grad_output[0]
    grads = [grad_own] + [
        lax.ppermute(grad_own, "tp", shift_pairs(tp_count, -step)) for step in range(1, tp_count)
    ]
    kv_send, q_theirs = part_heads(at, queries[0], key_heads[0], value_heads[0], ctx_count)
    kv_all = lax.all_to_all(kv_send, "ctx", split_axis=0, concat_axis=0, tiled=True)
    q_recv = lax.ppermute(q_theirs, "ctx", ctx_pairs(0, 1))
    first, key_mask, row_mask = prelude(
        at, block_pattern, global_offsets, grad_own, out_weight, (q_theirs,)
    )
    g_mine, g_theirs, grad_sends = grad_heads(
        at, columns_at, send_at, first, out_weight, grads, dp_count - 1, picked
    )
    g_recv = lax.ppermute(g_theirs, "ctx", ctx_pairs(0, 1))
    swapped = [
        lax.ppermute(send, "dp", shift_pairs(dp_count, step + 1))
        for step, send in enumerate(grad_sends)
    ]

    weights, inverse, attn_mine, attn_theirs, value_parts = forward(
        at, queries[0], q_recv, key_mask, row_mask, g_mine, g_recv, kv_all
    )

    attn = []
    for step in range(dp_count):
        for held, side in ((attn_mine, 0), (attn_theirs, 1)):
            pairs = ctx_pairs(0, side, step)
            axes = ("dp", "ctx") if step else "ctx"
            attn.append(lax.ppermute(held, axes, pairs) if step or side else held)

    def returned(parts):
        return [
            lax.ppermute(part, "ctx", ctx_pairs(-step, 0)) if step else part
            for step, part in enumerate(parts)
        ]

    value_parts = returned(value_parts)
    send = weight_terms(at, keep_at, attn, grads, swapped, outer, picked, True)
    weight_recv = lax.ppermute(send, "ctx", ctx_pairs(0, 1))
    dq_mine, dq_theirs, key_parts = key_terms(
        at, queries[0], q_recv, g_mine, g_recv, attn_mine, attn_theirs, inverse, weights, kv_all, (send,)
    )
    key_parts = returned(key_parts)
    dq_recv = lax.ppermute(dq_theirs, "ctx", ctx_pairs(0, 1))
    keep = weight_terms(at, keep_at, attn, grads, swapped, outer, picked, False, (dq_mine, *value_parts[1:]))
    weight_sums = weight_add(keep, weight_recv)
    grad_weight = weight_sums[0].astype(jnp.float32)
    for step in range(1, outer):
        grad_weight = grad_weight + lax.ppermute(
            weight_sums[step], "ctx", ctx_pairs(step, 0)
        ).astype(jnp.float32)

    terms_mine, terms_theirs = add_terms(key_parts, value_parts, (weight_sums[0],))
    terms_recv = lax.ppermute(terms_theirs, "ctx", ctx_pairs(0, 1))
    grad_q, grad_k, grad_v = join_heads(at, dq_mine, dq_recv, terms_mine, terms_recv)
    return grad_q[None], grad_k[None], grad_v[None], grad_weight.astype(jnp.bfloat16)


def solution(mesh):
    in_specs = (
        P("dp", "ctx", "tp"),
        P("dp", "ctx", "tp"),
        P("dp", "ctx", "tp"),
        P("dp", "ctx", "tp"),
        P("tp", None),
        P(),
        P(),
    )
    out_specs = (
        P("dp", "ctx", "tp"),
        P("dp", "ctx", "tp"),
        P("dp", "ctx", "tp"),
        P("tp", ("dp", "ctx")),
    )
    return jax.shard_map(
        per_device, mesh=mesh, in_specs=in_specs, out_specs=out_specs, check_vma=False
    )
```

```python
import functools

import jax
import jax.numpy as jnp
from jax import lax
from jax.experimental import pallas as pl
from jax.experimental.pallas import tpu as pltpu
from jax.sharding import PartitionSpec as P

HD = 128
MASKED = -1e30
INNER = 2
SOURCES = 3
ANY = pl.BlockSpec(memory_space=pl.ANY)
VMEM = pl.BlockSpec(memory_space=pltpu.VMEM)
SMEM = pl.BlockSpec(memory_space=pltpu.SMEM)


def against(left_op, right_op):
    return lax.dot_general(
        left_op, right_op, (((1,), (1,)), ((), ())), preferred_element_type=jnp.float32
    )


def product(left_op, right_op):
    return jnp.dot(left_op, right_op, preferred_element_type=jnp.float32)


def begin(source, target, semaphore):
    copy = pltpu.make_async_copy(source, target, semaphore)
    copy.start()
    return copy


def call(kernel, out_shape, in_specs, out_specs, scratch, micros, name, after=()):
    skipped = len(after)
    in_specs = [ANY] * skipped + in_specs
    run = pl.pallas_call(
        lambda *refs: kernel(*refs[skipped:]),
        out_shape=out_shape,
        in_specs=in_specs,
        out_specs=out_specs,
        scratch_shapes=scratch,
        compiler_params=pltpu.CompilerParams(vmem_limit_bytes=60 * 1024 * 1024),
        cost_estimate=pl.CostEstimate(
            flops=int(micros * 1e9), bytes_accessed=int(micros * 3e6), transcendentals=0
        ),
        name=name,
    )

    def placed(*args):
        args = [
            pltpu.with_memory_space_constraint(arg, pltpu.HBM) if spec is ANY else arg
            for spec, arg in zip(in_specs, (*after, *args))
        ]
        return run(*args)

    return placed


def bf16(*shape):
    return pltpu.HBM(shape, jnp.bfloat16)


def f32(*shape):
    return pltpu.HBM(shape, jnp.float32)


def part_kernel(at_ref, k_ref, v_ref, kv_mine, kv_theirs, held_s, in_sem, out_sem):
    half = kv_mine.shape[1] // 2
    loads = [begin(held, held_s.at[i], in_sem.at[i]) for i, held in enumerate((k_ref, v_ref))]
    mine = pl.ds(pl.multiple_of(at_ref[0] * half, half), half)
    theirs = pl.ds(pl.multiple_of((1 - at_ref[0]) * half, half), half)
    copies = []
    for index in range(2):
        loads[index].wait()
        place = slice(index * half, (index + 1) * half)
        for side, (cols, out) in enumerate(((mine, kv_mine), (theirs, kv_theirs))):
            sem = out_sem.at[2 * index + side]
            copies.append(begin(held_s.at[index, :, cols], out.at[:, place], sem))
    for copy in copies:
        copy.wait()


def part_heads(at, keys, values):
    rows, feats = keys.shape
    return call(
        part_kernel,
        [bf16(rows, feats), bf16(rows, feats)],
        [SMEM] + [ANY] * 2,
        [ANY] * 2,
        [
            pltpu.VMEM((2, rows, feats), jnp.bfloat16),
            pltpu.SemaphoreType.DMA((2,)),
            pltpu.SemaphoreType.DMA((4,)),
        ],
        2,
        "part_heads",
    )(at, keys, values)


def prelude_kernel(at_ref, pattern, offsets, q_ref, grad_ref, weight_ref, *refs):
    first, key_mask, row_mask, q_theirs = refs[:4]
    grad_s, weight_s, first_s, mask_s, row_s, q_s, sem, out_sem = refs[4:]
    half = q_theirs.shape[1]
    theirs = pl.ds(pl.multiple_of((1 - at_ref[0]) * half, half), half)
    q_load = begin(q_ref.at[:, theirs], q_s, sem.at[2])
    rows, width = grad_s.shape
    block_count, glob_count = offsets.shape
    start = pl.multiple_of(at_ref[2] * width, width)
    loads = [
        begin(grad_ref, grad_s, sem.at[0]),
        begin(weight_ref.at[:, pl.ds(start, width)], weight_s, sem.at[1]),
    ]
    q_load.wait()
    stores = [begin(q_s, q_theirs, out_sem.at[3])]
    own = at_ref[1] * INNER + at_ref[0]
    partner = at_ref[1] * INNER + 1 - at_ref[0]
    lane = lax.broadcasted_iota(jnp.int32, (1, HD), 1)
    row_at = lax.broadcasted_iota(jnp.int32, (rows, HD), 0)
    col_at = lax.broadcasted_iota(jnp.int32, (8, rows), 1)
    group_at = lax.broadcasted_iota(jnp.int32, (8, rows), 0)
    for index in range(block_count):
        block = at_ref[SOURCES + index]
        hidden = []
        for target in (own, partner):
            seen = jnp.abs(block - target) <= 1
            for r in range(pattern.shape[1]):
                seen = seen | (pattern[target, r] == block)
            hidden.append(jnp.where(seen, 0, 1))
        lane_hidden = jnp.where(lane == 0, hidden[0], jnp.where(lane == 1, hidden[1], 0))
        hidden_rows = jnp.broadcast_to(lane_hidden, (rows, HD))
        for r in range(glob_count):
            hidden_rows = jnp.where(row_at == offsets[block, r], 0, hidden_rows)
        mask_s[index * rows : (index + 1) * rows, :] = hidden_rows.astype(jnp.float32).astype(
            jnp.bfloat16
        )
    for group, target in enumerate((own, partner)):
        local = jnp.where(group_at == group, MASKED, 0.0)
        for r in range(glob_count):
            local = jnp.where(col_at == offsets[target, r], 0.0, local)
        row_s[:, group * rows : (group + 1) * rows] = local
    stores.append(begin(mask_s, key_mask, out_sem.at[0]))
    stores.append(begin(row_s, row_mask, out_sem.at[1]))
    for load in loads:
        load.wait()
    first_s[...] = against(weight_s[...], grad_s[...])
    stores.append(begin(first_s, first, out_sem.at[2]))
    for store in stores:
        store.wait()


def prelude(at, pattern, offsets, queries, grad_own, out_weight, after):
    rows, width = grad_own.shape
    feats = out_weight.shape[0]
    keys = offsets.shape[0] * rows
    half = queries.shape[1] // INNER
    return call(
        prelude_kernel,
        [
            f32(feats, rows),
            bf16(keys, HD),
            f32(8, 2 * rows),
            bf16(rows, half),
        ],
        [SMEM] * 3 + [ANY] * 3,
        [ANY] * 4,
        [
            pltpu.VMEM((rows, width), jnp.bfloat16),
            pltpu.VMEM((feats, width), jnp.bfloat16),
            pltpu.VMEM((feats, rows), jnp.float32),
            pltpu.VMEM((keys, HD), jnp.bfloat16),
            pltpu.VMEM((8, 2 * rows), jnp.float32),
            pltpu.VMEM((rows, half), jnp.bfloat16),
            pltpu.SemaphoreType.DMA((3,)),
            pltpu.SemaphoreType.DMA((4,)),
        ],
        4,
        "prelude",
        after,
    )(at, pattern, offsets, queries, grad_own, out_weight)


def forward_kernel(block_count, head_count, at_ref, q_ref, q_recv, key_mask, row_mask, *refs):
    g_mine, g_recv = refs[:2]
    kv_refs, refs = refs[2 : 2 + block_count], refs[2 + block_count :]
    e_out, inv_out, attn_mine, attn_theirs = refs[:4]
    part_out, refs = refs[4], refs[5:]
    q_s, g_s, mask_s, kv_s, e_s, s_ref, attn_s, inv_s, row_s, part_s = refs[:10]
    sem, kv_sem, e_sem, out_sem, part_sem = refs[10:]
    rows = q_recv.shape[0]
    feats = head_count * HD
    score_scale = HD ** (-0.5)
    mine = pl.ds(pl.multiple_of(at_ref[0] * feats, feats), feats)
    loads = [
        begin(q_ref.at[:, mine], q_s.at[0], sem.at[0]),
        begin(q_recv, q_s.at[1], sem.at[1]),
        begin(key_mask, mask_s, sem.at[2]),
        begin(row_mask, row_s, sem.at[3]),
    ]
    kv_loads = [begin(kv_refs[j], kv_s.at[j], kv_sem.at[j]) for j in range(block_count)]
    g_loads = [begin(g_mine, g_s.at[0], sem.at[4]), begin(g_recv, g_s.at[1], sem.at[5])]
    for load in loads:
        load.wait()
    rows_low = row_s[...].astype(jnp.bfloat16)
    hidden = jnp.concatenate([rows_low, jnp.zeros((HD - 8, 2 * rows), jnp.bfloat16)], axis=0)
    stores = []
    for head in range(head_count):
        cols = slice(head * HD, (head + 1) * HD)
        vcols = slice(feats + head * HD, feats + (head + 1) * HD)
        q_t = jnp.concatenate(
            [jnp.transpose(q_s[0, :, cols]), jnp.transpose(q_s[1, :, cols])], axis=1
        )
        q_t = jnp.concatenate([q_t, hidden], axis=0)
        top = jnp.full((1, 2 * rows), MASKED, jnp.float32)
        for j in range(block_count):
            if head == 0:
                kv_loads[j].wait()
            keys = slice(j * rows, (j + 1) * rows)
            scores = product(jnp.concatenate([kv_s[j, :, cols], mask_s[keys, :]], axis=1), q_t)
            s_ref[keys, :] = scores
            top = jnp.maximum(top, jnp.max(scores, axis=0, keepdims=True))
        total = jnp.zeros((1, 2 * rows), jnp.float32)
        attn_t = jnp.zeros((HD, 2 * rows), jnp.float32)
        for j in range(block_count):
            keys = slice(j * rows, (j + 1) * rows)
            weights = jnp.exp((s_ref[keys, :] - top) * score_scale)
            total = total + jnp.sum(weights, axis=0, keepdims=True)
            low = weights.astype(jnp.bfloat16)
            e_s[head, keys, :] = low
            stores.append(
                begin(e_s.at[head, keys], e_out.at[head, keys], e_sem.at[head * block_count + j])
            )
            attn_t = attn_t + product(jnp.transpose(kv_s[j, :, vcols]), low)
        inverse = 1.0 / total
        inv_s[head : head + 1, :] = inverse
        attn_low = (attn_t * inverse).astype(jnp.bfloat16)
        attn_s[0, cols, :] = attn_low[:, :rows]
        attn_s[1, cols, :] = attn_low[:, rows:]
        if head == 0:
            for load in g_loads:
                load.wait()
        if head == head_count - 1:
            stores.append(begin(attn_s.at[0], attn_mine, out_sem.at[0]))
            stores.append(begin(attn_s.at[1], attn_theirs, out_sem.at[1]))
            stores.append(begin(inv_s, inv_out, out_sem.at[2]))
        g_t = jnp.concatenate([g_s[0, cols, :], g_s[1, cols, :]], axis=1).astype(jnp.float32)
        grad = jnp.transpose((g_t * inverse).astype(jnp.bfloat16))
        for j in range(block_count):
            keys = slice(j * rows, (j + 1) * rows)
            part_s[j, :, cols] = product(e_s[head, keys, :], grad).astype(jnp.bfloat16)
            if head == head_count - 1:
                target = part_out.at[at_ref[SOURCES + j]]
                stores.append(begin(part_s.at[j], target, part_sem.at[j]))
    for store in stores:
        store.wait()


def forward(at, queries, q_recv, key_mask, row_mask, g_mine, g_recv, kv_blocks, after):
    block_count = len(kv_blocks)
    rows, feats = q_recv.shape
    heads = feats // HD
    keys = block_count * rows
    return call(
        functools.partial(forward_kernel, block_count, heads),
        [
            bf16(heads, keys, 2 * rows),
            f32(max(heads, 8), 2 * rows),
            bf16(feats, rows),
            bf16(feats, rows),
            bf16(block_count, rows, feats),
        ],
        [SMEM] + [ANY] * (6 + block_count),
        [ANY] * 5,
        [
            pltpu.VMEM((2, rows, feats), jnp.bfloat16),
            pltpu.VMEM((2, feats, rows), jnp.bfloat16),
            pltpu.VMEM((keys, HD), jnp.bfloat16),
            pltpu.VMEM((block_count, rows, 2 * feats), jnp.bfloat16),
            pltpu.VMEM((heads, keys, 2 * rows), jnp.bfloat16),
            pltpu.VMEM((keys, 2 * rows), jnp.float32),
            pltpu.VMEM((2, feats, rows), jnp.bfloat16),
            pltpu.VMEM((max(heads, 8), 2 * rows), jnp.float32),
            pltpu.VMEM((8, 2 * rows), jnp.float32),
            pltpu.VMEM((block_count, rows, feats), jnp.bfloat16),
            pltpu.SemaphoreType.DMA((6,)),
            pltpu.SemaphoreType.DMA((block_count,)),
            pltpu.SemaphoreType.DMA((heads * block_count,)),
            pltpu.SemaphoreType.DMA((3,)),
            pltpu.SemaphoreType.DMA((block_count,)),
        ],
        20,
        "forward",
        after,
    )(at, queries, q_recv, key_mask, row_mask, g_mine, g_recv, *kv_blocks)


def key_terms_kernel(block_count, at_ref, q_ref, q_recv, g_mine, g_recv, attn_mine, attn_theirs, *refs):
    inv_ref, e_ref = refs[:2]
    kv_refs, refs = refs[2 : 2 + block_count], refs[2 + block_count :]
    dq_mine, dq_theirs, part_out = refs[:3]
    refs = refs[3:]
    q_s, t_s, inv_s, kv_s, e_s, part_s, dq_s, sem, kv_sem, e_sem, part_sem, dq_sem = refs
    rows, feats = q_recv.shape
    head_count = feats // HD
    score_scale = HD ** (-0.5)
    mine = pl.ds(pl.multiple_of(at_ref[0] * feats, feats), feats)
    loads = [begin(q_ref.at[:, mine], q_s.at[0], sem.at[0]), begin(q_recv, q_s.at[1], sem.at[1])]
    for index, held in enumerate((g_mine, g_recv, attn_mine, attn_theirs)):
        loads.append(begin(held, t_s.at[index], sem.at[2 + index]))
    loads.append(begin(inv_ref, inv_s, sem.at[6]))
    kv_loads, e_loads, stores = [], {}, []
    for j in range(block_count):
        keys = slice(j * rows, (j + 1) * rows)
        kv_loads.append(begin(kv_refs[j], kv_s.at[j], kv_sem.at[j]))
        for head in range(head_count):
            e_loads[head, j] = begin(
                e_ref.at[head, keys], e_s.at[head, keys], e_sem.at[head * block_count + j]
            )
    for load in loads:
        load.wait()
    for head in range(head_count):
        cols = slice(head * HD, (head + 1) * HD)
        vcols = slice(feats + head * HD, feats + (head + 1) * HD)
        inverse = inv_s[head : head + 1, :]
        g_t = jnp.concatenate([t_s[0, cols, :], t_s[1, cols, :]], axis=1).astype(jnp.float32)
        attn_t = jnp.concatenate([t_s[2, cols, :], t_s[3, cols, :]], axis=1)
        row_dot = jnp.sum(g_t * attn_t.astype(jnp.float32), axis=0, keepdims=True) * inverse
        g_t = (g_t * inverse).astype(jnp.bfloat16)
        query = jnp.concatenate([q_s[0, :, cols], q_s[1, :, cols]], axis=0)
        dq_t = jnp.zeros((HD, 2 * rows), jnp.float32)
        for j in range(block_count):
            keys = slice(j * rows, (j + 1) * rows)
            if head == 0:
                kv_loads[j].wait()
            e_loads[head, j].wait()
            dprobs = product(kv_s[j, :, vcols], g_t)
            dscore = (e_s[head, keys, :].astype(jnp.float32) * (dprobs - row_dot)).astype(
                jnp.bfloat16
            )
            dq_t = dq_t + product(jnp.transpose(kv_s[j, :, cols]), dscore)
            part_s[j, :, cols] = (score_scale * product(dscore, query)).astype(jnp.bfloat16)
            if head == head_count - 1:
                target = part_out.at[at_ref[SOURCES + j]]
                stores.append(begin(part_s.at[j], target, part_sem.at[j]))
        dquery = (score_scale * jnp.transpose(dq_t)).astype(jnp.bfloat16)
        dq_s[0, :, cols] = dquery[:rows]
        dq_s[1, :, cols] = dquery[rows:]
    stores.append(begin(dq_s.at[0], dq_mine, dq_sem.at[0]))
    stores.append(begin(dq_s.at[1], dq_theirs, dq_sem.at[1]))
    for store in stores:
        store.wait()


def key_terms(at, queries, q_recv, g_mine, g_recv, attn_mine, attn_theirs, inverse, weights, kv_blocks, after):
    block_count = len(kv_blocks)
    rows, feats = q_recv.shape
    heads = feats // HD
    keys = block_count * rows
    return call(
        functools.partial(key_terms_kernel, block_count),
        [bf16(rows, feats)] * 2 + [bf16(block_count, rows, feats)],
        [SMEM] + [ANY] * (8 + block_count),
        [ANY] * 3,
        [
            pltpu.VMEM((2, rows, feats), jnp.bfloat16),
            pltpu.VMEM((4, feats, rows), jnp.bfloat16),
            pltpu.VMEM(inverse.shape, jnp.float32),
            pltpu.VMEM((block_count, rows, 2 * feats), jnp.bfloat16),
            pltpu.VMEM((heads, keys, 2 * rows), jnp.bfloat16),
            pltpu.VMEM((block_count, rows, feats), jnp.bfloat16),
            pltpu.VMEM((2, rows, feats), jnp.bfloat16),
            pltpu.SemaphoreType.DMA((7,)),
            pltpu.SemaphoreType.DMA((block_count,)),
            pltpu.SemaphoreType.DMA((heads * block_count,)),
            pltpu.SemaphoreType.DMA((block_count,)),
            pltpu.SemaphoreType.DMA((2,)),
        ],
        7,
        "key_terms",
        after,
    )(at, queries, q_recv, g_mine, g_recv, attn_mine, attn_theirs, inverse, weights, *kv_blocks)


def grad_heads_kernel(part_count, sends, picked, columns_at, send_at, at_ref, first_ref, weight_ref, *refs):
    grads, refs = refs[:part_count], refs[part_count:]
    outs, refs = refs[: 2 + sends], refs[2 + sends :]
    first_s, grad_s, weight_s, out_s, first_sem, weight_sem, grad_sem, send_sem, out_sem = refs
    half = out_s.shape[1]
    width = grads[0].shape[1]
    first_load = begin(first_ref, first_s, first_sem)
    weight_loads, grad_loads = [], []
    for k in range(part_count):
        grad_loads.append(begin(grads[k], grad_s.at[k], grad_sem.at[k]))
        if k:
            start = pl.multiple_of(at_ref[columns_at + k - 1] * width, width)
            columns = weight_ref.at[:, pl.ds(start, width)]
            weight_loads.append(begin(columns, weight_s.at[k - 1], weight_sem.at[k - 1]))
    for load in grad_loads:
        load.wait()
    copies = []
    for send in range(sends):
        for i in range(picked):
            place = send * picked + i
            target = outs[2 + send].at[:, i * width : (i + 1) * width]
            for k in range(part_count):

                @pl.when(at_ref[send_at + place] == k)
                def _():
                    begin(grad_s.at[k], target, send_sem.at[place])

            copies.append(pltpu.make_async_copy(grad_s.at[0], target, send_sem.at[place]))
    first_load.wait()
    summed = first_s[...]
    for k in range(1, part_count):
        weight_loads[k - 1].wait()
        summed = summed + against(weight_s[k - 1], grad_s[k])
    first_s[...] = summed
    for side, at in enumerate((at_ref[0], 1 - at_ref[0])):
        kept = first_s[pl.ds(pl.multiple_of(at * half, half), half), :]
        out_s[side] = kept.astype(jnp.bfloat16)
        copies.append(begin(out_s.at[side], outs[side], out_sem.at[side]))
    for copy in copies:
        copy.wait()


def grad_heads(at, columns_at, send_at, first, out_weight, grads, sends, picked):
    feats, rows = first.shape
    half = feats // INNER
    count = len(grads)
    width = grads[0].shape[1]
    out = call(
        functools.partial(grad_heads_kernel, count, sends, picked, columns_at, send_at),
        [bf16(half, rows), bf16(half, rows)] + [bf16(rows, picked * width)] * sends,
        [SMEM] + [ANY] * (2 + count),
        [ANY] * (2 + sends),
        [
            pltpu.VMEM((feats, rows), jnp.float32),
            pltpu.VMEM((count, rows, width), jnp.bfloat16),
            pltpu.VMEM((count - 1, feats, width), jnp.bfloat16),
            pltpu.VMEM((INNER, half, rows), jnp.bfloat16),
            pltpu.SemaphoreType.DMA,
            pltpu.SemaphoreType.DMA((count - 1,)),
            pltpu.SemaphoreType.DMA((count,)),
            pltpu.SemaphoreType.DMA((sends * picked,)),
            pltpu.SemaphoreType.DMA((INNER,)),
        ],
        3,
        "grad_heads",
    )(at, first, out_weight, *grads)
    return out[0], out[1], out[2:]


def weight_kernel(part_count, doc_count, sent, step_at, at_ref, *refs):
    attn, refs = refs[: INNER * doc_count], refs[INNER * doc_count :]
    grads, refs = refs[:part_count], refs[part_count:]
    swapped, refs = refs[: doc_count - 1], refs[doc_count - 1 :]
    if sent:
        out, refs = refs[0], refs[1:]
        outs = [out.at[k] for k in range(out.shape[0])]
    else:
        recv, refs = refs[0], refs[1:]
        outs, refs = refs[: recv.shape[0]], refs[recv.shape[0] :]
        recv_s, recv_sem, refs = refs[0], refs[1], refs[2:]
    attn_s, grad_s, out_s, attn_sem, grad_sem, out_sem = refs
    outer, feats, width = out_s.shape
    half = feats // INNER
    piece = grads[0].shape[1]
    pieces = piece // width
    here = (1 - at_ref[0]) if sent else at_ref[0]
    attn_loads, grad_loads = [], []
    for doc in range(doc_count):
        for side in range(INNER):
            at = (1 - at_ref[0]) if side else at_ref[0]
            index = doc * INNER + side
            target = attn_s.at[doc, pl.ds(pl.multiple_of(at * half, half), half)]
            attn_loads.append(begin(attn[index], target, attn_sem.at[index]))
    for k in range(outer):
        place = lax.rem(at_ref[1] + k, outer) * INNER + here
        which = at_ref[step_at + place // pieces]
        cols = pl.ds(pl.multiple_of(lax.rem(place, pieces) * width, width), width)
        for i in range(part_count):

            @pl.when(which == i)
            def _():
                begin(grads[i].at[:, cols], grad_s.at[0, k], grad_sem.at[k])

        loads = [pltpu.make_async_copy(grads[0].at[:, cols], grad_s.at[0, k], grad_sem.at[k])]
        cols = pl.ds(pl.multiple_of(place * width, width), width)
        for doc in range(1, doc_count):
            source = swapped[doc - 1].at[:, cols]
            loads.append(begin(source, grad_s.at[doc, k], grad_sem.at[doc * outer + k]))
        if not sent:
            loads.append(begin(recv.at[k], recv_s.at[k], recv_sem.at[k]))
        grad_loads.append(loads)
    for load in attn_loads:
        load.wait()
    stores = []
    for k in range(outer):
        term = 0.0
        for doc in range(doc_count):
            grad_loads[k][doc].wait()
            term = term + product(attn_s[doc], grad_s[doc, k])
        if not sent:
            grad_loads[k][doc_count].wait()
            term = term + recv_s[k].astype(jnp.float32)
        out_s[k] = term.astype(out_s.dtype)
        stores.append(begin(out_s.at[k], outs[k], out_sem.at[k]))
    for store in stores:
        store.wait()


def weight_terms(at, step_at, attn, grads, swapped, outer, picked, recv=None, after=()):
    half, rows = attn[0].shape
    feats = half * INNER
    doc_count = len(attn) // INNER
    width = picked * grads[0].shape[1] // (outer * INNER)
    sent = recv is None
    operands = [*attn, *grads, *swapped] + ([] if sent else [recv])
    scratch = [
        pltpu.VMEM((doc_count, feats, rows), jnp.bfloat16),
        pltpu.VMEM((doc_count, outer, rows, width), jnp.bfloat16),
        pltpu.VMEM((outer, feats, width), jnp.bfloat16),
        pltpu.SemaphoreType.DMA((len(attn),)),
        pltpu.SemaphoreType.DMA((doc_count * outer,)),
        pltpu.SemaphoreType.DMA((outer,)),
    ]
    if not sent:
        added = [pltpu.VMEM((outer, feats, width), jnp.bfloat16), pltpu.SemaphoreType.DMA((outer,))]
        scratch = added + scratch
    return call(
        functools.partial(weight_kernel, len(grads), doc_count, sent, step_at),
        bf16(outer, feats, width) if sent else [bf16(feats, width)] * outer,
        [SMEM] + [ANY] * len(operands),
        ANY if sent else [ANY] * outer,
        scratch,
        4,
        "weight_sent" if sent else "weight_kept",
        after,
    )(at, *operands)


def collect_kernel(joined, *refs):
    if joined:
        at_ref, dq_mine, dq_recv, terms, grad_q, out = refs[:6]
        dq_s, q_s, dq_sem, q_sem = refs[6:10]
        terms_s, out_s, sem, out_sem = refs[10:]
    else:
        terms, out, terms_s, out_s, sem, out_sem = refs
    count, rows, half = terms.shape
    loads = [begin(terms.at[c], terms_s.at[c], sem.at[c]) for c in range(count)]
    stores = []
    if joined:
        held = [begin(dq, dq_s.at[i], dq_sem.at[i]) for i, dq in enumerate((dq_mine, dq_recv))]
        for side, at in enumerate((at_ref[0], 1 - at_ref[0])):
            held[side].wait()
            q_s[:, pl.ds(pl.multiple_of(at * half, half), half)] = dq_s[side]
        stores.append(begin(q_s, grad_q, q_sem))
    for load in loads:
        load.wait()
    for side in range(INNER):
        summed = terms_s[side].astype(jnp.float32)
        for c in range(side + INNER, count, INNER):
            summed = summed + terms_s[c].astype(jnp.float32)
        out_s[:, side * half : (side + 1) * half] = summed.astype(jnp.bfloat16)
    stores.append(begin(out_s, out, out_sem))
    for store in stores:
        store.wait()


def collect(terms, name, joined=(), after=()):
    count, rows, half = terms.shape
    whole = bf16(rows, INNER * half)
    scratch = [
        pltpu.VMEM((count, rows, half), jnp.bfloat16),
        pltpu.VMEM((rows, INNER * half), jnp.bfloat16),
        pltpu.SemaphoreType.DMA((count,)),
        pltpu.SemaphoreType.DMA,
    ]
    if joined:
        scratch = [
            pltpu.VMEM((INNER, rows, half), jnp.bfloat16),
            pltpu.VMEM((rows, INNER * half), jnp.bfloat16),
            pltpu.SemaphoreType.DMA((INNER,)),
            pltpu.SemaphoreType.DMA,
        ] + scratch
    return call(
        functools.partial(collect_kernel, bool(joined)),
        [whole, whole] if joined else whole,
        [SMEM, ANY, ANY, ANY] if joined else [ANY],
        [ANY, ANY] if joined else ANY,
        scratch,
        2,
        name,
        after,
    )(*joined, terms)


def per_device(
    queries, key_heads, value_heads, grad_output, out_weight, block_pattern, global_offsets
):
    dp_count, ctx_count, tp_count = (lax.axis_size(name) for name in ("dp", "ctx", "tp"))
    dp_at, ctx_at, tp_at = (lax.axis_index(name) for name in ("dp", "ctx", "tp"))
    outer = ctx_count // INNER
    outer_at, inner_at = ctx_at // INNER, ctx_at % INNER
    picked = tp_count // dp_count

    def ctx_pairs(step, side, dp_step=0):
        moved = [(c + step * INNER) % ctx_count ^ side for c in range(ctx_count)]
        if not dp_step:
            return list(enumerate(moved))
        return [
            (d * ctx_count + c, (d + dp_step) % dp_count * ctx_count + moved[c])
            for d in range(dp_count)
            for c in range(ctx_count)
        ]

    def shift_pairs(count, step):
        return [(i, (i + step) % count) for i in range(count)]

    def dp_steps(which):
        return [(which * picked + i - tp_at) % tp_count for i in range(picked)]

    routes = [(step, side) for step in range(outer) for side in range(INNER)]
    sources = [
        ((outer_at - step) % outer) * INNER + (inner_at + side) % INNER for step, side in routes
    ]
    scalars = [inner_at, outer_at, tp_at] + sources
    columns_at = len(scalars)
    scalars = scalars + [(tp_at + step) % tp_count for step in range(1, tp_count)]
    send_at = len(scalars)
    for step in range(1, dp_count):
        scalars = scalars + dp_steps((dp_at + step) % dp_count)
    keep_at = len(scalars)
    at = jnp.stack(scalars + dp_steps(dp_at))

    grad_own = grad_output[0]
    grads = [grad_own] + [
        lax.ppermute(grad_own, "tp", shift_pairs(tp_count, -step)) for step in range(1, tp_count)
    ]
    kv_mine, kv_theirs = part_heads(at, key_heads[0], value_heads[0])
    kv_recv = lax.ppermute(kv_theirs, "ctx", ctx_pairs(0, 1))
    kv_blocks = [
        lax.ppermute(kv_recv if side else kv_mine, "ctx", ctx_pairs(step, 0))
        if step
        else (kv_recv if side else kv_mine)
        for step, side in routes
    ]
    first, key_mask, row_mask, q_theirs = prelude(
        at, block_pattern, global_offsets, queries[0], grad_own, out_weight, (kv_recv,)
    )
    q_recv = lax.ppermute(q_theirs, "ctx", ctx_pairs(0, 1))
    g_mine, g_theirs, grad_sends = grad_heads(
        at, columns_at, send_at, first, out_weight, grads, dp_count - 1, picked
    )
    g_recv = lax.ppermute(g_theirs, "ctx", ctx_pairs(0, 1))
    swapped = [
        lax.ppermute(send, "dp", shift_pairs(dp_count, step + 1))
        for step, send in enumerate(grad_sends)
    ]

    weights, inverse, attn_mine, attn_theirs, value_parts = forward(
        at, queries[0], q_recv, key_mask, row_mask, g_mine, g_recv, kv_blocks, ()
    )

    attn = []
    for step in range(dp_count):
        for held, side in ((attn_mine, 0), (attn_theirs, 1)):
            pairs = ctx_pairs(0, side, step)
            axes = ("dp", "ctx") if step else "ctx"
            attn.append(lax.ppermute(held, axes, pairs) if step or side else held)

    def returned(parts):
        return lax.all_to_all(parts, "ctx", split_axis=0, concat_axis=0, tiled=True)

    value_parts = returned(value_parts)
    send = weight_terms(at, keep_at, attn, grads, swapped, outer, picked)
    weight_recv = lax.ppermute(send, "ctx", ctx_pairs(0, 1))
    dq_mine, dq_theirs, key_parts = key_terms(
        at, queries[0], q_recv, g_mine, g_recv, attn_mine, attn_theirs, inverse, weights, kv_blocks, (send,)
    )
    key_parts = returned(key_parts)
    dq_recv = lax.ppermute(dq_theirs, "ctx", ctx_pairs(0, 1))
    weight_sums = weight_terms(
        at, keep_at, attn, grads, swapped, outer, picked, weight_recv, (dq_mine,)
    )
    grad_weight = weight_sums[0].astype(jnp.float32)
    for step in range(1, outer):
        grad_weight = grad_weight + lax.ppermute(
            weight_sums[step], "ctx", ctx_pairs(step, 0)
        ).astype(jnp.float32)

    grad_v = collect(value_parts, "collect_values", (), (weight_sums[0],))
    grad_q, grad_k = collect(key_parts, "collect_keys", (at, dq_mine, dq_recv), (grad_v,))
    return grad_q[None], grad_k[None], grad_v[None], grad_weight.astype(jnp.bfloat16)


def solution(mesh):
    in_specs = (
        P("dp", "ctx", "tp"),
        P("dp", "ctx", "tp"),
        P("dp", "ctx", "tp"),
        P("dp", "ctx", "tp"),
        P("tp", None),
        P(),
        P(),
    )
    out_specs = (
        P("dp", "ctx", "tp"),
        P("dp", "ctx", "tp"),
        P("dp", "ctx", "tp"),
        P("tp", ("dp", "ctx")),
    )
    return jax.shard_map(
        per_device, mesh=mesh, in_specs=in_specs, out_specs=out_specs, check_vma=False
    )
```

```python
import functools

import jax
import jax.numpy as jnp
from jax import lax
from jax.experimental import pallas as pl
from jax.experimental.pallas import tpu as pltpu
from jax.sharding import PartitionSpec as P

HD = 128
MASKED = -1e30
INNER = 2
SOURCES = 3
ANY = pl.BlockSpec(memory_space=pl.ANY)
VMEM = pl.BlockSpec(memory_space=pltpu.VMEM)
SMEM = pl.BlockSpec(memory_space=pltpu.SMEM)


def against(left_op, right_op):
    return lax.dot_general(
        left_op, right_op, (((1,), (1,)), ((), ())), preferred_element_type=jnp.float32
    )


def product(left_op, right_op):
    return jnp.dot(left_op, right_op, preferred_element_type=jnp.float32)


def begin(source, target, semaphore):
    copy = pltpu.make_async_copy(source, target, semaphore)
    copy.start()
    return copy


def call(kernel, out_shape, in_specs, out_specs, scratch, micros, name, after=()):
    skipped = len(after)
    in_specs = [ANY] * skipped + in_specs
    run = pl.pallas_call(
        lambda *refs: kernel(*refs[skipped:]),
        out_shape=out_shape,
        in_specs=in_specs,
        out_specs=out_specs,
        scratch_shapes=scratch,
        compiler_params=pltpu.CompilerParams(vmem_limit_bytes=64 * 1024 * 1024),
        cost_estimate=pl.CostEstimate(
            flops=int(micros * 1e9), bytes_accessed=int(micros * 3e6), transcendentals=0
        ),
        name=name,
    )

    def placed(*args):
        args = [
            pltpu.with_memory_space_constraint(arg, pltpu.HBM) if spec is ANY else arg
            for spec, arg in zip(in_specs, (*after, *args))
        ]
        return run(*args)

    return placed


def bf16(*shape):
    return pltpu.HBM(shape, jnp.bfloat16)


def f32(*shape):
    return pltpu.HBM(shape, jnp.float32)


def part_kernel(at_ref, k_ref, v_ref, kv_mine, kv_theirs, held_s, in_sem, out_sem):
    half = kv_mine.shape[1] // 2
    loads = [begin(held, held_s.at[i], in_sem.at[i]) for i, held in enumerate((k_ref, v_ref))]
    mine = pl.ds(pl.multiple_of(at_ref[0] * half, half), half)
    theirs = pl.ds(pl.multiple_of((1 - at_ref[0]) * half, half), half)
    copies = []
    for index in range(2):
        loads[index].wait()
        place = slice(index * half, (index + 1) * half)
        for side, (cols, out) in enumerate(((mine, kv_mine), (theirs, kv_theirs))):
            sem = out_sem.at[2 * index + side]
            copies.append(begin(held_s.at[index, :, cols], out.at[:, place], sem))
    for copy in copies:
        copy.wait()


def part_heads(at, keys, values):
    rows, feats = keys.shape
    return call(
        part_kernel,
        [bf16(rows, feats), bf16(rows, feats)],
        [SMEM] + [ANY] * 2,
        [ANY] * 2,
        [
            pltpu.VMEM((2, rows, feats), jnp.bfloat16),
            pltpu.SemaphoreType.DMA((2,)),
            pltpu.SemaphoreType.DMA((4,)),
        ],
        2,
        "part_heads",
    )(at, keys, values)


def prelude_kernel(at_ref, pattern, offsets, q_ref, grad_ref, weight_ref, *refs):
    first, key_mask, row_mask, q_theirs = refs[:4]
    grad_s, weight_s, first_s, mask_s, row_s, q_s, sem, out_sem = refs[4:]
    half = q_theirs.shape[1]
    theirs = pl.ds(pl.multiple_of((1 - at_ref[0]) * half, half), half)
    q_load = begin(q_ref.at[:, theirs], q_s, sem.at[2])
    rows, width = grad_s.shape
    block_count, glob_count = offsets.shape
    start = pl.multiple_of(at_ref[2] * width, width)
    loads = [
        begin(grad_ref, grad_s, sem.at[0]),
        begin(weight_ref.at[:, pl.ds(start, width)], weight_s, sem.at[1]),
    ]
    q_load.wait()
    stores = [begin(q_s, q_theirs, out_sem.at[3])]
    own = at_ref[1] * INNER + at_ref[0]
    partner = at_ref[1] * INNER + 1 - at_ref[0]
    lane = lax.broadcasted_iota(jnp.int32, (1, HD), 1)
    row_at = lax.broadcasted_iota(jnp.int32, (rows, HD), 0)
    col_at = lax.broadcasted_iota(jnp.int32, (8, rows), 1)
    group_at = lax.broadcasted_iota(jnp.int32, (8, rows), 0)
    for index in range(block_count):
        block = at_ref[SOURCES + index]
        hidden = []
        for target in (own, partner):
            seen = jnp.abs(block - target) <= 1
            for r in range(pattern.shape[1]):
                seen = seen | (pattern[target, r] == block)
            hidden.append(jnp.where(seen, 0, 1))
        lane_hidden = jnp.where(lane == 0, hidden[0], jnp.where(lane == 1, hidden[1], 0))
        hidden_rows = jnp.broadcast_to(lane_hidden, (rows, HD))
        for r in range(glob_count):
            hidden_rows = jnp.where(row_at == offsets[block, r], 0, hidden_rows)
        mask_s[index * rows : (index + 1) * rows, :] = hidden_rows.astype(jnp.float32).astype(
            jnp.bfloat16
        )
    for group, target in enumerate((own, partner)):
        local = jnp.where(group_at == group, MASKED, 0.0)
        for r in range(glob_count):
            local = jnp.where(col_at == offsets[target, r], 0.0, local)
        row_s[:, group * rows : (group + 1) * rows] = local
    stores.append(begin(mask_s, key_mask, out_sem.at[0]))
    stores.append(begin(row_s, row_mask, out_sem.at[1]))
    for load in loads:
        load.wait()
    first_s[...] = against(weight_s[...], grad_s[...])
    stores.append(begin(first_s, first, out_sem.at[2]))
    for store in stores:
        store.wait()


def prelude(at, pattern, offsets, queries, grad_own, out_weight, after):
    rows, width = grad_own.shape
    feats = out_weight.shape[0]
    keys = offsets.shape[0] * rows
    half = queries.shape[1] // INNER
    return call(
        prelude_kernel,
        [
            f32(feats, rows),
            bf16(keys, HD),
            f32(8, 2 * rows),
            bf16(rows, half),
        ],
        [SMEM] * 3 + [ANY] * 3,
        [ANY] * 4,
        [
            pltpu.VMEM((rows, width), jnp.bfloat16),
            pltpu.VMEM((feats, width), jnp.bfloat16),
            pltpu.VMEM((feats, rows), jnp.float32),
            pltpu.VMEM((keys, HD), jnp.bfloat16),
            pltpu.VMEM((8, 2 * rows), jnp.float32),
            pltpu.VMEM((rows, half), jnp.bfloat16),
            pltpu.SemaphoreType.DMA((3,)),
            pltpu.SemaphoreType.DMA((4,)),
        ],
        4,
        "prelude",
        after,
    )(at, pattern, offsets, queries, grad_own, out_weight)


def forward_kernel(block_count, head_count, at_ref, q_ref, q_recv, key_mask, row_mask, *refs):
    g_mine, g_recv = refs[:2]
    kv_refs, refs = refs[2 : 2 + block_count], refs[2 + block_count :]
    e_out, inv_out, attn_mine, attn_theirs = refs[:4]
    part_out, refs = refs[4], refs[5:]
    q_s, g_s, mask_s, kv_s, e_s, s_ref, attn_s, inv_s, row_s, part_s = refs[:10]
    sem, kv_sem, e_sem, out_sem, part_sem = refs[10:]
    rows = q_recv.shape[0]
    feats = head_count * HD
    score_scale = HD ** (-0.5)
    mine = pl.ds(pl.multiple_of(at_ref[0] * feats, feats), feats)
    loads = [
        begin(q_ref.at[:, mine], q_s.at[0], sem.at[0]),
        begin(q_recv, q_s.at[1], sem.at[1]),
        begin(key_mask, mask_s, sem.at[2]),
        begin(row_mask, row_s, sem.at[3]),
    ]
    kv_loads = [begin(kv_refs[j], kv_s.at[j], kv_sem.at[j]) for j in range(block_count)]
    g_loads = [begin(g_mine, g_s.at[0], sem.at[4]), begin(g_recv, g_s.at[1], sem.at[5])]
    for load in loads:
        load.wait()
    rows_low = row_s[...].astype(jnp.bfloat16)
    hidden = jnp.concatenate([rows_low, jnp.zeros((HD - 8, 2 * rows), jnp.bfloat16)], axis=0)
    stores = []
    for head in range(head_count):
        cols = slice(head * HD, (head + 1) * HD)
        vcols = slice(feats + head * HD, feats + (head + 1) * HD)
        q_t = jnp.concatenate(
            [jnp.transpose(q_s[0, :, cols]), jnp.transpose(q_s[1, :, cols])], axis=1
        )
        q_t = jnp.concatenate([q_t, hidden], axis=0)
        top = jnp.full((1, 2 * rows), MASKED, jnp.float32)
        for j in range(block_count):
            if head == 0:
                kv_loads[j].wait()
            keys = slice(j * rows, (j + 1) * rows)
            scores = product(jnp.concatenate([kv_s[j, :, cols], mask_s[keys, :]], axis=1), q_t)
            s_ref[keys, :] = scores
            top = jnp.maximum(top, jnp.max(scores, axis=0, keepdims=True))
        total = jnp.zeros((1, 2 * rows), jnp.float32)
        attn_t = jnp.zeros((HD, 2 * rows), jnp.float32)
        for j in range(block_count):
            keys = slice(j * rows, (j + 1) * rows)
            weights = jnp.exp((s_ref[keys, :] - top) * score_scale)
            total = total + jnp.sum(weights, axis=0, keepdims=True)
            low = weights.astype(jnp.bfloat16)
            e_s[head, keys, :] = low
            stores.append(
                begin(e_s.at[head, keys], e_out.at[head, keys], e_sem.at[head * block_count + j])
            )
            attn_t = attn_t + product(jnp.transpose(kv_s[j, :, vcols]), low)
        inverse = 1.0 / total
        inv_s[head : head + 1, :] = inverse
        attn_low = (attn_t * inverse).astype(jnp.bfloat16)
        attn_s[0, cols, :] = attn_low[:, :rows]
        attn_s[1, cols, :] = attn_low[:, rows:]
        if head == 0:
            for load in g_loads:
                load.wait()
        if head == head_count - 1:
            stores.append(begin(attn_s.at[0], attn_mine, out_sem.at[0]))
            stores.append(begin(attn_s.at[1], attn_theirs, out_sem.at[1]))
            stores.append(begin(inv_s, inv_out, out_sem.at[2]))
        g_t = jnp.concatenate([g_s[0, cols, :], g_s[1, cols, :]], axis=1).astype(jnp.float32)
        grad = jnp.transpose((g_t * inverse).astype(jnp.bfloat16))
        for j in range(block_count):
            keys = slice(j * rows, (j + 1) * rows)
            part_s[j, :, cols] = product(e_s[head, keys, :], grad).astype(jnp.bfloat16)
            if head == head_count - 1:
                target = part_out.at[at_ref[SOURCES + j]]
                stores.append(begin(part_s.at[j], target, part_sem.at[j]))
    for store in stores:
        store.wait()


def forward(at, queries, q_recv, key_mask, row_mask, g_mine, g_recv, kv_blocks, after):
    block_count = len(kv_blocks)
    rows, feats = q_recv.shape
    heads = feats // HD
    keys = block_count * rows
    return call(
        functools.partial(forward_kernel, block_count, heads),
        [
            bf16(heads, keys, 2 * rows),
            f32(max(heads, 8), 2 * rows),
            bf16(feats, rows),
            bf16(feats, rows),
            bf16(block_count, rows, feats),
        ],
        [SMEM] + [ANY] * (6 + block_count),
        [ANY] * 5,
        [
            pltpu.VMEM((2, rows, feats), jnp.bfloat16),
            pltpu.VMEM((2, feats, rows), jnp.bfloat16),
            pltpu.VMEM((keys, HD), jnp.bfloat16),
            pltpu.VMEM((block_count, rows, 2 * feats), jnp.bfloat16),
            pltpu.VMEM((heads, keys, 2 * rows), jnp.bfloat16),
            pltpu.VMEM((keys, 2 * rows), jnp.float32),
            pltpu.VMEM((2, feats, rows), jnp.bfloat16),
            pltpu.VMEM((max(heads, 8), 2 * rows), jnp.float32),
            pltpu.VMEM((8, 2 * rows), jnp.float32),
            pltpu.VMEM((block_count, rows, feats), jnp.bfloat16),
            pltpu.SemaphoreType.DMA((6,)),
            pltpu.SemaphoreType.DMA((block_count,)),
            pltpu.SemaphoreType.DMA((heads * block_count,)),
            pltpu.SemaphoreType.DMA((3,)),
            pltpu.SemaphoreType.DMA((block_count,)),
        ],
        20,
        "forward",
        after,
    )(at, queries, q_recv, key_mask, row_mask, g_mine, g_recv, *kv_blocks)


def key_terms_kernel(block_count, at_ref, q_ref, q_recv, g_mine, g_recv, attn_mine, attn_theirs, *refs):
    inv_ref, e_ref = refs[:2]
    kv_refs, refs = refs[2 : 2 + block_count], refs[2 + block_count :]
    dq_mine, dq_theirs, part_out = refs[:3]
    refs = refs[3:]
    q_s, t_s, inv_s, kv_s, e_s, part_s, dq_s, sem, kv_sem, e_sem, part_sem, dq_sem = refs
    rows, feats = q_recv.shape
    head_count = feats // HD
    score_scale = HD ** (-0.5)
    mine = pl.ds(pl.multiple_of(at_ref[0] * feats, feats), feats)
    loads = [begin(q_ref.at[:, mine], q_s.at[0], sem.at[0]), begin(q_recv, q_s.at[1], sem.at[1])]
    for index, held in enumerate((g_mine, g_recv, attn_mine, attn_theirs)):
        loads.append(begin(held, t_s.at[index], sem.at[2 + index]))
    loads.append(begin(inv_ref, inv_s, sem.at[6]))
    kv_loads, e_loads, stores = [], {}, []
    for j in range(block_count):
        keys = slice(j * rows, (j + 1) * rows)
        kv_loads.append(begin(kv_refs[j], kv_s.at[j], kv_sem.at[j]))
        for head in range(head_count):
            e_loads[head, j] = begin(
                e_ref.at[head, keys], e_s.at[head, keys], e_sem.at[head * block_count + j]
            )
    for load in loads:
        load.wait()
    for head in range(head_count):
        cols = slice(head * HD, (head + 1) * HD)
        vcols = slice(feats + head * HD, feats + (head + 1) * HD)
        inverse = inv_s[head : head + 1, :]
        g_t = jnp.concatenate([t_s[0, cols, :], t_s[1, cols, :]], axis=1).astype(jnp.float32)
        attn_t = jnp.concatenate([t_s[2, cols, :], t_s[3, cols, :]], axis=1)
        row_dot = jnp.sum(g_t * attn_t.astype(jnp.float32), axis=0, keepdims=True) * inverse
        g_t = (g_t * inverse).astype(jnp.bfloat16)
        query = jnp.concatenate([q_s[0, :, cols], q_s[1, :, cols]], axis=0)
        dq_t = jnp.zeros((HD, 2 * rows), jnp.float32)
        for j in range(block_count):
            keys = slice(j * rows, (j + 1) * rows)
            if head == 0:
                kv_loads[j].wait()
            e_loads[head, j].wait()
            dprobs = product(kv_s[j, :, vcols], g_t)
            dscore = (e_s[head, keys, :].astype(jnp.float32) * (dprobs - row_dot)).astype(
                jnp.bfloat16
            )
            dq_t = dq_t + product(jnp.transpose(kv_s[j, :, cols]), dscore)
            part_s[j, :, cols] = (score_scale * product(dscore, query)).astype(jnp.bfloat16)
            if head == head_count - 1:
                target = part_out.at[at_ref[SOURCES + j]]
                stores.append(begin(part_s.at[j], target, part_sem.at[j]))
        dquery = (score_scale * jnp.transpose(dq_t)).astype(jnp.bfloat16)
        dq_s[0, :, cols] = dquery[:rows]
        dq_s[1, :, cols] = dquery[rows:]
    stores.append(begin(dq_s.at[0], dq_mine, dq_sem.at[0]))
    stores.append(begin(dq_s.at[1], dq_theirs, dq_sem.at[1]))
    for store in stores:
        store.wait()


def key_terms(at, queries, q_recv, g_mine, g_recv, attn_mine, attn_theirs, inverse, weights, kv_blocks, after):
    block_count = len(kv_blocks)
    rows, feats = q_recv.shape
    heads = feats // HD
    keys = block_count * rows
    return call(
        functools.partial(key_terms_kernel, block_count),
        [bf16(rows, feats)] * 2 + [bf16(block_count, rows, feats)],
        [SMEM] + [ANY] * (8 + block_count),
        [ANY] * 3,
        [
            pltpu.VMEM((2, rows, feats), jnp.bfloat16),
            pltpu.VMEM((4, feats, rows), jnp.bfloat16),
            pltpu.VMEM(inverse.shape, jnp.float32),
            pltpu.VMEM((block_count, rows, 2 * feats), jnp.bfloat16),
            pltpu.VMEM((heads, keys, 2 * rows), jnp.bfloat16),
            pltpu.VMEM((block_count, rows, feats), jnp.bfloat16),
            pltpu.VMEM((2, rows, feats), jnp.bfloat16),
            pltpu.SemaphoreType.DMA((7,)),
            pltpu.SemaphoreType.DMA((block_count,)),
            pltpu.SemaphoreType.DMA((heads * block_count,)),
            pltpu.SemaphoreType.DMA((block_count,)),
            pltpu.SemaphoreType.DMA((2,)),
        ],
        7,
        "key_terms",
        after,
    )(at, queries, q_recv, g_mine, g_recv, attn_mine, attn_theirs, inverse, weights, *kv_blocks)


def grad_heads_kernel(part_count, sends, picked, columns_at, send_at, at_ref, first_ref, weight_ref, *refs):
    grads, refs = refs[:part_count], refs[part_count:]
    outs, refs = refs[: 2 + sends], refs[2 + sends :]
    first_s, grad_s, weight_s, out_s, first_sem, weight_sem, grad_sem, send_sem, out_sem = refs
    half = out_s.shape[1]
    width = grads[0].shape[1]
    first_load = begin(first_ref, first_s, first_sem)
    weight_loads, grad_loads = [], []
    for k in range(1, part_count):
        start = pl.multiple_of(at_ref[columns_at + k - 1] * width, width)
        columns = weight_ref.at[:, pl.ds(start, width)]
        weight_loads.append(begin(columns, weight_s.at[k - 1], weight_sem.at[k - 1]))
        grad_loads.append(begin(grads[k], grad_s.at[k], grad_sem.at[k]))
    own_load = begin(grads[0], grad_s.at[0], grad_sem.at[0])
    first_load.wait()
    summed = first_s[...]
    for k in range(1, part_count):
        weight_loads[k - 1].wait()
        grad_loads[k - 1].wait()
        summed = summed + against(weight_s[k - 1], grad_s[k])
    first_s[...] = summed
    copies = []
    for side, at in enumerate((at_ref[0], 1 - at_ref[0])):
        kept = first_s[pl.ds(pl.multiple_of(at * half, half), half), :]
        out_s[side] = kept.astype(jnp.bfloat16)
        copies.append(begin(out_s.at[side], outs[side], out_sem.at[side]))
    own_load.wait()
    for send in range(sends):
        for i in range(picked):
            place = send * picked + i
            target = outs[2 + send].at[:, i * width : (i + 1) * width]
            for k in range(part_count):

                @pl.when(at_ref[send_at + place] == k)
                def _():
                    begin(grad_s.at[k], target, send_sem.at[place])

            copies.append(pltpu.make_async_copy(grad_s.at[0], target, send_sem.at[place]))
    for copy in copies:
        copy.wait()


def grad_heads(at, columns_at, send_at, first, out_weight, grads, sends, picked):
    feats, rows = first.shape
    half = feats // INNER
    count = len(grads)
    width = grads[0].shape[1]
    out = call(
        functools.partial(grad_heads_kernel, count, sends, picked, columns_at, send_at),
        [bf16(half, rows), bf16(half, rows)] + [bf16(rows, picked * width)] * sends,
        [SMEM] + [ANY] * (2 + count),
        [ANY] * (2 + sends),
        [
            pltpu.VMEM((feats, rows), jnp.float32),
            pltpu.VMEM((count, rows, width), jnp.bfloat16),
            pltpu.VMEM((count - 1, feats, width), jnp.bfloat16),
            pltpu.VMEM((INNER, half, rows), jnp.bfloat16),
            pltpu.SemaphoreType.DMA,
            pltpu.SemaphoreType.DMA((count - 1,)),
            pltpu.SemaphoreType.DMA((count,)),
            pltpu.SemaphoreType.DMA((sends * picked,)),
            pltpu.SemaphoreType.DMA((INNER,)),
        ],
        3,
        "grad_heads",
    )(at, first, out_weight, *grads)
    return out[0], out[1], out[2:]


def weight_kernel(part_count, doc_count, sent, step_at, at_ref, *refs):
    attn, refs = refs[: INNER * doc_count], refs[INNER * doc_count :]
    grads, refs = refs[:part_count], refs[part_count:]
    swapped, refs = refs[: doc_count - 1], refs[doc_count - 1 :]
    if sent:
        out, refs = refs[0], refs[1:]
        outs = [out.at[k] for k in range(out.shape[0])]
    else:
        recv, passed, refs = refs[0], refs[1], refs[2:]
        outs, refs = refs[: recv.shape[0]], refs[recv.shape[0] :]
        passed_out, recv_s, passed_s, recv_sem, passed_sem = refs[:5]
        refs = refs[5:]
        passed_load = begin(passed, passed_s, passed_sem)
    attn_s, grad_s, out_s, attn_sem, grad_sem, out_sem = refs
    outer, feats, width = out_s.shape
    half = feats // INNER
    piece = grads[0].shape[1]
    pieces = piece // width
    here = (1 - at_ref[0]) if sent else at_ref[0]
    attn_loads, grad_loads = [], []
    for doc in range(doc_count):
        for side in range(INNER):
            at = (1 - at_ref[0]) if side else at_ref[0]
            index = doc * INNER + side
            target = attn_s.at[doc, pl.ds(pl.multiple_of(at * half, half), half)]
            attn_loads.append(begin(attn[index], target, attn_sem.at[index]))
    for k in range(outer):
        place = lax.rem(at_ref[1] + k, outer) * INNER + here
        which = at_ref[step_at + place // pieces]
        cols = pl.ds(pl.multiple_of(lax.rem(place, pieces) * width, width), width)
        for i in range(part_count):

            @pl.when(which == i)
            def _():
                begin(grads[i].at[:, cols], grad_s.at[0, k], grad_sem.at[k])

        loads = [pltpu.make_async_copy(grads[0].at[:, cols], grad_s.at[0, k], grad_sem.at[k])]
        cols = pl.ds(pl.multiple_of(place * width, width), width)
        for doc in range(1, doc_count):
            source = swapped[doc - 1].at[:, cols]
            loads.append(begin(source, grad_s.at[doc, k], grad_sem.at[doc * outer + k]))
        if not sent:
            loads.append(begin(recv.at[k], recv_s.at[k], recv_sem.at[k]))
        grad_loads.append(loads)
    for load in attn_loads:
        load.wait()
    stores = []
    if not sent:
        passed_load.wait()
        stores.append(begin(passed_s, passed_out, passed_sem))
    for k in range(outer):
        term = 0.0
        for doc in range(doc_count):
            grad_loads[k][doc].wait()
            term = term + product(attn_s[doc], grad_s[doc, k])
        if not sent:
            grad_loads[k][doc_count].wait()
            term = term + recv_s[k].astype(jnp.float32)
        out_s[k] = term.astype(out_s.dtype)
        stores.append(begin(out_s.at[k], outs[k], out_sem.at[k]))
    for store in stores:
        store.wait()


def weight_terms(at, step_at, attn, grads, swapped, outer, picked, recv=None, passed=None, after=()):
    half, rows = attn[0].shape
    feats = half * INNER
    doc_count = len(attn) // INNER
    width = picked * grads[0].shape[1] // (outer * INNER)
    sent = recv is None
    operands = [*attn, *grads, *swapped] + ([] if sent else [recv, passed])
    scratch = [
        pltpu.VMEM((doc_count, feats, rows), jnp.bfloat16),
        pltpu.VMEM((doc_count, outer, rows, width), jnp.bfloat16),
        pltpu.VMEM((outer, feats, width), jnp.bfloat16),
        pltpu.SemaphoreType.DMA((len(attn),)),
        pltpu.SemaphoreType.DMA((doc_count * outer,)),
        pltpu.SemaphoreType.DMA((outer,)),
    ]
    if not sent:
        scratch = [
            pltpu.VMEM((outer, feats, width), jnp.bfloat16),
            pltpu.VMEM(passed.shape, jnp.bfloat16),
            pltpu.SemaphoreType.DMA((outer,)),
            pltpu.SemaphoreType.DMA,
        ] + scratch
    return call(
        functools.partial(weight_kernel, len(grads), doc_count, sent, step_at),
        bf16(outer, feats, width) if sent else [bf16(feats, width)] * outer + [bf16(*passed.shape)],
        [SMEM] + [ANY] * len(operands),
        ANY if sent else [ANY] * (outer + 1),
        scratch,
        4,
        "weight_sent" if sent else "weight_kept",
        after,
    )(at, *operands)


def collect_kernel(joined, *refs):
    if joined:
        at_ref, dq_mine, dq_recv, terms, grad_q, out = refs[:6]
        dq_s, q_s, dq_sem, q_sem = refs[6:10]
        terms_s, out_s, sem, out_sem = refs[10:]
    else:
        terms, out, terms_s, out_s, sem, out_sem = refs
    count, rows, half = terms.shape
    loads = [begin(terms.at[c], terms_s.at[c], sem.at[c]) for c in range(count)]
    stores = []
    if joined:
        held = [begin(dq, dq_s.at[i], dq_sem.at[i]) for i, dq in enumerate((dq_mine, dq_recv))]
        for side, at in enumerate((at_ref[0], 1 - at_ref[0])):
            held[side].wait()
            q_s[:, pl.ds(pl.multiple_of(at * half, half), half)] = dq_s[side]
        stores.append(begin(q_s, grad_q, q_sem))
    for load in loads:
        load.wait()
    for side in range(INNER):
        summed = terms_s[side].astype(jnp.float32)
        for c in range(side + INNER, count, INNER):
            summed = summed + terms_s[c].astype(jnp.float32)
        out_s[:, side * half : (side + 1) * half] = summed.astype(jnp.bfloat16)
    stores.append(begin(out_s, out, out_sem))
    for store in stores:
        store.wait()


def collect(terms, name, joined=(), after=()):
    count, rows, half = terms.shape
    whole = bf16(rows, INNER * half)
    scratch = [
        pltpu.VMEM((count, rows, half), jnp.bfloat16),
        pltpu.VMEM((rows, INNER * half), jnp.bfloat16),
        pltpu.SemaphoreType.DMA((count,)),
        pltpu.SemaphoreType.DMA,
    ]
    if joined:
        scratch = [
            pltpu.VMEM((INNER, rows, half), jnp.bfloat16),
            pltpu.VMEM((rows, INNER * half), jnp.bfloat16),
            pltpu.SemaphoreType.DMA((INNER,)),
            pltpu.SemaphoreType.DMA,
        ] + scratch
    return call(
        functools.partial(collect_kernel, bool(joined)),
        [whole, whole] if joined else whole,
        [SMEM, ANY, ANY, ANY] if joined else [ANY],
        [ANY, ANY] if joined else ANY,
        scratch,
        2,
        name,
        after,
    )(*joined, terms)


def per_device(
    queries, key_heads, value_heads, grad_output, out_weight, block_pattern, global_offsets
):
    dp_count, ctx_count, tp_count = (lax.axis_size(name) for name in ("dp", "ctx", "tp"))
    dp_at, ctx_at, tp_at = (lax.axis_index(name) for name in ("dp", "ctx", "tp"))
    outer = ctx_count // INNER
    outer_at, inner_at = ctx_at // INNER, ctx_at % INNER
    picked = tp_count // dp_count

    def ctx_pairs(step, side, dp_step=0):
        moved = [(c + step * INNER) % ctx_count ^ side for c in range(ctx_count)]
        if not dp_step:
            return list(enumerate(moved))
        return [
            (d * ctx_count + c, (d + dp_step) % dp_count * ctx_count + moved[c])
            for d in range(dp_count)
            for c in range(ctx_count)
        ]

    def shift_pairs(count, step):
        return [(i, (i + step) % count) for i in range(count)]

    def dp_steps(which):
        return [(which * picked + i - tp_at) % tp_count for i in range(picked)]

    routes = [(step, side) for step in range(outer) for side in range(INNER)]
    sources = [
        ((outer_at - step) % outer) * INNER + (inner_at + side) % INNER for step, side in routes
    ]
    scalars = [inner_at, outer_at, tp_at] + sources
    columns_at = len(scalars)
    scalars = scalars + [(tp_at + step) % tp_count for step in range(1, tp_count)]
    send_at = len(scalars)
    for step in range(1, dp_count):
        scalars = scalars + dp_steps((dp_at + step) % dp_count)
    keep_at = len(scalars)
    at = jnp.stack(scalars + dp_steps(dp_at))

    grad_own = grad_output[0]
    grads = [grad_own] + [
        lax.ppermute(grad_own, "tp", shift_pairs(tp_count, -step)) for step in range(1, tp_count)
    ]
    kv_mine, kv_theirs = part_heads(at, key_heads[0], value_heads[0])
    kv_recv = lax.ppermute(kv_theirs, "ctx", ctx_pairs(0, 1))
    kv_blocks = [
        lax.ppermute(kv_recv if side else kv_mine, "ctx", ctx_pairs(step, 0))
        if step
        else (kv_recv if side else kv_mine)
        for step, side in routes
    ]
    first, key_mask, row_mask, q_theirs = prelude(
        at, block_pattern, global_offsets, queries[0], grad_own, out_weight, (kv_recv,)
    )
    q_recv = lax.ppermute(q_theirs, "ctx", ctx_pairs(0, 1))
    g_mine, g_theirs, grad_sends = grad_heads(
        at, columns_at, send_at, first, out_weight, grads, dp_count - 1, picked
    )
    g_recv = lax.ppermute(g_theirs, "ctx", ctx_pairs(0, 1))
    swapped = [
        lax.ppermute(send, "dp", shift_pairs(dp_count, step + 1))
        for step, send in enumerate(grad_sends)
    ]

    weights, inverse, attn_mine, attn_theirs, value_parts = forward(
        at, queries[0], q_recv, key_mask, row_mask, g_mine, g_recv, kv_blocks, ()
    )

    attn = []
    for step in range(dp_count):
        for held, side in ((attn_mine, 0), (attn_theirs, 1)):
            pairs = ctx_pairs(0, side, step)
            axes = ("dp", "ctx") if step else "ctx"
            attn.append(lax.ppermute(held, axes, pairs) if step or side else held)

    def returned(parts):
        return lax.all_to_all(parts, "ctx", split_axis=0, concat_axis=0, tiled=True)

    value_parts = returned(value_parts)
    send = weight_terms(at, keep_at, attn, grads, swapped, outer, picked)
    weight_recv = lax.ppermute(send, "ctx", ctx_pairs(0, 1))
    dq_mine, dq_theirs, key_parts = key_terms(
        at, queries[0], q_recv, g_mine, g_recv, attn_mine, attn_theirs, inverse, weights, kv_blocks, (send,)
    )
    key_parts = returned(key_parts)
    *weight_sums, dq_theirs = weight_terms(
        at, keep_at, attn, grads, swapped, outer, picked, weight_recv, dq_theirs
    )
    weight_parts = [
        lax.ppermute(weight_sums[step], "ctx", ctx_pairs(step, 0)) for step in range(1, outer)
    ]
    dq_recv = lax.ppermute(dq_theirs, "ctx", ctx_pairs(0, 1))
    grad_v = collect(value_parts, "collect_values", (), (weight_sums[0],))
    grad_q, grad_k = collect(key_parts, "collect_keys", (at, dq_mine, dq_recv), (grad_v,))
    weight_parts, grad_k = lax.optimization_barrier((weight_parts, grad_k))
    grad_weight = weight_sums[0].astype(jnp.float32)
    for part in weight_parts:
        grad_weight = grad_weight + part.astype(jnp.float32)

    return grad_q[None], grad_k[None], grad_v[None], grad_weight.astype(jnp.bfloat16)


def solution(mesh):
    in_specs = (
        P("dp", "ctx", "tp"),
        P("dp", "ctx", "tp"),
        P("dp", "ctx", "tp"),
        P("dp", "ctx", "tp"),
        P("tp", None),
        P(),
        P(),
    )
    out_specs = (
        P("dp", "ctx", "tp"),
        P("dp", "ctx", "tp"),
        P("dp", "ctx", "tp"),
        P("tp", ("dp", "ctx")),
    )
    return jax.shard_map(
        per_device, mesh=mesh, in_specs=in_specs, out_specs=out_specs, check_vma=False
    )
```

```python
import functools

import jax
import jax.numpy as jnp
from jax import lax
from jax.experimental import pallas as pl
from jax.experimental.pallas import tpu as pltpu
from jax.sharding import PartitionSpec as P

HD = 128
MASKED = -1e30
INNER = 2
SOURCES = 3
ANY = pl.BlockSpec(memory_space=pl.ANY)
VMEM = pl.BlockSpec(memory_space=pltpu.VMEM)
SMEM = pl.BlockSpec(memory_space=pltpu.SMEM)


def against(left_op, right_op):
    return lax.dot_general(
        left_op, right_op, (((1,), (1,)), ((), ())), preferred_element_type=jnp.float32
    )


def product(left_op, right_op):
    return jnp.dot(left_op, right_op, preferred_element_type=jnp.float32)


def begin(source, target, semaphore):
    copy = pltpu.make_async_copy(source, target, semaphore)
    copy.start()
    return copy


def call(kernel, out_shape, in_specs, out_specs, scratch, micros, name, after=()):
    skipped = len(after)
    in_specs = [ANY] * skipped + in_specs
    run = pl.pallas_call(
        lambda *refs: kernel(*refs[skipped:]),
        out_shape=out_shape,
        in_specs=in_specs,
        out_specs=out_specs,
        scratch_shapes=scratch,
        compiler_params=pltpu.CompilerParams(vmem_limit_bytes=64 * 1024 * 1024),
        cost_estimate=pl.CostEstimate(
            flops=int(micros * 1e9), bytes_accessed=int(micros * 3e6), transcendentals=0
        ),
        name=name,
    )

    def placed(*args):
        args = [
            pltpu.with_memory_space_constraint(arg, pltpu.HBM) if spec is ANY else arg
            for spec, arg in zip(in_specs, (*after, *args))
        ]
        return run(*args)

    return placed


def bf16(*shape):
    return pltpu.HBM(shape, jnp.bfloat16)


def f32(*shape):
    return pltpu.HBM(shape, jnp.float32)


def part_kernel(at_ref, k_ref, v_ref, kv_mine, kv_theirs, held_s, in_sem, out_sem):
    half = kv_mine.shape[1] // 2
    loads = [begin(held, held_s.at[i], in_sem.at[i]) for i, held in enumerate((k_ref, v_ref))]
    mine = pl.ds(pl.multiple_of(at_ref[0] * half, half), half)
    theirs = pl.ds(pl.multiple_of((1 - at_ref[0]) * half, half), half)
    copies = []
    for index in range(2):
        loads[index].wait()
        place = slice(index * half, (index + 1) * half)
        for side, (cols, out) in enumerate(((mine, kv_mine), (theirs, kv_theirs))):
            sem = out_sem.at[2 * index + side]
            copies.append(begin(held_s.at[index, :, cols], out.at[:, place], sem))
    for copy in copies:
        copy.wait()


def part_heads(at, keys, values):
    rows, feats = keys.shape
    return call(
        part_kernel,
        [bf16(rows, feats), bf16(rows, feats)],
        [SMEM] + [ANY] * 2,
        [ANY] * 2,
        [
            pltpu.VMEM((2, rows, feats), jnp.bfloat16),
            pltpu.SemaphoreType.DMA((2,)),
            pltpu.SemaphoreType.DMA((4,)),
        ],
        2,
        "part_heads",
    )(at, keys, values)


def prelude_kernel(at_ref, pattern, offsets, q_ref, grad_ref, weight_ref, *refs):
    first, key_mask, row_mask, q_theirs = refs[:4]
    grad_s, weight_s, first_s, mask_s, row_s, q_s, sem, out_sem = refs[4:]
    half = q_theirs.shape[1]
    theirs = pl.ds(pl.multiple_of((1 - at_ref[0]) * half, half), half)
    q_load = begin(q_ref.at[:, theirs], q_s, sem.at[2])
    rows, width = grad_s.shape
    block_count, glob_count = offsets.shape
    start = pl.multiple_of(at_ref[2] * width, width)
    loads = [
        begin(grad_ref, grad_s, sem.at[0]),
        begin(weight_ref.at[:, pl.ds(start, width)], weight_s, sem.at[1]),
    ]
    q_load.wait()
    stores = [begin(q_s, q_theirs, out_sem.at[3])]
    own = at_ref[1] * INNER + at_ref[0]
    partner = at_ref[1] * INNER + 1 - at_ref[0]
    lane = lax.broadcasted_iota(jnp.int32, (1, HD), 1)
    row_at = lax.broadcasted_iota(jnp.int32, (rows, HD), 0)
    col_at = lax.broadcasted_iota(jnp.int32, (8, rows), 1)
    group_at = lax.broadcasted_iota(jnp.int32, (8, rows), 0)
    for index in range(block_count):
        block = at_ref[SOURCES + index]
        hidden = []
        for target in (own, partner):
            seen = jnp.abs(block - target) <= 1
            for r in range(pattern.shape[1]):
                seen = seen | (pattern[target, r] == block)
            hidden.append(jnp.where(seen, 0, 1))
        lane_hidden = jnp.where(lane == 0, hidden[0], jnp.where(lane == 1, hidden[1], 0))
        hidden_rows = jnp.broadcast_to(lane_hidden, (rows, HD))
        for r in range(glob_count):
            hidden_rows = jnp.where(row_at == offsets[block, r], 0, hidden_rows)
        mask_s[index * rows : (index + 1) * rows, :] = hidden_rows.astype(jnp.float32).astype(
            jnp.bfloat16
        )
    for group, target in enumerate((own, partner)):
        local = jnp.where(group_at == group, MASKED, 0.0)
        for r in range(glob_count):
            local = jnp.where(col_at == offsets[target, r], 0.0, local)
        row_s[:, group * rows : (group + 1) * rows] = local
    stores.append(begin(mask_s, key_mask, out_sem.at[0]))
    stores.append(begin(row_s, row_mask, out_sem.at[1]))
    for load in loads:
        load.wait()
    first_s[...] = against(weight_s[...], grad_s[...])
    stores.append(begin(first_s, first, out_sem.at[2]))
    for store in stores:
        store.wait()


def prelude(at, pattern, offsets, queries, grad_own, out_weight, after):
    rows, width = grad_own.shape
    feats = out_weight.shape[0]
    keys = offsets.shape[0] * rows
    half = queries.shape[1] // INNER
    return call(
        prelude_kernel,
        [
            f32(feats, rows),
            bf16(keys, HD),
            f32(8, 2 * rows),
            bf16(rows, half),
        ],
        [SMEM] * 3 + [ANY] * 3,
        [ANY] * 4,
        [
            pltpu.VMEM((rows, width), jnp.bfloat16),
            pltpu.VMEM((feats, width), jnp.bfloat16),
            pltpu.VMEM((feats, rows), jnp.float32),
            pltpu.VMEM((keys, HD), jnp.bfloat16),
            pltpu.VMEM((8, 2 * rows), jnp.float32),
            pltpu.VMEM((rows, half), jnp.bfloat16),
            pltpu.SemaphoreType.DMA((3,)),
            pltpu.SemaphoreType.DMA((4,)),
        ],
        4,
        "prelude",
        after,
    )(at, pattern, offsets, queries, grad_own, out_weight)


def forward_kernel(block_count, head_count, at_ref, q_ref, q_recv, key_mask, row_mask, *refs):
    kv_refs, refs = refs[:block_count], refs[block_count:]
    e_out, inv_out, attn_out = refs[:3]
    q_s, mask_s, kv_s, e_s, s_ref, attn_s, inv_s, row_s, sem, kv_sem, e_sem, out_sem = refs[3:]
    rows = q_recv.shape[0]
    feats = head_count * HD
    score_scale = HD ** (-0.5)
    mine = pl.ds(pl.multiple_of(at_ref[0] * feats, feats), feats)
    loads = [
        begin(q_ref.at[:, mine], q_s.at[0], sem.at[0]),
        begin(q_recv, q_s.at[1], sem.at[1]),
        begin(key_mask, mask_s, sem.at[2]),
        begin(row_mask, row_s, sem.at[3]),
    ]
    kv_loads = [begin(kv_refs[j], kv_s.at[j], kv_sem.at[j]) for j in range(block_count)]
    for load in loads:
        load.wait()
    rows_low = row_s[...].astype(jnp.bfloat16)
    hidden = jnp.concatenate([rows_low, jnp.zeros((HD - 8, 2 * rows), jnp.bfloat16)], axis=0)
    stores = []
    for head in range(head_count):
        cols = slice(head * HD, (head + 1) * HD)
        vcols = slice(feats + head * HD, feats + (head + 1) * HD)
        q_t = jnp.concatenate(
            [jnp.transpose(q_s[0, :, cols]), jnp.transpose(q_s[1, :, cols])], axis=1
        )
        q_t = jnp.concatenate([q_t, hidden], axis=0)
        top = jnp.full((1, 2 * rows), MASKED, jnp.float32)
        for j in range(block_count):
            if head == 0:
                kv_loads[j].wait()
            keys = slice(j * rows, (j + 1) * rows)
            scores = product(jnp.concatenate([kv_s[j, :, cols], mask_s[keys, :]], axis=1), q_t)
            s_ref[keys, :] = scores
            top = jnp.maximum(top, jnp.max(scores, axis=0, keepdims=True))
        total = jnp.zeros((1, 2 * rows), jnp.float32)
        attn_t = jnp.zeros((HD, 2 * rows), jnp.float32)
        for j in range(block_count):
            keys = slice(j * rows, (j + 1) * rows)
            weights = jnp.exp((s_ref[keys, :] - top) * score_scale)
            total = total + jnp.sum(weights, axis=0, keepdims=True)
            low = weights.astype(jnp.bfloat16)
            e_s[head, keys, :] = low
            stores.append(
                begin(e_s.at[head, keys], e_out.at[head, keys], e_sem.at[head * block_count + j])
            )
            attn_t = attn_t + product(jnp.transpose(kv_s[j, :, vcols]), low)
        inverse = 1.0 / total
        inv_s[head : head + 1, :] = inverse
        attn_low = (attn_t * inverse).astype(jnp.bfloat16)
        attn_s[0, cols, :] = attn_low[:, :rows]
        attn_s[1, cols, :] = attn_low[:, rows:]
    stores.append(begin(attn_s, attn_out, out_sem.at[0]))
    stores.append(begin(inv_s, inv_out, out_sem.at[1]))
    for store in stores:
        store.wait()


def forward(at, queries, q_recv, key_mask, row_mask, kv_blocks, after=()):
    block_count = len(kv_blocks)
    rows, feats = q_recv.shape
    heads = feats // HD
    keys = block_count * rows
    return call(
        functools.partial(forward_kernel, block_count, heads),
        [
            bf16(heads, keys, 2 * rows),
            f32(max(heads, 8), 2 * rows),
            bf16(INNER, feats, rows),
        ],
        [SMEM] + [ANY] * (4 + block_count),
        [ANY] * 3,
        [
            pltpu.VMEM((2, rows, feats), jnp.bfloat16),
            pltpu.VMEM((keys, HD), jnp.bfloat16),
            pltpu.VMEM((block_count, rows, 2 * feats), jnp.bfloat16),
            pltpu.VMEM((heads, keys, 2 * rows), jnp.bfloat16),
            pltpu.VMEM((keys, 2 * rows), jnp.float32),
            pltpu.VMEM((2, feats, rows), jnp.bfloat16),
            pltpu.VMEM((max(heads, 8), 2 * rows), jnp.float32),
            pltpu.VMEM((8, 2 * rows), jnp.float32),
            pltpu.SemaphoreType.DMA((4,)),
            pltpu.SemaphoreType.DMA((block_count,)),
            pltpu.SemaphoreType.DMA((heads * block_count,)),
            pltpu.SemaphoreType.DMA((2,)),
        ],
        6,
        "forward",
        after,
    )(at, queries, q_recv, key_mask, row_mask, *kv_blocks)


def backward_kernel(block_count, head_count, at_ref, *refs):
    q_ref, q_recv, g_mine, g_recv, attn_ref, inv_ref, e_ref = refs[:7]
    kv_refs, refs = refs[7 : 7 + block_count], refs[7 + block_count :]
    dq_mine, dq_theirs, part_out, attn_out = refs[:4]
    q_s, t_s, attn_s, inv_s, kv_s, e_s, part_s, dq_s, sem, kv_sem, e_sem, part_sem, dq_sem = refs[4:]
    rows = q_recv.shape[0]
    feats = head_count * HD
    score_scale = HD ** (-0.5)
    mine = pl.ds(pl.multiple_of(at_ref[0] * feats, feats), feats)
    loads = [begin(q_ref.at[:, mine], q_s.at[0], sem.at[0]), begin(q_recv, q_s.at[1], sem.at[1])]
    for index, held in enumerate((g_mine, g_recv)):
        loads.append(begin(held, t_s.at[index], sem.at[2 + index]))
    loads.append(begin(attn_ref, attn_s, sem.at[4]))
    loads.append(begin(inv_ref, inv_s, sem.at[5]))
    kv_loads, e_loads, stores = [], {}, []
    for j in range(block_count):
        keys = slice(j * rows, (j + 1) * rows)
        kv_loads.append(begin(kv_refs[j], kv_s.at[j], kv_sem.at[j]))
        for head in range(head_count):
            e_loads[head, j] = begin(
                e_ref.at[head, keys], e_s.at[head, keys], e_sem.at[head * block_count + j]
            )
    for load in loads:
        load.wait()
    stores.append(begin(attn_s, attn_out, dq_sem.at[2]))
    for head in range(head_count):
        cols = slice(head * HD, (head + 1) * HD)
        vcols = slice(feats + head * HD, feats + (head + 1) * HD)
        inverse = inv_s[head : head + 1, :]
        g_t = jnp.concatenate([t_s[0, cols, :], t_s[1, cols, :]], axis=1).astype(jnp.float32)
        attn_t = jnp.concatenate([attn_s[0, cols, :], attn_s[1, cols, :]], axis=1)
        row_dot = jnp.sum(g_t * attn_t.astype(jnp.float32), axis=0, keepdims=True) * inverse
        g_t = (g_t * inverse).astype(jnp.bfloat16)
        grad = jnp.transpose(g_t)
        query = jnp.concatenate([q_s[0, :, cols], q_s[1, :, cols]], axis=0)
        dq_t = jnp.zeros((HD, 2 * rows), jnp.float32)
        for j in range(block_count):
            keys = slice(j * rows, (j + 1) * rows)
            if head == 0:
                kv_loads[j].wait()
            e_loads[head, j].wait()
            low = e_s[head, keys, :]
            dprobs = product(kv_s[j, :, vcols], g_t)
            dscore = (low.astype(jnp.float32) * (dprobs - row_dot)).astype(jnp.bfloat16)
            dq_t = dq_t + product(jnp.transpose(kv_s[j, :, cols]), dscore)
            part_s[j, :, cols] = (score_scale * product(dscore, query)).astype(jnp.bfloat16)
            part_s[j, :, vcols] = product(low, grad).astype(jnp.bfloat16)
            if head == head_count - 1:
                stores.append(begin(part_s.at[j], part_out.at[at_ref[SOURCES + j]], part_sem.at[j]))
        dquery = (score_scale * jnp.transpose(dq_t)).astype(jnp.bfloat16)
        dq_s[0, :, cols] = dquery[:rows]
        dq_s[1, :, cols] = dquery[rows:]
    stores.append(begin(dq_s.at[0], dq_mine, dq_sem.at[0]))
    stores.append(begin(dq_s.at[1], dq_theirs, dq_sem.at[1]))
    for store in stores:
        store.wait()


def backward(at, queries, q_recv, g_mine, g_recv, attn, inverse, weights, kv_blocks):
    block_count = len(kv_blocks)
    rows, feats = q_recv.shape
    heads = feats // HD
    keys = block_count * rows
    return call(
        functools.partial(backward_kernel, block_count, heads),
        [bf16(rows, feats)] * 2 + [bf16(block_count, rows, 2 * feats), bf16(*attn.shape)],
        [SMEM] + [ANY] * (7 + block_count),
        [ANY] * 4,
        [
            pltpu.VMEM((2, rows, feats), jnp.bfloat16),
            pltpu.VMEM((2, feats, rows), jnp.bfloat16),
            pltpu.VMEM(attn.shape, jnp.bfloat16),
            pltpu.VMEM(inverse.shape, jnp.float32),
            pltpu.VMEM((block_count, rows, 2 * feats), jnp.bfloat16),
            pltpu.VMEM((heads, keys, 2 * rows), jnp.bfloat16),
            pltpu.VMEM((block_count, rows, 2 * feats), jnp.bfloat16),
            pltpu.VMEM((2, rows, feats), jnp.bfloat16),
            pltpu.SemaphoreType.DMA((6,)),
            pltpu.SemaphoreType.DMA((block_count,)),
            pltpu.SemaphoreType.DMA((heads * block_count,)),
            pltpu.SemaphoreType.DMA((block_count,)),
            pltpu.SemaphoreType.DMA((3,)),
        ],
        8,
        "backward",
    )(at, queries, q_recv, g_mine, g_recv, attn, inverse, weights, *kv_blocks)


def chunk(at_ref, steps_at, parts, place, width, target, semaphore):
    pieces = parts[0].shape[1] // width
    which = at_ref[steps_at + place // pieces]
    cols = pl.ds(pl.multiple_of(lax.rem(place, pieces) * width, width), width)
    for k, part in enumerate(parts):

        @pl.when(which == k)
        def _():
            begin(part.at[:, cols], target, semaphore)

    return pltpu.make_async_copy(parts[0].at[:, cols], target, semaphore)


def grad_heads_kernel(part_count, routes, picked, columns_at, groups_at, at_ref, first_ref, weight_ref, *refs):
    grads, refs = refs[:part_count], refs[part_count:]
    outs, sends, refs = refs[:2], refs[2 : 2 + len(routes)], refs[2 + len(routes) :]
    first_s, grad_s, weight_s, out_s, first_sem, weight_sem, grad_sem, send_sem, out_sem = refs
    half = out_s.shape[1]
    width = grads[0].shape[1]
    first_load = begin(first_ref, first_s, first_sem)
    weight_loads, grad_loads = [], []
    for k in range(1, part_count):
        start = pl.multiple_of(at_ref[columns_at + k - 1] * width, width)
        columns = weight_ref.at[:, pl.ds(start, width)]
        weight_loads.append(begin(columns, weight_s.at[k - 1], weight_sem.at[k - 1]))
        grad_loads.append(begin(grads[k], grad_s.at[k], grad_sem.at[k]))
    own_load = begin(grads[0], grad_s.at[0], grad_sem.at[0])
    first_load.wait()
    summed = first_s[...]
    for k in range(1, part_count):
        weight_loads[k - 1].wait()
        grad_loads[k - 1].wait()
        summed = summed + against(weight_s[k - 1], grad_s[k])
    first_s[...] = summed
    copies = []
    for side, at in enumerate((at_ref[0], 1 - at_ref[0])):
        kept = first_s[pl.ds(pl.multiple_of(at * half, half), half), :]
        out_s[side] = kept.astype(jnp.bfloat16)
        copies.append(begin(out_s.at[side], outs[side], out_sem.at[side]))
    own_load.wait()
    parts = [grad_s.at[k] for k in range(part_count)]
    for index, (step, side) in enumerate(routes):
        outer, _, block = sends[index].shape
        here = (1 - at_ref[0]) if side else at_ref[0]
        for k in range(outer):
            place = lax.rem(at_ref[1] + k, outer) * INNER + here
            target, sem = sends[index].at[k], send_sem.at[index * outer + k]
            copies.append(chunk(at_ref, groups_at + step * picked, parts, place, block, target, sem))
    for copy in copies:
        copy.wait()


def grad_heads(at, columns_at, groups_at, first, out_weight, grads, routes, outer, picked):
    feats, rows = first.shape
    half = feats // INNER
    count = len(grads)
    width = grads[0].shape[1]
    block = picked * width // (outer * INNER)
    out = call(
        functools.partial(grad_heads_kernel, count, routes, picked, columns_at, groups_at),
        [bf16(half, rows), bf16(half, rows)] + [bf16(outer, rows, block)] * len(routes),
        [SMEM] + [ANY] * (2 + count),
        [ANY] * (2 + len(routes)),
        [
            pltpu.VMEM((feats, rows), jnp.float32),
            pltpu.VMEM((count, rows, width), jnp.bfloat16),
            pltpu.VMEM((count - 1, feats, width), jnp.bfloat16),
            pltpu.VMEM((INNER, half, rows), jnp.bfloat16),
            pltpu.SemaphoreType.DMA,
            pltpu.SemaphoreType.DMA((count - 1,)),
            pltpu.SemaphoreType.DMA((count,)),
            pltpu.SemaphoreType.DMA((len(routes) * outer,)),
            pltpu.SemaphoreType.DMA((INNER,)),
        ],
        4,
        "grad_heads",
    )(at, first, out_weight, *grads)
    return out[0], out[1], out[2:]


def weight_kernel(part_count, doc_count, groups_at, at_ref, *refs):
    route_count = INNER * doc_count
    attn, refs = refs[:route_count], refs[route_count:]
    grads, refs = refs[:part_count], refs[part_count:]
    swapped, refs = refs[: route_count - 1], refs[route_count - 1 :]
    attn_s, grad_s, out_s, attn_sem, grad_sem, out_sem = refs[-6:]
    outs = refs[:-6]
    outer, feats, width = out_s.shape
    half = feats // INNER
    attn_loads, grad_loads = [], []
    for doc in range(doc_count):
        for side in range(INNER):
            for group, at in enumerate((at_ref[0], 1 - at_ref[0])):
                source = attn[doc * INNER + group].at[side ^ group]
                target = attn_s.at[doc * INNER + side, pl.ds(pl.multiple_of(at * half, half), half)]
                sem = attn_sem.at[(doc * INNER + side) * INNER + group]
                attn_loads.append(begin(source, target, sem))
    for k in range(outer):
        place = lax.rem(at_ref[1] + k, outer) * INNER + at_ref[0]
        target, sem = grad_s.at[0, k], grad_sem.at[k]
        loads = [chunk(at_ref, groups_at, grads, place, width, target, sem)]
        for index, held in enumerate(swapped):
            sem = grad_sem.at[(index + 1) * outer + k]
            loads.append(begin(held.at[k], grad_s.at[index + 1, k], sem))
        grad_loads.append(loads)
    for load in attn_loads:
        load.wait()
    stores = []
    for k in range(outer):
        term = 0.0
        for index in range(route_count):
            grad_loads[k][index].wait()
            term = term + product(attn_s[index], grad_s[index, k])
        out_s[k] = term.astype(out_s.dtype)
        stores.append(begin(out_s.at[k], outs[k], out_sem.at[k]))
    for store in stores:
        store.wait()


def weight_terms(at, groups_at, attn, grads, swapped, after=()):
    _, half, rows = attn[0].shape
    outer, _, width = swapped[0].shape
    feats = half * INNER
    routes = len(attn)
    operands = [*attn, *grads, *swapped]
    return call(
        functools.partial(weight_kernel, len(grads), routes // INNER, groups_at),
        [bf16(feats, width)] * outer,
        [SMEM] + [ANY] * len(operands),
        [ANY] * outer,
        [
            pltpu.VMEM((routes, feats, rows), jnp.bfloat16),
            pltpu.VMEM((routes, outer, rows, width), jnp.bfloat16),
            pltpu.VMEM((outer, feats, width), jnp.bfloat16),
            pltpu.SemaphoreType.DMA((routes * INNER,)),
            pltpu.SemaphoreType.DMA((routes * outer,)),
            pltpu.SemaphoreType.DMA((outer,)),
        ],
        5,
        "weight_terms",
        after,
    )(at, *operands)


def collect_kernel(at_ref, dq_mine, dq_recv, terms, *refs):
    outs, (dq_s, terms_s, out_s, dq_sem, sem, out_sem) = refs[:3], refs[3:]
    count, rows, both = terms.shape
    half = both // 2
    loads = [begin(terms.at[c], terms_s.at[c], sem.at[c]) for c in range(count)]
    held = [begin(dq, dq_s.at[i], dq_sem.at[i]) for i, dq in enumerate((dq_mine, dq_recv))]
    for side, at in enumerate((at_ref[0], 1 - at_ref[0])):
        held[side].wait()
        out_s[0, :, pl.ds(pl.multiple_of(at * half, half), half)] = dq_s[side]
    stores = [begin(out_s.at[0], outs[0], out_sem.at[0])]
    for load in loads:
        load.wait()
    for side in range(INNER):
        summed = terms_s[side].astype(jnp.float32)
        for c in range(side + INNER, count, INNER):
            summed = summed + terms_s[c].astype(jnp.float32)
        summed = summed.astype(jnp.bfloat16)
        for kind in range(2):
            cols = slice(side * half, (side + 1) * half)
            out_s[1 + kind, :, cols] = summed[:, kind * half : (kind + 1) * half]
    for index in (1, 2):
        stores.append(begin(out_s.at[index], outs[index], out_sem.at[index]))
    for store in stores:
        store.wait()


def collect(at, dq_mine, dq_recv, terms):
    count, rows, both = terms.shape
    half = both // 2
    return call(
        collect_kernel,
        [bf16(rows, INNER * half)] * 3,
        [SMEM] + [ANY] * 3,
        [ANY] * 3,
        [
            pltpu.VMEM((INNER, rows, half), jnp.bfloat16),
            pltpu.VMEM((count, rows, both), jnp.bfloat16),
            pltpu.VMEM((3, rows, INNER * half), jnp.bfloat16),
            pltpu.SemaphoreType.DMA((INNER,)),
            pltpu.SemaphoreType.DMA((count,)),
            pltpu.SemaphoreType.DMA((3,)),
        ],
        3,
        "collect",
    )(at, dq_mine, dq_recv, terms)


def per_device(
    queries, key_heads, value_heads, grad_output, out_weight, block_pattern, global_offsets
):
    dp_count, ctx_count, tp_count = (lax.axis_size(name) for name in ("dp", "ctx", "tp"))
    dp_at, ctx_at, tp_at = (lax.axis_index(name) for name in ("dp", "ctx", "tp"))
    outer = ctx_count // INNER
    outer_at, inner_at = ctx_at // INNER, ctx_at % INNER
    picked = tp_count // dp_count

    def ctx_pairs(step, side, dp_step=0):
        moved = [(c + step * INNER) % ctx_count ^ side for c in range(ctx_count)]
        if not dp_step:
            return list(enumerate(moved))
        return [
            (d * ctx_count + c, (d + dp_step) % dp_count * ctx_count + moved[c])
            for d in range(dp_count)
            for c in range(ctx_count)
        ]

    def shift_pairs(count, step):
        return [(i, (i + step) % count) for i in range(count)]

    def dp_steps(which):
        return [(which * picked + i - tp_at) % tp_count for i in range(picked)]

    routes = [(step, side) for step in range(outer) for side in range(INNER)]
    sources = [
        ((outer_at - step) % outer) * INNER + (inner_at + side) % INNER for step, side in routes
    ]
    scalars = [inner_at, outer_at, tp_at] + sources
    columns_at = len(scalars)
    scalars = scalars + [(tp_at + step) % tp_count for step in range(1, tp_count)]
    groups_at = len(scalars)
    for step in range(dp_count):
        scalars = scalars + dp_steps((dp_at + step) % dp_count)
    at = jnp.stack(scalars)

    grad_own = grad_output[0]
    grads = [grad_own] + [
        lax.ppermute(grad_own, "tp", shift_pairs(tp_count, -step)) for step in range(1, tp_count)
    ]
    kv_mine, kv_theirs = part_heads(at, key_heads[0], value_heads[0])
    kv_recv = lax.ppermute(kv_theirs, "ctx", ctx_pairs(0, 1))
    kv_blocks = [
        lax.ppermute(kv_recv if side else kv_mine, "ctx", ctx_pairs(step, 0))
        if step
        else (kv_recv if side else kv_mine)
        for step, side in routes
    ]
    first, key_mask, row_mask, q_theirs = prelude(
        at, block_pattern, global_offsets, queries[0], grad_own, out_weight, (kv_recv,)
    )
    q_recv = lax.ppermute(q_theirs, "ctx", ctx_pairs(0, 1))
    partners = [(step, side) for step in range(dp_count) for side in range(INNER)][1:]

    def to_partners(arrays):
        return [
            lax.ppermute(held, ("dp", "ctx") if step else "ctx", ctx_pairs(0, side, step))
            for (step, side), held in zip(partners, arrays)
        ]

    g_mine, g_theirs, grad_sends = grad_heads(
        at, columns_at, groups_at, first, out_weight, grads, partners, outer, picked
    )
    g_recv = lax.ppermute(g_theirs, "ctx", ctx_pairs(0, 1))
    swapped = to_partners(grad_sends)

    weights, inverse, attn = forward(at, queries[0], q_recv, key_mask, row_mask, kv_blocks)
    dq_mine, dq_theirs, parts, attn = backward(
        at, queries[0], q_recv, g_mine, g_recv, attn, inverse, weights, kv_blocks
    )
    terms = lax.all_to_all(parts, "ctx", split_axis=0, concat_axis=0, tiled=True)
    dq_recv = lax.ppermute(dq_theirs, "ctx", ctx_pairs(0, 1))

    attn_all = [attn] + to_partners([attn] * len(partners))
    weight_sums = weight_terms(at, groups_at, attn_all, grads, swapped)
    weight_parts = [
        lax.ppermute(weight_sums[step], "ctx", ctx_pairs(step, 0)) for step in range(1, outer)
    ]
    grad_q, grad_k, grad_v = collect(at, dq_mine, dq_recv, terms)
    grad_weight = weight_sums[0].astype(jnp.float32)
    for part in weight_parts:
        grad_weight = grad_weight + part.astype(jnp.float32)

    return grad_q[None], grad_k[None], grad_v[None], grad_weight.astype(jnp.bfloat16)


def solution(mesh):
    in_specs = (
        P("dp", "ctx", "tp"),
        P("dp", "ctx", "tp"),
        P("dp", "ctx", "tp"),
        P("dp", "ctx", "tp"),
        P("tp", None),
        P(),
        P(),
    )
    out_specs = (
        P("dp", "ctx", "tp"),
        P("dp", "ctx", "tp"),
        P("dp", "ctx", "tp"),
        P("tp", ("dp", "ctx")),
    )
    return jax.shard_map(
        per_device, mesh=mesh, in_specs=in_specs, out_specs=out_specs, check_vma=False
    )
```

```python
import functools

import jax
import jax.numpy as jnp
from jax import lax
from jax.experimental import pallas as pl
from jax.experimental.pallas import tpu as pltpu
from jax.sharding import PartitionSpec as P

HD = 128
MASKED = -1e30
INNER = 2
SOURCES = 3
ANY = pl.BlockSpec(memory_space=pl.ANY)
VMEM = pl.BlockSpec(memory_space=pltpu.VMEM)
SMEM = pl.BlockSpec(memory_space=pltpu.SMEM)


def against(left_op, right_op):
    return lax.dot_general(
        left_op, right_op, (((1,), (1,)), ((), ())), preferred_element_type=jnp.float32
    )


def product(left_op, right_op):
    return jnp.dot(left_op, right_op, preferred_element_type=jnp.float32)


def begin(source, target, semaphore):
    copy = pltpu.make_async_copy(source, target, semaphore)
    copy.start()
    return copy


def call(kernel, out_shape, in_specs, out_specs, scratch, micros, name, after=()):
    skipped = len(after)
    in_specs = [ANY] * skipped + in_specs
    run = pl.pallas_call(
        lambda *refs: kernel(*refs[skipped:]),
        out_shape=out_shape,
        in_specs=in_specs,
        out_specs=out_specs,
        scratch_shapes=scratch,
        compiler_params=pltpu.CompilerParams(vmem_limit_bytes=64 * 1024 * 1024),
        cost_estimate=pl.CostEstimate(
            flops=int(micros * 1e9), bytes_accessed=int(micros * 3e6), transcendentals=0
        ),
        name=name,
    )

    def placed(*args):
        args = [
            pltpu.with_memory_space_constraint(arg, pltpu.HBM) if spec is ANY else arg
            for spec, arg in zip(in_specs, (*after, *args))
        ]
        return run(*args)

    return placed


def bf16(*shape):
    return pltpu.HBM(shape, jnp.bfloat16)


def f32(*shape):
    return pltpu.HBM(shape, jnp.float32)


def part_kernel(at_ref, k_ref, v_ref, kv_mine, kv_theirs, held_s, in_sem, out_sem):
    half = kv_mine.shape[1] // 2
    loads = [begin(held, held_s.at[i], in_sem.at[i]) for i, held in enumerate((k_ref, v_ref))]
    mine = pl.ds(pl.multiple_of(at_ref[0] * half, half), half)
    theirs = pl.ds(pl.multiple_of((1 - at_ref[0]) * half, half), half)
    copies = []
    for index in range(2):
        loads[index].wait()
        place = slice(index * half, (index + 1) * half)
        for side, (cols, out) in enumerate(((mine, kv_mine), (theirs, kv_theirs))):
            sem = out_sem.at[2 * index + side]
            copies.append(begin(held_s.at[index, :, cols], out.at[:, place], sem))
    for copy in copies:
        copy.wait()


def part_heads(at, keys, values):
    rows, feats = keys.shape
    return call(
        part_kernel,
        [bf16(rows, feats), bf16(rows, feats)],
        [SMEM] + [ANY] * 2,
        [ANY] * 2,
        [
            pltpu.VMEM((2, rows, feats), jnp.bfloat16),
            pltpu.SemaphoreType.DMA((2,)),
            pltpu.SemaphoreType.DMA((4,)),
        ],
        2,
        "part_heads",
    )(at, keys, values)


def prelude_kernel(at_ref, pattern, offsets, q_ref, grad_ref, weight_ref, *refs):
    first, key_mask, row_mask, q_theirs = refs[:4]
    grad_s, weight_s, first_s, mask_s, row_s, q_s, sem, out_sem = refs[4:]
    half = q_theirs.shape[1]
    theirs = pl.ds(pl.multiple_of((1 - at_ref[0]) * half, half), half)
    q_load = begin(q_ref.at[:, theirs], q_s, sem.at[2])
    rows, width = grad_s.shape
    block_count, glob_count = offsets.shape
    start = pl.multiple_of(at_ref[2] * width, width)
    loads = [
        begin(grad_ref, grad_s, sem.at[0]),
        begin(weight_ref.at[:, pl.ds(start, width)], weight_s, sem.at[1]),
    ]
    q_load.wait()
    stores = [begin(q_s, q_theirs, out_sem.at[3])]
    own = at_ref[1] * INNER + at_ref[0]
    partner = at_ref[1] * INNER + 1 - at_ref[0]
    lane = lax.broadcasted_iota(jnp.int32, (1, HD), 1)
    row_at = lax.broadcasted_iota(jnp.int32, (rows, HD), 0)
    col_at = lax.broadcasted_iota(jnp.int32, (8, rows), 1)
    group_at = lax.broadcasted_iota(jnp.int32, (8, rows), 0)
    for index in range(block_count):
        block = at_ref[SOURCES + index]
        hidden = []
        for target in (own, partner):
            seen = jnp.abs(block - target) <= 1
            for r in range(pattern.shape[1]):
                seen = seen | (pattern[target, r] == block)
            hidden.append(jnp.where(seen, 0, 1))
        lane_hidden = jnp.where(lane == 0, hidden[0], jnp.where(lane == 1, hidden[1], 0))
        hidden_rows = jnp.broadcast_to(lane_hidden, (rows, HD))
        for r in range(glob_count):
            hidden_rows = jnp.where(row_at == offsets[block, r], 0, hidden_rows)
        mask_s[index * rows : (index + 1) * rows, :] = hidden_rows.astype(jnp.float32).astype(
            jnp.bfloat16
        )
    for group, target in enumerate((own, partner)):
        local = jnp.where(group_at == group, MASKED, 0.0)
        for r in range(glob_count):
            local = jnp.where(col_at == offsets[target, r], 0.0, local)
        row_s[:, group * rows : (group + 1) * rows] = local
    stores.append(begin(mask_s, key_mask, out_sem.at[0]))
    stores.append(begin(row_s, row_mask, out_sem.at[1]))
    for load in loads:
        load.wait()
    first_s[...] = against(weight_s[...], grad_s[...])
    stores.append(begin(first_s, first, out_sem.at[2]))
    for store in stores:
        store.wait()


def prelude(at, pattern, offsets, queries, grad_own, out_weight, after):
    rows, width = grad_own.shape
    feats = out_weight.shape[0]
    keys = offsets.shape[0] * rows
    half = queries.shape[1] // INNER
    return call(
        prelude_kernel,
        [
            f32(feats, rows),
            bf16(keys, HD),
            f32(8, 2 * rows),
            bf16(rows, half),
        ],
        [SMEM] * 3 + [ANY] * 3,
        [ANY] * 4,
        [
            pltpu.VMEM((rows, width), jnp.bfloat16),
            pltpu.VMEM((feats, width), jnp.bfloat16),
            pltpu.VMEM((feats, rows), jnp.float32),
            pltpu.VMEM((keys, HD), jnp.bfloat16),
            pltpu.VMEM((8, 2 * rows), jnp.float32),
            pltpu.VMEM((rows, half), jnp.bfloat16),
            pltpu.SemaphoreType.DMA((3,)),
            pltpu.SemaphoreType.DMA((4,)),
        ],
        4,
        "prelude",
        after,
    )(at, pattern, offsets, queries, grad_own, out_weight)


def forward_kernel(block_count, head_count, at_ref, q_ref, q_recv, key_mask, row_mask, *refs):
    kv_refs, refs = refs[:block_count], refs[block_count:]
    e_out, inv_out, attn_out = refs[:3]
    q_s, mask_s, kv_s, e_s, s_ref, attn_s, inv_s, row_s, sem, kv_sem, e_sem, out_sem = refs[3:]
    rows = q_recv.shape[0]
    feats = head_count * HD
    score_scale = HD ** (-0.5)
    mine = pl.ds(pl.multiple_of(at_ref[0] * feats, feats), feats)
    loads = [
        begin(q_ref.at[:, mine], q_s.at[0], sem.at[0]),
        begin(q_recv, q_s.at[1], sem.at[1]),
        begin(key_mask, mask_s, sem.at[2]),
        begin(row_mask, row_s, sem.at[3]),
    ]
    kv_loads = [begin(kv_refs[j], kv_s.at[j], kv_sem.at[j]) for j in range(block_count)]
    for load in loads:
        load.wait()
    rows_low = row_s[...].astype(jnp.bfloat16)
    hidden = jnp.concatenate([rows_low, jnp.zeros((HD - 8, 2 * rows), jnp.bfloat16)], axis=0)
    stores = []
    for head in range(head_count):
        cols = slice(head * HD, (head + 1) * HD)
        vcols = slice(feats + head * HD, feats + (head + 1) * HD)
        q_t = jnp.concatenate(
            [jnp.transpose(q_s[0, :, cols]), jnp.transpose(q_s[1, :, cols])], axis=1
        )
        q_t = jnp.concatenate([q_t, hidden], axis=0)
        top = jnp.full((1, 2 * rows), MASKED, jnp.float32)
        for j in range(block_count):
            if head == 0:
                kv_loads[j].wait()
            keys = slice(j * rows, (j + 1) * rows)
            scores = product(jnp.concatenate([kv_s[j, :, cols], mask_s[keys, :]], axis=1), q_t)
            s_ref[keys, :] = scores
            top = jnp.maximum(top, jnp.max(scores, axis=0, keepdims=True))
        total = jnp.zeros((1, 2 * rows), jnp.float32)
        attn_t = jnp.zeros((HD, 2 * rows), jnp.float32)
        for j in range(block_count):
            keys = slice(j * rows, (j + 1) * rows)
            weights = jnp.exp((s_ref[keys, :] - top) * score_scale)
            total = total + jnp.sum(weights, axis=0, keepdims=True)
            low = weights.astype(jnp.bfloat16)
            e_s[head, keys, :] = low
            stores.append(
                begin(e_s.at[head, keys], e_out.at[head, keys], e_sem.at[head * block_count + j])
            )
            attn_t = attn_t + product(jnp.transpose(kv_s[j, :, vcols]), low)
        inverse = 1.0 / total
        inv_s[head : head + 1, :] = inverse
        attn_low = (attn_t * inverse).astype(jnp.bfloat16)
        attn_s[0, cols, :] = attn_low[:, :rows]
        attn_s[1, cols, :] = attn_low[:, rows:]
    stores.append(begin(attn_s, attn_out, out_sem.at[0]))
    stores.append(begin(inv_s, inv_out, out_sem.at[1]))
    for store in stores:
        store.wait()


def forward(at, queries, q_recv, key_mask, row_mask, kv_blocks, after=()):
    block_count = len(kv_blocks)
    rows, feats = q_recv.shape
    heads = feats // HD
    keys = block_count * rows
    return call(
        functools.partial(forward_kernel, block_count, heads),
        [
            bf16(heads, keys, 2 * rows),
            f32(max(heads, 8), 2 * rows),
            bf16(INNER, feats, rows),
        ],
        [SMEM] + [ANY] * (4 + block_count),
        [ANY] * 3,
        [
            pltpu.VMEM((2, rows, feats), jnp.bfloat16),
            pltpu.VMEM((keys, HD), jnp.bfloat16),
            pltpu.VMEM((block_count, rows, 2 * feats), jnp.bfloat16),
            pltpu.VMEM((heads, keys, 2 * rows), jnp.bfloat16),
            pltpu.VMEM((keys, 2 * rows), jnp.float32),
            pltpu.VMEM((2, feats, rows), jnp.bfloat16),
            pltpu.VMEM((max(heads, 8), 2 * rows), jnp.float32),
            pltpu.VMEM((8, 2 * rows), jnp.float32),
            pltpu.SemaphoreType.DMA((4,)),
            pltpu.SemaphoreType.DMA((block_count,)),
            pltpu.SemaphoreType.DMA((heads * block_count,)),
            pltpu.SemaphoreType.DMA((2,)),
        ],
        6,
        "forward",
        after,
    )(at, queries, q_recv, key_mask, row_mask, *kv_blocks)


def backward_kernel(block_count, head_count, at_ref, *refs):
    q_ref, q_recv, g_mine, g_recv, attn_ref, inv_ref, e_ref = refs[:7]
    kv_refs, refs = refs[7 : 7 + block_count], refs[7 + block_count :]
    outer = block_count // INNER
    dq_mine, dq_theirs, attn_out = refs[:3]
    part_outs, refs = refs[3 : 3 + outer], refs[3 + outer :]
    q_s, t_s, attn_s, inv_s, kv_s, e_s, part_s, dq_s, sem, kv_sem, e_sem, part_sem, dq_sem = refs
    rows = q_recv.shape[0]
    feats = head_count * HD
    score_scale = HD ** (-0.5)
    mine = pl.ds(pl.multiple_of(at_ref[0] * feats, feats), feats)
    loads = [begin(q_ref.at[:, mine], q_s.at[0], sem.at[0]), begin(q_recv, q_s.at[1], sem.at[1])]
    for index, held in enumerate((g_mine, g_recv)):
        loads.append(begin(held, t_s.at[index], sem.at[2 + index]))
    loads.append(begin(attn_ref, attn_s, sem.at[4]))
    loads.append(begin(inv_ref, inv_s, sem.at[5]))
    kv_loads, e_loads, stores = [], {}, []
    for j in range(block_count):
        keys = slice(j * rows, (j + 1) * rows)
        kv_loads.append(begin(kv_refs[j], kv_s.at[j], kv_sem.at[j]))
        for head in range(head_count):
            e_loads[head, j] = begin(
                e_ref.at[head, keys], e_s.at[head, keys], e_sem.at[head * block_count + j]
            )
    for load in loads:
        load.wait()
    stores.append(begin(attn_s, attn_out, dq_sem.at[2]))
    for head in range(head_count):
        cols = slice(head * HD, (head + 1) * HD)
        vcols = slice(feats + head * HD, feats + (head + 1) * HD)
        inverse = inv_s[head : head + 1, :]
        g_t = jnp.concatenate([t_s[0, cols, :], t_s[1, cols, :]], axis=1).astype(jnp.float32)
        attn_t = jnp.concatenate([attn_s[0, cols, :], attn_s[1, cols, :]], axis=1)
        row_dot = jnp.sum(g_t * attn_t.astype(jnp.float32), axis=0, keepdims=True) * inverse
        g_t = (g_t * inverse).astype(jnp.bfloat16)
        grad = jnp.transpose(g_t)
        query = jnp.concatenate([q_s[0, :, cols], q_s[1, :, cols]], axis=0)
        dq_t = jnp.zeros((HD, 2 * rows), jnp.float32)
        for j in range(block_count):
            keys = slice(j * rows, (j + 1) * rows)
            if head == 0:
                kv_loads[j].wait()
            e_loads[head, j].wait()
            low = e_s[head, keys, :]
            dprobs = product(kv_s[j, :, vcols], g_t)
            dscore = (low.astype(jnp.float32) * (dprobs - row_dot)).astype(jnp.bfloat16)
            dq_t = dq_t + product(jnp.transpose(kv_s[j, :, cols]), dscore)
            part_s[j, :, cols] = (score_scale * product(dscore, query)).astype(jnp.bfloat16)
            part_s[j, :, vcols] = product(low, grad).astype(jnp.bfloat16)
            if head == head_count - 1:
                stores.append(begin(part_s.at[j], part_outs[j // INNER].at[j % INNER], part_sem.at[j]))
        dquery = (score_scale * jnp.transpose(dq_t)).astype(jnp.bfloat16)
        dq_s[0, :, cols] = dquery[:rows]
        dq_s[1, :, cols] = dquery[rows:]
    stores.append(begin(dq_s.at[0], dq_mine, dq_sem.at[0]))
    stores.append(begin(dq_s.at[1], dq_theirs, dq_sem.at[1]))
    for store in stores:
        store.wait()


def backward(at, queries, q_recv, g_mine, g_recv, attn, inverse, weights, kv_blocks):
    block_count = len(kv_blocks)
    rows, feats = q_recv.shape
    heads = feats // HD
    keys = block_count * rows
    outer = block_count // INNER
    out = call(
        functools.partial(backward_kernel, block_count, heads),
        [bf16(rows, feats)] * 2 + [bf16(*attn.shape)] + [bf16(INNER, rows, 2 * feats)] * outer,
        [SMEM] + [ANY] * (7 + block_count),
        [ANY] * (3 + outer),
        [
            pltpu.VMEM((2, rows, feats), jnp.bfloat16),
            pltpu.VMEM((2, feats, rows), jnp.bfloat16),
            pltpu.VMEM(attn.shape, jnp.bfloat16),
            pltpu.VMEM(inverse.shape, jnp.float32),
            pltpu.VMEM((block_count, rows, 2 * feats), jnp.bfloat16),
            pltpu.VMEM((heads, keys, 2 * rows), jnp.bfloat16),
            pltpu.VMEM((block_count, rows, 2 * feats), jnp.bfloat16),
            pltpu.VMEM((2, rows, feats), jnp.bfloat16),
            pltpu.SemaphoreType.DMA((6,)),
            pltpu.SemaphoreType.DMA((block_count,)),
            pltpu.SemaphoreType.DMA((heads * block_count,)),
            pltpu.SemaphoreType.DMA((block_count,)),
            pltpu.SemaphoreType.DMA((3,)),
        ],
        8,
        "backward",
    )(at, queries, q_recv, g_mine, g_recv, attn, inverse, weights, *kv_blocks)
    return out[0], out[1], out[2], out[3:]


def chunk(at_ref, steps_at, parts, place, width, target, semaphore):
    pieces = parts[0].shape[1] // width
    which = at_ref[steps_at + place // pieces]
    cols = pl.ds(pl.multiple_of(lax.rem(place, pieces) * width, width), width)
    for k, part in enumerate(parts):

        @pl.when(which == k)
        def _():
            begin(part.at[:, cols], target, semaphore)

    return pltpu.make_async_copy(parts[0].at[:, cols], target, semaphore)


def grad_heads_kernel(part_count, picked, columns_at, groups_at, at_ref, first_ref, weight_ref, *refs):
    grads, refs = refs[:part_count], refs[part_count:]
    outs, sends, refs = refs[:2], refs[2], refs[3:]
    first_s, grad_s, weight_s, out_s, first_sem, weight_sem, grad_sem, send_sem, out_sem = refs
    half = out_s.shape[1]
    width = grads[0].shape[1]
    first_load = begin(first_ref, first_s, first_sem)
    weight_loads, grad_loads = [], []
    for k in range(1, part_count):
        start = pl.multiple_of(at_ref[columns_at + k - 1] * width, width)
        columns = weight_ref.at[:, pl.ds(start, width)]
        weight_loads.append(begin(columns, weight_s.at[k - 1], weight_sem.at[k - 1]))
        grad_loads.append(begin(grads[k], grad_s.at[k], grad_sem.at[k]))
    own_load = begin(grads[0], grad_s.at[0], grad_sem.at[0])
    first_load.wait()
    summed = first_s[...]
    for k in range(1, part_count):
        weight_loads[k - 1].wait()
        grad_loads[k - 1].wait()
        summed = summed + against(weight_s[k - 1], grad_s[k])
    first_s[...] = summed
    copies = []
    for side, at in enumerate((at_ref[0], 1 - at_ref[0])):
        kept = first_s[pl.ds(pl.multiple_of(at * half, half), half), :]
        out_s[side] = kept.astype(jnp.bfloat16)
        copies.append(begin(out_s.at[side], outs[side], out_sem.at[side]))
    own_load.wait()
    parts = [grad_s.at[k] for k in range(part_count)]
    route_count, outer, _, block = sends.shape
    for index in range(route_count):
        for k in range(outer):
            place = lax.rem(at_ref[1] + k, outer) * INNER + index % INNER
            target, sem = sends.at[index, k], send_sem.at[index * outer + k]
            steps_at = groups_at + index // INNER * picked
            copies.append(chunk(at_ref, steps_at, parts, place, block, target, sem))
    for copy in copies:
        copy.wait()


def grad_heads(at, columns_at, groups_at, first, out_weight, grads, route_count, outer, picked):
    feats, rows = first.shape
    half = feats // INNER
    count = len(grads)
    width = grads[0].shape[1]
    block = picked * width // (outer * INNER)
    return call(
        functools.partial(grad_heads_kernel, count, picked, columns_at, groups_at),
        [bf16(half, rows), bf16(half, rows), bf16(route_count, outer, rows, block)],
        [SMEM] + [ANY] * (2 + count),
        [ANY] * 3,
        [
            pltpu.VMEM((feats, rows), jnp.float32),
            pltpu.VMEM((count, rows, width), jnp.bfloat16),
            pltpu.VMEM((count - 1, feats, width), jnp.bfloat16),
            pltpu.VMEM((INNER, half, rows), jnp.bfloat16),
            pltpu.SemaphoreType.DMA,
            pltpu.SemaphoreType.DMA((count - 1,)),
            pltpu.SemaphoreType.DMA((count,)),
            pltpu.SemaphoreType.DMA((route_count * outer,)),
            pltpu.SemaphoreType.DMA((INNER,)),
        ],
        4,
        "grad_heads",
    )(at, first, out_weight, *grads)


def weight_kernel(doc_count, doc_at, at_ref, *refs):
    route_count = INNER * doc_count
    attn, grads, refs = refs[:route_count], refs[route_count], refs[route_count + 1 :]
    attn_s, grad_s, out_s, attn_sem, grad_sem, out_sem = refs[-6:]
    outs = refs[:-6]
    outer, feats, width = out_s.shape
    half = feats // INNER
    attn_loads, grad_loads = [], []
    for doc in range(doc_count):
        for side in range(INNER):
            for group, at in enumerate((at_ref[0], 1 - at_ref[0])):
                source = attn[doc * INNER + group].at[side ^ group]
                target = attn_s.at[doc * INNER + side, pl.ds(pl.multiple_of(at * half, half), half)]
                sem = attn_sem.at[(doc * INNER + side) * INNER + group]
                attn_loads.append(begin(source, target, sem))
    for k in range(outer):
        loads = []
        for index in range(route_count):
            doc = lax.rem(at_ref[doc_at] + doc_count - index // INNER, doc_count)
            at = (1 - at_ref[0]) if index % INNER else at_ref[0]
            sem = grad_sem.at[index * outer + k]
            loads.append(begin(grads.at[doc * INNER + at, k], grad_s.at[index, k], sem))
        grad_loads.append(loads)
    for load in attn_loads:
        load.wait()
    stores = []
    for k in range(outer):
        term = 0.0
        for index in range(route_count):
            grad_loads[k][index].wait()
            term = term + product(attn_s[index], grad_s[index, k])
        out_s[k] = term.astype(out_s.dtype)
        stores.append(begin(out_s.at[k], outs[k], out_sem.at[k]))
    for store in stores:
        store.wait()


def weight_terms(at, doc_at, attn, grads, after=()):
    _, half, rows = attn[0].shape
    _, outer, _, width = grads.shape
    feats = half * INNER
    routes = len(attn)
    return call(
        functools.partial(weight_kernel, routes // INNER, doc_at),
        [bf16(feats, width)] * outer,
        [SMEM] + [ANY] * (routes + 1),
        [ANY] * outer,
        [
            pltpu.VMEM((routes, feats, rows), jnp.bfloat16),
            pltpu.VMEM((routes, outer, rows, width), jnp.bfloat16),
            pltpu.VMEM((outer, feats, width), jnp.bfloat16),
            pltpu.SemaphoreType.DMA((routes * INNER,)),
            pltpu.SemaphoreType.DMA((routes * outer,)),
            pltpu.SemaphoreType.DMA((outer,)),
        ],
        5,
        "weight_terms",
        after,
    )(at, *attn, grads)


def add_kernel(count, *refs):
    terms, (mine, theirs) = refs[:count], refs[count : count + 2]
    terms_s, out_s, term_sem, out_sem = refs[count + 2 :]
    loads = [
        begin(terms[c].at[side], terms_s.at[c, side], term_sem.at[c * INNER + side])
        for side in (1, 0)
        for c in range(count)
    ]
    stores = []
    for index, (side, out) in enumerate(((1, theirs), (0, mine))):
        for load in loads[index * count : (index + 1) * count]:
            load.wait()
        summed = terms_s[0, side].astype(jnp.float32)
        for c in range(1, count):
            summed = summed + terms_s[c, side].astype(jnp.float32)
        out_s[side] = summed.astype(jnp.bfloat16)
        stores.append(begin(out_s.at[side], out, out_sem.at[side]))
    for store in stores:
        store.wait()


def add_terms(terms, after):
    _, rows, width = terms[0].shape
    count = len(terms)
    return call(
        functools.partial(add_kernel, count),
        [bf16(rows, width)] * 2,
        [ANY] * count,
        [ANY] * 2,
        [
            pltpu.VMEM((count, INNER, rows, width), jnp.bfloat16),
            pltpu.VMEM((INNER, rows, width), jnp.bfloat16),
            pltpu.SemaphoreType.DMA((count * INNER,)),
            pltpu.SemaphoreType.DMA((INNER,)),
        ],
        2,
        "add_terms",
        after,
    )(*terms)


def join_kernel(at_ref, dq_mine, dq_recv, mine, recv, *refs):
    outs, (held_s, out_s, sem, out_sem) = refs[:3], refs[3:]
    half = dq_mine.shape[1]
    loads = [
        begin(dq_mine, held_s.at[0, 0], sem.at[0]),
        begin(dq_recv, held_s.at[1, 0], sem.at[1]),
    ]
    for side, held in enumerate((mine, recv)):
        for index in range(2):
            source = held.at[:, index * half : (index + 1) * half]
            loads.append(begin(source, held_s.at[side, 1 + index], sem.at[2 + 2 * side + index]))
    for load in loads:
        load.wait()
    stores = []
    for index, out in enumerate(outs):
        for side, at in enumerate((at_ref[0], 1 - at_ref[0])):
            cols = pl.ds(pl.multiple_of(at * half, half), half)
            out_s[index, :, cols] = held_s[side, index]
        stores.append(begin(out_s.at[index], out, out_sem.at[index]))
    for store in stores:
        store.wait()


def join_heads(at, dq_mine, dq_recv, mine, recv):
    rows, half = dq_mine.shape
    return call(
        join_kernel,
        [bf16(rows, INNER * half)] * 3,
        [SMEM] + [ANY] * 4,
        [ANY] * 3,
        [
            pltpu.VMEM((INNER, 3, rows, half), jnp.bfloat16),
            pltpu.VMEM((3, rows, INNER * half), jnp.bfloat16),
            pltpu.SemaphoreType.DMA((6,)),
            pltpu.SemaphoreType.DMA((3,)),
        ],
        2,
        "join_heads",
    )(at, dq_mine, dq_recv, mine, recv)


def per_device(
    queries, key_heads, value_heads, grad_output, out_weight, block_pattern, global_offsets
):
    dp_count, ctx_count, tp_count = (lax.axis_size(name) for name in ("dp", "ctx", "tp"))
    dp_at, ctx_at, tp_at = (lax.axis_index(name) for name in ("dp", "ctx", "tp"))
    outer = ctx_count // INNER
    outer_at, inner_at = ctx_at // INNER, ctx_at % INNER
    picked = tp_count // dp_count

    def ctx_pairs(step, side, dp_step=0):
        moved = [(c + step * INNER) % ctx_count ^ side for c in range(ctx_count)]
        if not dp_step:
            return list(enumerate(moved))
        return [
            (d * ctx_count + c, (d + dp_step) % dp_count * ctx_count + moved[c])
            for d in range(dp_count)
            for c in range(ctx_count)
        ]

    def shift_pairs(count, step):
        return [(i, (i + step) % count) for i in range(count)]

    def dp_steps(which):
        return [(which * picked + i - tp_at) % tp_count for i in range(picked)]

    routes = [(step, side) for step in range(outer) for side in range(INNER)]
    sources = [
        ((outer_at - step) % outer) * INNER + (inner_at + side) % INNER for step, side in routes
    ]
    scalars = [inner_at, outer_at, tp_at] + sources
    columns_at = len(scalars)
    scalars = scalars + [(tp_at + step) % tp_count for step in range(1, tp_count)]
    groups_at = len(scalars)
    for step in range(dp_count):
        scalars = scalars + dp_steps(step)
    doc_at = len(scalars)
    at = jnp.stack(scalars + [dp_at])

    grad_own = grad_output[0]
    grads = [grad_own] + [
        lax.ppermute(grad_own, "tp", shift_pairs(tp_count, -step)) for step in range(1, tp_count)
    ]
    kv_mine, kv_theirs = part_heads(at, key_heads[0], value_heads[0])
    kv_recv = lax.ppermute(kv_theirs, "ctx", ctx_pairs(0, 1))
    kv_blocks = [
        lax.ppermute(kv_recv if side else kv_mine, "ctx", ctx_pairs(step, 0))
        if step
        else (kv_recv if side else kv_mine)
        for step, side in routes
    ]
    first, key_mask, row_mask, q_theirs = prelude(
        at, block_pattern, global_offsets, queries[0], grad_own, out_weight, (kv_recv,)
    )
    q_recv = lax.ppermute(q_theirs, "ctx", ctx_pairs(0, 1))
    g_mine, g_theirs, sends = grad_heads(
        at, columns_at, groups_at, first, out_weight, grads, dp_count * INNER, outer, picked
    )
    g_recv = lax.ppermute(g_theirs, "ctx", ctx_pairs(0, 1))
    sharers = [
        [d * ctx_count + o * INNER + i for d in range(dp_count) for i in range(INNER)]
        for o in range(outer)
    ]
    columns = lax.all_to_all(
        sends, ("dp", "ctx"), split_axis=0, concat_axis=0, axis_index_groups=sharers, tiled=True
    )

    weights, inverse, attn = forward(at, queries[0], q_recv, key_mask, row_mask, kv_blocks)
    dq_mine, dq_theirs, attn, parts = backward(
        at, queries[0], q_recv, g_mine, g_recv, attn, inverse, weights, kv_blocks
    )
    terms = [
        lax.ppermute(part, "ctx", ctx_pairs(-step, 0)) if step else part
        for step, part in enumerate(parts)
    ]

    attn_all = [attn, lax.ppermute(attn, "ctx", ctx_pairs(0, 1))]
    for step in range(1, dp_count):
        pairs = shift_pairs(dp_count, step)
        attn_all = attn_all + [lax.ppermute(held, "dp", pairs) for held in attn_all[:INNER]]
    weight_sums = weight_terms(at, doc_at, attn_all, columns)
    weight_parts = [
        lax.ppermute(weight_sums[step], "ctx", ctx_pairs(step, 0)) for step in range(1, outer)
    ]

    dq_recv = lax.ppermute(dq_theirs, "ctx", ctx_pairs(0, 1))
    terms_mine, terms_theirs = add_terms(terms, (weight_sums[0],))
    terms_recv = lax.ppermute(terms_theirs, "ctx", ctx_pairs(0, 1))
    grad_q, grad_k, grad_v = join_heads(at, dq_mine, dq_recv, terms_mine, terms_recv)
    grad_weight = weight_sums[0].astype(jnp.float32)
    for part in weight_parts:
        grad_weight = grad_weight + part.astype(jnp.float32)
    grad_weight = grad_weight.astype(jnp.bfloat16)
    return grad_q[None], grad_k[None], grad_v[None], grad_weight


def solution(mesh):
    in_specs = (
        P("dp", "ctx", "tp"),
        P("dp", "ctx", "tp"),
        P("dp", "ctx", "tp"),
        P("dp", "ctx", "tp"),
        P("tp", None),
        P(),
        P(),
    )
    out_specs = (
        P("dp", "ctx", "tp"),
        P("dp", "ctx", "tp"),
        P("dp", "ctx", "tp"),
        P("tp", ("dp", "ctx")),
    )
    return jax.shard_map(
        per_device, mesh=mesh, in_specs=in_specs, out_specs=out_specs, check_vma=False
    )
```

```python
import functools

import jax
import jax.numpy as jnp
from jax import lax
from jax.experimental import pallas as pl
from jax.experimental.pallas import tpu as pltpu
from jax.sharding import PartitionSpec as P

HD = 128
MASKED = -1e30
INNER = 2
SOURCES = 3
ANY = pl.BlockSpec(memory_space=pl.ANY)
VMEM = pl.BlockSpec(memory_space=pltpu.VMEM)
SMEM = pl.BlockSpec(memory_space=pltpu.SMEM)


def against(left_op, right_op):
    return lax.dot_general(
        left_op, right_op, (((1,), (1,)), ((), ())), preferred_element_type=jnp.float32
    )


def product(left_op, right_op):
    return jnp.dot(left_op, right_op, preferred_element_type=jnp.float32)


def begin(source, target, semaphore):
    copy = pltpu.make_async_copy(source, target, semaphore)
    copy.start()
    return copy


def call(kernel, out_shape, in_specs, out_specs, scratch, micros, name, after=()):
    skipped = len(after)
    in_specs = [ANY] * skipped + in_specs
    run = pl.pallas_call(
        lambda *refs: kernel(*refs[skipped:]),
        out_shape=out_shape,
        in_specs=in_specs,
        out_specs=out_specs,
        scratch_shapes=scratch,
        compiler_params=pltpu.CompilerParams(vmem_limit_bytes=64 * 1024 * 1024),
        cost_estimate=pl.CostEstimate(
            flops=int(micros * 1e9), bytes_accessed=int(micros * 3e6), transcendentals=0
        ),
        name=name,
    )

    def placed(*args):
        args = [
            pltpu.with_memory_space_constraint(arg, pltpu.HBM) if spec is ANY else arg
            for spec, arg in zip(in_specs, (*after, *args))
        ]
        return run(*args)

    return placed


def bf16(*shape):
    return pltpu.HBM(shape, jnp.bfloat16)


def f32(*shape):
    return pltpu.HBM(shape, jnp.float32)


def part_kernel(at_ref, k_ref, v_ref, kv_mine, kv_theirs, held_s, in_sem, out_sem):
    half = kv_mine.shape[1] // 2
    loads = [begin(held, held_s.at[i], in_sem.at[i]) for i, held in enumerate((k_ref, v_ref))]
    mine = pl.ds(pl.multiple_of(at_ref[0] * half, half), half)
    theirs = pl.ds(pl.multiple_of((1 - at_ref[0]) * half, half), half)
    copies = []
    for index in range(2):
        loads[index].wait()
        place = slice(index * half, (index + 1) * half)
        for side, (cols, out) in enumerate(((mine, kv_mine), (theirs, kv_theirs))):
            sem = out_sem.at[2 * index + side]
            copies.append(begin(held_s.at[index, :, cols], out.at[:, place], sem))
    for copy in copies:
        copy.wait()


def part_heads(at, keys, values):
    rows, feats = keys.shape
    return call(
        part_kernel,
        [bf16(rows, feats), bf16(rows, feats)],
        [SMEM] + [ANY] * 2,
        [ANY] * 2,
        [
            pltpu.VMEM((2, rows, feats), jnp.bfloat16),
            pltpu.SemaphoreType.DMA((2,)),
            pltpu.SemaphoreType.DMA((4,)),
        ],
        2,
        "part_heads",
    )(at, keys, values)


def prelude_kernel(at_ref, pattern, offsets, grad_ref, weight_ref, *refs):
    first, key_mask, row_mask = refs[:3]
    grad_s, weight_s, first_s, mask_s, row_s, sem, out_sem = refs[3:]
    rows, width = grad_s.shape
    block_count, glob_count = offsets.shape
    start = pl.multiple_of(at_ref[2] * width, width)
    loads = [
        begin(grad_ref, grad_s, sem.at[0]),
        begin(weight_ref.at[:, pl.ds(start, width)], weight_s, sem.at[1]),
    ]
    stores = []
    own = at_ref[1] * INNER + at_ref[0]
    partner = at_ref[1] * INNER + 1 - at_ref[0]
    lane = lax.broadcasted_iota(jnp.int32, (1, HD), 1)
    row_at = lax.broadcasted_iota(jnp.int32, (rows, HD), 0)
    col_at = lax.broadcasted_iota(jnp.int32, (8, rows), 1)
    group_at = lax.broadcasted_iota(jnp.int32, (8, rows), 0)
    for index in range(block_count):
        block = at_ref[SOURCES + index]
        hidden = []
        for target in (own, partner):
            seen = jnp.abs(block - target) <= 1
            for r in range(pattern.shape[1]):
                seen = seen | (pattern[target, r] == block)
            hidden.append(jnp.where(seen, 0, 1))
        lane_hidden = jnp.where(lane == 0, hidden[0], jnp.where(lane == 1, hidden[1], 0))
        hidden_rows = jnp.broadcast_to(lane_hidden, (rows, HD))
        for r in range(glob_count):
            hidden_rows = jnp.where(row_at == offsets[block, r], 0, hidden_rows)
        mask_s[index * rows : (index + 1) * rows, :] = hidden_rows.astype(jnp.float32).astype(
            jnp.bfloat16
        )
    for group, target in enumerate((own, partner)):
        local = jnp.where(group_at == group, MASKED, 0.0)
        for r in range(glob_count):
            local = jnp.where(col_at == offsets[target, r], 0.0, local)
        row_s[:, group * rows : (group + 1) * rows] = local
    stores.append(begin(mask_s, key_mask, out_sem.at[0]))
    stores.append(begin(row_s, row_mask, out_sem.at[1]))
    for load in loads:
        load.wait()
    first_s[...] = against(weight_s[...], grad_s[...])
    stores.append(begin(first_s, first, out_sem.at[2]))
    for store in stores:
        store.wait()


def prelude(at, pattern, offsets, grad_own, out_weight, after):
    rows, width = grad_own.shape
    feats = out_weight.shape[0]
    keys = offsets.shape[0] * rows
    return call(
        prelude_kernel,
        [
            f32(feats, rows),
            bf16(keys, HD),
            f32(8, 2 * rows),
        ],
        [SMEM] * 3 + [ANY] * 2,
        [ANY] * 3,
        [
            pltpu.VMEM((rows, width), jnp.bfloat16),
            pltpu.VMEM((feats, width), jnp.bfloat16),
            pltpu.VMEM((feats, rows), jnp.float32),
            pltpu.VMEM((keys, HD), jnp.bfloat16),
            pltpu.VMEM((8, 2 * rows), jnp.float32),
            pltpu.SemaphoreType.DMA((2,)),
            pltpu.SemaphoreType.DMA((3,)),
        ],
        4,
        "prelude",
        after,
    )(at, pattern, offsets, grad_own, out_weight)


def attention_kernel(block_count, head_count, at_ref, q_ref, recv_ref, g_mine, key_mask, row_mask, *refs):
    kv_refs, refs = refs[:block_count], refs[block_count:]
    attn_mine, attn_theirs, dq_mine, dq_theirs, part_out = refs[:5]
    q_s, recv_s, g_s, mask_s, row_s, kv_s, e_s, s_ref, attn_s, dq_s, part_s = refs[5:16]
    sem, kv_sem, out_sem, part_sem = refs[16:]
    rows = q_ref.shape[0]
    feats = head_count * HD
    score_scale = HD ** (-0.5)
    mine = pl.ds(pl.multiple_of(at_ref[0] * feats, feats), feats)
    loads = [
        begin(q_ref.at[:, mine], q_s, sem.at[0]),
        begin(recv_ref, recv_s, sem.at[1]),
        begin(key_mask, mask_s, sem.at[2]),
        begin(row_mask, row_s, sem.at[3]),
        begin(g_mine, g_s, sem.at[4]),
    ]
    kv_loads = [begin(kv_refs[j], kv_s.at[j], kv_sem.at[j]) for j in range(block_count)]
    for load in loads:
        load.wait()
    rows_low = row_s[...].astype(jnp.bfloat16)
    hidden = jnp.concatenate([rows_low, jnp.zeros((HD - 8, 2 * rows), jnp.bfloat16)], axis=0)
    stores = []
    for head in range(head_count):
        cols = slice(head * HD, (head + 1) * HD)
        vcols = slice(feats + head * HD, feats + (head + 1) * HD)
        query_recv = recv_s[1, cols, :]
        q_t = jnp.concatenate([jnp.transpose(q_s[:, cols]), query_recv], axis=1)
        q_t = jnp.concatenate([q_t, hidden], axis=0)
        top = jnp.full((1, 2 * rows), MASKED, jnp.float32)
        for j in range(block_count):
            if head == 0:
                kv_loads[j].wait()
            keys = slice(j * rows, (j + 1) * rows)
            scores = product(jnp.concatenate([kv_s[j, :, cols], mask_s[keys, :]], axis=1), q_t)
            s_ref[keys, :] = scores
            top = jnp.maximum(top, jnp.max(scores, axis=0, keepdims=True))
        total = jnp.zeros((1, 2 * rows), jnp.float32)
        attn_t = jnp.zeros((HD, 2 * rows), jnp.float32)
        for j in range(block_count):
            keys = slice(j * rows, (j + 1) * rows)
            weights = jnp.exp((s_ref[keys, :] - top) * score_scale)
            total = total + jnp.sum(weights, axis=0, keepdims=True)
            low = weights.astype(jnp.bfloat16)
            e_s[keys, :] = low
            attn_t = attn_t + product(jnp.transpose(kv_s[j, :, vcols]), low)
        inverse = 1.0 / total
        attn_low = (attn_t * inverse).astype(jnp.bfloat16)
        attn_s[0, cols, :] = attn_low[:, :rows]
        attn_s[1, cols, :] = attn_low[:, rows:]
        if head == head_count - 1:
            stores.append(begin(attn_s.at[0], attn_mine, out_sem.at[0]))
            stores.append(begin(attn_s.at[1], attn_theirs, out_sem.at[1]))
        g_t = jnp.concatenate([g_s[cols, :], recv_s[0, cols, :]], axis=1).astype(jnp.float32)
        row_dot = jnp.sum(g_t * attn_low.astype(jnp.float32), axis=0, keepdims=True) * inverse
        g_t = (g_t * inverse).astype(jnp.bfloat16)
        grad = jnp.transpose(g_t)
        query = jnp.concatenate([q_s[:, cols], jnp.transpose(query_recv)], axis=0)
        dq_t = jnp.zeros((HD, 2 * rows), jnp.float32)
        for j in range(block_count):
            keys = slice(j * rows, (j + 1) * rows)
            low = e_s[keys, :]
            dprobs = product(kv_s[j, :, vcols], g_t)
            dscore = (low.astype(jnp.float32) * (dprobs - row_dot)).astype(jnp.bfloat16)
            dq_t = dq_t + product(jnp.transpose(kv_s[j, :, cols]), dscore)
            part_s[j, :, cols] = (score_scale * product(dscore, query)).astype(jnp.bfloat16)
            part_s[j, :, vcols] = product(low, grad).astype(jnp.bfloat16)
            if head == head_count - 1:
                target = part_out.at[at_ref[SOURCES + j]]
                stores.append(begin(part_s.at[j], target, part_sem.at[j]))
        dquery = (score_scale * jnp.transpose(dq_t)).astype(jnp.bfloat16)
        dq_s[0, :, cols] = dquery[:rows]
        dq_s[1, :, cols] = dquery[rows:]
    stores.append(begin(dq_s.at[0], dq_mine, out_sem.at[2]))
    stores.append(begin(dq_s.at[1], dq_theirs, out_sem.at[3]))
    for store in stores:
        store.wait()


def attention(at, queries, recv, g_mine, key_mask, row_mask, kv_blocks):
    block_count = len(kv_blocks)
    feats, rows = g_mine.shape
    heads = feats // HD
    keys = block_count * rows
    return call(
        functools.partial(attention_kernel, block_count, heads),
        [bf16(feats, rows)] * 2 + [bf16(rows, feats)] * 2 + [bf16(block_count, rows, 2 * feats)],
        [SMEM] + [ANY] * (5 + block_count),
        [ANY] * 5,
        [
            pltpu.VMEM((rows, feats), jnp.bfloat16),
            pltpu.VMEM((2, feats, rows), jnp.bfloat16),
            pltpu.VMEM((feats, rows), jnp.bfloat16),
            pltpu.VMEM((keys, HD), jnp.bfloat16),
            pltpu.VMEM((8, 2 * rows), jnp.float32),
            pltpu.VMEM((block_count, rows, 2 * feats), jnp.bfloat16),
            pltpu.VMEM((keys, 2 * rows), jnp.bfloat16),
            pltpu.VMEM((keys, 2 * rows), jnp.float32),
            pltpu.VMEM((2, feats, rows), jnp.bfloat16),
            pltpu.VMEM((2, rows, feats), jnp.bfloat16),
            pltpu.VMEM((block_count, rows, 2 * feats), jnp.bfloat16),
            pltpu.SemaphoreType.DMA((5,)),
            pltpu.SemaphoreType.DMA((block_count,)),
            pltpu.SemaphoreType.DMA((4,)),
            pltpu.SemaphoreType.DMA((block_count,)),
        ],
        20,
        "attention",
    )(at, queries, recv, g_mine, key_mask, row_mask, *kv_blocks)


def grad_heads_kernel(part_count, place, at_ref, first_ref, q_ref, weight_ref, *refs):
    grads, refs = refs[: part_count - 1], refs[part_count - 1 :]
    mine, theirs = refs[:2]
    first_s, q_s, grad_s, weight_s, out_s, sem, weight_sem, grad_sem, out_sem = refs[2:]
    half = out_s.shape[1]
    width = grads[0].shape[1]
    first_load = begin(first_ref, first_s, sem.at[0])
    cols = pl.ds(pl.multiple_of((1 - at_ref[0]) * half, half), half)
    q_load = begin(q_ref.at[:, cols], q_s, sem.at[1])
    loads = []
    for k in range(part_count - 1):
        start = pl.multiple_of(at_ref[place + k] * width, width)
        columns = weight_ref.at[:, pl.ds(start, width)]
        loads.append(begin(grads[k], grad_s.at[k], grad_sem.at[k]))
        loads.append(begin(columns, weight_s.at[k], weight_sem.at[k]))
    q_load.wait()
    out_s[2] = jnp.transpose(q_s[...])
    copies = [begin(out_s.at[2], theirs.at[1], out_sem.at[2])]
    first_load.wait()
    summed = first_s[...]
    for k in range(part_count - 1):
        loads[2 * k].wait()
        loads[2 * k + 1].wait()
        summed = summed + against(weight_s[k], grad_s[k])
    first_s[...] = summed
    for side, target in enumerate((mine, theirs.at[0])):
        at = (1 - at_ref[0]) if side else at_ref[0]
        kept = first_s[pl.ds(pl.multiple_of(at * half, half), half), :]
        out_s[side] = kept.astype(jnp.bfloat16)
        copies.append(begin(out_s.at[side], target, out_sem.at[side]))
    for copy in copies:
        copy.wait()


def grad_heads(at, place, first, queries, out_weight, grads):
    feats, rows = first.shape
    half = feats // INNER
    count = len(grads)
    width = grads[0].shape[1]
    return call(
        functools.partial(grad_heads_kernel, count, place),
        [bf16(half, rows), bf16(2, half, rows)],
        [SMEM] + [ANY] * (2 + count),
        [ANY] * 2,
        [
            pltpu.VMEM((feats, rows), jnp.float32),
            pltpu.VMEM((rows, half), jnp.bfloat16),
            pltpu.VMEM((count - 1, rows, width), jnp.bfloat16),
            pltpu.VMEM((count - 1, feats, width), jnp.bfloat16),
            pltpu.VMEM((3, half, rows), jnp.bfloat16),
            pltpu.SemaphoreType.DMA((2,)),
            pltpu.SemaphoreType.DMA((count - 1,)),
            pltpu.SemaphoreType.DMA((count - 1,)),
            pltpu.SemaphoreType.DMA((3,)),
        ],
        3,
        "grad_heads",
    )(at, first, queries, out_weight, *grads[1:])


def pick_kernel(part_count, place, at_ref, *refs):
    grads, (out, held_s, sem, out_sem) = refs[:part_count], refs[part_count:]
    width = grads[0].shape[1]
    picked = out.shape[1] // width
    for i in range(picked):
        for k in range(part_count):

            @pl.when(at_ref[place + i] == k)
            def _():
                begin(grads[k], held_s.at[i], sem.at[i])

    stores = []
    for i in range(picked):
        pltpu.make_async_copy(grads[0], held_s.at[i], sem.at[i]).wait()
        target = out.at[:, i * width : (i + 1) * width]
        stores.append(begin(held_s.at[i], target, out_sem.at[i]))
    for store in stores:
        store.wait()


def pick_columns(at, place, grads, picked, after):
    rows, width = grads[0].shape
    return call(
        functools.partial(pick_kernel, len(grads), place),
        bf16(rows, picked * width),
        [SMEM] + [ANY] * len(grads),
        ANY,
        [
            pltpu.VMEM((picked, rows, width), jnp.bfloat16),
            pltpu.SemaphoreType.DMA((picked,)),
            pltpu.SemaphoreType.DMA((picked,)),
        ],
        2,
        "pick_columns",
        after,
    )(at, *grads)


def weight_kernel(part_count, doc_count, sent, step_at, at_ref, *refs):
    attn, refs = refs[: INNER * doc_count], refs[INNER * doc_count :]
    grads, refs = refs[:part_count], refs[part_count:]
    swapped, refs = refs[: doc_count - 1], refs[doc_count - 1 :]
    if sent:
        out, refs = refs[0], refs[1:]
        outs = [out.at[k] for k in range(out.shape[0])]
    else:
        recv, passed, refs = refs[0], refs[1], refs[2:]
        outs, refs = refs[: recv.shape[0]], refs[recv.shape[0] :]
        passed_out, recv_s, passed_s, recv_sem, passed_sem = refs[:5]
        refs = refs[5:]
        passed_load = begin(passed, passed_s, passed_sem)
    attn_s, grad_s, out_s, attn_sem, grad_sem, out_sem = refs
    outer, feats, width = out_s.shape
    half = feats // INNER
    piece = grads[0].shape[1]
    pieces = piece // width
    here = (1 - at_ref[0]) if sent else at_ref[0]
    attn_loads, grad_loads = [], []
    for doc in range(doc_count):
        for side in range(INNER):
            at = (1 - at_ref[0]) if side else at_ref[0]
            index = doc * INNER + side
            target = attn_s.at[doc, pl.ds(pl.multiple_of(at * half, half), half)]
            attn_loads.append(begin(attn[index], target, attn_sem.at[index]))
    for k in range(outer):
        place = lax.rem(at_ref[1] + k, outer) * INNER + here
        which = at_ref[step_at + place // pieces]
        cols = pl.ds(pl.multiple_of(lax.rem(place, pieces) * width, width), width)
        for i in range(part_count):

            @pl.when(which == i)
            def _():
                begin(grads[i].at[:, cols], grad_s.at[0, k], grad_sem.at[k])

        loads = [pltpu.make_async_copy(grads[0].at[:, cols], grad_s.at[0, k], grad_sem.at[k])]
        cols = pl.ds(pl.multiple_of(place * width, width), width)
        for doc in range(1, doc_count):
            source = swapped[doc - 1].at[:, cols]
            loads.append(begin(source, grad_s.at[doc, k], grad_sem.at[doc * outer + k]))
        if not sent:
            loads.append(begin(recv.at[k], recv_s.at[k], recv_sem.at[k]))
        grad_loads.append(loads)
    for load in attn_loads:
        load.wait()
    stores = []
    if not sent:
        passed_load.wait()
        stores.append(begin(passed_s, passed_out, passed_sem))
    for k in range(outer):
        term = 0.0
        for doc in range(doc_count):
            grad_loads[k][doc].wait()
            term = term + product(attn_s[doc], grad_s[doc, k])
        if not sent:
            grad_loads[k][doc_count].wait()
            term = term + recv_s[k].astype(jnp.float32)
        out_s[k] = term.astype(out_s.dtype)
        stores.append(begin(out_s.at[k], outs[k], out_sem.at[k]))
    for store in stores:
        store.wait()


def weight_terms(at, step_at, attn, grads, swapped, outer, picked, recv=None, passed=None, after=()):
    half, rows = attn[0].shape
    feats = half * INNER
    doc_count = len(attn) // INNER
    width = picked * grads[0].shape[1] // (outer * INNER)
    sent = recv is None
    operands = [*attn, *grads, *swapped] + ([] if sent else [recv, passed])
    scratch = [
        pltpu.VMEM((doc_count, feats, rows), jnp.bfloat16),
        pltpu.VMEM((doc_count, outer, rows, width), jnp.bfloat16),
        pltpu.VMEM((outer, feats, width), jnp.bfloat16),
        pltpu.SemaphoreType.DMA((len(attn),)),
        pltpu.SemaphoreType.DMA((doc_count * outer,)),
        pltpu.SemaphoreType.DMA((outer,)),
    ]
    if not sent:
        scratch = [
            pltpu.VMEM((outer, feats, width), jnp.bfloat16),
            pltpu.VMEM(passed.shape, jnp.bfloat16),
            pltpu.SemaphoreType.DMA((outer,)),
            pltpu.SemaphoreType.DMA,
        ] + scratch
    return call(
        functools.partial(weight_kernel, len(grads), doc_count, sent, step_at),
        bf16(outer, feats, width) if sent else [bf16(feats, width)] * outer + [bf16(*passed.shape)],
        [SMEM] + [ANY] * len(operands),
        ANY if sent else [ANY] * (outer + 1),
        scratch,
        4,
        "weight_sent" if sent else "weight_kept",
        after,
    )(at, *operands)


def collect_kernel(at_ref, dq_mine, dq_recv, terms, *refs):
    outs, (dq_s, terms_s, out_s, dq_sem, sem, out_sem) = refs[:3], refs[3:]
    count, rows, both = terms.shape
    half = both // 2
    loads = [begin(terms.at[c], terms_s.at[c], sem.at[c]) for c in range(count)]
    held = [begin(dq, dq_s.at[i], dq_sem.at[i]) for i, dq in enumerate((dq_mine, dq_recv))]
    for side, at in enumerate((at_ref[0], 1 - at_ref[0])):
        held[side].wait()
        out_s[0, :, pl.ds(pl.multiple_of(at * half, half), half)] = dq_s[side]
    stores = [begin(out_s.at[0], outs[0], out_sem.at[0])]
    for load in loads:
        load.wait()
    for side in range(INNER):
        summed = terms_s[side].astype(jnp.float32)
        for c in range(side + INNER, count, INNER):
            summed = summed + terms_s[c].astype(jnp.float32)
        summed = summed.astype(jnp.bfloat16)
        for kind in range(2):
            cols = slice(side * half, (side + 1) * half)
            out_s[1 + kind, :, cols] = summed[:, kind * half : (kind + 1) * half]
    for index in (1, 2):
        stores.append(begin(out_s.at[index], outs[index], out_sem.at[index]))
    for store in stores:
        store.wait()


def collect(at, dq_mine, dq_recv, terms):
    count, rows, both = terms.shape
    half = both // 2
    return call(
        collect_kernel,
        [bf16(rows, INNER * half)] * 3,
        [SMEM] + [ANY] * 3,
        [ANY] * 3,
        [
            pltpu.VMEM((INNER, rows, half), jnp.bfloat16),
            pltpu.VMEM((count, rows, both), jnp.bfloat16),
            pltpu.VMEM((3, rows, INNER * half), jnp.bfloat16),
            pltpu.SemaphoreType.DMA((INNER,)),
            pltpu.SemaphoreType.DMA((count,)),
            pltpu.SemaphoreType.DMA((3,)),
        ],
        3,
        "collect",
    )(at, dq_mine, dq_recv, terms)


def per_device(
    queries, key_heads, value_heads, grad_output, out_weight, block_pattern, global_offsets
):
    dp_count, ctx_count, tp_count = (lax.axis_size(name) for name in ("dp", "ctx", "tp"))
    dp_at, ctx_at, tp_at = (lax.axis_index(name) for name in ("dp", "ctx", "tp"))
    outer = ctx_count // INNER
    outer_at, inner_at = ctx_at // INNER, ctx_at % INNER
    picked = tp_count // dp_count

    def ctx_pairs(step, side, dp_step=0):
        moved = [(c + step * INNER) % ctx_count ^ side for c in range(ctx_count)]
        if not dp_step:
            return list(enumerate(moved))
        return [
            (d * ctx_count + c, (d + dp_step) % dp_count * ctx_count + moved[c])
            for d in range(dp_count)
            for c in range(ctx_count)
        ]

    def shift_pairs(count, step):
        return [(i, (i + step) % count) for i in range(count)]

    def dp_steps(which):
        return [(which * picked + i - tp_at) % tp_count for i in range(picked)]

    routes = [(step, side) for step in range(outer) for side in range(INNER)]
    sources = [
        ((outer_at - step) % outer) * INNER + (inner_at + side) % INNER for step, side in routes
    ]
    scalars = [inner_at, outer_at, tp_at] + sources
    columns_at = len(scalars)
    scalars = scalars + [(tp_at + step) % tp_count for step in range(1, tp_count)]
    send_at = len(scalars)
    for step in range(1, dp_count):
        scalars = scalars + dp_steps((dp_at + step) % dp_count)
    keep_at = len(scalars)
    at = jnp.stack(scalars + dp_steps(dp_at))

    grad_own = grad_output[0]
    grads = [grad_own] + [
        lax.ppermute(grad_own, "tp", shift_pairs(tp_count, -step)) for step in range(1, tp_count)
    ]
    kv_mine, kv_theirs = part_heads(at, key_heads[0], value_heads[0])
    kv_recv = lax.ppermute(kv_theirs, "ctx", ctx_pairs(0, 1))
    kv_blocks = [
        lax.ppermute(kv_recv if side else kv_mine, "ctx", ctx_pairs(step, 0))
        if step
        else (kv_recv if side else kv_mine)
        for step, side in routes
    ]
    first, key_mask, row_mask = prelude(
        at, block_pattern, global_offsets, grad_own, out_weight, (kv_recv, *kv_blocks[INNER::INNER])
    )
    g_mine, theirs = grad_heads(at, columns_at, first, queries[0], out_weight, grads)
    recv = lax.ppermute(theirs, "ctx", ctx_pairs(0, 1))
    grad_sends = [
        pick_columns(at, send_at + step * picked, grads, picked, (g_mine,))
        for step in range(dp_count - 1)
    ]
    swapped = [
        lax.ppermute(send, "dp", shift_pairs(dp_count, step + 1))
        for step, send in enumerate(grad_sends)
    ]

    attn_mine, attn_theirs, dq_mine, dq_theirs, parts = attention(
        at, queries[0], recv, g_mine, key_mask, row_mask, kv_blocks
    )
    terms = lax.all_to_all(parts, "ctx", split_axis=0, concat_axis=0, tiled=True)

    attn = []
    for step in range(dp_count):
        for held, side in ((attn_mine, 0), (attn_theirs, 1)):
            pairs = ctx_pairs(0, side, step)
            axes = ("dp", "ctx") if step else "ctx"
            attn.append(lax.ppermute(held, axes, pairs) if step or side else held)

    send = weight_terms(at, keep_at, attn, grads, swapped, outer, picked)
    weight_recv = lax.ppermute(send, "ctx", ctx_pairs(0, 1))
    *weight_sums, dq_theirs = weight_terms(
        at, keep_at, attn, grads, swapped, outer, picked, weight_recv, dq_theirs
    )
    weight_parts = [
        lax.ppermute(weight_sums[step], "ctx", ctx_pairs(step, 0)) for step in range(1, outer)
    ]
    dq_recv = lax.ppermute(dq_theirs, "ctx", ctx_pairs(0, 1))
    grad_q, grad_k, grad_v = collect(at, dq_mine, dq_recv, terms)
    weight_parts, grad_k = lax.optimization_barrier((weight_parts, grad_k))
    grad_weight = weight_sums[0].astype(jnp.float32)
    for part in weight_parts:
        grad_weight = grad_weight + part.astype(jnp.float32)

    return grad_q[None], grad_k[None], grad_v[None], grad_weight.astype(jnp.bfloat16)


def solution(mesh):
    in_specs = (
        P("dp", "ctx", "tp"),
        P("dp", "ctx", "tp"),
        P("dp", "ctx", "tp"),
        P("dp", "ctx", "tp"),
        P("tp", None),
        P(),
        P(),
    )
    out_specs = (
        P("dp", "ctx", "tp"),
        P("dp", "ctx", "tp"),
        P("dp", "ctx", "tp"),
        P("tp", ("dp", "ctx")),
    )
    return jax.shard_map(
        per_device, mesh=mesh, in_specs=in_specs, out_specs=out_specs, check_vma=False
    )
```

```python
import functools

import jax
import jax.numpy as jnp
from jax import lax
from jax.experimental import pallas as pl
from jax.experimental.pallas import tpu as pltpu
from jax.sharding import PartitionSpec as P

HD = 128
MASKED = -1e30
INNER = 2
SOURCES = 3
ANY = pl.BlockSpec(memory_space=pl.ANY)
VMEM = pl.BlockSpec(memory_space=pltpu.VMEM)
SMEM = pl.BlockSpec(memory_space=pltpu.SMEM)


def against(left_op, right_op):
    return lax.dot_general(
        left_op, right_op, (((1,), (1,)), ((), ())), preferred_element_type=jnp.float32
    )


def product(left_op, right_op):
    return jnp.dot(left_op, right_op, preferred_element_type=jnp.float32)


def begin(source, target, semaphore):
    copy = pltpu.make_async_copy(source, target, semaphore)
    copy.start()
    return copy


def call(kernel, out_shape, in_specs, out_specs, scratch, micros, name, after=()):
    skipped = len(after)
    in_specs = [ANY] * skipped + in_specs
    run = pl.pallas_call(
        lambda *refs: kernel(*refs[skipped:]),
        out_shape=out_shape,
        in_specs=in_specs,
        out_specs=out_specs,
        scratch_shapes=scratch,
        compiler_params=pltpu.CompilerParams(vmem_limit_bytes=64 * 1024 * 1024),
        cost_estimate=pl.CostEstimate(
            flops=int(micros * 1e9), bytes_accessed=int(micros * 3e6), transcendentals=0
        ),
        name=name,
    )

    def placed(*args):
        args = [
            pltpu.with_memory_space_constraint(arg, pltpu.HBM) if spec is ANY else arg
            for spec, arg in zip(in_specs, (*after, *args))
        ]
        return run(*args)

    return placed


def bf16(*shape):
    return pltpu.HBM(shape, jnp.bfloat16)


def f32(*shape):
    return pltpu.HBM(shape, jnp.float32)


def part_kernel(at_ref, k_ref, v_ref, kv_mine, kv_theirs, held_s, in_sem, out_sem):
    half = kv_mine.shape[1] // 2
    loads = [begin(held, held_s.at[i], in_sem.at[i]) for i, held in enumerate((k_ref, v_ref))]
    mine = pl.ds(pl.multiple_of(at_ref[0] * half, half), half)
    theirs = pl.ds(pl.multiple_of((1 - at_ref[0]) * half, half), half)
    copies = []
    for index in range(2):
        loads[index].wait()
        place = slice(index * half, (index + 1) * half)
        for side, (cols, out) in enumerate(((mine, kv_mine), (theirs, kv_theirs))):
            sem = out_sem.at[2 * index + side]
            copies.append(begin(held_s.at[index, :, cols], out.at[:, place], sem))
    for copy in copies:
        copy.wait()


def part_heads(at, keys, values):
    rows, feats = keys.shape
    return call(
        part_kernel,
        [bf16(rows, feats), bf16(rows, feats)],
        [SMEM] + [ANY] * 2,
        [ANY] * 2,
        [
            pltpu.VMEM((2, rows, feats), jnp.bfloat16),
            pltpu.SemaphoreType.DMA((2,)),
            pltpu.SemaphoreType.DMA((4,)),
        ],
        2,
        "part_heads",
    )(at, keys, values)


def prelude_kernel(at_ref, pattern, offsets, grad_ref, weight_ref, *refs):
    first, key_mask, row_mask = refs[:3]
    grad_s, weight_s, first_s, mask_s, row_s, sem, out_sem = refs[3:]
    rows, width = grad_s.shape
    block_count, glob_count = offsets.shape
    start = pl.multiple_of(at_ref[2] * width, width)
    loads = [
        begin(grad_ref, grad_s, sem.at[0]),
        begin(weight_ref.at[:, pl.ds(start, width)], weight_s, sem.at[1]),
    ]
    stores = []
    own = at_ref[1] * INNER + at_ref[0]
    partner = at_ref[1] * INNER + 1 - at_ref[0]
    lane = lax.broadcasted_iota(jnp.int32, (1, HD), 1)
    row_at = lax.broadcasted_iota(jnp.int32, (rows, HD), 0)
    col_at = lax.broadcasted_iota(jnp.int32, (8, rows), 1)
    group_at = lax.broadcasted_iota(jnp.int32, (8, rows), 0)
    for index in range(block_count):
        block = at_ref[SOURCES + index]
        hidden = []
        for target in (own, partner):
            seen = jnp.abs(block - target) <= 1
            for r in range(pattern.shape[1]):
                seen = seen | (pattern[target, r] == block)
            hidden.append(jnp.where(seen, 0, 1))
        lane_hidden = jnp.where(lane == 0, hidden[0], jnp.where(lane == 1, hidden[1], 0))
        hidden_rows = jnp.broadcast_to(lane_hidden, (rows, HD))
        for r in range(glob_count):
            hidden_rows = jnp.where(row_at == offsets[block, r], 0, hidden_rows)
        mask_s[index * rows : (index + 1) * rows, :] = hidden_rows.astype(jnp.float32).astype(
            jnp.bfloat16
        )
    for group, target in enumerate((own, partner)):
        local = jnp.where(group_at == group, MASKED, 0.0)
        for r in range(glob_count):
            local = jnp.where(col_at == offsets[target, r], 0.0, local)
        row_s[:, group * rows : (group + 1) * rows] = local
    stores.append(begin(mask_s, key_mask, out_sem.at[0]))
    stores.append(begin(row_s, row_mask, out_sem.at[1]))
    for load in loads:
        load.wait()
    first_s[...] = against(weight_s[...], grad_s[...])
    stores.append(begin(first_s, first, out_sem.at[2]))
    for store in stores:
        store.wait()


def prelude(at, pattern, offsets, grad_own, out_weight, after):
    rows, width = grad_own.shape
    feats = out_weight.shape[0]
    keys = offsets.shape[0] * rows
    return call(
        prelude_kernel,
        [
            f32(feats, rows),
            bf16(keys, HD),
            f32(8, 2 * rows),
        ],
        [SMEM] * 3 + [ANY] * 2,
        [ANY] * 3,
        [
            pltpu.VMEM((rows, width), jnp.bfloat16),
            pltpu.VMEM((feats, width), jnp.bfloat16),
            pltpu.VMEM((feats, rows), jnp.float32),
            pltpu.VMEM((keys, HD), jnp.bfloat16),
            pltpu.VMEM((8, 2 * rows), jnp.float32),
            pltpu.SemaphoreType.DMA((2,)),
            pltpu.SemaphoreType.DMA((3,)),
        ],
        4,
        "prelude",
        after,
    )(at, pattern, offsets, grad_own, out_weight)


def attention_kernel(block_count, head_count, at_ref, q_ref, recv_ref, g_mine, key_mask, row_mask, *refs):
    kv_refs, refs = refs[:block_count], refs[block_count:]
    outer = block_count // INNER
    attn_mine, attn_theirs, dq_mine, dq_theirs = refs[:4]
    part_outs, refs = refs[4 : 4 + outer], refs[4 + outer :]
    q_s, recv_s, g_s, mask_s, row_s, kv_s, e_s, s_ref, attn_s, dq_s, part_s = refs[:11]
    sem, kv_sem, out_sem, part_sem = refs[11:]
    rows = q_ref.shape[0]
    feats = head_count * HD
    score_scale = HD ** (-0.5)
    mine = pl.ds(pl.multiple_of(at_ref[0] * feats, feats), feats)
    loads = [
        begin(q_ref.at[:, mine], q_s, sem.at[0]),
        begin(recv_ref, recv_s, sem.at[1]),
        begin(key_mask, mask_s, sem.at[2]),
        begin(row_mask, row_s, sem.at[3]),
        begin(g_mine, g_s, sem.at[4]),
    ]
    kv_loads = [begin(kv_refs[j], kv_s.at[j], kv_sem.at[j]) for j in range(block_count)]
    for load in loads:
        load.wait()
    rows_low = row_s[...].astype(jnp.bfloat16)
    hidden = jnp.concatenate([rows_low, jnp.zeros((HD - 8, 2 * rows), jnp.bfloat16)], axis=0)
    stores = []
    for head in range(head_count):
        cols = slice(head * HD, (head + 1) * HD)
        vcols = slice(feats + head * HD, feats + (head + 1) * HD)
        query_recv = recv_s[1, cols, :]
        q_t = jnp.concatenate([jnp.transpose(q_s[:, cols]), query_recv], axis=1)
        q_t = jnp.concatenate([q_t, hidden], axis=0)
        top = jnp.full((1, 2 * rows), MASKED, jnp.float32)
        for j in range(block_count):
            if head == 0:
                kv_loads[j].wait()
            keys = slice(j * rows, (j + 1) * rows)
            scores = product(jnp.concatenate([kv_s[j, :, cols], mask_s[keys, :]], axis=1), q_t)
            s_ref[keys, :] = scores
            top = jnp.maximum(top, jnp.max(scores, axis=0, keepdims=True))
        total = jnp.zeros((1, 2 * rows), jnp.float32)
        attn_t = jnp.zeros((HD, 2 * rows), jnp.float32)
        for j in range(block_count):
            keys = slice(j * rows, (j + 1) * rows)
            weights = jnp.exp((s_ref[keys, :] - top) * score_scale)
            total = total + jnp.sum(weights, axis=0, keepdims=True)
            low = weights.astype(jnp.bfloat16)
            e_s[keys, :] = low
            attn_t = attn_t + product(jnp.transpose(kv_s[j, :, vcols]), low)
        inverse = 1.0 / total
        attn_low = (attn_t * inverse).astype(jnp.bfloat16)
        attn_s[0, cols, :] = attn_low[:, :rows]
        attn_s[1, cols, :] = attn_low[:, rows:]
        if head == head_count - 1:
            stores.append(begin(attn_s.at[0], attn_mine, out_sem.at[0]))
            stores.append(begin(attn_s.at[1], attn_theirs, out_sem.at[1]))
        g_t = jnp.concatenate([g_s[cols, :], recv_s[0, cols, :]], axis=1).astype(jnp.float32)
        row_dot = jnp.sum(g_t * attn_low.astype(jnp.float32), axis=0, keepdims=True) * inverse
        g_t = (g_t * inverse).astype(jnp.bfloat16)
        grad = jnp.transpose(g_t)
        query = jnp.concatenate([q_s[:, cols], jnp.transpose(query_recv)], axis=0)
        dq_t = jnp.zeros((HD, 2 * rows), jnp.float32)
        for j in range(block_count):
            keys = slice(j * rows, (j + 1) * rows)
            low = e_s[keys, :]
            dprobs = product(kv_s[j, :, vcols], g_t)
            dscore = (low.astype(jnp.float32) * (dprobs - row_dot)).astype(jnp.bfloat16)
            dq_t = dq_t + product(jnp.transpose(kv_s[j, :, cols]), dscore)
            part_s[j, :, cols] = (score_scale * product(dscore, query)).astype(jnp.bfloat16)
            part_s[j, :, vcols] = product(low, grad).astype(jnp.bfloat16)
            if head == head_count - 1:
                target = part_outs[j // INNER].at[j % INNER]
                stores.append(begin(part_s.at[j], target, part_sem.at[j]))
        dquery = (score_scale * jnp.transpose(dq_t)).astype(jnp.bfloat16)
        dq_s[0, :, cols] = dquery[:rows]
        dq_s[1, :, cols] = dquery[rows:]
    stores.append(begin(dq_s.at[0], dq_mine, out_sem.at[2]))
    stores.append(begin(dq_s.at[1], dq_theirs, out_sem.at[3]))
    for store in stores:
        store.wait()


def attention(at, queries, recv, g_mine, key_mask, row_mask, kv_blocks):
    block_count = len(kv_blocks)
    feats, rows = g_mine.shape
    heads = feats // HD
    keys = block_count * rows
    outer = block_count // INNER
    out = call(
        functools.partial(attention_kernel, block_count, heads),
        [bf16(feats, rows)] * 2 + [bf16(rows, feats)] * 2 + [bf16(INNER, rows, 2 * feats)] * outer,
        [SMEM] + [ANY] * (5 + block_count),
        [ANY] * (4 + outer),
        [
            pltpu.VMEM((rows, feats), jnp.bfloat16),
            pltpu.VMEM((2, feats, rows), jnp.bfloat16),
            pltpu.VMEM((feats, rows), jnp.bfloat16),
            pltpu.VMEM((keys, HD), jnp.bfloat16),
            pltpu.VMEM((8, 2 * rows), jnp.float32),
            pltpu.VMEM((block_count, rows, 2 * feats), jnp.bfloat16),
            pltpu.VMEM((keys, 2 * rows), jnp.bfloat16),
            pltpu.VMEM((keys, 2 * rows), jnp.float32),
            pltpu.VMEM((2, feats, rows), jnp.bfloat16),
            pltpu.VMEM((2, rows, feats), jnp.bfloat16),
            pltpu.VMEM((block_count, rows, 2 * feats), jnp.bfloat16),
            pltpu.SemaphoreType.DMA((5,)),
            pltpu.SemaphoreType.DMA((block_count,)),
            pltpu.SemaphoreType.DMA((4,)),
            pltpu.SemaphoreType.DMA((block_count,)),
        ],
        20,
        "attention",
    )(at, queries, recv, g_mine, key_mask, row_mask, *kv_blocks)
    return *out[:4], out[4:]


def grad_heads_kernel(part_count, place, at_ref, first_ref, q_ref, weight_ref, *refs):
    grads, refs = refs[: part_count - 1], refs[part_count - 1 :]
    mine, theirs = refs[:2]
    first_s, q_s, grad_s, weight_s, out_s, sem, weight_sem, grad_sem, out_sem = refs[2:]
    half = out_s.shape[1]
    width = grads[0].shape[1]
    first_load = begin(first_ref, first_s, sem.at[0])
    cols = pl.ds(pl.multiple_of((1 - at_ref[0]) * half, half), half)
    q_load = begin(q_ref.at[:, cols], q_s, sem.at[1])
    loads = []
    for k in range(part_count - 1):
        start = pl.multiple_of(at_ref[place + k] * width, width)
        columns = weight_ref.at[:, pl.ds(start, width)]
        loads.append(begin(grads[k], grad_s.at[k], grad_sem.at[k]))
        loads.append(begin(columns, weight_s.at[k], weight_sem.at[k]))
    q_load.wait()
    out_s[2] = jnp.transpose(q_s[...])
    copies = [begin(out_s.at[2], theirs.at[1], out_sem.at[2])]
    first_load.wait()
    summed = first_s[...]
    for k in range(part_count - 1):
        loads[2 * k].wait()
        loads[2 * k + 1].wait()
        summed = summed + against(weight_s[k], grad_s[k])
    first_s[...] = summed
    for side, target in enumerate((mine, theirs.at[0])):
        at = (1 - at_ref[0]) if side else at_ref[0]
        kept = first_s[pl.ds(pl.multiple_of(at * half, half), half), :]
        out_s[side] = kept.astype(jnp.bfloat16)
        copies.append(begin(out_s.at[side], target, out_sem.at[side]))
    for copy in copies:
        copy.wait()


def grad_heads(at, place, first, queries, out_weight, grads):
    feats, rows = first.shape
    half = feats // INNER
    count = len(grads)
    width = grads[0].shape[1]
    return call(
        functools.partial(grad_heads_kernel, count, place),
        [bf16(half, rows), bf16(2, half, rows)],
        [SMEM] + [ANY] * (2 + count),
        [ANY] * 2,
        [
            pltpu.VMEM((feats, rows), jnp.float32),
            pltpu.VMEM((rows, half), jnp.bfloat16),
            pltpu.VMEM((count - 1, rows, width), jnp.bfloat16),
            pltpu.VMEM((count - 1, feats, width), jnp.bfloat16),
            pltpu.VMEM((3, half, rows), jnp.bfloat16),
            pltpu.SemaphoreType.DMA((2,)),
            pltpu.SemaphoreType.DMA((count - 1,)),
            pltpu.SemaphoreType.DMA((count - 1,)),
            pltpu.SemaphoreType.DMA((3,)),
        ],
        3,
        "grad_heads",
    )(at, first, queries, out_weight, *grads[1:])


def pick_kernel(part_count, picked, places, at_ref, *refs):
    grads, refs = refs[:part_count], refs[part_count:]
    outs, (held_s, sem, out_sem) = refs[: len(places)], refs[len(places) :]
    _, outer, _, block = outs[0].shape
    pieces = grads[0].shape[1] // block
    loads = [begin(grads[k], held_s.at[k], sem.at[k]) for k in range(part_count)]
    for load in loads:
        load.wait()
    stores = []
    for index, steps_at in enumerate(places):
        for side in range(INNER):
            here = (1 - at_ref[0]) if side else at_ref[0]
            for k in range(outer):
                place = lax.rem(at_ref[1] + k, outer) * INNER + here
                cols = pl.ds(pl.multiple_of(lax.rem(place, pieces) * block, block), block)
                source = held_s.at[at_ref[steps_at + place // pieces], :, cols]
                order = (index * INNER + side) * outer + k
                stores.append(begin(source, outs[index].at[side, k], out_sem.at[order]))
    for store in stores:
        store.wait()


def pick_columns(at, places, grads, outer, picked, after):
    rows, width = grads[0].shape
    block = picked * width // (outer * INNER)
    return call(
        functools.partial(pick_kernel, len(grads), picked, places),
        [bf16(INNER, outer, rows, block)] * len(places),
        [SMEM] + [ANY] * len(grads),
        [ANY] * len(places),
        [
            pltpu.VMEM((len(grads), rows, width), jnp.bfloat16),
            pltpu.SemaphoreType.DMA((len(grads),)),
            pltpu.SemaphoreType.DMA((len(places) * INNER * outer,)),
        ],
        3,
        "pick_columns",
        after,
    )(at, *grads)


def weight_kernel(doc_count, sent, at_ref, *refs):
    attn, refs = refs[: INNER * doc_count], refs[INNER * doc_count :]
    grads, refs = refs[:doc_count], refs[doc_count:]
    if sent:
        out, refs = refs[0], refs[1:]
        outs = [out.at[k] for k in range(out.shape[0])]
    else:
        recv, refs = refs[0], refs[1:]
        outs, refs = refs[: recv.shape[0]], refs[recv.shape[0] :]
        recv_s, recv_sem, refs = refs[0], refs[1], refs[2:]
    attn_s, grad_s, out_s, attn_sem, grad_sem, out_sem = refs
    outer, feats, _ = out_s.shape
    half = feats // INNER
    attn_loads, grad_loads = [], []
    for doc in range(doc_count):
        for side in range(INNER):
            at = (1 - at_ref[0]) if side else at_ref[0]
            index = doc * INNER + side
            target = attn_s.at[doc, pl.ds(pl.multiple_of(at * half, half), half)]
            attn_loads.append(begin(attn[index], target, attn_sem.at[index]))
    for k in range(outer):
        loads = [
            begin(grads[doc].at[int(sent), k], grad_s.at[doc, k], grad_sem.at[doc * outer + k])
            for doc in range(doc_count)
        ]
        if not sent:
            loads.append(begin(recv.at[k], recv_s.at[k], recv_sem.at[k]))
        grad_loads.append(loads)
    for load in attn_loads:
        load.wait()
    stores = []
    for k in range(outer):
        term = 0.0
        for doc in range(doc_count):
            grad_loads[k][doc].wait()
            term = term + product(attn_s[doc], grad_s[doc, k])
        if not sent:
            grad_loads[k][doc_count].wait()
            term = term + recv_s[k].astype(jnp.float32)
        out_s[k] = term.astype(out_s.dtype)
        stores.append(begin(out_s.at[k], outs[k], out_sem.at[k]))
    for store in stores:
        store.wait()


def weight_terms(at, attn, grads, recv=None, after=()):
    half, rows = attn[0].shape
    feats = half * INNER
    doc_count = len(grads)
    _, outer, _, width = grads[0].shape
    sent = recv is None
    operands = [*attn, *grads] + ([] if sent else [recv])
    scratch = [
        pltpu.VMEM((doc_count, feats, rows), jnp.bfloat16),
        pltpu.VMEM((doc_count, outer, rows, width), jnp.bfloat16),
        pltpu.VMEM((outer, feats, width), jnp.bfloat16),
        pltpu.SemaphoreType.DMA((len(attn),)),
        pltpu.SemaphoreType.DMA((doc_count * outer,)),
        pltpu.SemaphoreType.DMA((outer,)),
    ]
    if not sent:
        added = [pltpu.VMEM((outer, feats, width), jnp.bfloat16), pltpu.SemaphoreType.DMA((outer,))]
        scratch = added + scratch
    return call(
        functools.partial(weight_kernel, doc_count, sent),
        bf16(outer, feats, width) if sent else [bf16(feats, width)] * outer,
        [SMEM] + [ANY] * len(operands),
        ANY if sent else [ANY] * outer,
        scratch,
        4,
        "weight_sent" if sent else "weight_kept",
        after,
    )(at, *operands)


def add_kernel(count, dq_theirs, *refs):
    terms, (mine, theirs) = refs[:count], refs[count : count + 2]
    terms_s, mine_s, theirs_s, dq_s, term_sem, out_sem, dq_sem = refs[count + 2 :]
    both = mine.shape[1]
    dq_load = begin(dq_theirs, dq_s, dq_sem)
    loads = {
        (side, c): begin(terms[c].at[side], terms_s.at[c, side], term_sem.at[c * INNER + side])
        for side in (1, 0)
        for c in range(count)
    }
    stores = []
    for side, (held_s, out) in ((1, (theirs_s, theirs)), (0, (mine_s, mine))):
        summed = 0.0
        for c in range(count):
            loads[side, c].wait()
            summed = summed + terms_s[c, side].astype(jnp.float32)
        held_s[:, :both] = summed.astype(jnp.bfloat16)
        if side:
            dq_load.wait()
            held_s[:, both:] = dq_s[...]
        stores.append(begin(held_s, out, out_sem.at[side]))
    for store in stores:
        store.wait()


def add_terms(dq_theirs, terms, after):
    _, rows, both = terms[0].shape
    half = both // 2
    count = len(terms)
    return call(
        functools.partial(add_kernel, count),
        [bf16(rows, both), bf16(rows, both + half)],
        [ANY] * (1 + count),
        [ANY] * 2,
        [
            pltpu.VMEM((count, INNER, rows, both), jnp.bfloat16),
            pltpu.VMEM((rows, both), jnp.bfloat16),
            pltpu.VMEM((rows, both + half), jnp.bfloat16),
            pltpu.VMEM((rows, half), jnp.bfloat16),
            pltpu.SemaphoreType.DMA((count * INNER,)),
            pltpu.SemaphoreType.DMA((INNER,)),
            pltpu.SemaphoreType.DMA,
        ],
        2,
        "add_terms",
        after,
    )(dq_theirs, *terms)


def join_kernel(at_ref, dq_mine, mine, recv, *refs):
    outs, (dq_s, mine_s, recv_s, out_s, sem, out_sem) = refs[:3], refs[3:]
    half = dq_mine.shape[1]
    loads = [
        begin(dq_mine, dq_s, sem.at[0]),
        begin(mine, mine_s, sem.at[1]),
        begin(recv, recv_s, sem.at[2]),
    ]
    here = pl.ds(pl.multiple_of(at_ref[0] * half, half), half)
    there = pl.ds(pl.multiple_of((1 - at_ref[0]) * half, half), half)
    for load in loads:
        load.wait()
    out_s[0, :, here] = dq_s[...]
    out_s[0, :, there] = recv_s[:, 2 * half :]
    for kind in range(2):
        cols = slice(kind * half, (kind + 1) * half)
        out_s[1 + kind, :, here] = mine_s[:, cols]
        out_s[1 + kind, :, there] = recv_s[:, cols]
    stores = [begin(out_s.at[index], out, out_sem.at[index]) for index, out in enumerate(outs)]
    for store in stores:
        store.wait()


def join_heads(at, dq_mine, mine, recv):
    rows, half = dq_mine.shape
    return call(
        join_kernel,
        [bf16(rows, INNER * half)] * 3,
        [SMEM] + [ANY] * 3,
        [ANY] * 3,
        [
            pltpu.VMEM(dq_mine.shape, jnp.bfloat16),
            pltpu.VMEM(mine.shape, jnp.bfloat16),
            pltpu.VMEM(recv.shape, jnp.bfloat16),
            pltpu.VMEM((3, rows, INNER * half), jnp.bfloat16),
            pltpu.SemaphoreType.DMA((3,)),
            pltpu.SemaphoreType.DMA((3,)),
        ],
        2,
        "join_heads",
    )(at, dq_mine, mine, recv)


def per_device(
    queries, key_heads, value_heads, grad_output, out_weight, block_pattern, global_offsets
):
    dp_count, ctx_count, tp_count = (lax.axis_size(name) for name in ("dp", "ctx", "tp"))
    dp_at, ctx_at, tp_at = (lax.axis_index(name) for name in ("dp", "ctx", "tp"))
    outer = ctx_count // INNER
    outer_at, inner_at = ctx_at // INNER, ctx_at % INNER
    picked = tp_count // dp_count

    def ctx_pairs(step, side, dp_step=0):
        moved = [(c + step * INNER) % ctx_count ^ side for c in range(ctx_count)]
        if not dp_step:
            return list(enumerate(moved))
        return [
            (d * ctx_count + c, (d + dp_step) % dp_count * ctx_count + moved[c])
            for d in range(dp_count)
            for c in range(ctx_count)
        ]

    def shift_pairs(count, step):
        return [(i, (i + step) % count) for i in range(count)]

    def dp_steps(which):
        return [(which * picked + i - tp_at) % tp_count for i in range(picked)]

    routes = [(step, side) for step in range(outer) for side in range(INNER)]
    sources = [
        ((outer_at - step) % outer) * INNER + (inner_at + side) % INNER for step, side in routes
    ]
    scalars = [inner_at, outer_at, tp_at] + sources
    columns_at = len(scalars)
    scalars = scalars + [(tp_at + step) % tp_count for step in range(1, tp_count)]
    groups_at = []
    for step in range(dp_count):
        groups_at.append(len(scalars))
        scalars = scalars + dp_steps((dp_at + step) % dp_count)
    at = jnp.stack(scalars)

    grad_own = grad_output[0]
    grads = [grad_own] + [
        lax.ppermute(grad_own, "tp", shift_pairs(tp_count, -step)) for step in range(1, tp_count)
    ]
    kv_mine, kv_theirs = part_heads(at, key_heads[0], value_heads[0])
    kv_recv = lax.ppermute(kv_theirs, "ctx", ctx_pairs(0, 1))
    kv_blocks = [
        lax.ppermute(kv_recv if side else kv_mine, "ctx", ctx_pairs(step, 0))
        if step
        else (kv_recv if side else kv_mine)
        for step, side in routes
    ]
    first, key_mask, row_mask = prelude(
        at, block_pattern, global_offsets, grad_own, out_weight, (kv_recv, kv_blocks[INNER], kv_blocks[-INNER])
    )
    g_mine, theirs = grad_heads(at, columns_at, first, queries[0], out_weight, grads)
    recv = lax.ppermute(theirs, "ctx", ctx_pairs(0, 1))
    kept, *sends = pick_columns(at, tuple(groups_at), grads, outer, picked, (g_mine,))
    grad_blocks = [kept] + [
        lax.ppermute(send, "dp", shift_pairs(dp_count, step + 1)) for step, send in enumerate(sends)
    ]

    attn_mine, attn_theirs, dq_mine, dq_theirs, parts = attention(
        at, queries[0], recv, g_mine, key_mask, row_mask, kv_blocks
    )
    terms = [
        lax.ppermute(part, "ctx", ctx_pairs(-step, 0)) if step else part
        for step, part in enumerate(parts)
    ]

    attn = []
    for step in range(dp_count):
        for held, side in ((attn_mine, 0), (attn_theirs, 1)):
            pairs = ctx_pairs(0, side, step)
            axes = ("dp", "ctx") if step else "ctx"
            attn.append(lax.ppermute(held, axes, pairs) if step or side else held)

    send = weight_terms(at, attn, grad_blocks)
    weight_recv = lax.ppermute(send, "ctx", ctx_pairs(0, 1))
    weight_sums = weight_terms(at, attn, grad_blocks, weight_recv)
    weight_parts = [
        lax.ppermute(weight_sums[step], "ctx", ctx_pairs(step, 0)) for step in range(1, outer)
    ]
    terms_mine, terms_theirs = add_terms(dq_theirs, terms, (weight_sums[0],))
    terms_recv = lax.ppermute(terms_theirs, "ctx", ctx_pairs(0, 1))
    grad_q, grad_k, grad_v = join_heads(at, dq_mine, terms_mine, terms_recv)
    grad_weight = weight_sums[0].astype(jnp.float32)
    for part in weight_parts:
        grad_weight = grad_weight + part.astype(jnp.float32)

    return grad_q[None], grad_k[None], grad_v[None], grad_weight.astype(jnp.bfloat16)


def solution(mesh):
    in_specs = (
        P("dp", "ctx", "tp"),
        P("dp", "ctx", "tp"),
        P("dp", "ctx", "tp"),
        P("dp", "ctx", "tp"),
        P("tp", None),
        P(),
        P(),
    )
    out_specs = (
        P("dp", "ctx", "tp"),
        P("dp", "ctx", "tp"),
        P("dp", "ctx", "tp"),
        P("tp", ("dp", "ctx")),
    )
    return jax.shard_map(
        per_device, mesh=mesh, in_specs=in_specs, out_specs=out_specs, check_vma=False
    )
```

```python
import functools

import jax
import jax.numpy as jnp
from jax import lax
from jax.experimental import pallas as pl
from jax.experimental.pallas import tpu as pltpu
from jax.sharding import PartitionSpec as P

HD = 128
MASKED = -1e30
INNER = 2
SOURCES = 3
ANY = pl.BlockSpec(memory_space=pl.ANY)
VMEM = pl.BlockSpec(memory_space=pltpu.VMEM)
SMEM = pl.BlockSpec(memory_space=pltpu.SMEM)


def against(left_op, right_op):
    return lax.dot_general(
        left_op, right_op, (((1,), (1,)), ((), ())), preferred_element_type=jnp.float32
    )


def product(left_op, right_op):
    return jnp.dot(left_op, right_op, preferred_element_type=jnp.float32)


def begin(source, target, semaphore):
    copy = pltpu.make_async_copy(source, target, semaphore)
    copy.start()
    return copy


def call(kernel, out_shape, in_specs, out_specs, scratch, micros, name, after=()):
    skipped = len(after)
    in_specs = [ANY] * skipped + in_specs
    run = pl.pallas_call(
        lambda *refs: kernel(*refs[skipped:]),
        out_shape=out_shape,
        in_specs=in_specs,
        out_specs=out_specs,
        scratch_shapes=scratch,
        compiler_params=pltpu.CompilerParams(vmem_limit_bytes=64 * 1024 * 1024),
        cost_estimate=pl.CostEstimate(
            flops=int(micros * 1e9), bytes_accessed=int(micros * 3e6), transcendentals=0
        ),
        name=name,
    )

    def placed(*args):
        args = [
            pltpu.with_memory_space_constraint(arg, pltpu.HBM) if spec is ANY else arg
            for spec, arg in zip(in_specs, (*after, *args))
        ]
        return run(*args)

    return placed


def bf16(*shape):
    return pltpu.HBM(shape, jnp.bfloat16)


def f32(*shape):
    return pltpu.HBM(shape, jnp.float32)


def part_kernel(at_ref, k_ref, v_ref, kv_mine, kv_theirs, held_s, in_sem, out_sem):
    half = kv_mine.shape[1] // 2
    loads = [begin(held, held_s.at[i], in_sem.at[i]) for i, held in enumerate((k_ref, v_ref))]
    mine = pl.ds(pl.multiple_of(at_ref[0] * half, half), half)
    theirs = pl.ds(pl.multiple_of((1 - at_ref[0]) * half, half), half)
    copies = []
    for index in range(2):
        loads[index].wait()
        place = slice(index * half, (index + 1) * half)
        for side, (cols, out) in enumerate(((mine, kv_mine), (theirs, kv_theirs))):
            sem = out_sem.at[2 * index + side]
            copies.append(begin(held_s.at[index, :, cols], out.at[:, place], sem))
    for copy in copies:
        copy.wait()


def part_heads(at, keys, values):
    rows, feats = keys.shape
    return call(
        part_kernel,
        [bf16(rows, feats), bf16(rows, feats)],
        [SMEM] + [ANY] * 2,
        [ANY] * 2,
        [
            pltpu.VMEM((2, rows, feats), jnp.bfloat16),
            pltpu.SemaphoreType.DMA((2,)),
            pltpu.SemaphoreType.DMA((4,)),
        ],
        2,
        "part_heads",
    )(at, keys, values)


def prelude_kernel(at_ref, pattern, offsets, grad_ref, weight_ref, *refs):
    first, key_mask, row_mask = refs[:3]
    grad_s, weight_s, first_s, mask_s, row_s, sem, out_sem = refs[3:]
    rows, width = grad_s.shape
    block_count, glob_count = offsets.shape
    start = pl.multiple_of(at_ref[2] * width, width)
    loads = [
        begin(grad_ref, grad_s, sem.at[0]),
        begin(weight_ref.at[:, pl.ds(start, width)], weight_s, sem.at[1]),
    ]
    stores = []
    own = at_ref[1] * INNER + at_ref[0]
    partner = at_ref[1] * INNER + 1 - at_ref[0]
    lane = lax.broadcasted_iota(jnp.int32, (1, HD), 1)
    row_at = lax.broadcasted_iota(jnp.int32, (rows, HD), 0)
    col_at = lax.broadcasted_iota(jnp.int32, (8, rows), 1)
    group_at = lax.broadcasted_iota(jnp.int32, (8, rows), 0)
    for index in range(block_count):
        block = at_ref[SOURCES + index]
        hidden = []
        for target in (own, partner):
            seen = jnp.abs(block - target) <= 1
            for r in range(pattern.shape[1]):
                seen = seen | (pattern[target, r] == block)
            hidden.append(jnp.where(seen, 0, 1))
        lane_hidden = jnp.where(lane == 0, hidden[0], jnp.where(lane == 1, hidden[1], 0))
        hidden_rows = jnp.broadcast_to(lane_hidden, (rows, HD))
        for r in range(glob_count):
            hidden_rows = jnp.where(row_at == offsets[block, r], 0, hidden_rows)
        mask_s[index * rows : (index + 1) * rows, :] = hidden_rows.astype(jnp.float32).astype(
            jnp.bfloat16
        )
    for group, target in enumerate((own, partner)):
        local = jnp.where(group_at == group, MASKED, 0.0)
        for r in range(glob_count):
            local = jnp.where(col_at == offsets[target, r], 0.0, local)
        row_s[:, group * rows : (group + 1) * rows] = local
    stores.append(begin(mask_s, key_mask, out_sem.at[0]))
    stores.append(begin(row_s, row_mask, out_sem.at[1]))
    for load in loads:
        load.wait()
    first_s[...] = against(weight_s[...], grad_s[...])
    stores.append(begin(first_s, first, out_sem.at[2]))
    for store in stores:
        store.wait()


def prelude(at, pattern, offsets, grad_own, out_weight, after):
    rows, width = grad_own.shape
    feats = out_weight.shape[0]
    keys = offsets.shape[0] * rows
    return call(
        prelude_kernel,
        [
            f32(feats, rows),
            bf16(keys, HD),
            f32(8, 2 * rows),
        ],
        [SMEM] * 3 + [ANY] * 2,
        [ANY] * 3,
        [
            pltpu.VMEM((rows, width), jnp.bfloat16),
            pltpu.VMEM((feats, width), jnp.bfloat16),
            pltpu.VMEM((feats, rows), jnp.float32),
            pltpu.VMEM((keys, HD), jnp.bfloat16),
            pltpu.VMEM((8, 2 * rows), jnp.float32),
            pltpu.SemaphoreType.DMA((2,)),
            pltpu.SemaphoreType.DMA((3,)),
        ],
        4,
        "prelude",
        after,
    )(at, pattern, offsets, grad_own, out_weight)


def attention_kernel(block_count, head_count, at_ref, q_ref, recv_ref, g_mine, key_mask, row_mask, *refs):
    kv_refs, refs = refs[:block_count], refs[block_count:]
    attn_mine, attn_theirs, dq_mine, dq_theirs, part_out = refs[:5]
    refs = refs[5:]
    q_s, recv_s, g_s, mask_s, row_s, kv_s, e_s, s_ref, attn_s, dq_s, part_s = refs[:11]
    sem, kv_sem, out_sem, part_sem = refs[11:]
    rows = q_ref.shape[0]
    feats = head_count * HD
    score_scale = HD ** (-0.5)
    mine = pl.ds(pl.multiple_of(at_ref[0] * feats, feats), feats)
    loads = [
        begin(q_ref.at[:, mine], q_s, sem.at[0]),
        begin(recv_ref, recv_s, sem.at[1]),
        begin(key_mask, mask_s, sem.at[2]),
        begin(row_mask, row_s, sem.at[3]),
        begin(g_mine, g_s, sem.at[4]),
    ]
    kv_loads = [begin(kv_refs[j], kv_s.at[j], kv_sem.at[j]) for j in range(block_count)]
    for load in loads:
        load.wait()
    rows_low = row_s[...].astype(jnp.bfloat16)
    hidden = jnp.concatenate([rows_low, jnp.zeros((HD - 8, 2 * rows), jnp.bfloat16)], axis=0)
    stores = []
    for head in range(head_count):
        cols = slice(head * HD, (head + 1) * HD)
        vcols = slice(feats + head * HD, feats + (head + 1) * HD)
        query_recv = recv_s[1, cols, :]
        q_t = jnp.concatenate([jnp.transpose(q_s[:, cols]), query_recv], axis=1)
        q_t = jnp.concatenate([q_t, hidden], axis=0)
        top = jnp.full((1, 2 * rows), MASKED, jnp.float32)
        for j in range(block_count):
            if head == 0:
                kv_loads[j].wait()
            keys = slice(j * rows, (j + 1) * rows)
            scores = product(jnp.concatenate([kv_s[j, :, cols], mask_s[keys, :]], axis=1), q_t)
            s_ref[keys, :] = scores
            top = jnp.maximum(top, jnp.max(scores, axis=0, keepdims=True))
        total = jnp.zeros((1, 2 * rows), jnp.float32)
        attn_t = jnp.zeros((HD, 2 * rows), jnp.float32)
        for j in range(block_count):
            keys = slice(j * rows, (j + 1) * rows)
            weights = jnp.exp((s_ref[keys, :] - top) * score_scale)
            total = total + jnp.sum(weights, axis=0, keepdims=True)
            low = weights.astype(jnp.bfloat16)
            e_s[keys, :] = low
            attn_t = attn_t + product(jnp.transpose(kv_s[j, :, vcols]), low)
        inverse = 1.0 / total
        attn_low = (attn_t * inverse).astype(jnp.bfloat16)
        attn_s[0, cols, :] = attn_low[:, :rows]
        attn_s[1, cols, :] = attn_low[:, rows:]
        if head == head_count - 1:
            stores.append(begin(attn_s.at[0], attn_mine, out_sem.at[0]))
            stores.append(begin(attn_s.at[1], attn_theirs, out_sem.at[1]))
        g_t = jnp.concatenate([g_s[cols, :], recv_s[0, cols, :]], axis=1).astype(jnp.float32)
        row_dot = jnp.sum(g_t * attn_low.astype(jnp.float32), axis=0, keepdims=True) * inverse
        g_t = (g_t * inverse).astype(jnp.bfloat16)
        grad = jnp.transpose(g_t)
        query = jnp.concatenate([q_s[:, cols], jnp.transpose(query_recv)], axis=0)
        dq_t = jnp.zeros((HD, 2 * rows), jnp.float32)
        for j in range(block_count):
            keys = slice(j * rows, (j + 1) * rows)
            low = e_s[keys, :]
            dprobs = product(kv_s[j, :, vcols], g_t)
            dscore = (low.astype(jnp.float32) * (dprobs - row_dot)).astype(jnp.bfloat16)
            dq_t = dq_t + product(jnp.transpose(kv_s[j, :, cols]), dscore)
            part_s[j, :, cols] = (score_scale * product(dscore, query)).astype(jnp.bfloat16)
            part_s[j, :, vcols] = product(low, grad).astype(jnp.bfloat16)
            if head == head_count - 1:
                target = part_out.at[at_ref[SOURCES + j] // INNER, j % INNER]
                stores.append(begin(part_s.at[j], target, part_sem.at[j]))
        dquery = (score_scale * jnp.transpose(dq_t)).astype(jnp.bfloat16)
        dq_s[0, :, cols] = dquery[:rows]
        dq_s[1, :, cols] = dquery[rows:]
    stores.append(begin(dq_s.at[0], dq_mine, out_sem.at[2]))
    stores.append(begin(dq_s.at[1], dq_theirs, out_sem.at[3]))
    for store in stores:
        store.wait()


def attention(at, queries, recv, g_mine, key_mask, row_mask, kv_blocks):
    block_count = len(kv_blocks)
    feats, rows = g_mine.shape
    heads = feats // HD
    keys = block_count * rows
    parts = bf16(block_count // INNER, INNER, rows, 2 * feats)
    return call(
        functools.partial(attention_kernel, block_count, heads),
        [bf16(feats, rows)] * 2 + [bf16(rows, feats)] * 2 + [parts],
        [SMEM] + [ANY] * (5 + block_count),
        [ANY] * 5,
        [
            pltpu.VMEM((rows, feats), jnp.bfloat16),
            pltpu.VMEM((2, feats, rows), jnp.bfloat16),
            pltpu.VMEM((feats, rows), jnp.bfloat16),
            pltpu.VMEM((keys, HD), jnp.bfloat16),
            pltpu.VMEM((8, 2 * rows), jnp.float32),
            pltpu.VMEM((block_count, rows, 2 * feats), jnp.bfloat16),
            pltpu.VMEM((keys, 2 * rows), jnp.bfloat16),
            pltpu.VMEM((keys, 2 * rows), jnp.float32),
            pltpu.VMEM((2, feats, rows), jnp.bfloat16),
            pltpu.VMEM((2, rows, feats), jnp.bfloat16),
            pltpu.VMEM((block_count, rows, 2 * feats), jnp.bfloat16),
            pltpu.SemaphoreType.DMA((5,)),
            pltpu.SemaphoreType.DMA((block_count,)),
            pltpu.SemaphoreType.DMA((4,)),
            pltpu.SemaphoreType.DMA((block_count,)),
        ],
        20,
        "attention",
    )(at, queries, recv, g_mine, key_mask, row_mask, *kv_blocks)


def grad_heads_kernel(part_count, place, at_ref, first_ref, q_ref, weight_ref, *refs):
    grads, refs = refs[: part_count - 1], refs[part_count - 1 :]
    mine, theirs = refs[:2]
    first_s, q_s, grad_s, weight_s, out_s, sem, weight_sem, grad_sem, out_sem = refs[2:]
    half = out_s.shape[1]
    width = grads[0].shape[1]
    first_load = begin(first_ref, first_s, sem.at[0])
    cols = pl.ds(pl.multiple_of((1 - at_ref[0]) * half, half), half)
    q_load = begin(q_ref.at[:, cols], q_s, sem.at[1])
    loads = []
    for k in range(part_count - 1):
        start = pl.multiple_of(at_ref[place + k] * width, width)
        columns = weight_ref.at[:, pl.ds(start, width)]
        loads.append(begin(grads[k], grad_s.at[k], grad_sem.at[k]))
        loads.append(begin(columns, weight_s.at[k], weight_sem.at[k]))
    q_load.wait()
    out_s[2] = jnp.transpose(q_s[...])
    copies = [begin(out_s.at[2], theirs.at[1], out_sem.at[2])]
    first_load.wait()
    summed = first_s[...]
    for k in range(part_count - 1):
        loads[2 * k].wait()
        loads[2 * k + 1].wait()
        summed = summed + against(weight_s[k], grad_s[k])
    first_s[...] = summed
    for side, target in enumerate((mine, theirs.at[0])):
        at = (1 - at_ref[0]) if side else at_ref[0]
        kept = first_s[pl.ds(pl.multiple_of(at * half, half), half), :]
        out_s[side] = kept.astype(jnp.bfloat16)
        copies.append(begin(out_s.at[side], target, out_sem.at[side]))
    for copy in copies:
        copy.wait()


def grad_heads(at, place, first, queries, out_weight, grads):
    feats, rows = first.shape
    half = feats // INNER
    count = len(grads)
    width = grads[0].shape[1]
    return call(
        functools.partial(grad_heads_kernel, count, place),
        [bf16(half, rows), bf16(2, half, rows)],
        [SMEM] + [ANY] * (2 + count),
        [ANY] * 2,
        [
            pltpu.VMEM((feats, rows), jnp.float32),
            pltpu.VMEM((rows, half), jnp.bfloat16),
            pltpu.VMEM((count - 1, rows, width), jnp.bfloat16),
            pltpu.VMEM((count - 1, feats, width), jnp.bfloat16),
            pltpu.VMEM((3, half, rows), jnp.bfloat16),
            pltpu.SemaphoreType.DMA((2,)),
            pltpu.SemaphoreType.DMA((count - 1,)),
            pltpu.SemaphoreType.DMA((count - 1,)),
            pltpu.SemaphoreType.DMA((3,)),
        ],
        3,
        "grad_heads",
    )(at, first, queries, out_weight, *grads[1:])


def pick_kernel(part_count, picked, places, at_ref, *refs):
    grads, refs = refs[:part_count], refs[part_count:]
    outs, (held_s, sem, out_sem) = refs[: len(places)], refs[len(places) :]
    _, outer, _, block = outs[0].shape
    pieces = grads[0].shape[1] // block
    loads = [begin(grads[k], held_s.at[k], sem.at[k]) for k in range(part_count)]
    for load in loads:
        load.wait()
    stores = []
    for index, steps_at in enumerate(places):
        for side in range(INNER):
            here = (1 - at_ref[0]) if side else at_ref[0]
            for k in range(outer):
                place = lax.rem(at_ref[1] + k, outer) * INNER + here
                cols = pl.ds(pl.multiple_of(lax.rem(place, pieces) * block, block), block)
                source = held_s.at[at_ref[steps_at + place // pieces], :, cols]
                order = (index * INNER + side) * outer + k
                stores.append(begin(source, outs[index].at[side, k], out_sem.at[order]))
    for store in stores:
        store.wait()


def pick_columns(at, places, grads, outer, picked, after):
    rows, width = grads[0].shape
    block = picked * width // (outer * INNER)
    return call(
        functools.partial(pick_kernel, len(grads), picked, places),
        [bf16(INNER, outer, rows, block)] * len(places),
        [SMEM] + [ANY] * len(grads),
        [ANY] * len(places),
        [
            pltpu.VMEM((len(grads), rows, width), jnp.bfloat16),
            pltpu.SemaphoreType.DMA((len(grads),)),
            pltpu.SemaphoreType.DMA((len(places) * INNER * outer,)),
        ],
        3,
        "pick_columns",
        after,
    )(at, *grads)


def weight_kernel(doc_count, sent, at_ref, *refs):
    attn, refs = refs[: INNER * doc_count], refs[INNER * doc_count :]
    grads, refs = refs[:doc_count], refs[doc_count:]
    if sent:
        out, refs = refs[0], refs[1:]
        outs = [out.at[k] for k in range(out.shape[0])]
    else:
        recv, refs = refs[0], refs[1:]
        outs, refs = refs[: recv.shape[0]], refs[recv.shape[0] :]
        recv_s, recv_sem, refs = refs[0], refs[1], refs[2:]
    attn_s, grad_s, out_s, attn_sem, grad_sem, out_sem = refs
    outer, feats, _ = out_s.shape
    half = feats // INNER
    attn_loads, grad_loads = [], []
    for doc in range(doc_count):
        for side in range(INNER):
            at = (1 - at_ref[0]) if side else at_ref[0]
            index = doc * INNER + side
            target = attn_s.at[doc, pl.ds(pl.multiple_of(at * half, half), half)]
            attn_loads.append(begin(attn[index], target, attn_sem.at[index]))
    for k in range(outer):
        loads = [
            begin(grads[doc].at[int(sent), k], grad_s.at[doc, k], grad_sem.at[doc * outer + k])
            for doc in range(doc_count)
        ]
        if not sent:
            loads.append(begin(recv.at[k], recv_s.at[k], recv_sem.at[k]))
        grad_loads.append(loads)
    for load in attn_loads:
        load.wait()
    stores = []
    for k in range(outer):
        term = 0.0
        for doc in range(doc_count):
            grad_loads[k][doc].wait()
            term = term + product(attn_s[doc], grad_s[doc, k])
        if not sent:
            grad_loads[k][doc_count].wait()
            term = term + recv_s[k].astype(jnp.float32)
        out_s[k] = term.astype(out_s.dtype)
        stores.append(begin(out_s.at[k], outs[k], out_sem.at[k]))
    for store in stores:
        store.wait()


def weight_terms(at, attn, grads, recv=None, after=()):
    half, rows = attn[0].shape
    feats = half * INNER
    doc_count = len(grads)
    _, outer, _, width = grads[0].shape
    sent = recv is None
    operands = [*attn, *grads] + ([] if sent else [recv])
    scratch = [
        pltpu.VMEM((doc_count, feats, rows), jnp.bfloat16),
        pltpu.VMEM((doc_count, outer, rows, width), jnp.bfloat16),
        pltpu.VMEM((outer, feats, width), jnp.bfloat16),
        pltpu.SemaphoreType.DMA((len(attn),)),
        pltpu.SemaphoreType.DMA((doc_count * outer,)),
        pltpu.SemaphoreType.DMA((outer,)),
    ]
    if not sent:
        added = [pltpu.VMEM((outer, feats, width), jnp.bfloat16), pltpu.SemaphoreType.DMA((outer,))]
        scratch = added + scratch
    return call(
        functools.partial(weight_kernel, doc_count, sent),
        bf16(outer, feats, width) if sent else [bf16(feats, width)] * outer,
        [SMEM] + [ANY] * len(operands),
        ANY if sent else [ANY] * outer,
        scratch,
        4,
        "weight_sent" if sent else "weight_kept",
        after,
    )(at, *operands)


def add_kernel(dq_theirs, terms, mine, theirs, *scratch):
    terms_s, mine_s, theirs_s, dq_s, term_sem, out_sem, dq_sem = scratch
    count, _, _, both = terms.shape
    dq_load = begin(dq_theirs, dq_s, dq_sem)
    loads = {
        (side, c): begin(terms.at[c, side], terms_s.at[c, side], term_sem.at[c * INNER + side])
        for side in (1, 0)
        for c in range(count)
    }
    stores = []
    for side, (held_s, out) in ((1, (theirs_s, theirs)), (0, (mine_s, mine))):
        summed = 0.0
        for c in range(count):
            loads[side, c].wait()
            summed = summed + terms_s[c, side].astype(jnp.float32)
        held_s[:, :both] = summed.astype(jnp.bfloat16)
        if side:
            dq_load.wait()
            held_s[:, both:] = dq_s[...]
        stores.append(begin(held_s, out, out_sem.at[side]))
    for store in stores:
        store.wait()


def add_terms(dq_theirs, terms, after):
    count, _, rows, both = terms.shape
    half = both // 2
    return call(
        add_kernel,
        [bf16(rows, both), bf16(rows, both + half)],
        [ANY] * 2,
        [ANY] * 2,
        [
            pltpu.VMEM((count, INNER, rows, both), jnp.bfloat16),
            pltpu.VMEM((rows, both), jnp.bfloat16),
            pltpu.VMEM((rows, both + half), jnp.bfloat16),
            pltpu.VMEM((rows, half), jnp.bfloat16),
            pltpu.SemaphoreType.DMA((count * INNER,)),
            pltpu.SemaphoreType.DMA((INNER,)),
            pltpu.SemaphoreType.DMA,
        ],
        2,
        "add_terms",
        after,
    )(dq_theirs, terms)


def join_kernel(at_ref, dq_mine, mine, recv, *refs):
    outs, (dq_s, mine_s, recv_s, out_s, sem, out_sem) = refs[:3], refs[3:]
    half = dq_mine.shape[1]
    loads = [
        begin(dq_mine, dq_s, sem.at[0]),
        begin(mine, mine_s, sem.at[1]),
        begin(recv, recv_s, sem.at[2]),
    ]
    here = pl.ds(pl.multiple_of(at_ref[0] * half, half), half)
    there = pl.ds(pl.multiple_of((1 - at_ref[0]) * half, half), half)
    for load in loads:
        load.wait()
    out_s[0, :, here] = dq_s[...]
    out_s[0, :, there] = recv_s[:, 2 * half :]
    for kind in range(2):
        cols = slice(kind * half, (kind + 1) * half)
        out_s[1 + kind, :, here] = mine_s[:, cols]
        out_s[1 + kind, :, there] = recv_s[:, cols]
    stores = [begin(out_s.at[index], out, out_sem.at[index]) for index, out in enumerate(outs)]
    for store in stores:
        store.wait()


def join_heads(at, dq_mine, mine, recv):
    rows, half = dq_mine.shape
    return call(
        join_kernel,
        [bf16(rows, INNER * half)] * 3,
        [SMEM] + [ANY] * 3,
        [ANY] * 3,
        [
            pltpu.VMEM(dq_mine.shape, jnp.bfloat16),
            pltpu.VMEM(mine.shape, jnp.bfloat16),
            pltpu.VMEM(recv.shape, jnp.bfloat16),
            pltpu.VMEM((3, rows, INNER * half), jnp.bfloat16),
            pltpu.SemaphoreType.DMA((3,)),
            pltpu.SemaphoreType.DMA((3,)),
        ],
        2,
        "join_heads",
    )(at, dq_mine, mine, recv)


def per_device(
    queries, key_heads, value_heads, grad_output, out_weight, block_pattern, global_offsets
):
    dp_count, ctx_count, tp_count = (lax.axis_size(name) for name in ("dp", "ctx", "tp"))
    dp_at, ctx_at, tp_at = (lax.axis_index(name) for name in ("dp", "ctx", "tp"))
    outer = ctx_count // INNER
    outer_at, inner_at = ctx_at // INNER, ctx_at % INNER
    picked = tp_count // dp_count

    def ctx_pairs(step, side, dp_step=0):
        moved = [(c + step * INNER) % ctx_count ^ side for c in range(ctx_count)]
        if not dp_step:
            return list(enumerate(moved))
        return [
            (d * ctx_count + c, (d + dp_step) % dp_count * ctx_count + moved[c])
            for d in range(dp_count)
            for c in range(ctx_count)
        ]

    def shift_pairs(count, step):
        return [(i, (i + step) % count) for i in range(count)]

    def dp_steps(which):
        return [(which * picked + i - tp_at) % tp_count for i in range(picked)]

    routes = [(step, side) for step in range(outer) for side in range(INNER)]
    sources = [
        ((outer_at - step) % outer) * INNER + (inner_at + side) % INNER for step, side in routes
    ]
    scalars = [inner_at, outer_at, tp_at] + sources
    columns_at = len(scalars)
    scalars = scalars + [(tp_at + step) % tp_count for step in range(1, tp_count)]
    groups_at = []
    for step in range(dp_count):
        groups_at.append(len(scalars))
        scalars = scalars + dp_steps((dp_at + step) % dp_count)
    at = jnp.stack(scalars)

    grad_own = grad_output[0]
    grads = [grad_own] + [
        lax.ppermute(grad_own, "tp", shift_pairs(tp_count, -step)) for step in range(1, tp_count)
    ]
    kv_mine, kv_theirs = part_heads(at, key_heads[0], value_heads[0])
    kv_recv = lax.ppermute(kv_theirs, "ctx", ctx_pairs(0, 1))
    kv_blocks = [
        lax.ppermute(kv_recv if side else kv_mine, "ctx", ctx_pairs(step, 0))
        if step
        else (kv_recv if side else kv_mine)
        for step, side in routes
    ]
    first, key_mask, row_mask = prelude(
        at, block_pattern, global_offsets, grad_own, out_weight, (kv_recv, kv_blocks[INNER], kv_blocks[-INNER])
    )
    g_mine, theirs = grad_heads(at, columns_at, first, queries[0], out_weight, grads)
    recv = lax.ppermute(theirs, "ctx", ctx_pairs(0, 1))
    kept, *sends = pick_columns(at, tuple(groups_at), grads, outer, picked, (g_mine,))
    grad_blocks = [kept] + [
        lax.ppermute(send, "dp", shift_pairs(dp_count, step + 1)) for step, send in enumerate(sends)
    ]

    attn_mine, attn_theirs, dq_mine, dq_theirs, parts = attention(
        at, queries[0], recv, g_mine, key_mask, row_mask, kv_blocks
    )
    columns = [[o * INNER + i for o in range(outer)] for i in range(INNER)]
    terms = lax.all_to_all(
        parts, "ctx", split_axis=0, concat_axis=0, axis_index_groups=columns, tiled=True
    )

    attn = []
    for step in range(dp_count):
        for held, side in ((attn_mine, 0), (attn_theirs, 1)):
            pairs = ctx_pairs(0, side, step)
            axes = ("dp", "ctx") if step else "ctx"
            attn.append(lax.ppermute(held, axes, pairs) if step or side else held)

    send = weight_terms(at, attn, grad_blocks)
    weight_recv = lax.ppermute(send, "ctx", ctx_pairs(0, 1))
    weight_sums = weight_terms(at, attn, grad_blocks, weight_recv)
    weight_parts = [
        lax.ppermute(weight_sums[step], "ctx", ctx_pairs(step, 0)) for step in range(1, outer)
    ]
    terms_mine, terms_theirs = add_terms(dq_theirs, terms, (weight_sums[0],))
    terms_recv = lax.ppermute(terms_theirs, "ctx", ctx_pairs(0, 1))
    grad_q, grad_k, grad_v = join_heads(at, dq_mine, terms_mine, terms_recv)
    grad_weight = weight_sums[0].astype(jnp.float32)
    for part in weight_parts:
        grad_weight = grad_weight + part.astype(jnp.float32)

    return grad_q[None], grad_k[None], grad_v[None], grad_weight.astype(jnp.bfloat16)


def solution(mesh):
    in_specs = (
        P("dp", "ctx", "tp"),
        P("dp", "ctx", "tp"),
        P("dp", "ctx", "tp"),
        P("dp", "ctx", "tp"),
        P("tp", None),
        P(),
        P(),
    )
    out_specs = (
        P("dp", "ctx", "tp"),
        P("dp", "ctx", "tp"),
        P("dp", "ctx", "tp"),
        P("tp", ("dp", "ctx")),
    )
    return jax.shard_map(
        per_device, mesh=mesh, in_specs=in_specs, out_specs=out_specs, check_vma=False
    )
```

```python
import functools

import jax
import jax.numpy as jnp
from jax import lax
from jax.experimental import pallas as pl
from jax.experimental.pallas import tpu as pltpu
from jax.sharding import PartitionSpec as P

HD = 128
MASKED = -1e30
INNER = 2
SOURCES = 3
ANY = pl.BlockSpec(memory_space=pl.ANY)
VMEM = pl.BlockSpec(memory_space=pltpu.VMEM)
SMEM = pl.BlockSpec(memory_space=pltpu.SMEM)


def against(left_op, right_op):
    return lax.dot_general(
        left_op, right_op, (((1,), (1,)), ((), ())), preferred_element_type=jnp.float32
    )


def product(left_op, right_op):
    return jnp.dot(left_op, right_op, preferred_element_type=jnp.float32)


def begin(source, target, semaphore):
    copy = pltpu.make_async_copy(source, target, semaphore)
    copy.start()
    return copy


def call(kernel, out_shape, in_specs, out_specs, scratch, micros, name, after=()):
    skipped = len(after)
    in_specs = [ANY] * skipped + in_specs
    run = pl.pallas_call(
        lambda *refs: kernel(*refs[skipped:]),
        out_shape=out_shape,
        in_specs=in_specs,
        out_specs=out_specs,
        scratch_shapes=scratch,
        compiler_params=pltpu.CompilerParams(vmem_limit_bytes=64 * 1024 * 1024),
        cost_estimate=pl.CostEstimate(
            flops=int(micros * 1e9), bytes_accessed=int(micros * 3e6), transcendentals=0
        ),
        name=name,
    )

    def placed(*args):
        args = [
            pltpu.with_memory_space_constraint(arg, pltpu.HBM) if spec is ANY else arg
            for spec, arg in zip(in_specs, (*after, *args))
        ]
        return run(*args)

    return placed


def bf16(*shape):
    return pltpu.HBM(shape, jnp.bfloat16)


def f32(*shape):
    return pltpu.HBM(shape, jnp.float32)


def part_kernel(at_ref, k_ref, v_ref, kv_mine, kv_theirs, held_s, in_sem, out_sem):
    half = kv_mine.shape[1] // 2
    loads = [begin(held, held_s.at[i], in_sem.at[i]) for i, held in enumerate((k_ref, v_ref))]
    mine = pl.ds(pl.multiple_of(at_ref[0] * half, half), half)
    theirs = pl.ds(pl.multiple_of((1 - at_ref[0]) * half, half), half)
    copies = []
    for index in range(2):
        loads[index].wait()
        place = slice(index * half, (index + 1) * half)
        for side, (cols, out) in enumerate(((mine, kv_mine), (theirs, kv_theirs))):
            sem = out_sem.at[2 * index + side]
            copies.append(begin(held_s.at[index, :, cols], out.at[:, place], sem))
    for copy in copies:
        copy.wait()


def part_heads(at, keys, values):
    rows, feats = keys.shape
    return call(
        part_kernel,
        [bf16(rows, feats), bf16(rows, feats)],
        [SMEM] + [ANY] * 2,
        [ANY] * 2,
        [
            pltpu.VMEM((2, rows, feats), jnp.bfloat16),
            pltpu.SemaphoreType.DMA((2,)),
            pltpu.SemaphoreType.DMA((4,)),
        ],
        2,
        "part_heads",
    )(at, keys, values)


def prelude_kernel(at_ref, pattern, offsets, grad_ref, weight_ref, *refs):
    first, key_mask, row_mask = refs[:3]
    grad_s, weight_s, first_s, mask_s, row_s, sem, out_sem = refs[3:]
    rows, width = grad_s.shape
    block_count, glob_count = offsets.shape
    start = pl.multiple_of(at_ref[2] * width, width)
    loads = [
        begin(grad_ref, grad_s, sem.at[0]),
        begin(weight_ref.at[:, pl.ds(start, width)], weight_s, sem.at[1]),
    ]
    stores = []
    own = at_ref[1] * INNER + at_ref[0]
    partner = at_ref[1] * INNER + 1 - at_ref[0]
    lane = lax.broadcasted_iota(jnp.int32, (1, HD), 1)
    row_at = lax.broadcasted_iota(jnp.int32, (rows, HD), 0)
    col_at = lax.broadcasted_iota(jnp.int32, (8, rows), 1)
    group_at = lax.broadcasted_iota(jnp.int32, (8, rows), 0)
    for index in range(block_count):
        block = at_ref[SOURCES + index]
        hidden = []
        for target in (own, partner):
            seen = jnp.abs(block - target) <= 1
            for r in range(pattern.shape[1]):
                seen = seen | (pattern[target, r] == block)
            hidden.append(jnp.where(seen, 0, 1))
        lane_hidden = jnp.where(lane == 0, hidden[0], jnp.where(lane == 1, hidden[1], 0))
        hidden_rows = jnp.broadcast_to(lane_hidden, (rows, HD))
        for r in range(glob_count):
            hidden_rows = jnp.where(row_at == offsets[block, r], 0, hidden_rows)
        mask_s[index * rows : (index + 1) * rows, :] = hidden_rows.astype(jnp.float32).astype(
            jnp.bfloat16
        )
    for group, target in enumerate((own, partner)):
        local = jnp.where(group_at == group, MASKED, 0.0)
        for r in range(glob_count):
            local = jnp.where(col_at == offsets[target, r], 0.0, local)
        row_s[:, group * rows : (group + 1) * rows] = local
    stores.append(begin(mask_s, key_mask, out_sem.at[0]))
    stores.append(begin(row_s, row_mask, out_sem.at[1]))
    for load in loads:
        load.wait()
    first_s[...] = against(weight_s[...], grad_s[...])
    stores.append(begin(first_s, first, out_sem.at[2]))
    for store in stores:
        store.wait()


def prelude(at, pattern, offsets, grad_own, out_weight, after):
    rows, width = grad_own.shape
    feats = out_weight.shape[0]
    keys = offsets.shape[0] * rows
    return call(
        prelude_kernel,
        [
            f32(feats, rows),
            bf16(keys, HD),
            f32(8, 2 * rows),
        ],
        [SMEM] * 3 + [ANY] * 2,
        [ANY] * 3,
        [
            pltpu.VMEM((rows, width), jnp.bfloat16),
            pltpu.VMEM((feats, width), jnp.bfloat16),
            pltpu.VMEM((feats, rows), jnp.float32),
            pltpu.VMEM((keys, HD), jnp.bfloat16),
            pltpu.VMEM((8, 2 * rows), jnp.float32),
            pltpu.SemaphoreType.DMA((2,)),
            pltpu.SemaphoreType.DMA((3,)),
        ],
        4,
        "prelude",
        after,
    )(at, pattern, offsets, grad_own, out_weight)


def attention_kernel(block_count, head_count, at_ref, q_ref, recv_ref, g_mine, key_mask, row_mask, *refs):
    kv_refs, refs = refs[:block_count], refs[block_count:]
    attn_mine, attn_theirs, dq_mine, dq_theirs, part_out = refs[:5]
    refs = refs[5:]
    q_s, recv_s, g_s, mask_s, row_s, kv_s, e_s, s_ref, attn_s, dq_s, part_s = refs[:11]
    sem, kv_sem, out_sem, part_sem = refs[11:]
    rows = q_ref.shape[0]
    feats = head_count * HD
    score_scale = HD ** (-0.5)
    mine = pl.ds(pl.multiple_of(at_ref[0] * feats, feats), feats)
    loads = [
        begin(q_ref.at[:, mine], q_s, sem.at[0]),
        begin(recv_ref, recv_s, sem.at[1]),
        begin(key_mask, mask_s, sem.at[2]),
        begin(row_mask, row_s, sem.at[3]),
        begin(g_mine, g_s, sem.at[4]),
    ]
    kv_loads = [begin(kv_refs[j], kv_s.at[j], kv_sem.at[j]) for j in range(block_count)]
    for load in loads:
        load.wait()
    rows_low = row_s[...].astype(jnp.bfloat16)
    hidden = jnp.concatenate([rows_low, jnp.zeros((HD - 8, 2 * rows), jnp.bfloat16)], axis=0)
    stores = []
    for head in range(head_count):
        cols = slice(head * HD, (head + 1) * HD)
        vcols = slice(feats + head * HD, feats + (head + 1) * HD)
        query_recv = recv_s[1, cols, :]
        q_t = jnp.concatenate([jnp.transpose(q_s[:, cols]), query_recv], axis=1)
        q_t = jnp.concatenate([q_t, hidden], axis=0)
        top = jnp.full((1, 2 * rows), MASKED, jnp.float32)
        for j in range(block_count):
            if head == 0:
                kv_loads[j].wait()
            keys = slice(j * rows, (j + 1) * rows)
            scores = product(jnp.concatenate([kv_s[j, :, cols], mask_s[keys, :]], axis=1), q_t)
            s_ref[keys, :] = scores
            top = jnp.maximum(top, jnp.max(scores, axis=0, keepdims=True))
        total = jnp.zeros((1, 2 * rows), jnp.float32)
        attn_t = jnp.zeros((HD, 2 * rows), jnp.float32)
        for j in range(block_count):
            keys = slice(j * rows, (j + 1) * rows)
            weights = jnp.exp((s_ref[keys, :] - top) * score_scale)
            total = total + jnp.sum(weights, axis=0, keepdims=True)
            low = weights.astype(jnp.bfloat16)
            e_s[keys, :] = low
            attn_t = attn_t + product(jnp.transpose(kv_s[j, :, vcols]), low)
        inverse = 1.0 / total
        attn_low = (attn_t * inverse).astype(jnp.bfloat16)
        attn_s[0, cols, :] = attn_low[:, :rows]
        attn_s[1, cols, :] = attn_low[:, rows:]
        if head == head_count - 1:
            stores.append(begin(attn_s.at[0], attn_mine, out_sem.at[0]))
            stores.append(begin(attn_s.at[1], attn_theirs, out_sem.at[1]))
        g_t = jnp.concatenate([g_s[cols, :], recv_s[0, cols, :]], axis=1).astype(jnp.float32)
        row_dot = jnp.sum(g_t * attn_low.astype(jnp.float32), axis=0, keepdims=True) * inverse
        g_t = (g_t * inverse).astype(jnp.bfloat16)
        grad = jnp.transpose(g_t)
        query = jnp.concatenate([q_s[:, cols], jnp.transpose(query_recv)], axis=0)
        dq_t = jnp.zeros((HD, 2 * rows), jnp.float32)
        for j in range(block_count):
            keys = slice(j * rows, (j + 1) * rows)
            low = e_s[keys, :]
            dprobs = product(kv_s[j, :, vcols], g_t)
            dscore = (low.astype(jnp.float32) * (dprobs - row_dot)).astype(jnp.bfloat16)
            dq_t = dq_t + product(jnp.transpose(kv_s[j, :, cols]), dscore)
            part_s[j, :, cols] = (score_scale * product(dscore, query)).astype(jnp.bfloat16)
            part_s[j, :, vcols] = product(low, grad).astype(jnp.bfloat16)
            if head == head_count - 1:
                target = part_out.at[at_ref[SOURCES + j] // INNER, j % INNER]
                stores.append(begin(part_s.at[j], target, part_sem.at[j]))
        dquery = (score_scale * jnp.transpose(dq_t)).astype(jnp.bfloat16)
        dq_s[0, :, cols] = dquery[:rows]
        dq_s[1, :, cols] = dquery[rows:]
    stores.append(begin(dq_s.at[0], dq_mine, out_sem.at[2]))
    stores.append(begin(dq_s.at[1], dq_theirs, out_sem.at[3]))
    for store in stores:
        store.wait()


def attention(at, queries, recv, g_mine, key_mask, row_mask, kv_blocks):
    block_count = len(kv_blocks)
    feats, rows = g_mine.shape
    heads = feats // HD
    keys = block_count * rows
    parts = bf16(block_count // INNER, INNER, rows, 2 * feats)
    return call(
        functools.partial(attention_kernel, block_count, heads),
        [bf16(feats, rows)] * 2 + [bf16(rows, feats)] * 2 + [parts],
        [SMEM] + [ANY] * (5 + block_count),
        [ANY] * 5,
        [
            pltpu.VMEM((rows, feats), jnp.bfloat16),
            pltpu.VMEM((2, feats, rows), jnp.bfloat16),
            pltpu.VMEM((feats, rows), jnp.bfloat16),
            pltpu.VMEM((keys, HD), jnp.bfloat16),
            pltpu.VMEM((8, 2 * rows), jnp.float32),
            pltpu.VMEM((block_count, rows, 2 * feats), jnp.bfloat16),
            pltpu.VMEM((keys, 2 * rows), jnp.bfloat16),
            pltpu.VMEM((keys, 2 * rows), jnp.float32),
            pltpu.VMEM((2, feats, rows), jnp.bfloat16),
            pltpu.VMEM((2, rows, feats), jnp.bfloat16),
            pltpu.VMEM((block_count, rows, 2 * feats), jnp.bfloat16),
            pltpu.SemaphoreType.DMA((5,)),
            pltpu.SemaphoreType.DMA((block_count,)),
            pltpu.SemaphoreType.DMA((4,)),
            pltpu.SemaphoreType.DMA((block_count,)),
        ],
        20,
        "attention",
    )(at, queries, recv, g_mine, key_mask, row_mask, *kv_blocks)


def grad_heads_kernel(part_count, place, at_ref, first_ref, q_ref, weight_ref, *refs):
    grads, refs = refs[: part_count - 1], refs[part_count - 1 :]
    mine, theirs = refs[:2]
    first_s, q_s, grad_s, weight_s, out_s, sem, weight_sem, grad_sem, out_sem = refs[2:]
    half = out_s.shape[1]
    width = grads[0].shape[1]
    first_load = begin(first_ref, first_s, sem.at[0])
    cols = pl.ds(pl.multiple_of((1 - at_ref[0]) * half, half), half)
    q_load = begin(q_ref.at[:, cols], q_s, sem.at[1])
    loads = []
    for k in range(part_count - 1):
        start = pl.multiple_of(at_ref[place + k] * width, width)
        columns = weight_ref.at[:, pl.ds(start, width)]
        loads.append(begin(grads[k], grad_s.at[k], grad_sem.at[k]))
        loads.append(begin(columns, weight_s.at[k], weight_sem.at[k]))
    q_load.wait()
    out_s[2] = jnp.transpose(q_s[...])
    copies = [begin(out_s.at[2], theirs.at[1], out_sem.at[2])]
    first_load.wait()
    summed = first_s[...]
    for k in range(part_count - 1):
        loads[2 * k].wait()
        loads[2 * k + 1].wait()
        summed = summed + against(weight_s[k], grad_s[k])
    first_s[...] = summed
    for side, target in enumerate((mine, theirs.at[0])):
        at = (1 - at_ref[0]) if side else at_ref[0]
        kept = first_s[pl.ds(pl.multiple_of(at * half, half), half), :]
        out_s[side] = kept.astype(jnp.bfloat16)
        copies.append(begin(out_s.at[side], target, out_sem.at[side]))
    for copy in copies:
        copy.wait()


def grad_heads(at, place, first, queries, out_weight, grads):
    feats, rows = first.shape
    half = feats // INNER
    count = len(grads)
    width = grads[0].shape[1]
    return call(
        functools.partial(grad_heads_kernel, count, place),
        [bf16(half, rows), bf16(2, half, rows)],
        [SMEM] + [ANY] * (2 + count),
        [ANY] * 2,
        [
            pltpu.VMEM((feats, rows), jnp.float32),
            pltpu.VMEM((rows, half), jnp.bfloat16),
            pltpu.VMEM((count - 1, rows, width), jnp.bfloat16),
            pltpu.VMEM((count - 1, feats, width), jnp.bfloat16),
            pltpu.VMEM((3, half, rows), jnp.bfloat16),
            pltpu.SemaphoreType.DMA((2,)),
            pltpu.SemaphoreType.DMA((count - 1,)),
            pltpu.SemaphoreType.DMA((count - 1,)),
            pltpu.SemaphoreType.DMA((3,)),
        ],
        3,
        "grad_heads",
    )(at, first, queries, out_weight, *grads[1:])


def pick_kernel(part_count, picked, places, at_ref, *refs):
    grads, refs = refs[:part_count], refs[part_count:]
    outs, (held_s, sem, out_sem) = refs[: len(places)], refs[len(places) :]
    _, outer, _, block = outs[0].shape
    pieces = grads[0].shape[1] // block
    loads = [begin(grads[k], held_s.at[k], sem.at[k]) for k in range(part_count)]
    for load in loads:
        load.wait()
    stores = []
    for index, steps_at in enumerate(places):
        for side in range(INNER):
            here = (1 - at_ref[0]) if side else at_ref[0]
            for k in range(outer):
                place = lax.rem(at_ref[1] + k, outer) * INNER + here
                cols = pl.ds(pl.multiple_of(lax.rem(place, pieces) * block, block), block)
                source = held_s.at[at_ref[steps_at + place // pieces], :, cols]
                order = (index * INNER + side) * outer + k
                stores.append(begin(source, outs[index].at[side, k], out_sem.at[order]))
    for store in stores:
        store.wait()


def pick_columns(at, places, grads, outer, picked, after):
    rows, width = grads[0].shape
    block = picked * width // (outer * INNER)
    return call(
        functools.partial(pick_kernel, len(grads), picked, places),
        [bf16(INNER, outer, rows, block)] * len(places),
        [SMEM] + [ANY] * len(grads),
        [ANY] * len(places),
        [
            pltpu.VMEM((len(grads), rows, width), jnp.bfloat16),
            pltpu.SemaphoreType.DMA((len(grads),)),
            pltpu.SemaphoreType.DMA((len(places) * INNER * outer,)),
        ],
        3,
        "pick_columns",
        after,
    )(at, *grads)


def weight_kernel(doc_count, side, steps, at_ref, *refs):
    attn, refs = refs[: INNER * doc_count], refs[INNER * doc_count :]
    grads, refs = refs[:doc_count], refs[doc_count:]
    out, attn_s, grad_s, out_s, attn_sem, grad_sem, out_sem = refs
    half = out.shape[1] // INNER
    attn_loads, grad_loads = [], []
    for doc in range(doc_count):
        for group in range(INNER):
            at = (1 - at_ref[0]) if group else at_ref[0]
            index = doc * INNER + group
            target = attn_s.at[doc, pl.ds(pl.multiple_of(at * half, half), half)]
            attn_loads.append(begin(attn[index], target, attn_sem.at[index]))
    for index, step in enumerate(steps):
        for doc in range(doc_count):
            sem = grad_sem.at[doc * len(steps) + index]
            grad_loads.append(begin(grads[doc].at[side, step], grad_s.at[doc, index], sem))
    for load in attn_loads:
        load.wait()
    stores = []
    for index in range(len(steps)):
        term = 0.0
        for doc in range(doc_count):
            grad_loads[index * doc_count + doc].wait()
            term = term + product(attn_s[doc], grad_s[doc, index])
        out_s[index] = term.astype(out_s.dtype)
        stores.append(begin(out_s.at[index], out.at[index], out_sem.at[index]))
    for store in stores:
        store.wait()


def weight_terms(at, attn, grads, side, steps, name, after=()):
    half, rows = attn[0].shape
    feats = half * INNER
    doc_count, count = len(grads), len(steps)
    width = grads[0].shape[3]
    return call(
        functools.partial(weight_kernel, doc_count, side, steps),
        bf16(count, feats, width),
        [SMEM] + [ANY] * (len(attn) + doc_count),
        ANY,
        [
            pltpu.VMEM((doc_count, feats, rows), jnp.bfloat16),
            pltpu.VMEM((doc_count, count, rows, width), jnp.bfloat16),
            pltpu.VMEM((count, feats, width), jnp.bfloat16),
            pltpu.SemaphoreType.DMA((len(attn),)),
            pltpu.SemaphoreType.DMA((doc_count * count,)),
            pltpu.SemaphoreType.DMA((count,)),
        ],
        4,
        name,
        after,
    )(at, *attn, *grads)


def weight_add_kernel(first, keep, recv, *refs):
    count = recv.shape[0]
    outs, (held_s, out_s, sem, out_sem) = refs[:count], refs[count:]
    loads = []
    for index in range(count):
        loads.append(begin(keep.at[first + index], held_s.at[0, index], sem.at[2 * index]))
        loads.append(begin(recv.at[index], held_s.at[1, index], sem.at[2 * index + 1]))
    stores = []
    for index in range(count):
        loads[2 * index].wait()
        loads[2 * index + 1].wait()
        summed = held_s[0, index].astype(jnp.float32) + held_s[1, index].astype(jnp.float32)
        out_s[index] = summed.astype(jnp.bfloat16)
        stores.append(begin(out_s.at[index], outs[index], out_sem.at[index]))
    for store in stores:
        store.wait()


def weight_add(first, keep, recv, after):
    count, feats, width = recv.shape
    return call(
        functools.partial(weight_add_kernel, first),
        [bf16(feats, width)] * count,
        [ANY] * 2,
        [ANY] * count,
        [
            pltpu.VMEM((2, count, feats, width), jnp.bfloat16),
            pltpu.VMEM((count, feats, width), jnp.bfloat16),
            pltpu.SemaphoreType.DMA((2 * count,)),
            pltpu.SemaphoreType.DMA((count,)),
        ],
        2,
        "weight_add",
        after,
    )(keep, recv)


def add_kernel(dq_theirs, terms, mine, theirs, *scratch):
    terms_s, mine_s, theirs_s, dq_s, term_sem, out_sem, dq_sem = scratch
    count, _, _, both = terms.shape
    dq_load = begin(dq_theirs, dq_s, dq_sem)
    loads = {
        (side, c): begin(terms.at[c, side], terms_s.at[c, side], term_sem.at[c * INNER + side])
        for side in (1, 0)
        for c in range(count)
    }
    stores = []
    for side, (held_s, out) in ((1, (theirs_s, theirs)), (0, (mine_s, mine))):
        summed = 0.0
        for c in range(count):
            loads[side, c].wait()
            summed = summed + terms_s[c, side].astype(jnp.float32)
        held_s[:, :both] = summed.astype(jnp.bfloat16)
        if side:
            dq_load.wait()
            held_s[:, both:] = dq_s[...]
        stores.append(begin(held_s, out, out_sem.at[side]))
    for store in stores:
        store.wait()


def add_terms(dq_theirs, terms, after):
    count, _, rows, both = terms.shape
    half = both // 2
    return call(
        add_kernel,
        [bf16(rows, both), bf16(rows, both + half)],
        [ANY] * 2,
        [ANY] * 2,
        [
            pltpu.VMEM((count, INNER, rows, both), jnp.bfloat16),
            pltpu.VMEM((rows, both), jnp.bfloat16),
            pltpu.VMEM((rows, both + half), jnp.bfloat16),
            pltpu.VMEM((rows, half), jnp.bfloat16),
            pltpu.SemaphoreType.DMA((count * INNER,)),
            pltpu.SemaphoreType.DMA((INNER,)),
            pltpu.SemaphoreType.DMA,
        ],
        2,
        "add_terms",
        after,
    )(dq_theirs, terms)


def join_kernel(at_ref, dq_mine, mine, recv, *refs):
    outs, (dq_s, mine_s, recv_s, out_s, sem, out_sem) = refs[:3], refs[3:]
    half = dq_mine.shape[1]
    loads = [
        begin(dq_mine, dq_s, sem.at[0]),
        begin(mine, mine_s, sem.at[1]),
        begin(recv, recv_s, sem.at[2]),
    ]
    here = pl.ds(pl.multiple_of(at_ref[0] * half, half), half)
    there = pl.ds(pl.multiple_of((1 - at_ref[0]) * half, half), half)
    for load in loads:
        load.wait()
    out_s[0, :, here] = dq_s[...]
    out_s[0, :, there] = recv_s[:, 2 * half :]
    for kind in range(2):
        cols = slice(kind * half, (kind + 1) * half)
        out_s[1 + kind, :, here] = mine_s[:, cols]
        out_s[1 + kind, :, there] = recv_s[:, cols]
    stores = [begin(out_s.at[index], out, out_sem.at[index]) for index, out in enumerate(outs)]
    for store in stores:
        store.wait()


def join_heads(at, dq_mine, mine, recv):
    rows, half = dq_mine.shape
    return call(
        join_kernel,
        [bf16(rows, INNER * half)] * 3,
        [SMEM] + [ANY] * 3,
        [ANY] * 3,
        [
            pltpu.VMEM(dq_mine.shape, jnp.bfloat16),
            pltpu.VMEM(mine.shape, jnp.bfloat16),
            pltpu.VMEM(recv.shape, jnp.bfloat16),
            pltpu.VMEM((3, rows, INNER * half), jnp.bfloat16),
            pltpu.SemaphoreType.DMA((3,)),
            pltpu.SemaphoreType.DMA((3,)),
        ],
        2,
        "join_heads",
    )(at, dq_mine, mine, recv)


def per_device(
    queries, key_heads, value_heads, grad_output, out_weight, block_pattern, global_offsets
):
    dp_count, ctx_count, tp_count = (lax.axis_size(name) for name in ("dp", "ctx", "tp"))
    dp_at, ctx_at, tp_at = (lax.axis_index(name) for name in ("dp", "ctx", "tp"))
    outer = ctx_count // INNER
    outer_at, inner_at = ctx_at // INNER, ctx_at % INNER
    picked = tp_count // dp_count

    def ctx_pairs(step, side, dp_step=0):
        moved = [(c + step * INNER) % ctx_count ^ side for c in range(ctx_count)]
        if not dp_step:
            return list(enumerate(moved))
        return [
            (d * ctx_count + c, (d + dp_step) % dp_count * ctx_count + moved[c])
            for d in range(dp_count)
            for c in range(ctx_count)
        ]

    def shift_pairs(count, step):
        return [(i, (i + step) % count) for i in range(count)]

    def dp_steps(which):
        return [(which * picked + i - tp_at) % tp_count for i in range(picked)]

    routes = [(step, side) for step in range(outer) for side in range(INNER)]
    sources = [
        ((outer_at - step) % outer) * INNER + (inner_at + side) % INNER for step, side in routes
    ]
    scalars = [inner_at, outer_at, tp_at] + sources
    columns_at = len(scalars)
    scalars = scalars + [(tp_at + step) % tp_count for step in range(1, tp_count)]
    groups_at = []
    for step in range(dp_count):
        groups_at.append(len(scalars))
        scalars = scalars + dp_steps((dp_at + step) % dp_count)
    at = jnp.stack(scalars)

    grad_own = grad_output[0]
    grads = [grad_own] + [
        lax.ppermute(grad_own, "tp", shift_pairs(tp_count, -step)) for step in range(1, tp_count)
    ]
    kv_mine, kv_theirs = part_heads(at, key_heads[0], value_heads[0])
    kv_recv = lax.ppermute(kv_theirs, "ctx", ctx_pairs(0, 1))
    kv_blocks = [
        lax.ppermute(kv_recv if side else kv_mine, "ctx", ctx_pairs(step, 0))
        if step
        else (kv_recv if side else kv_mine)
        for step, side in routes
    ]
    first, key_mask, row_mask = prelude(
        at, block_pattern, global_offsets, grad_own, out_weight, (kv_recv, kv_blocks[INNER], kv_blocks[-INNER])
    )
    g_mine, theirs = grad_heads(at, columns_at, first, queries[0], out_weight, grads)
    recv = lax.ppermute(theirs, "ctx", ctx_pairs(0, 1))
    kept, *sends = pick_columns(at, tuple(groups_at), grads, outer, picked, (g_mine,))
    grad_blocks = [kept] + [
        lax.ppermute(send, "dp", shift_pairs(dp_count, step + 1)) for step, send in enumerate(sends)
    ]

    attn_mine, attn_theirs, dq_mine, dq_theirs, parts = attention(
        at, queries[0], recv, g_mine, key_mask, row_mask, kv_blocks
    )
    columns = [[o * INNER + i for o in range(outer)] for i in range(INNER)]
    terms = lax.all_to_all(
        parts, "ctx", split_axis=0, concat_axis=0, axis_index_groups=columns, tiled=True
    )

    attn = []
    for step in range(dp_count):
        for held, side in ((attn_mine, 0), (attn_theirs, 1)):
            pairs = ctx_pairs(0, side, step)
            axes = ("dp", "ctx") if step else "ctx"
            attn.append(lax.ppermute(held, axes, pairs) if step or side else held)

    order = list(range(1, outer)) + [0]
    halves = [order[: outer // 2], order[outer // 2 :]]
    recvs, previous = [], ()
    for steps in halves:
        send = weight_terms(at, attn, grad_blocks, 1, steps, "weight_sent", previous)
        recvs.append(lax.ppermute(send, "ctx", ctx_pairs(0, 1)))
        previous = (send,)
    keep = weight_terms(at, attn, grad_blocks, 0, order, "weight_kept", previous)
    weight_sums = []
    for recv in recvs:
        weight_sums = [*weight_sums, *weight_add(len(weight_sums), keep, recv, weight_sums[-1:])]
    weight_parts = [
        lax.ppermute(held, "ctx", ctx_pairs(step, 0)) for step, held in zip(order[:-1], weight_sums)
    ]
    terms_mine, terms_theirs = add_terms(dq_theirs, terms, (weight_sums[-1],))
    terms_recv = lax.ppermute(terms_theirs, "ctx", ctx_pairs(0, 1))
    grad_q, grad_k, grad_v = join_heads(at, dq_mine, terms_mine, terms_recv)
    grad_weight = weight_sums[-1].astype(jnp.float32)
    for part in weight_parts:
        grad_weight = grad_weight + part.astype(jnp.float32)

    return grad_q[None], grad_k[None], grad_v[None], grad_weight.astype(jnp.bfloat16)


def solution(mesh):
    in_specs = (
        P("dp", "ctx", "tp"),
        P("dp", "ctx", "tp"),
        P("dp", "ctx", "tp"),
        P("dp", "ctx", "tp"),
        P("tp", None),
        P(),
        P(),
    )
    out_specs = (
        P("dp", "ctx", "tp"),
        P("dp", "ctx", "tp"),
        P("dp", "ctx", "tp"),
        P("tp", ("dp", "ctx")),
    )
    return jax.shard_map(
        per_device, mesh=mesh, in_specs=in_specs, out_specs=out_specs, check_vma=False
    )
```

```python
import functools

import jax
import jax.numpy as jnp
from jax import lax
from jax.experimental import pallas as pl
from jax.experimental.pallas import tpu as pltpu
from jax.sharding import PartitionSpec as P

HD = 128
MASKED = -1e30
INNER = 2
SOURCES = 3
ANY = pl.BlockSpec(memory_space=pl.ANY)
VMEM = pl.BlockSpec(memory_space=pltpu.VMEM)
SMEM = pl.BlockSpec(memory_space=pltpu.SMEM)


def against(left_op, right_op):
    return lax.dot_general(
        left_op, right_op, (((1,), (1,)), ((), ())), preferred_element_type=jnp.float32
    )


def product(left_op, right_op):
    return jnp.dot(left_op, right_op, preferred_element_type=jnp.float32)


def begin(source, target, semaphore):
    copy = pltpu.make_async_copy(source, target, semaphore)
    copy.start()
    return copy


def call(kernel, out_shape, in_specs, out_specs, scratch, micros, name, after=()):
    skipped = len(after)
    in_specs = [ANY] * skipped + in_specs
    run = pl.pallas_call(
        lambda *refs: kernel(*refs[skipped:]),
        out_shape=out_shape,
        in_specs=in_specs,
        out_specs=out_specs,
        scratch_shapes=scratch,
        compiler_params=pltpu.CompilerParams(vmem_limit_bytes=64 * 1024 * 1024),
        cost_estimate=pl.CostEstimate(
            flops=int(micros * 1e9), bytes_accessed=int(micros * 3e6), transcendentals=0
        ),
        name=name,
    )

    def placed(*args):
        args = [
            pltpu.with_memory_space_constraint(arg, pltpu.HBM) if spec is ANY else arg
            for spec, arg in zip(in_specs, (*after, *args))
        ]
        return run(*args)

    return placed


def bf16(*shape):
    return pltpu.HBM(shape, jnp.bfloat16)


def f32(*shape):
    return pltpu.HBM(shape, jnp.float32)


def part_kernel(at_ref, k_ref, v_ref, kv_mine, kv_theirs, held_s, in_sem, out_sem):
    half = kv_mine.shape[1] // 2
    loads = [begin(held, held_s.at[i], in_sem.at[i]) for i, held in enumerate((k_ref, v_ref))]
    mine = pl.ds(pl.multiple_of(at_ref[0] * half, half), half)
    theirs = pl.ds(pl.multiple_of((1 - at_ref[0]) * half, half), half)
    copies = []
    for index in range(2):
        loads[index].wait()
        place = slice(index * half, (index + 1) * half)
        for side, (cols, out) in enumerate(((mine, kv_mine), (theirs, kv_theirs))):
            sem = out_sem.at[2 * index + side]
            copies.append(begin(held_s.at[index, :, cols], out.at[:, place], sem))
    for copy in copies:
        copy.wait()


def part_heads(at, keys, values):
    rows, feats = keys.shape
    return call(
        part_kernel,
        [bf16(rows, feats), bf16(rows, feats)],
        [SMEM] + [ANY] * 2,
        [ANY] * 2,
        [
            pltpu.VMEM((2, rows, feats), jnp.bfloat16),
            pltpu.SemaphoreType.DMA((2,)),
            pltpu.SemaphoreType.DMA((4,)),
        ],
        2,
        "part_heads",
    )(at, keys, values)


def prelude_kernel(at_ref, pattern, offsets, grad_ref, weight_ref, *refs):
    first, key_mask, row_mask = refs[:3]
    grad_s, weight_s, first_s, mask_s, row_s, sem, out_sem = refs[3:]
    rows, width = grad_s.shape
    block_count, glob_count = offsets.shape
    start = pl.multiple_of(at_ref[2] * width, width)
    loads = [
        begin(grad_ref, grad_s, sem.at[0]),
        begin(weight_ref.at[:, pl.ds(start, width)], weight_s, sem.at[1]),
    ]
    stores = []
    own = at_ref[1] * INNER + at_ref[0]
    partner = at_ref[1] * INNER + 1 - at_ref[0]
    lane = lax.broadcasted_iota(jnp.int32, (1, HD), 1)
    row_at = lax.broadcasted_iota(jnp.int32, (rows, HD), 0)
    col_at = lax.broadcasted_iota(jnp.int32, (8, rows), 1)
    group_at = lax.broadcasted_iota(jnp.int32, (8, rows), 0)
    for index in range(block_count):
        block = at_ref[SOURCES + index]
        hidden = []
        for target in (own, partner):
            seen = jnp.abs(block - target) <= 1
            for r in range(pattern.shape[1]):
                seen = seen | (pattern[target, r] == block)
            hidden.append(jnp.where(seen, 0, 1))
        lane_hidden = jnp.where(lane == 0, hidden[0], jnp.where(lane == 1, hidden[1], 0))
        hidden_rows = jnp.broadcast_to(lane_hidden, (rows, HD))
        for r in range(glob_count):
            hidden_rows = jnp.where(row_at == offsets[block, r], 0, hidden_rows)
        mask_s[index * rows : (index + 1) * rows, :] = hidden_rows.astype(jnp.float32).astype(
            jnp.bfloat16
        )
    for group, target in enumerate((own, partner)):
        local = jnp.where(group_at == group, MASKED, 0.0)
        for r in range(glob_count):
            local = jnp.where(col_at == offsets[target, r], 0.0, local)
        row_s[:, group * rows : (group + 1) * rows] = local
    stores.append(begin(mask_s, key_mask, out_sem.at[0]))
    stores.append(begin(row_s, row_mask, out_sem.at[1]))
    for load in loads:
        load.wait()
    first_s[...] = against(weight_s[...], grad_s[...])
    stores.append(begin(first_s, first, out_sem.at[2]))
    for store in stores:
        store.wait()


def prelude(at, pattern, offsets, grad_own, out_weight, after):
    rows, width = grad_own.shape
    feats = out_weight.shape[0]
    keys = offsets.shape[0] * rows
    return call(
        prelude_kernel,
        [
            f32(feats, rows),
            bf16(keys, HD),
            f32(8, 2 * rows),
        ],
        [SMEM] * 3 + [ANY] * 2,
        [ANY] * 3,
        [
            pltpu.VMEM((rows, width), jnp.bfloat16),
            pltpu.VMEM((feats, width), jnp.bfloat16),
            pltpu.VMEM((feats, rows), jnp.float32),
            pltpu.VMEM((keys, HD), jnp.bfloat16),
            pltpu.VMEM((8, 2 * rows), jnp.float32),
            pltpu.SemaphoreType.DMA((2,)),
            pltpu.SemaphoreType.DMA((3,)),
        ],
        4,
        "prelude",
        after,
    )(at, pattern, offsets, grad_own, out_weight)


def attention_kernel(block_count, head_count, at_ref, q_ref, recv_ref, g_mine, key_mask, row_mask, *refs):
    kv_refs, refs = refs[:block_count], refs[block_count:]
    outer = block_count // INNER
    attn_mine, attn_theirs, dq_mine, dq_theirs = refs[:4]
    part_outs, refs = refs[4 : 4 + outer], refs[4 + outer :]
    q_s, recv_s, g_s, mask_s, row_s, kv_s, e_s, s_ref, attn_s, dq_s, part_s = refs[:11]
    sem, kv_sem, out_sem, part_sem = refs[11:]
    rows = q_ref.shape[0]
    feats = head_count * HD
    score_scale = HD ** (-0.5)
    mine = pl.ds(pl.multiple_of(at_ref[0] * feats, feats), feats)
    loads = [
        begin(q_ref.at[:, mine], q_s, sem.at[0]),
        begin(recv_ref, recv_s, sem.at[1]),
        begin(key_mask, mask_s, sem.at[2]),
        begin(row_mask, row_s, sem.at[3]),
        begin(g_mine, g_s, sem.at[4]),
    ]
    kv_loads = [begin(kv_refs[j], kv_s.at[j], kv_sem.at[j]) for j in range(block_count)]
    for load in loads:
        load.wait()
    rows_low = row_s[...].astype(jnp.bfloat16)
    hidden = jnp.concatenate([rows_low, jnp.zeros((HD - 8, 2 * rows), jnp.bfloat16)], axis=0)
    stores = []
    for head in range(head_count):
        cols = slice(head * HD, (head + 1) * HD)
        vcols = slice(feats + head * HD, feats + (head + 1) * HD)
        query_recv = recv_s[1, cols, :]
        q_t = jnp.concatenate([jnp.transpose(q_s[:, cols]), query_recv], axis=1)
        q_t = jnp.concatenate([q_t, hidden], axis=0)
        top = jnp.full((1, 2 * rows), MASKED, jnp.float32)
        for j in range(block_count):
            if head == 0:
                kv_loads[j].wait()
            keys = slice(j * rows, (j + 1) * rows)
            scores = product(jnp.concatenate([kv_s[j, :, cols], mask_s[keys, :]], axis=1), q_t)
            s_ref[keys, :] = scores
            top = jnp.maximum(top, jnp.max(scores, axis=0, keepdims=True))
        total = jnp.zeros((1, 2 * rows), jnp.float32)
        attn_t = jnp.zeros((HD, 2 * rows), jnp.float32)
        for j in range(block_count):
            keys = slice(j * rows, (j + 1) * rows)
            weights = jnp.exp((s_ref[keys, :] - top) * score_scale)
            total = total + jnp.sum(weights, axis=0, keepdims=True)
            low = weights.astype(jnp.bfloat16)
            e_s[keys, :] = low
            attn_t = attn_t + product(jnp.transpose(kv_s[j, :, vcols]), low)
        inverse = 1.0 / total
        attn_low = (attn_t * inverse).astype(jnp.bfloat16)
        attn_s[0, cols, :] = attn_low[:, :rows]
        attn_s[1, cols, :] = attn_low[:, rows:]
        if head == head_count - 1:
            stores.append(begin(attn_s.at[0], attn_mine, out_sem.at[0]))
            stores.append(begin(attn_s.at[1], attn_theirs, out_sem.at[1]))
        g_t = jnp.concatenate([g_s[cols, :], recv_s[0, cols, :]], axis=1).astype(jnp.float32)
        row_dot = jnp.sum(g_t * attn_low.astype(jnp.float32), axis=0, keepdims=True) * inverse
        g_t = (g_t * inverse).astype(jnp.bfloat16)
        grad = jnp.transpose(g_t)
        query = jnp.concatenate([q_s[:, cols], jnp.transpose(query_recv)], axis=0)
        dq_t = jnp.zeros((HD, 2 * rows), jnp.float32)
        for j in range(block_count):
            keys = slice(j * rows, (j + 1) * rows)
            low = e_s[keys, :]
            dprobs = product(kv_s[j, :, vcols], g_t)
            dscore = (low.astype(jnp.float32) * (dprobs - row_dot)).astype(jnp.bfloat16)
            dq_t = dq_t + product(jnp.transpose(kv_s[j, :, cols]), dscore)
            part_s[j, :, cols] = (score_scale * product(dscore, query)).astype(jnp.bfloat16)
            part_s[j, :, vcols] = product(low, grad).astype(jnp.bfloat16)
            if head == head_count - 1:
                target = part_outs[j // INNER].at[j % INNER]
                stores.append(begin(part_s.at[j], target, part_sem.at[j]))
        dquery = (score_scale * jnp.transpose(dq_t)).astype(jnp.bfloat16)
        dq_s[0, :, cols] = dquery[:rows]
        dq_s[1, :, cols] = dquery[rows:]
    stores.append(begin(dq_s.at[0], dq_mine, out_sem.at[2]))
    stores.append(begin(dq_s.at[1], dq_theirs, out_sem.at[3]))
    for store in stores:
        store.wait()


def attention(at, queries, recv, g_mine, key_mask, row_mask, kv_blocks):
    block_count = len(kv_blocks)
    feats, rows = g_mine.shape
    heads = feats // HD
    keys = block_count * rows
    outer = block_count // INNER
    out = call(
        functools.partial(attention_kernel, block_count, heads),
        [bf16(feats, rows)] * 2 + [bf16(rows, feats)] * 2 + [bf16(INNER, rows, 2 * feats)] * outer,
        [SMEM] + [ANY] * (5 + block_count),
        [ANY] * (4 + outer),
        [
            pltpu.VMEM((rows, feats), jnp.bfloat16),
            pltpu.VMEM((2, feats, rows), jnp.bfloat16),
            pltpu.VMEM((feats, rows), jnp.bfloat16),
            pltpu.VMEM((keys, HD), jnp.bfloat16),
            pltpu.VMEM((8, 2 * rows), jnp.float32),
            pltpu.VMEM((block_count, rows, 2 * feats), jnp.bfloat16),
            pltpu.VMEM((keys, 2 * rows), jnp.bfloat16),
            pltpu.VMEM((keys, 2 * rows), jnp.float32),
            pltpu.VMEM((2, feats, rows), jnp.bfloat16),
            pltpu.VMEM((2, rows, feats), jnp.bfloat16),
            pltpu.VMEM((block_count, rows, 2 * feats), jnp.bfloat16),
            pltpu.SemaphoreType.DMA((5,)),
            pltpu.SemaphoreType.DMA((block_count,)),
            pltpu.SemaphoreType.DMA((4,)),
            pltpu.SemaphoreType.DMA((block_count,)),
        ],
        20,
        "attention",
    )(at, queries, recv, g_mine, key_mask, row_mask, *kv_blocks)
    return *out[:4], out[4:]


def grad_heads_kernel(part_count, place, at_ref, first_ref, q_ref, weight_ref, *refs):
    grads, refs = refs[: part_count - 1], refs[part_count - 1 :]
    mine, theirs = refs[:2]
    first_s, q_s, grad_s, weight_s, out_s, sem, weight_sem, grad_sem, out_sem = refs[2:]
    half = out_s.shape[1]
    width = grads[0].shape[1]
    first_load = begin(first_ref, first_s, sem.at[0])
    cols = pl.ds(pl.multiple_of((1 - at_ref[0]) * half, half), half)
    q_load = begin(q_ref.at[:, cols], q_s, sem.at[1])
    loads = []
    for k in range(part_count - 1):
        start = pl.multiple_of(at_ref[place + k] * width, width)
        columns = weight_ref.at[:, pl.ds(start, width)]
        loads.append(begin(grads[k], grad_s.at[k], grad_sem.at[k]))
        loads.append(begin(columns, weight_s.at[k], weight_sem.at[k]))
    q_load.wait()
    out_s[2] = jnp.transpose(q_s[...])
    copies = [begin(out_s.at[2], theirs.at[1], out_sem.at[2])]
    first_load.wait()
    summed = first_s[...]
    for k in range(part_count - 1):
        loads[2 * k].wait()
        loads[2 * k + 1].wait()
        summed = summed + against(weight_s[k], grad_s[k])
    first_s[...] = summed
    for side, target in enumerate((mine, theirs.at[0])):
        at = (1 - at_ref[0]) if side else at_ref[0]
        kept = first_s[pl.ds(pl.multiple_of(at * half, half), half), :]
        out_s[side] = kept.astype(jnp.bfloat16)
        copies.append(begin(out_s.at[side], target, out_sem.at[side]))
    for copy in copies:
        copy.wait()


def grad_heads(at, place, first, queries, out_weight, grads):
    feats, rows = first.shape
    half = feats // INNER
    count = len(grads)
    width = grads[0].shape[1]
    return call(
        functools.partial(grad_heads_kernel, count, place),
        [bf16(half, rows), bf16(2, half, rows)],
        [SMEM] + [ANY] * (2 + count),
        [ANY] * 2,
        [
            pltpu.VMEM((feats, rows), jnp.float32),
            pltpu.VMEM((rows, half), jnp.bfloat16),
            pltpu.VMEM((count - 1, rows, width), jnp.bfloat16),
            pltpu.VMEM((count - 1, feats, width), jnp.bfloat16),
            pltpu.VMEM((3, half, rows), jnp.bfloat16),
            pltpu.SemaphoreType.DMA((2,)),
            pltpu.SemaphoreType.DMA((count - 1,)),
            pltpu.SemaphoreType.DMA((count - 1,)),
            pltpu.SemaphoreType.DMA((3,)),
        ],
        3,
        "grad_heads",
    )(at, first, queries, out_weight, *grads[1:])


def pick_kernel(part_count, picked, places, at_ref, *refs):
    grads, refs = refs[:part_count], refs[part_count:]
    outs, (held_s, sem, out_sem) = refs[: len(places)], refs[len(places) :]
    _, outer, _, block = outs[0].shape
    pieces = grads[0].shape[1] // block
    loads = [begin(grads[k], held_s.at[k], sem.at[k]) for k in range(part_count)]
    for load in loads:
        load.wait()
    stores = []
    for index, steps_at in enumerate(places):
        for side in range(INNER):
            here = (1 - at_ref[0]) if side else at_ref[0]
            for k in range(outer):
                place = lax.rem(at_ref[1] + k, outer) * INNER + here
                cols = pl.ds(pl.multiple_of(lax.rem(place, pieces) * block, block), block)
                source = held_s.at[at_ref[steps_at + place // pieces], :, cols]
                order = (index * INNER + side) * outer + k
                stores.append(begin(source, outs[index].at[side, k], out_sem.at[order]))
    for store in stores:
        store.wait()


def pick_columns(at, places, grads, outer, picked, after):
    rows, width = grads[0].shape
    block = picked * width // (outer * INNER)
    return call(
        functools.partial(pick_kernel, len(grads), picked, places),
        [bf16(INNER, outer, rows, block)] * len(places),
        [SMEM] + [ANY] * len(grads),
        [ANY] * len(places),
        [
            pltpu.VMEM((len(grads), rows, width), jnp.bfloat16),
            pltpu.SemaphoreType.DMA((len(grads),)),
            pltpu.SemaphoreType.DMA((len(places) * INNER * outer,)),
        ],
        3,
        "pick_columns",
        after,
    )(at, *grads)


def weight_kernel(doc_count, side, steps, at_ref, *refs):
    attn, refs = refs[: INNER * doc_count], refs[INNER * doc_count :]
    grads, refs = refs[:doc_count], refs[doc_count:]
    out, attn_s, grad_s, out_s, attn_sem, grad_sem, out_sem = refs
    half = out.shape[1] // INNER
    attn_loads, grad_loads = [], []
    for doc in range(doc_count):
        for group in range(INNER):
            at = (1 - at_ref[0]) if group else at_ref[0]
            index = doc * INNER + group
            target = attn_s.at[doc, pl.ds(pl.multiple_of(at * half, half), half)]
            attn_loads.append(begin(attn[index], target, attn_sem.at[index]))
    for index, step in enumerate(steps):
        for doc in range(doc_count):
            sem = grad_sem.at[doc * len(steps) + index]
            grad_loads.append(begin(grads[doc].at[side, step], grad_s.at[doc, index], sem))
    for load in attn_loads:
        load.wait()
    stores = []
    for index in range(len(steps)):
        term = 0.0
        for doc in range(doc_count):
            grad_loads[index * doc_count + doc].wait()
            term = term + product(attn_s[doc], grad_s[doc, index])
        out_s[index] = term.astype(out_s.dtype)
        stores.append(begin(out_s.at[index], out.at[index], out_sem.at[index]))
    for store in stores:
        store.wait()


def weight_terms(at, attn, grads, side, steps, name, after=()):
    half, rows = attn[0].shape
    feats = half * INNER
    doc_count, count = len(grads), len(steps)
    width = grads[0].shape[3]
    return call(
        functools.partial(weight_kernel, doc_count, side, steps),
        bf16(count, feats, width),
        [SMEM] + [ANY] * (len(attn) + doc_count),
        ANY,
        [
            pltpu.VMEM((doc_count, feats, rows), jnp.bfloat16),
            pltpu.VMEM((doc_count, count, rows, width), jnp.bfloat16),
            pltpu.VMEM((count, feats, width), jnp.bfloat16),
            pltpu.SemaphoreType.DMA((len(attn),)),
            pltpu.SemaphoreType.DMA((doc_count * count,)),
            pltpu.SemaphoreType.DMA((count,)),
        ],
        4,
        name,
        after,
    )(at, *attn, *grads)


def weight_add_kernel(first, keep, recv, *refs):
    count = recv.shape[0]
    outs, (held_s, out_s, sem, out_sem) = refs[:count], refs[count:]
    loads = []
    for index in range(count):
        loads.append(begin(keep.at[first + index], held_s.at[0, index], sem.at[2 * index]))
        loads.append(begin(recv.at[index], held_s.at[1, index], sem.at[2 * index + 1]))
    stores = []
    for index in range(count):
        loads[2 * index].wait()
        loads[2 * index + 1].wait()
        summed = held_s[0, index].astype(jnp.float32) + held_s[1, index].astype(jnp.float32)
        out_s[index] = summed.astype(jnp.bfloat16)
        stores.append(begin(out_s.at[index], outs[index], out_sem.at[index]))
    for store in stores:
        store.wait()


def weight_add(first, keep, recv, after):
    count, feats, width = recv.shape
    return call(
        functools.partial(weight_add_kernel, first),
        [bf16(feats, width)] * count,
        [ANY] * 2,
        [ANY] * count,
        [
            pltpu.VMEM((2, count, feats, width), jnp.bfloat16),
            pltpu.VMEM((count, feats, width), jnp.bfloat16),
            pltpu.SemaphoreType.DMA((2 * count,)),
            pltpu.SemaphoreType.DMA((count,)),
        ],
        2,
        "weight_add",
        after,
    )(keep, recv)


def add_kernel(count, dq_theirs, *refs):
    terms, mine, theirs, scratch = refs[:count], refs[count], refs[count + 1], refs[count + 2 :]
    terms_s, mine_s, theirs_s, dq_s, term_sem, out_sem, dq_sem = scratch
    both = mine.shape[1]
    dq_load = begin(dq_theirs, dq_s, dq_sem)
    loads = {
        (side, c): begin(terms[c].at[side], terms_s.at[c, side], term_sem.at[c * INNER + side])
        for side in (1, 0)
        for c in range(count)
    }
    stores = []
    for side, (held_s, out) in ((1, (theirs_s, theirs)), (0, (mine_s, mine))):
        summed = 0.0
        for c in range(count):
            loads[side, c].wait()
            summed = summed + terms_s[c, side].astype(jnp.float32)
        held_s[:, :both] = summed.astype(jnp.bfloat16)
        if side:
            dq_load.wait()
            held_s[:, both:] = dq_s[...]
        stores.append(begin(held_s, out, out_sem.at[side]))
    for store in stores:
        store.wait()


def add_terms(dq_theirs, terms, after):
    _, rows, both = terms[0].shape
    half = both // 2
    count = len(terms)
    return call(
        functools.partial(add_kernel, count),
        [bf16(rows, both), bf16(rows, both + half)],
        [ANY] * (1 + count),
        [ANY] * 2,
        [
            pltpu.VMEM((count, INNER, rows, both), jnp.bfloat16),
            pltpu.VMEM((rows, both), jnp.bfloat16),
            pltpu.VMEM((rows, both + half), jnp.bfloat16),
            pltpu.VMEM((rows, half), jnp.bfloat16),
            pltpu.SemaphoreType.DMA((count * INNER,)),
            pltpu.SemaphoreType.DMA((INNER,)),
            pltpu.SemaphoreType.DMA,
        ],
        2,
        "add_terms",
        after,
    )(dq_theirs, *terms)


def join_kernel(at_ref, dq_mine, mine, recv, *refs):
    outs, (dq_s, mine_s, recv_s, out_s, sem, out_sem) = refs[:3], refs[3:]
    half = dq_mine.shape[1]
    loads = [
        begin(dq_mine, dq_s, sem.at[0]),
        begin(mine, mine_s, sem.at[1]),
        begin(recv, recv_s, sem.at[2]),
    ]
    here = pl.ds(pl.multiple_of(at_ref[0] * half, half), half)
    there = pl.ds(pl.multiple_of((1 - at_ref[0]) * half, half), half)
    for load in loads:
        load.wait()
    out_s[0, :, here] = dq_s[...]
    out_s[0, :, there] = recv_s[:, 2 * half :]
    for kind in range(2):
        cols = slice(kind * half, (kind + 1) * half)
        out_s[1 + kind, :, here] = mine_s[:, cols]
        out_s[1 + kind, :, there] = recv_s[:, cols]
    stores = [begin(out_s.at[index], out, out_sem.at[index]) for index, out in enumerate(outs)]
    for store in stores:
        store.wait()


def join_heads(at, dq_mine, mine, recv):
    rows, half = dq_mine.shape
    return call(
        join_kernel,
        [bf16(rows, INNER * half)] * 3,
        [SMEM] + [ANY] * 3,
        [ANY] * 3,
        [
            pltpu.VMEM(dq_mine.shape, jnp.bfloat16),
            pltpu.VMEM(mine.shape, jnp.bfloat16),
            pltpu.VMEM(recv.shape, jnp.bfloat16),
            pltpu.VMEM((3, rows, INNER * half), jnp.bfloat16),
            pltpu.SemaphoreType.DMA((3,)),
            pltpu.SemaphoreType.DMA((3,)),
        ],
        2,
        "join_heads",
    )(at, dq_mine, mine, recv)


def per_device(
    queries, key_heads, value_heads, grad_output, out_weight, block_pattern, global_offsets
):
    dp_count, ctx_count, tp_count = (lax.axis_size(name) for name in ("dp", "ctx", "tp"))
    dp_at, ctx_at, tp_at = (lax.axis_index(name) for name in ("dp", "ctx", "tp"))
    outer = ctx_count // INNER
    outer_at, inner_at = ctx_at // INNER, ctx_at % INNER
    picked = tp_count // dp_count

    def ctx_pairs(step, side, dp_step=0):
        moved = [(c + step * INNER) % ctx_count ^ side for c in range(ctx_count)]
        if not dp_step:
            return list(enumerate(moved))
        return [
            (d * ctx_count + c, (d + dp_step) % dp_count * ctx_count + moved[c])
            for d in range(dp_count)
            for c in range(ctx_count)
        ]

    def shift_pairs(count, step):
        return [(i, (i + step) % count) for i in range(count)]

    def dp_steps(which):
        return [(which * picked + i - tp_at) % tp_count for i in range(picked)]

    routes = [(step, side) for step in range(outer) for side in range(INNER)]
    sources = [
        ((outer_at - step) % outer) * INNER + (inner_at + side) % INNER for step, side in routes
    ]
    scalars = [inner_at, outer_at, tp_at] + sources
    columns_at = len(scalars)
    scalars = scalars + [(tp_at + step) % tp_count for step in range(1, tp_count)]
    groups_at = []
    for step in range(dp_count):
        groups_at.append(len(scalars))
        scalars = scalars + dp_steps((dp_at + step) % dp_count)
    at = jnp.stack(scalars)

    grad_own = grad_output[0]
    grads = [grad_own] + [
        lax.ppermute(grad_own, "tp", shift_pairs(tp_count, -step)) for step in range(1, tp_count)
    ]
    kv_mine, kv_theirs = part_heads(at, key_heads[0], value_heads[0])
    kv_recv = lax.ppermute(kv_theirs, "ctx", ctx_pairs(0, 1))
    kv_blocks = [
        lax.ppermute(kv_recv if side else kv_mine, "ctx", ctx_pairs(step, 0))
        if step
        else (kv_recv if side else kv_mine)
        for step, side in routes
    ]
    first, key_mask, row_mask = prelude(
        at, block_pattern, global_offsets, grad_own, out_weight, (kv_recv, kv_blocks[INNER], kv_blocks[-INNER])
    )
    g_mine, theirs = grad_heads(at, columns_at, first, queries[0], out_weight, grads)
    recv = lax.ppermute(theirs, "ctx", ctx_pairs(0, 1))
    kept, *sends = pick_columns(at, tuple(groups_at), grads, outer, picked, (g_mine,))
    grad_blocks = [kept] + [
        lax.ppermute(send, "dp", shift_pairs(dp_count, step + 1)) for step, send in enumerate(sends)
    ]

    attn_mine, attn_theirs, dq_mine, dq_theirs, parts = attention(
        at, queries[0], recv, g_mine, key_mask, row_mask, kv_blocks
    )
    attn = []
    for step in range(dp_count):
        for held, side in ((attn_mine, 0), (attn_theirs, 1)):
            pairs = ctx_pairs(0, side, step)
            axes = ("dp", "ctx") if step else "ctx"
            attn.append(lax.ppermute(held, axes, pairs) if step or side else held)

    parts, _ = lax.optimization_barrier((parts, attn[1:]))
    terms = [
        lax.ppermute(part, "ctx", ctx_pairs(-step, 0)) if step else part
        for step, part in enumerate(parts)
    ]

    order = list(range(1, outer)) + [0]
    send = weight_terms(at, attn, grad_blocks, 1, order[:-1], "weight_sent")
    weight_recv = lax.ppermute(send, "ctx", ctx_pairs(0, 1))
    own_send = weight_terms(at, attn, grad_blocks, 1, order[-1:], "weight_own", (send,))
    own_recv = lax.ppermute(own_send, "ctx", ctx_pairs(0, 1))
    keep = weight_terms(at, attn, grad_blocks, 0, order, "weight_kept", (own_send,))
    weight_sums = weight_add(0, keep, weight_recv, ())
    weight_parts = [
        lax.ppermute(held, "ctx", ctx_pairs(step, 0)) for step, held in zip(order, weight_sums)
    ]
    terms_mine, terms_theirs = add_terms(dq_theirs, terms, weight_sums[-1:])
    terms_recv = lax.ppermute(terms_theirs, "ctx", ctx_pairs(0, 1))
    grad_q, grad_k, grad_v = join_heads(at, dq_mine, terms_mine, terms_recv)
    grad_weight = keep[-1].astype(jnp.float32) + own_recv[0].astype(jnp.float32)
    for part in weight_parts:
        grad_weight = grad_weight + part.astype(jnp.float32)
    grad_weight = grad_weight.astype(jnp.bfloat16)
    return grad_q[None], grad_k[None], grad_v[None], grad_weight.astype(jnp.bfloat16)


def solution(mesh):
    in_specs = (
        P("dp", "ctx", "tp"),
        P("dp", "ctx", "tp"),
        P("dp", "ctx", "tp"),
        P("dp", "ctx", "tp"),
        P("tp", None),
        P(),
        P(),
    )
    out_specs = (
        P("dp", "ctx", "tp"),
        P("dp", "ctx", "tp"),
        P("dp", "ctx", "tp"),
        P("tp", ("dp", "ctx")),
    )
    return jax.shard_map(
        per_device, mesh=mesh, in_specs=in_specs, out_specs=out_specs, check_vma=False
    )
```

```python
import functools

import jax
import jax.numpy as jnp
from jax import lax
from jax.experimental import pallas as pl
from jax.experimental.pallas import tpu as pltpu
from jax.sharding import PartitionSpec as P

HD = 128
MASKED = -1e30
INNER = 2
SOURCES = 3
ANY = pl.BlockSpec(memory_space=pl.ANY)
VMEM = pl.BlockSpec(memory_space=pltpu.VMEM)
SMEM = pl.BlockSpec(memory_space=pltpu.SMEM)


def against(left_op, right_op):
    return lax.dot_general(
        left_op, right_op, (((1,), (1,)), ((), ())), preferred_element_type=jnp.float32
    )


def product(left_op, right_op):
    return jnp.dot(left_op, right_op, preferred_element_type=jnp.float32)


def begin(source, target, semaphore):
    copy = pltpu.make_async_copy(source, target, semaphore)
    copy.start()
    return copy


def call(kernel, out_shape, in_specs, out_specs, scratch, micros, name, after=()):
    skipped = len(after)
    in_specs = [ANY] * skipped + in_specs
    run = pl.pallas_call(
        lambda *refs: kernel(*refs[skipped:]),
        out_shape=out_shape,
        in_specs=in_specs,
        out_specs=out_specs,
        scratch_shapes=scratch,
        compiler_params=pltpu.CompilerParams(vmem_limit_bytes=64 * 1024 * 1024),
        cost_estimate=pl.CostEstimate(
            flops=int(micros * 1e9), bytes_accessed=int(micros * 3e6), transcendentals=0
        ),
        name=name,
    )

    def placed(*args):
        args = [
            pltpu.with_memory_space_constraint(arg, pltpu.HBM) if spec is ANY else arg
            for spec, arg in zip(in_specs, (*after, *args))
        ]
        return run(*args)

    return placed


def bf16(*shape):
    return pltpu.HBM(shape, jnp.bfloat16)


def f32(*shape):
    return pltpu.HBM(shape, jnp.float32)


def part_kernel(at_ref, k_ref, v_ref, kv_mine, kv_theirs, held_s, in_sem, out_sem):
    half = kv_mine.shape[1] // 2
    loads = [begin(held, held_s.at[i], in_sem.at[i]) for i, held in enumerate((k_ref, v_ref))]
    mine = pl.ds(pl.multiple_of(at_ref[0] * half, half), half)
    theirs = pl.ds(pl.multiple_of((1 - at_ref[0]) * half, half), half)
    copies = []
    for index in range(2):
        loads[index].wait()
        place = slice(index * half, (index + 1) * half)
        for side, (cols, out) in enumerate(((mine, kv_mine), (theirs, kv_theirs))):
            sem = out_sem.at[2 * index + side]
            copies.append(begin(held_s.at[index, :, cols], out.at[:, place], sem))
    for copy in copies:
        copy.wait()


def part_heads(at, keys, values):
    rows, feats = keys.shape
    return call(
        part_kernel,
        [bf16(rows, feats), bf16(rows, feats)],
        [SMEM] + [ANY] * 2,
        [ANY] * 2,
        [
            pltpu.VMEM((2, rows, feats), jnp.bfloat16),
            pltpu.SemaphoreType.DMA((2,)),
            pltpu.SemaphoreType.DMA((4,)),
        ],
        2,
        "part_heads",
    )(at, keys, values)


def prelude_kernel(at_ref, pattern, offsets, grad_ref, weight_ref, *refs):
    first, key_mask, row_mask = refs[:3]
    grad_s, weight_s, first_s, mask_s, row_s, sem, out_sem = refs[3:]
    rows, width = grad_s.shape
    block_count, glob_count = offsets.shape
    start = pl.multiple_of(at_ref[2] * width, width)
    loads = [
        begin(grad_ref, grad_s, sem.at[0]),
        begin(weight_ref.at[:, pl.ds(start, width)], weight_s, sem.at[1]),
    ]
    stores = []
    own = at_ref[1] * INNER + at_ref[0]
    partner = at_ref[1] * INNER + 1 - at_ref[0]
    lane = lax.broadcasted_iota(jnp.int32, (1, HD), 1)
    row_at = lax.broadcasted_iota(jnp.int32, (rows, HD), 0)
    col_at = lax.broadcasted_iota(jnp.int32, (8, rows), 1)
    group_at = lax.broadcasted_iota(jnp.int32, (8, rows), 0)
    for index in range(block_count):
        block = at_ref[SOURCES + index]
        hidden = []
        for target in (own, partner):
            seen = jnp.abs(block - target) <= 1
            for r in range(pattern.shape[1]):
                seen = seen | (pattern[target, r] == block)
            hidden.append(jnp.where(seen, 0, 1))
        lane_hidden = jnp.where(lane == 0, hidden[0], jnp.where(lane == 1, hidden[1], 0))
        hidden_rows = jnp.broadcast_to(lane_hidden, (rows, HD))
        for r in range(glob_count):
            hidden_rows = jnp.where(row_at == offsets[block, r], 0, hidden_rows)
        mask_s[index * rows : (index + 1) * rows, :] = hidden_rows.astype(jnp.float32).astype(
            jnp.bfloat16
        )
    for group, target in enumerate((own, partner)):
        local = jnp.where(group_at == group, MASKED, 0.0)
        for r in range(glob_count):
            local = jnp.where(col_at == offsets[target, r], 0.0, local)
        row_s[:, group * rows : (group + 1) * rows] = local
    stores.append(begin(mask_s, key_mask, out_sem.at[0]))
    stores.append(begin(row_s, row_mask, out_sem.at[1]))
    for load in loads:
        load.wait()
    first_s[...] = against(weight_s[...], grad_s[...])
    stores.append(begin(first_s, first, out_sem.at[2]))
    for store in stores:
        store.wait()


def prelude(at, pattern, offsets, grad_own, out_weight, after):
    rows, width = grad_own.shape
    feats = out_weight.shape[0]
    keys = offsets.shape[0] * rows
    return call(
        prelude_kernel,
        [
            f32(feats, rows),
            bf16(keys, HD),
            f32(8, 2 * rows),
        ],
        [SMEM] * 3 + [ANY] * 2,
        [ANY] * 3,
        [
            pltpu.VMEM((rows, width), jnp.bfloat16),
            pltpu.VMEM((feats, width), jnp.bfloat16),
            pltpu.VMEM((feats, rows), jnp.float32),
            pltpu.VMEM((keys, HD), jnp.bfloat16),
            pltpu.VMEM((8, 2 * rows), jnp.float32),
            pltpu.SemaphoreType.DMA((2,)),
            pltpu.SemaphoreType.DMA((3,)),
        ],
        4,
        "prelude",
        after,
    )(at, pattern, offsets, grad_own, out_weight)


def attention_kernel(block_count, head_count, at_ref, q_ref, recv_ref, g_mine, key_mask, row_mask, *refs):
    kv_refs, refs = refs[:block_count], refs[block_count:]
    outer = block_count // INNER
    attn_mine, attn_theirs, dq_mine, dq_theirs = refs[:4]
    part_outs, refs = refs[4 : 4 + outer], refs[4 + outer :]
    q_s, recv_s, g_s, mask_s, row_s, kv_s, e_s, s_ref, attn_s, dq_s, part_s = refs[:11]
    sem, kv_sem, out_sem, part_sem = refs[11:]
    rows = q_ref.shape[0]
    feats = head_count * HD
    score_scale = HD ** (-0.5)
    mine = pl.ds(pl.multiple_of(at_ref[0] * feats, feats), feats)
    loads = [
        begin(q_ref.at[:, mine], q_s, sem.at[0]),
        begin(recv_ref, recv_s, sem.at[1]),
        begin(key_mask, mask_s, sem.at[2]),
        begin(row_mask, row_s, sem.at[3]),
        begin(g_mine, g_s, sem.at[4]),
    ]
    kv_loads = [begin(kv_refs[j], kv_s.at[j], kv_sem.at[j]) for j in range(block_count)]
    for load in loads:
        load.wait()
    rows_low = row_s[...].astype(jnp.bfloat16)
    hidden = jnp.concatenate([rows_low, jnp.zeros((HD - 8, 2 * rows), jnp.bfloat16)], axis=0)
    stores = []
    for head in range(head_count):
        cols = slice(head * HD, (head + 1) * HD)
        vcols = slice(feats + head * HD, feats + (head + 1) * HD)
        query_recv = recv_s[1, cols, :]
        q_t = jnp.concatenate([jnp.transpose(q_s[:, cols]), query_recv], axis=1)
        q_t = jnp.concatenate([q_t, hidden], axis=0)
        top = jnp.full((1, 2 * rows), MASKED, jnp.float32)
        for j in range(block_count):
            if head == 0:
                kv_loads[j].wait()
            keys = slice(j * rows, (j + 1) * rows)
            scores = product(jnp.concatenate([kv_s[j, :, cols], mask_s[keys, :]], axis=1), q_t)
            s_ref[keys, :] = scores
            top = jnp.maximum(top, jnp.max(scores, axis=0, keepdims=True))
        total = jnp.zeros((1, 2 * rows), jnp.float32)
        attn_t = jnp.zeros((HD, 2 * rows), jnp.float32)
        for j in range(block_count):
            keys = slice(j * rows, (j + 1) * rows)
            weights = jnp.exp((s_ref[keys, :] - top) * score_scale)
            total = total + jnp.sum(weights, axis=0, keepdims=True)
            low = weights.astype(jnp.bfloat16)
            e_s[keys, :] = low
            attn_t = attn_t + product(jnp.transpose(kv_s[j, :, vcols]), low)
        inverse = 1.0 / total
        attn_low = (attn_t * inverse).astype(jnp.bfloat16)
        attn_s[0, cols, :] = attn_low[:, :rows]
        attn_s[1, cols, :] = attn_low[:, rows:]
        if head == head_count - 1:
            stores.append(begin(attn_s.at[0], attn_mine, out_sem.at[0]))
            stores.append(begin(attn_s.at[1], attn_theirs, out_sem.at[1]))
        g_t = jnp.concatenate([g_s[cols, :], recv_s[0, cols, :]], axis=1).astype(jnp.float32)
        row_dot = jnp.sum(g_t * attn_low.astype(jnp.float32), axis=0, keepdims=True) * inverse
        g_t = (g_t * inverse).astype(jnp.bfloat16)
        grad = jnp.transpose(g_t)
        query = jnp.concatenate([q_s[:, cols], jnp.transpose(query_recv)], axis=0)
        dq_t = jnp.zeros((HD, 2 * rows), jnp.float32)
        for j in range(block_count):
            keys = slice(j * rows, (j + 1) * rows)
            low = e_s[keys, :]
            dprobs = product(kv_s[j, :, vcols], g_t)
            dscore = (low.astype(jnp.float32) * (dprobs - row_dot)).astype(jnp.bfloat16)
            dq_t = dq_t + product(jnp.transpose(kv_s[j, :, cols]), dscore)
            part_s[j, :, cols] = (score_scale * product(dscore, query)).astype(jnp.bfloat16)
            part_s[j, :, vcols] = product(low, grad).astype(jnp.bfloat16)
            if head == head_count - 1:
                target = part_outs[j // INNER].at[j % INNER]
                stores.append(begin(part_s.at[j], target, part_sem.at[j]))
        dquery = (score_scale * jnp.transpose(dq_t)).astype(jnp.bfloat16)
        dq_s[0, :, cols] = dquery[:rows]
        dq_s[1, :, cols] = dquery[rows:]
    stores.append(begin(dq_s.at[0], dq_mine, out_sem.at[2]))
    stores.append(begin(dq_s.at[1], dq_theirs, out_sem.at[3]))
    for store in stores:
        store.wait()


def attention(at, queries, recv, g_mine, key_mask, row_mask, kv_blocks):
    block_count = len(kv_blocks)
    feats, rows = g_mine.shape
    heads = feats // HD
    keys = block_count * rows
    outer = block_count // INNER
    out = call(
        functools.partial(attention_kernel, block_count, heads),
        [bf16(feats, rows)] * 2 + [bf16(rows, feats)] * 2 + [bf16(INNER, rows, 2 * feats)] * outer,
        [SMEM] + [ANY] * (5 + block_count),
        [ANY] * (4 + outer),
        [
            pltpu.VMEM((rows, feats), jnp.bfloat16),
            pltpu.VMEM((2, feats, rows), jnp.bfloat16),
            pltpu.VMEM((feats, rows), jnp.bfloat16),
            pltpu.VMEM((keys, HD), jnp.bfloat16),
            pltpu.VMEM((8, 2 * rows), jnp.float32),
            pltpu.VMEM((block_count, rows, 2 * feats), jnp.bfloat16),
            pltpu.VMEM((keys, 2 * rows), jnp.bfloat16),
            pltpu.VMEM((keys, 2 * rows), jnp.float32),
            pltpu.VMEM((2, feats, rows), jnp.bfloat16),
            pltpu.VMEM((2, rows, feats), jnp.bfloat16),
            pltpu.VMEM((block_count, rows, 2 * feats), jnp.bfloat16),
            pltpu.SemaphoreType.DMA((5,)),
            pltpu.SemaphoreType.DMA((block_count,)),
            pltpu.SemaphoreType.DMA((4,)),
            pltpu.SemaphoreType.DMA((block_count,)),
        ],
        20,
        "attention",
    )(at, queries, recv, g_mine, key_mask, row_mask, *kv_blocks)
    return *out[:4], out[4:]


def grad_heads_kernel(part_count, place, at_ref, first_ref, q_ref, weight_ref, *refs):
    grads, refs = refs[: part_count - 1], refs[part_count - 1 :]
    mine, theirs = refs[:2]
    first_s, q_s, grad_s, weight_s, out_s, sem, weight_sem, grad_sem, out_sem = refs[2:]
    half = out_s.shape[1]
    width = grads[0].shape[1]
    first_load = begin(first_ref, first_s, sem.at[0])
    cols = pl.ds(pl.multiple_of((1 - at_ref[0]) * half, half), half)
    q_load = begin(q_ref.at[:, cols], q_s, sem.at[1])
    loads = []
    for k in range(part_count - 1):
        start = pl.multiple_of(at_ref[place + k] * width, width)
        columns = weight_ref.at[:, pl.ds(start, width)]
        loads.append(begin(grads[k], grad_s.at[k], grad_sem.at[k]))
        loads.append(begin(columns, weight_s.at[k], weight_sem.at[k]))
    q_load.wait()
    out_s[2] = jnp.transpose(q_s[...])
    copies = [begin(out_s.at[2], theirs.at[1], out_sem.at[2])]
    first_load.wait()
    summed = first_s[...]
    for k in range(part_count - 1):
        loads[2 * k].wait()
        loads[2 * k + 1].wait()
        summed = summed + against(weight_s[k], grad_s[k])
    first_s[...] = summed
    for side, target in enumerate((mine, theirs.at[0])):
        at = (1 - at_ref[0]) if side else at_ref[0]
        kept = first_s[pl.ds(pl.multiple_of(at * half, half), half), :]
        out_s[side] = kept.astype(jnp.bfloat16)
        copies.append(begin(out_s.at[side], target, out_sem.at[side]))
    for copy in copies:
        copy.wait()


def grad_heads(at, place, first, queries, out_weight, grads):
    feats, rows = first.shape
    half = feats // INNER
    count = len(grads)
    width = grads[0].shape[1]
    return call(
        functools.partial(grad_heads_kernel, count, place),
        [bf16(half, rows), bf16(2, half, rows)],
        [SMEM] + [ANY] * (2 + count),
        [ANY] * 2,
        [
            pltpu.VMEM((feats, rows), jnp.float32),
            pltpu.VMEM((rows, half), jnp.bfloat16),
            pltpu.VMEM((count - 1, rows, width), jnp.bfloat16),
            pltpu.VMEM((count - 1, feats, width), jnp.bfloat16),
            pltpu.VMEM((3, half, rows), jnp.bfloat16),
            pltpu.SemaphoreType.DMA((2,)),
            pltpu.SemaphoreType.DMA((count - 1,)),
            pltpu.SemaphoreType.DMA((count - 1,)),
            pltpu.SemaphoreType.DMA((3,)),
        ],
        3,
        "grad_heads",
    )(at, first, queries, out_weight, *grads[1:])


def pick_kernel(part_count, picked, places, at_ref, *refs):
    grads, refs = refs[:part_count], refs[part_count:]
    outs, (held_s, sem, out_sem) = refs[: len(places)], refs[len(places) :]
    _, outer, _, block = outs[0].shape
    pieces = grads[0].shape[1] // block
    loads = [begin(grads[k], held_s.at[k], sem.at[k]) for k in range(part_count)]
    for load in loads:
        load.wait()
    stores = []
    for index, steps_at in enumerate(places):
        for side in range(INNER):
            here = (1 - at_ref[0]) if side else at_ref[0]
            for k in range(outer):
                place = lax.rem(at_ref[1] + k, outer) * INNER + here
                cols = pl.ds(pl.multiple_of(lax.rem(place, pieces) * block, block), block)
                source = held_s.at[at_ref[steps_at + place // pieces], :, cols]
                order = (index * INNER + side) * outer + k
                stores.append(begin(source, outs[index].at[side, k], out_sem.at[order]))
    for store in stores:
        store.wait()


def pick_columns(at, places, grads, outer, picked, after):
    rows, width = grads[0].shape
    block = picked * width // (outer * INNER)
    return call(
        functools.partial(pick_kernel, len(grads), picked, places),
        [bf16(INNER, outer, rows, block)] * len(places),
        [SMEM] + [ANY] * len(grads),
        [ANY] * len(places),
        [
            pltpu.VMEM((len(grads), rows, width), jnp.bfloat16),
            pltpu.SemaphoreType.DMA((len(grads),)),
            pltpu.SemaphoreType.DMA((len(places) * INNER * outer,)),
        ],
        3,
        "pick_columns",
        after,
    )(at, *grads)


def weight_kernel(doc_count, side, steps, at_ref, *refs):
    attn, refs = refs[: INNER * doc_count], refs[INNER * doc_count :]
    grads, refs = refs[:doc_count], refs[doc_count:]
    out, attn_s, grad_s, out_s, attn_sem, grad_sem, out_sem = refs
    half = out.shape[1] // INNER
    attn_loads, grad_loads = [], []
    for doc in range(doc_count):
        for group in range(INNER):
            at = (1 - at_ref[0]) if group else at_ref[0]
            index = doc * INNER + group
            target = attn_s.at[doc, pl.ds(pl.multiple_of(at * half, half), half)]
            attn_loads.append(begin(attn[index], target, attn_sem.at[index]))
    for index, step in enumerate(steps):
        for doc in range(doc_count):
            sem = grad_sem.at[doc * len(steps) + index]
            grad_loads.append(begin(grads[doc].at[side, step], grad_s.at[doc, index], sem))
    for load in attn_loads:
        load.wait()
    stores = []
    for index in range(len(steps)):
        term = 0.0
        for doc in range(doc_count):
            grad_loads[index * doc_count + doc].wait()
            term = term + product(attn_s[doc], grad_s[doc, index])
        out_s[index] = term.astype(out_s.dtype)
        stores.append(begin(out_s.at[index], out.at[index], out_sem.at[index]))
    for store in stores:
        store.wait()


def weight_terms(at, attn, grads, side, steps, name, after=()):
    half, rows = attn[0].shape
    feats = half * INNER
    doc_count, count = len(grads), len(steps)
    width = grads[0].shape[3]
    return call(
        functools.partial(weight_kernel, doc_count, side, steps),
        bf16(count, feats, width),
        [SMEM] + [ANY] * (len(attn) + doc_count),
        ANY,
        [
            pltpu.VMEM((doc_count, feats, rows), jnp.bfloat16),
            pltpu.VMEM((doc_count, count, rows, width), jnp.bfloat16),
            pltpu.VMEM((count, feats, width), jnp.bfloat16),
            pltpu.SemaphoreType.DMA((len(attn),)),
            pltpu.SemaphoreType.DMA((doc_count * count,)),
            pltpu.SemaphoreType.DMA((count,)),
        ],
        4,
        name,
        after,
    )(at, *attn, *grads)


def weight_add_kernel(first, keep, recv, *refs):
    count = recv.shape[0]
    outs, (held_s, out_s, sem, out_sem) = refs[:count], refs[count:]
    loads = []
    for index in range(count):
        loads.append(begin(keep.at[first + index], held_s.at[0, index], sem.at[2 * index]))
        loads.append(begin(recv.at[index], held_s.at[1, index], sem.at[2 * index + 1]))
    stores = []
    for index in range(count):
        loads[2 * index].wait()
        loads[2 * index + 1].wait()
        summed = held_s[0, index].astype(jnp.float32) + held_s[1, index].astype(jnp.float32)
        out_s[index] = summed.astype(jnp.bfloat16)
        stores.append(begin(out_s.at[index], outs[index], out_sem.at[index]))
    for store in stores:
        store.wait()


def weight_add(first, keep, recv, after):
    count, feats, width = recv.shape
    return call(
        functools.partial(weight_add_kernel, first),
        [bf16(feats, width)] * count,
        [ANY] * 2,
        [ANY] * count,
        [
            pltpu.VMEM((2, count, feats, width), jnp.bfloat16),
            pltpu.VMEM((count, feats, width), jnp.bfloat16),
            pltpu.SemaphoreType.DMA((2 * count,)),
            pltpu.SemaphoreType.DMA((count,)),
        ],
        2,
        "weight_add",
        after,
    )(keep, recv)


def add_kernel(count, dq_theirs, *refs):
    terms, mine, theirs, scratch = refs[:count], refs[count], refs[count + 1], refs[count + 2 :]
    terms_s, mine_s, theirs_s, dq_s, term_sem, out_sem, dq_sem = scratch
    both = mine.shape[1]
    dq_load = begin(dq_theirs, dq_s, dq_sem)
    loads = {
        (side, c): begin(terms[c].at[side], terms_s.at[c, side], term_sem.at[c * INNER + side])
        for side in (1, 0)
        for c in range(count)
    }
    stores = []
    for side, (held_s, out) in ((1, (theirs_s, theirs)), (0, (mine_s, mine))):
        summed = 0.0
        for c in range(count):
            loads[side, c].wait()
            summed = summed + terms_s[c, side].astype(jnp.float32)
        held_s[:, :both] = summed.astype(jnp.bfloat16)
        if side:
            dq_load.wait()
            held_s[:, both:] = dq_s[...]
        stores.append(begin(held_s, out, out_sem.at[side]))
    for store in stores:
        store.wait()


def add_terms(dq_theirs, terms, after):
    _, rows, both = terms[0].shape
    half = both // 2
    count = len(terms)
    return call(
        functools.partial(add_kernel, count),
        [bf16(rows, both), bf16(rows, both + half)],
        [ANY] * (1 + count),
        [ANY] * 2,
        [
            pltpu.VMEM((count, INNER, rows, both), jnp.bfloat16),
            pltpu.VMEM((rows, both), jnp.bfloat16),
            pltpu.VMEM((rows, both + half), jnp.bfloat16),
            pltpu.VMEM((rows, half), jnp.bfloat16),
            pltpu.SemaphoreType.DMA((count * INNER,)),
            pltpu.SemaphoreType.DMA((INNER,)),
            pltpu.SemaphoreType.DMA,
        ],
        2,
        "add_terms",
        after,
    )(dq_theirs, *terms)


def join_kernel(at_ref, dq_mine, mine, recv, *refs):
    outs, (dq_s, mine_s, recv_s, out_s, sem, out_sem) = refs[:3], refs[3:]
    half = dq_mine.shape[1]
    loads = [
        begin(dq_mine, dq_s, sem.at[0]),
        begin(mine, mine_s, sem.at[1]),
        begin(recv, recv_s, sem.at[2]),
    ]
    here = pl.ds(pl.multiple_of(at_ref[0] * half, half), half)
    there = pl.ds(pl.multiple_of((1 - at_ref[0]) * half, half), half)
    for load in loads:
        load.wait()
    out_s[0, :, here] = dq_s[...]
    out_s[0, :, there] = recv_s[:, 2 * half :]
    for kind in range(2):
        cols = slice(kind * half, (kind + 1) * half)
        out_s[1 + kind, :, here] = mine_s[:, cols]
        out_s[1 + kind, :, there] = recv_s[:, cols]
    stores = [begin(out_s.at[index], out, out_sem.at[index]) for index, out in enumerate(outs)]
    for store in stores:
        store.wait()


def join_heads(at, dq_mine, mine, recv):
    rows, half = dq_mine.shape
    return call(
        join_kernel,
        [bf16(rows, INNER * half)] * 3,
        [SMEM] + [ANY] * 3,
        [ANY] * 3,
        [
            pltpu.VMEM(dq_mine.shape, jnp.bfloat16),
            pltpu.VMEM(mine.shape, jnp.bfloat16),
            pltpu.VMEM(recv.shape, jnp.bfloat16),
            pltpu.VMEM((3, rows, INNER * half), jnp.bfloat16),
            pltpu.SemaphoreType.DMA((3,)),
            pltpu.SemaphoreType.DMA((3,)),
        ],
        2,
        "join_heads",
    )(at, dq_mine, mine, recv)


def per_device(
    queries, key_heads, value_heads, grad_output, out_weight, block_pattern, global_offsets
):
    dp_count, ctx_count, tp_count = (lax.axis_size(name) for name in ("dp", "ctx", "tp"))
    dp_at, ctx_at, tp_at = (lax.axis_index(name) for name in ("dp", "ctx", "tp"))
    outer = ctx_count // INNER
    outer_at, inner_at = ctx_at // INNER, ctx_at % INNER
    picked = tp_count // dp_count

    def ctx_pairs(step, side, dp_step=0):
        moved = [(c + step * INNER) % ctx_count ^ side for c in range(ctx_count)]
        if not dp_step:
            return list(enumerate(moved))
        return [
            (d * ctx_count + c, (d + dp_step) % dp_count * ctx_count + moved[c])
            for d in range(dp_count)
            for c in range(ctx_count)
        ]

    def shift_pairs(count, step):
        return [(i, (i + step) % count) for i in range(count)]

    def dp_steps(which):
        return [(which * picked + i - tp_at) % tp_count for i in range(picked)]

    routes = [(step, side) for step in range(outer) for side in range(INNER)]
    sources = [
        ((outer_at - step) % outer) * INNER + (inner_at + side) % INNER for step, side in routes
    ]
    scalars = [inner_at, outer_at, tp_at] + sources
    columns_at = len(scalars)
    scalars = scalars + [(tp_at + step) % tp_count for step in range(1, tp_count)]
    groups_at = []
    for step in range(dp_count):
        groups_at.append(len(scalars))
        scalars = scalars + dp_steps((dp_at + step) % dp_count)
    at = jnp.stack(scalars)

    grad_own = grad_output[0]
    grads = [grad_own] + [
        lax.ppermute(grad_own, "tp", shift_pairs(tp_count, -step)) for step in range(1, tp_count)
    ]
    kv_mine, kv_theirs = part_heads(at, key_heads[0], value_heads[0])
    kv_recv = lax.ppermute(kv_theirs, "ctx", ctx_pairs(0, 1))
    kv_blocks = [
        lax.ppermute(kv_recv if side else kv_mine, "ctx", ctx_pairs(step, 0))
        if step
        else (kv_recv if side else kv_mine)
        for step, side in routes
    ]
    first, key_mask, row_mask = prelude(
        at, block_pattern, global_offsets, grad_own, out_weight, (kv_recv, kv_blocks[INNER], kv_blocks[-INNER])
    )
    g_mine, theirs = grad_heads(at, columns_at, first, queries[0], out_weight, grads)
    recv = lax.ppermute(theirs, "ctx", ctx_pairs(0, 1))
    kept, *sends = pick_columns(at, tuple(groups_at), grads, outer, picked, (g_mine,))
    grad_blocks = [kept] + [
        lax.ppermute(send, "dp", shift_pairs(dp_count, step + 1)) for step, send in enumerate(sends)
    ]

    attn_mine, attn_theirs, dq_mine, dq_theirs, parts = attention(
        at, queries[0], recv, g_mine, key_mask, row_mask, kv_blocks
    )
    attn_mine, attn_theirs, grad_blocks = lax.optimization_barrier(
        (attn_mine, attn_theirs, grad_blocks)
    )
    attn = []
    for step in range(dp_count):
        for held, side in ((attn_mine, 0), (attn_theirs, 1)):
            pairs = ctx_pairs(0, side, step)
            axes = ("dp", "ctx") if step else "ctx"
            attn.append(lax.ppermute(held, axes, pairs) if step or side else held)

    terms = [
        lax.ppermute(part, "ctx", ctx_pairs(-step, 0)) if step else part
        for step, part in enumerate(parts)
    ]

    order = list(range(1, outer)) + [0]
    send = weight_terms(at, attn, grad_blocks, 1, order[:-1], "weight_sent")
    weight_recv = lax.ppermute(send, "ctx", ctx_pairs(0, 1))
    own_send = weight_terms(at, attn, grad_blocks, 1, order[-1:], "weight_own", (send,))
    own_recv = lax.ppermute(own_send, "ctx", ctx_pairs(0, 1))
    keep = weight_terms(at, attn, grad_blocks, 0, order, "weight_kept", (own_send,))
    weight_sums = weight_add(0, keep, weight_recv, ())
    weight_parts = [
        lax.ppermute(held, "ctx", ctx_pairs(step, 0)) for step, held in zip(order, weight_sums)
    ]
    terms_mine, terms_theirs = add_terms(dq_theirs, terms, weight_sums[-1:])
    terms_recv = lax.ppermute(terms_theirs, "ctx", ctx_pairs(0, 1))
    grad_q, grad_k, grad_v = join_heads(at, dq_mine, terms_mine, terms_recv)
    grad_weight = keep[-1].astype(jnp.float32) + own_recv[0].astype(jnp.float32)
    for part in weight_parts:
        grad_weight = grad_weight + part.astype(jnp.float32)
    grad_weight = grad_weight.astype(jnp.bfloat16)
    return grad_q[None], grad_k[None], grad_v[None], grad_weight.astype(jnp.bfloat16)


def solution(mesh):
    in_specs = (
        P("dp", "ctx", "tp"),
        P("dp", "ctx", "tp"),
        P("dp", "ctx", "tp"),
        P("dp", "ctx", "tp"),
        P("tp", None),
        P(),
        P(),
    )
    out_specs = (
        P("dp", "ctx", "tp"),
        P("dp", "ctx", "tp"),
        P("dp", "ctx", "tp"),
        P("tp", ("dp", "ctx")),
    )
    return jax.shard_map(
        per_device, mesh=mesh, in_specs=in_specs, out_specs=out_specs, check_vma=False
    )
```

```python
import functools

import jax
import jax.numpy as jnp
from jax import lax
from jax.experimental import pallas as pl
from jax.experimental.pallas import tpu as pltpu
from jax.sharding import PartitionSpec as P

HD = 128
MASKED = -1e30
INNER = 2
SOURCES = 3
ANY = pl.BlockSpec(memory_space=pl.ANY)
VMEM = pl.BlockSpec(memory_space=pltpu.VMEM)
SMEM = pl.BlockSpec(memory_space=pltpu.SMEM)


def against(left_op, right_op):
    return lax.dot_general(
        left_op, right_op, (((1,), (1,)), ((), ())), preferred_element_type=jnp.float32
    )


def product(left_op, right_op):
    return jnp.dot(left_op, right_op, preferred_element_type=jnp.float32)


def begin(source, target, semaphore):
    copy = pltpu.make_async_copy(source, target, semaphore)
    copy.start()
    return copy


def call(kernel, out_shape, in_specs, out_specs, scratch, micros, name, after=()):
    skipped = len(after)
    in_specs = [ANY] * skipped + in_specs
    run = pl.pallas_call(
        lambda *refs: kernel(*refs[skipped:]),
        out_shape=out_shape,
        in_specs=in_specs,
        out_specs=out_specs,
        scratch_shapes=scratch,
        compiler_params=pltpu.CompilerParams(vmem_limit_bytes=64 * 1024 * 1024),
        cost_estimate=pl.CostEstimate(
            flops=int(micros * 1e9), bytes_accessed=int(micros * 3e6), transcendentals=0
        ),
        name=name,
    )

    def placed(*args):
        args = [
            pltpu.with_memory_space_constraint(arg, pltpu.HBM) if spec is ANY else arg
            for spec, arg in zip(in_specs, (*after, *args))
        ]
        return run(*args)

    return placed


def bf16(*shape):
    return pltpu.HBM(shape, jnp.bfloat16)


def f32(*shape):
    return pltpu.HBM(shape, jnp.float32)


def part_kernel(at_ref, k_ref, v_ref, kv_mine, kv_theirs, held_s, in_sem, out_sem):
    half = kv_mine.shape[1] // 2
    loads = [begin(held, held_s.at[i], in_sem.at[i]) for i, held in enumerate((k_ref, v_ref))]
    mine = pl.ds(pl.multiple_of(at_ref[0] * half, half), half)
    theirs = pl.ds(pl.multiple_of((1 - at_ref[0]) * half, half), half)
    copies = []
    for index in range(2):
        loads[index].wait()
        place = slice(index * half, (index + 1) * half)
        for side, (cols, out) in enumerate(((mine, kv_mine), (theirs, kv_theirs))):
            sem = out_sem.at[2 * index + side]
            copies.append(begin(held_s.at[index, :, cols], out.at[:, place], sem))
    for copy in copies:
        copy.wait()


def part_heads(at, keys, values):
    rows, feats = keys.shape
    return call(
        part_kernel,
        [bf16(rows, feats), bf16(rows, feats)],
        [SMEM] + [ANY] * 2,
        [ANY] * 2,
        [
            pltpu.VMEM((2, rows, feats), jnp.bfloat16),
            pltpu.SemaphoreType.DMA((2,)),
            pltpu.SemaphoreType.DMA((4,)),
        ],
        2,
        "part_heads",
    )(at, keys, values)


def prelude_kernel(at_ref, pattern, offsets, grad_ref, weight_ref, *refs):
    first, key_mask, row_mask = refs[:3]
    grad_s, weight_s, first_s, mask_s, row_s, sem, out_sem = refs[3:]
    rows, width = grad_s.shape
    block_count, glob_count = offsets.shape
    start = pl.multiple_of(at_ref[2] * width, width)
    loads = [
        begin(grad_ref, grad_s, sem.at[0]),
        begin(weight_ref.at[:, pl.ds(start, width)], weight_s, sem.at[1]),
    ]
    stores = []
    own = at_ref[1] * INNER + at_ref[0]
    partner = at_ref[1] * INNER + 1 - at_ref[0]
    lane = lax.broadcasted_iota(jnp.int32, (1, HD), 1)
    row_at = lax.broadcasted_iota(jnp.int32, (rows, HD), 0)
    col_at = lax.broadcasted_iota(jnp.int32, (8, rows), 1)
    group_at = lax.broadcasted_iota(jnp.int32, (8, rows), 0)
    for index in range(block_count):
        block = at_ref[SOURCES + index]
        hidden = []
        for target in (own, partner):
            seen = jnp.abs(block - target) <= 1
            for r in range(pattern.shape[1]):
                seen = seen | (pattern[target, r] == block)
            hidden.append(jnp.where(seen, 0, 1))
        lane_hidden = jnp.where(lane == 0, hidden[0], jnp.where(lane == 1, hidden[1], 0))
        hidden_rows = jnp.broadcast_to(lane_hidden, (rows, HD))
        for r in range(glob_count):
            hidden_rows = jnp.where(row_at == offsets[block, r], 0, hidden_rows)
        mask_s[index * rows : (index + 1) * rows, :] = hidden_rows.astype(jnp.float32).astype(
            jnp.bfloat16
        )
    for group, target in enumerate((own, partner)):
        local = jnp.where(group_at == group, MASKED, 0.0)
        for r in range(glob_count):
            local = jnp.where(col_at == offsets[target, r], 0.0, local)
        row_s[:, group * rows : (group + 1) * rows] = local
    stores.append(begin(mask_s, key_mask, out_sem.at[0]))
    stores.append(begin(row_s, row_mask, out_sem.at[1]))
    for load in loads:
        load.wait()
    first_s[...] = against(weight_s[...], grad_s[...])
    stores.append(begin(first_s, first, out_sem.at[2]))
    for store in stores:
        store.wait()


def prelude(at, pattern, offsets, grad_own, out_weight, after):
    rows, width = grad_own.shape
    feats = out_weight.shape[0]
    keys = offsets.shape[0] * rows
    return call(
        prelude_kernel,
        [
            f32(feats, rows),
            bf16(keys, HD),
            f32(8, 2 * rows),
        ],
        [SMEM] * 3 + [ANY] * 2,
        [ANY] * 3,
        [
            pltpu.VMEM((rows, width), jnp.bfloat16),
            pltpu.VMEM((feats, width), jnp.bfloat16),
            pltpu.VMEM((feats, rows), jnp.float32),
            pltpu.VMEM((keys, HD), jnp.bfloat16),
            pltpu.VMEM((8, 2 * rows), jnp.float32),
            pltpu.SemaphoreType.DMA((2,)),
            pltpu.SemaphoreType.DMA((3,)),
        ],
        4,
        "prelude",
        after,
    )(at, pattern, offsets, grad_own, out_weight)


def attention_kernel(block_count, head_count, at_ref, q_ref, recv_ref, g_mine, key_mask, row_mask, *refs):
    kv_refs, refs = refs[:block_count], refs[block_count:]
    outer = block_count // INNER
    attn_mine, attn_theirs, dq_mine, dq_theirs = refs[:4]
    part_outs, refs = refs[4 : 4 + outer], refs[4 + outer :]
    q_s, recv_s, g_s, mask_s, row_s, kv_s, e_s, s_ref, attn_s, dq_s, part_s = refs[:11]
    sem, kv_sem, out_sem, part_sem = refs[11:]
    rows = q_ref.shape[0]
    feats = head_count * HD
    score_scale = HD ** (-0.5)
    mine = pl.ds(pl.multiple_of(at_ref[0] * feats, feats), feats)
    loads = [
        begin(q_ref.at[:, mine], q_s, sem.at[0]),
        begin(recv_ref, recv_s, sem.at[1]),
        begin(key_mask, mask_s, sem.at[2]),
        begin(row_mask, row_s, sem.at[3]),
        begin(g_mine, g_s, sem.at[4]),
    ]
    kv_loads = [begin(kv_refs[j], kv_s.at[j], kv_sem.at[j]) for j in range(block_count)]
    for load in loads:
        load.wait()
    rows_low = row_s[...].astype(jnp.bfloat16)
    hidden = jnp.concatenate([rows_low, jnp.zeros((HD - 8, 2 * rows), jnp.bfloat16)], axis=0)
    stores = []
    for head in range(head_count):
        cols = slice(head * HD, (head + 1) * HD)
        vcols = slice(feats + head * HD, feats + (head + 1) * HD)
        query_recv = recv_s[1, cols, :]
        q_t = jnp.concatenate([jnp.transpose(q_s[:, cols]), query_recv], axis=1)
        q_t = jnp.concatenate([q_t, hidden], axis=0)
        top = jnp.full((1, 2 * rows), MASKED, jnp.float32)
        for j in range(block_count):
            if head == 0:
                kv_loads[j].wait()
            keys = slice(j * rows, (j + 1) * rows)
            scores = product(jnp.concatenate([kv_s[j, :, cols], mask_s[keys, :]], axis=1), q_t)
            s_ref[keys, :] = scores
            top = jnp.maximum(top, jnp.max(scores, axis=0, keepdims=True))
        total = jnp.zeros((1, 2 * rows), jnp.float32)
        attn_t = jnp.zeros((HD, 2 * rows), jnp.float32)
        for j in range(block_count):
            keys = slice(j * rows, (j + 1) * rows)
            weights = jnp.exp((s_ref[keys, :] - top) * score_scale)
            total = total + jnp.sum(weights, axis=0, keepdims=True)
            low = weights.astype(jnp.bfloat16)
            e_s[keys, :] = low
            attn_t = attn_t + product(jnp.transpose(kv_s[j, :, vcols]), low)
        inverse = 1.0 / total
        attn_low = (attn_t * inverse).astype(jnp.bfloat16)
        attn_s[0, cols, :] = attn_low[:, :rows]
        attn_s[1, cols, :] = attn_low[:, rows:]
        if head == head_count - 1:
            stores.append(begin(attn_s.at[0], attn_mine, out_sem.at[0]))
            stores.append(begin(attn_s.at[1], attn_theirs, out_sem.at[1]))
        g_t = jnp.concatenate([g_s[cols, :], recv_s[0, cols, :]], axis=1).astype(jnp.float32)
        row_dot = jnp.sum(g_t * attn_low.astype(jnp.float32), axis=0, keepdims=True) * inverse
        g_t = (g_t * inverse).astype(jnp.bfloat16)
        grad = jnp.transpose(g_t)
        query = jnp.concatenate([q_s[:, cols], jnp.transpose(query_recv)], axis=0)
        dq_t = jnp.zeros((HD, 2 * rows), jnp.float32)
        for j in range(block_count):
            keys = slice(j * rows, (j + 1) * rows)
            low = e_s[keys, :]
            dprobs = product(kv_s[j, :, vcols], g_t)
            dscore = (low.astype(jnp.float32) * (dprobs - row_dot)).astype(jnp.bfloat16)
            dq_t = dq_t + product(jnp.transpose(kv_s[j, :, cols]), dscore)
            part_s[j, :, cols] = (score_scale * product(dscore, query)).astype(jnp.bfloat16)
            part_s[j, :, vcols] = product(low, grad).astype(jnp.bfloat16)
            if head == head_count - 1:
                target = part_outs[j // INNER].at[j % INNER]
                stores.append(begin(part_s.at[j], target, part_sem.at[j]))
        dquery = (score_scale * jnp.transpose(dq_t)).astype(jnp.bfloat16)
        dq_s[0, :, cols] = dquery[:rows]
        dq_s[1, :, cols] = dquery[rows:]
    stores.append(begin(dq_s.at[0], dq_mine, out_sem.at[2]))
    stores.append(begin(dq_s.at[1], dq_theirs, out_sem.at[3]))
    for store in stores:
        store.wait()


def attention(at, queries, recv, g_mine, key_mask, row_mask, kv_blocks):
    block_count = len(kv_blocks)
    feats, rows = g_mine.shape
    heads = feats // HD
    keys = block_count * rows
    outer = block_count // INNER
    out = call(
        functools.partial(attention_kernel, block_count, heads),
        [bf16(feats, rows)] * 2 + [bf16(rows, feats)] * 2 + [bf16(INNER, rows, 2 * feats)] * outer,
        [SMEM] + [ANY] * (5 + block_count),
        [ANY] * (4 + outer),
        [
            pltpu.VMEM((rows, feats), jnp.bfloat16),
            pltpu.VMEM((2, feats, rows), jnp.bfloat16),
            pltpu.VMEM((feats, rows), jnp.bfloat16),
            pltpu.VMEM((keys, HD), jnp.bfloat16),
            pltpu.VMEM((8, 2 * rows), jnp.float32),
            pltpu.VMEM((block_count, rows, 2 * feats), jnp.bfloat16),
            pltpu.VMEM((keys, 2 * rows), jnp.bfloat16),
            pltpu.VMEM((keys, 2 * rows), jnp.float32),
            pltpu.VMEM((2, feats, rows), jnp.bfloat16),
            pltpu.VMEM((2, rows, feats), jnp.bfloat16),
            pltpu.VMEM((block_count, rows, 2 * feats), jnp.bfloat16),
            pltpu.SemaphoreType.DMA((5,)),
            pltpu.SemaphoreType.DMA((block_count,)),
            pltpu.SemaphoreType.DMA((4,)),
            pltpu.SemaphoreType.DMA((block_count,)),
        ],
        20,
        "attention",
    )(at, queries, recv, g_mine, key_mask, row_mask, *kv_blocks)
    return *out[:4], out[4:]


def grad_heads_kernel(part_count, place, at_ref, first_ref, q_ref, weight_ref, *refs):
    grads, refs = refs[: part_count - 1], refs[part_count - 1 :]
    mine, theirs = refs[:2]
    first_s, q_s, grad_s, weight_s, out_s, sem, weight_sem, grad_sem, out_sem = refs[2:]
    half = out_s.shape[1]
    width = grads[0].shape[1]
    first_load = begin(first_ref, first_s, sem.at[0])
    cols = pl.ds(pl.multiple_of((1 - at_ref[0]) * half, half), half)
    q_load = begin(q_ref.at[:, cols], q_s, sem.at[1])
    loads = []
    for k in range(part_count - 1):
        start = pl.multiple_of(at_ref[place + k] * width, width)
        columns = weight_ref.at[:, pl.ds(start, width)]
        loads.append(begin(grads[k], grad_s.at[k], grad_sem.at[k]))
        loads.append(begin(columns, weight_s.at[k], weight_sem.at[k]))
    q_load.wait()
    out_s[2] = jnp.transpose(q_s[...])
    copies = [begin(out_s.at[2], theirs.at[1], out_sem.at[2])]
    first_load.wait()
    summed = first_s[...]
    for k in range(part_count - 1):
        loads[2 * k].wait()
        loads[2 * k + 1].wait()
        summed = summed + against(weight_s[k], grad_s[k])
    first_s[...] = summed
    for side, target in enumerate((mine, theirs.at[0])):
        at = (1 - at_ref[0]) if side else at_ref[0]
        kept = first_s[pl.ds(pl.multiple_of(at * half, half), half), :]
        out_s[side] = kept.astype(jnp.bfloat16)
        copies.append(begin(out_s.at[side], target, out_sem.at[side]))
    for copy in copies:
        copy.wait()


def grad_heads(at, place, first, queries, out_weight, grads):
    feats, rows = first.shape
    half = feats // INNER
    count = len(grads)
    width = grads[0].shape[1]
    return call(
        functools.partial(grad_heads_kernel, count, place),
        [bf16(half, rows), bf16(2, half, rows)],
        [SMEM] + [ANY] * (2 + count),
        [ANY] * 2,
        [
            pltpu.VMEM((feats, rows), jnp.float32),
            pltpu.VMEM((rows, half), jnp.bfloat16),
            pltpu.VMEM((count - 1, rows, width), jnp.bfloat16),
            pltpu.VMEM((count - 1, feats, width), jnp.bfloat16),
            pltpu.VMEM((3, half, rows), jnp.bfloat16),
            pltpu.SemaphoreType.DMA((2,)),
            pltpu.SemaphoreType.DMA((count - 1,)),
            pltpu.SemaphoreType.DMA((count - 1,)),
            pltpu.SemaphoreType.DMA((3,)),
        ],
        3,
        "grad_heads",
    )(at, first, queries, out_weight, *grads[1:])


def pick_kernel(part_count, picked, places, at_ref, *refs):
    grads, refs = refs[:part_count], refs[part_count:]
    outs, (held_s, sem, out_sem) = refs[: len(places)], refs[len(places) :]
    _, outer, _, block = outs[0].shape
    pieces = grads[0].shape[1] // block
    loads = [begin(grads[k], held_s.at[k], sem.at[k]) for k in range(part_count)]
    for load in loads:
        load.wait()
    stores = []
    for index, steps_at in enumerate(places):
        for side in range(INNER):
            here = (1 - at_ref[0]) if side else at_ref[0]
            for k in range(outer):
                place = lax.rem(at_ref[1] + k, outer) * INNER + here
                cols = pl.ds(pl.multiple_of(lax.rem(place, pieces) * block, block), block)
                source = held_s.at[at_ref[steps_at + place // pieces], :, cols]
                order = (index * INNER + side) * outer + k
                stores.append(begin(source, outs[index].at[side, k], out_sem.at[order]))
    for store in stores:
        store.wait()


def pick_columns(at, places, grads, outer, picked, after):
    rows, width = grads[0].shape
    block = picked * width // (outer * INNER)
    return call(
        functools.partial(pick_kernel, len(grads), picked, places),
        [bf16(INNER, outer, rows, block)] * len(places),
        [SMEM] + [ANY] * len(grads),
        [ANY] * len(places),
        [
            pltpu.VMEM((len(grads), rows, width), jnp.bfloat16),
            pltpu.SemaphoreType.DMA((len(grads),)),
            pltpu.SemaphoreType.DMA((len(places) * INNER * outer,)),
        ],
        3,
        "pick_columns",
        after,
    )(at, *grads)


def weight_kernel(doc_count, side, steps, at_ref, *refs):
    attn, refs = refs[: INNER * doc_count], refs[INNER * doc_count :]
    grads, refs = refs[:doc_count], refs[doc_count:]
    out, attn_s, grad_s, out_s, attn_sem, grad_sem, out_sem = refs
    half = out.shape[1] // INNER
    attn_loads, grad_loads = [], []
    for doc in range(doc_count):
        for group in range(INNER):
            at = (1 - at_ref[0]) if group else at_ref[0]
            index = doc * INNER + group
            target = attn_s.at[doc, pl.ds(pl.multiple_of(at * half, half), half)]
            attn_loads.append(begin(attn[index], target, attn_sem.at[index]))
    for index, step in enumerate(steps):
        for doc in range(doc_count):
            sem = grad_sem.at[doc * len(steps) + index]
            grad_loads.append(begin(grads[doc].at[side, step], grad_s.at[doc, index], sem))
    for load in attn_loads:
        load.wait()
    stores = []
    for index in range(len(steps)):
        term = 0.0
        for doc in range(doc_count):
            grad_loads[index * doc_count + doc].wait()
            term = term + product(attn_s[doc], grad_s[doc, index])
        out_s[index] = term.astype(out_s.dtype)
        stores.append(begin(out_s.at[index], out.at[index], out_sem.at[index]))
    for store in stores:
        store.wait()


def weight_terms(at, attn, grads, side, steps, name, after=()):
    half, rows = attn[0].shape
    feats = half * INNER
    doc_count, count = len(grads), len(steps)
    width = grads[0].shape[3]
    return call(
        functools.partial(weight_kernel, doc_count, side, steps),
        bf16(count, feats, width),
        [SMEM] + [ANY] * (len(attn) + doc_count),
        ANY,
        [
            pltpu.VMEM((doc_count, feats, rows), jnp.bfloat16),
            pltpu.VMEM((doc_count, count, rows, width), jnp.bfloat16),
            pltpu.VMEM((count, feats, width), jnp.bfloat16),
            pltpu.SemaphoreType.DMA((len(attn),)),
            pltpu.SemaphoreType.DMA((doc_count * count,)),
            pltpu.SemaphoreType.DMA((count,)),
        ],
        4,
        name,
        after,
    )(at, *attn, *grads)


def weight_add_kernel(first, keep, recv, *refs):
    count = recv.shape[0]
    outs, (held_s, out_s, sem, out_sem) = refs[:count], refs[count:]
    loads = []
    for index in range(count):
        loads.append(begin(keep.at[first + index], held_s.at[0, index], sem.at[2 * index]))
        loads.append(begin(recv.at[index], held_s.at[1, index], sem.at[2 * index + 1]))
    stores = []
    for index in range(count):
        loads[2 * index].wait()
        loads[2 * index + 1].wait()
        summed = held_s[0, index].astype(jnp.float32) + held_s[1, index].astype(jnp.float32)
        out_s[index] = summed.astype(jnp.bfloat16)
        stores.append(begin(out_s.at[index], outs[index], out_sem.at[index]))
    for store in stores:
        store.wait()


def weight_add(first, keep, recv, after):
    count, feats, width = recv.shape
    return call(
        functools.partial(weight_add_kernel, first),
        [bf16(feats, width)] * count,
        [ANY] * 2,
        [ANY] * count,
        [
            pltpu.VMEM((2, count, feats, width), jnp.bfloat16),
            pltpu.VMEM((count, feats, width), jnp.bfloat16),
            pltpu.SemaphoreType.DMA((2 * count,)),
            pltpu.SemaphoreType.DMA((count,)),
        ],
        2,
        "weight_add",
        after,
    )(keep, recv)


def add_kernel(count, dq_theirs, *refs):
    terms, mine, theirs, scratch = refs[:count], refs[count], refs[count + 1], refs[count + 2 :]
    terms_s, mine_s, theirs_s, dq_s, term_sem, out_sem, dq_sem = scratch
    both = mine.shape[1]
    dq_load = begin(dq_theirs, dq_s, dq_sem)
    loads = {
        (side, c): begin(terms[c].at[side], terms_s.at[c, side], term_sem.at[c * INNER + side])
        for side in (1, 0)
        for c in range(count)
    }
    stores = []
    for side, (held_s, out) in ((1, (theirs_s, theirs)), (0, (mine_s, mine))):
        summed = 0.0
        for c in range(count):
            loads[side, c].wait()
            summed = summed + terms_s[c, side].astype(jnp.float32)
        held_s[:, :both] = summed.astype(jnp.bfloat16)
        if side:
            dq_load.wait()
            held_s[:, both:] = dq_s[...]
        stores.append(begin(held_s, out, out_sem.at[side]))
    for store in stores:
        store.wait()


def add_terms(dq_theirs, terms, after):
    _, rows, both = terms[0].shape
    half = both // 2
    count = len(terms)
    return call(
        functools.partial(add_kernel, count),
        [bf16(rows, both), bf16(rows, both + half)],
        [ANY] * (1 + count),
        [ANY] * 2,
        [
            pltpu.VMEM((count, INNER, rows, both), jnp.bfloat16),
            pltpu.VMEM((rows, both), jnp.bfloat16),
            pltpu.VMEM((rows, both + half), jnp.bfloat16),
            pltpu.VMEM((rows, half), jnp.bfloat16),
            pltpu.SemaphoreType.DMA((count * INNER,)),
            pltpu.SemaphoreType.DMA((INNER,)),
            pltpu.SemaphoreType.DMA,
        ],
        2,
        "add_terms",
        after,
    )(dq_theirs, *terms)


def join_kernel(at_ref, dq_mine, mine, recv, *refs):
    outs, (dq_s, mine_s, recv_s, out_s, sem, out_sem) = refs[:3], refs[3:]
    half = dq_mine.shape[1]
    loads = [
        begin(dq_mine, dq_s, sem.at[0]),
        begin(mine, mine_s, sem.at[1]),
        begin(recv, recv_s, sem.at[2]),
    ]
    here = pl.ds(pl.multiple_of(at_ref[0] * half, half), half)
    there = pl.ds(pl.multiple_of((1 - at_ref[0]) * half, half), half)
    for load in loads:
        load.wait()
    out_s[0, :, here] = dq_s[...]
    out_s[0, :, there] = recv_s[:, 2 * half :]
    for kind in range(2):
        cols = slice(kind * half, (kind + 1) * half)
        out_s[1 + kind, :, here] = mine_s[:, cols]
        out_s[1 + kind, :, there] = recv_s[:, cols]
    stores = [begin(out_s.at[index], out, out_sem.at[index]) for index, out in enumerate(outs)]
    for store in stores:
        store.wait()


def join_heads(at, dq_mine, mine, recv):
    rows, half = dq_mine.shape
    return call(
        join_kernel,
        [bf16(rows, INNER * half)] * 3,
        [SMEM] + [ANY] * 3,
        [ANY] * 3,
        [
            pltpu.VMEM(dq_mine.shape, jnp.bfloat16),
            pltpu.VMEM(mine.shape, jnp.bfloat16),
            pltpu.VMEM(recv.shape, jnp.bfloat16),
            pltpu.VMEM((3, rows, INNER * half), jnp.bfloat16),
            pltpu.SemaphoreType.DMA((3,)),
            pltpu.SemaphoreType.DMA((3,)),
        ],
        2,
        "join_heads",
    )(at, dq_mine, mine, recv)


def per_device(
    queries, key_heads, value_heads, grad_output, out_weight, block_pattern, global_offsets
):
    dp_count, ctx_count, tp_count = (lax.axis_size(name) for name in ("dp", "ctx", "tp"))
    dp_at, ctx_at, tp_at = (lax.axis_index(name) for name in ("dp", "ctx", "tp"))
    outer = ctx_count // INNER
    outer_at, inner_at = ctx_at // INNER, ctx_at % INNER
    picked = tp_count // dp_count

    def ctx_pairs(step, side, dp_step=0):
        moved = [(c + step * INNER) % ctx_count ^ side for c in range(ctx_count)]
        if not dp_step:
            return list(enumerate(moved))
        return [
            (d * ctx_count + c, (d + dp_step) % dp_count * ctx_count + moved[c])
            for d in range(dp_count)
            for c in range(ctx_count)
        ]

    def shift_pairs(count, step):
        return [(i, (i + step) % count) for i in range(count)]

    def dp_steps(which):
        return [(which * picked + i - tp_at) % tp_count for i in range(picked)]

    routes = [(step, side) for step in range(outer) for side in range(INNER)]
    sources = [
        ((outer_at - step) % outer) * INNER + (inner_at + side) % INNER for step, side in routes
    ]
    scalars = [inner_at, outer_at, tp_at] + sources
    columns_at = len(scalars)
    scalars = scalars + [(tp_at + step) % tp_count for step in range(1, tp_count)]
    groups_at = []
    for step in range(dp_count):
        groups_at.append(len(scalars))
        scalars = scalars + dp_steps((dp_at + step) % dp_count)
    at = jnp.stack(scalars)

    grad_own = grad_output[0]
    grads = [grad_own] + [
        lax.ppermute(grad_own, "tp", shift_pairs(tp_count, -step)) for step in range(1, tp_count)
    ]
    kv_mine, kv_theirs = part_heads(at, key_heads[0], value_heads[0])
    kv_recv = lax.ppermute(kv_theirs, "ctx", ctx_pairs(0, 1))
    kv_blocks = [
        lax.ppermute(kv_recv if side else kv_mine, "ctx", ctx_pairs(step, 0))
        if step
        else (kv_recv if side else kv_mine)
        for step, side in routes
    ]
    first, key_mask, row_mask = prelude(
        at, block_pattern, global_offsets, grad_own, out_weight, (kv_recv, kv_blocks[INNER], kv_blocks[-INNER])
    )
    g_mine, theirs = grad_heads(at, columns_at, first, queries[0], out_weight, grads)
    recv = lax.ppermute(theirs, "ctx", ctx_pairs(0, 1))
    kept, *sends = pick_columns(at, tuple(groups_at), grads, outer, picked, (g_mine,))
    grad_blocks = [kept] + [
        lax.ppermute(send, "dp", shift_pairs(dp_count, step + 1)) for step, send in enumerate(sends)
    ]

    attn_mine, attn_theirs, dq_mine, dq_theirs, parts = attention(
        at, queries[0], recv, g_mine, key_mask, row_mask, kv_blocks
    )
    attn_mine, attn_theirs, grad_blocks = lax.optimization_barrier(
        (attn_mine, attn_theirs, grad_blocks)
    )
    attn = []
    for step in range(dp_count):
        for held, side in ((attn_mine, 0), (attn_theirs, 1)):
            pairs = ctx_pairs(0, side, step)
            axes = ("dp", "ctx") if step else "ctx"
            attn.append(lax.ppermute(held, axes, pairs) if step or side else held)

    far_first = sorted(range(1, outer), key=lambda step: -min(step, outer - step))
    terms = [lax.ppermute(parts[step], "ctx", ctx_pairs(-step, 0)) for step in far_first]
    terms = [parts[0], *terms]

    order = list(range(1, outer)) + [0]
    send = weight_terms(at, attn, grad_blocks, 1, order[:-1], "weight_sent")
    weight_recv = lax.ppermute(send, "ctx", ctx_pairs(0, 1))
    own_send = weight_terms(at, attn, grad_blocks, 1, order[-1:], "weight_own", (send,))
    own_recv = lax.ppermute(own_send, "ctx", ctx_pairs(0, 1))
    keep = weight_terms(at, attn, grad_blocks, 0, order, "weight_kept", (own_send,))
    weight_sums = weight_add(0, keep, weight_recv, ())
    weight_parts = [
        lax.ppermute(held, "ctx", ctx_pairs(step, 0)) for step, held in zip(order, weight_sums)
    ]
    terms_mine, terms_theirs = add_terms(dq_theirs, terms, weight_sums[-1:])
    terms_recv = lax.ppermute(terms_theirs, "ctx", ctx_pairs(0, 1))
    grad_q, grad_k, grad_v = join_heads(at, dq_mine, terms_mine, terms_recv)
    grad_weight = keep[-1].astype(jnp.float32) + own_recv[0].astype(jnp.float32)
    for part in weight_parts:
        grad_weight = grad_weight + part.astype(jnp.float32)
    grad_weight = grad_weight.astype(jnp.bfloat16)
    return grad_q[None], grad_k[None], grad_v[None], grad_weight.astype(jnp.bfloat16)


def solution(mesh):
    in_specs = (
        P("dp", "ctx", "tp"),
        P("dp", "ctx", "tp"),
        P("dp", "ctx", "tp"),
        P("dp", "ctx", "tp"),
        P("tp", None),
        P(),
        P(),
    )
    out_specs = (
        P("dp", "ctx", "tp"),
        P("dp", "ctx", "tp"),
        P("dp", "ctx", "tp"),
        P("tp", ("dp", "ctx")),
    )
    return jax.shard_map(
        per_device, mesh=mesh, in_specs=in_specs, out_specs=out_specs, check_vma=False
    )
```

```python
import functools

import jax
import jax.numpy as jnp
from jax import lax
from jax.experimental import pallas as pl
from jax.experimental.pallas import tpu as pltpu
from jax.sharding import PartitionSpec as P

HD = 128
MASKED = -1e30
INNER = 2
SOURCES = 3
ANY = pl.BlockSpec(memory_space=pl.ANY)
VMEM = pl.BlockSpec(memory_space=pltpu.VMEM)
SMEM = pl.BlockSpec(memory_space=pltpu.SMEM)


def against(left_op, right_op):
    return lax.dot_general(
        left_op, right_op, (((1,), (1,)), ((), ())), preferred_element_type=jnp.float32
    )


def product(left_op, right_op):
    return jnp.dot(left_op, right_op, preferred_element_type=jnp.float32)


def begin(source, target, semaphore):
    copy = pltpu.make_async_copy(source, target, semaphore)
    copy.start()
    return copy


def call(kernel, out_shape, in_specs, out_specs, scratch, micros, name, after=()):
    skipped = len(after)
    in_specs = [ANY] * skipped + in_specs
    run = pl.pallas_call(
        lambda *refs: kernel(*refs[skipped:]),
        out_shape=out_shape,
        in_specs=in_specs,
        out_specs=out_specs,
        scratch_shapes=scratch,
        compiler_params=pltpu.CompilerParams(vmem_limit_bytes=64 * 1024 * 1024),
        cost_estimate=pl.CostEstimate(
            flops=int(micros * 1e9), bytes_accessed=int(micros * 3e6), transcendentals=0
        ),
        name=name,
    )

    def placed(*args):
        args = [
            pltpu.with_memory_space_constraint(arg, pltpu.HBM) if spec is ANY else arg
            for spec, arg in zip(in_specs, (*after, *args))
        ]
        return run(*args)

    return placed


def bf16(*shape):
    return pltpu.HBM(shape, jnp.bfloat16)


def f32(*shape):
    return pltpu.HBM(shape, jnp.float32)


def part_kernel(at_ref, k_ref, v_ref, kv_mine, kv_theirs, held_s, in_sem, out_sem):
    half = kv_mine.shape[1] // 2
    loads = [begin(held, held_s.at[i], in_sem.at[i]) for i, held in enumerate((k_ref, v_ref))]
    mine = pl.ds(pl.multiple_of(at_ref[0] * half, half), half)
    theirs = pl.ds(pl.multiple_of((1 - at_ref[0]) * half, half), half)
    copies = []
    for index in range(2):
        loads[index].wait()
        place = slice(index * half, (index + 1) * half)
        for side, (cols, out) in enumerate(((mine, kv_mine), (theirs, kv_theirs))):
            sem = out_sem.at[2 * index + side]
            copies.append(begin(held_s.at[index, :, cols], out.at[:, place], sem))
    for copy in copies:
        copy.wait()


def part_heads(at, keys, values):
    rows, feats = keys.shape
    return call(
        part_kernel,
        [bf16(rows, feats), bf16(rows, feats)],
        [SMEM] + [ANY] * 2,
        [ANY] * 2,
        [
            pltpu.VMEM((2, rows, feats), jnp.bfloat16),
            pltpu.SemaphoreType.DMA((2,)),
            pltpu.SemaphoreType.DMA((4,)),
        ],
        2,
        "part_heads",
    )(at, keys, values)


def prelude_kernel(at_ref, pattern, offsets, grad_ref, weight_ref, *refs):
    first, key_mask, row_mask = refs[:3]
    grad_s, weight_s, first_s, mask_s, row_s, sem, out_sem = refs[3:]
    rows, width = grad_s.shape
    block_count, glob_count = offsets.shape
    start = pl.multiple_of(at_ref[2] * width, width)
    loads = [
        begin(grad_ref, grad_s, sem.at[0]),
        begin(weight_ref.at[:, pl.ds(start, width)], weight_s, sem.at[1]),
    ]
    stores = []
    own = at_ref[1] * INNER + at_ref[0]
    partner = at_ref[1] * INNER + 1 - at_ref[0]
    lane = lax.broadcasted_iota(jnp.int32, (1, HD), 1)
    row_at = lax.broadcasted_iota(jnp.int32, (rows, HD), 0)
    col_at = lax.broadcasted_iota(jnp.int32, (8, rows), 1)
    group_at = lax.broadcasted_iota(jnp.int32, (8, rows), 0)
    for index in range(block_count):
        block = at_ref[SOURCES + index]
        hidden = []
        for target in (own, partner):
            seen = jnp.abs(block - target) <= 1
            for r in range(pattern.shape[1]):
                seen = seen | (pattern[target, r] == block)
            hidden.append(jnp.where(seen, 0, 1))
        lane_hidden = jnp.where(lane == 0, hidden[0], jnp.where(lane == 1, hidden[1], 0))
        hidden_rows = jnp.broadcast_to(lane_hidden, (rows, HD))
        for r in range(glob_count):
            hidden_rows = jnp.where(row_at == offsets[block, r], 0, hidden_rows)
        mask_s[index * rows : (index + 1) * rows, :] = hidden_rows.astype(jnp.float32).astype(
            jnp.bfloat16
        )
    for group, target in enumerate((own, partner)):
        local = jnp.where(group_at == group, MASKED, 0.0)
        for r in range(glob_count):
            local = jnp.where(col_at == offsets[target, r], 0.0, local)
        row_s[:, group * rows : (group + 1) * rows] = local
    stores.append(begin(mask_s, key_mask, out_sem.at[0]))
    stores.append(begin(row_s, row_mask, out_sem.at[1]))
    for load in loads:
        load.wait()
    first_s[...] = against(weight_s[...], grad_s[...])
    stores.append(begin(first_s, first, out_sem.at[2]))
    for store in stores:
        store.wait()


def prelude(at, pattern, offsets, grad_own, out_weight, after):
    rows, width = grad_own.shape
    feats = out_weight.shape[0]
    keys = offsets.shape[0] * rows
    return call(
        prelude_kernel,
        [
            f32(feats, rows),
            bf16(keys, HD),
            f32(8, 2 * rows),
        ],
        [SMEM] * 3 + [ANY] * 2,
        [ANY] * 3,
        [
            pltpu.VMEM((rows, width), jnp.bfloat16),
            pltpu.VMEM((feats, width), jnp.bfloat16),
            pltpu.VMEM((feats, rows), jnp.float32),
            pltpu.VMEM((keys, HD), jnp.bfloat16),
            pltpu.VMEM((8, 2 * rows), jnp.float32),
            pltpu.SemaphoreType.DMA((2,)),
            pltpu.SemaphoreType.DMA((3,)),
        ],
        4,
        "prelude",
        after,
    )(at, pattern, offsets, grad_own, out_weight)


def attention_kernel(block_count, head_count, at_ref, q_ref, recv_ref, g_mine, key_mask, row_mask, *refs):
    kv_refs, refs = refs[:block_count], refs[block_count:]
    outer = block_count // INNER
    attn_mine, attn_theirs, dq_mine, dq_theirs = refs[:4]
    part_outs, refs = refs[4 : 4 + outer], refs[4 + outer :]
    q_s, recv_s, g_s, mask_s, row_s, kv_s, e_s, s_ref, attn_s, dq_s, part_s = refs[:11]
    sem, kv_sem, out_sem, part_sem = refs[11:]
    rows = q_ref.shape[0]
    feats = head_count * HD
    score_scale = HD ** (-0.5)
    mine = pl.ds(pl.multiple_of(at_ref[0] * feats, feats), feats)
    loads = [
        begin(q_ref.at[:, mine], q_s, sem.at[0]),
        begin(recv_ref, recv_s, sem.at[1]),
        begin(key_mask, mask_s, sem.at[2]),
        begin(row_mask, row_s, sem.at[3]),
        begin(g_mine, g_s, sem.at[4]),
    ]
    kv_loads = [begin(kv_refs[j], kv_s.at[j], kv_sem.at[j]) for j in range(block_count)]
    for load in loads:
        load.wait()
    rows_low = row_s[...].astype(jnp.bfloat16)
    hidden = jnp.concatenate([rows_low, jnp.zeros((HD - 8, 2 * rows), jnp.bfloat16)], axis=0)
    stores = []
    for head in range(head_count):
        cols = slice(head * HD, (head + 1) * HD)
        vcols = slice(feats + head * HD, feats + (head + 1) * HD)
        query_recv = recv_s[1, cols, :]
        q_t = jnp.concatenate([jnp.transpose(q_s[:, cols]), query_recv], axis=1)
        q_t = jnp.concatenate([q_t, hidden], axis=0)
        top = jnp.full((1, 2 * rows), MASKED, jnp.float32)
        for j in range(block_count):
            if head == 0:
                kv_loads[j].wait()
            keys = slice(j * rows, (j + 1) * rows)
            scores = product(jnp.concatenate([kv_s[j, :, cols], mask_s[keys, :]], axis=1), q_t)
            s_ref[keys, :] = scores
            top = jnp.maximum(top, jnp.max(scores, axis=0, keepdims=True))
        total = jnp.zeros((1, 2 * rows), jnp.float32)
        attn_t = jnp.zeros((HD, 2 * rows), jnp.float32)
        for j in range(block_count):
            keys = slice(j * rows, (j + 1) * rows)
            weights = jnp.exp((s_ref[keys, :] - top) * score_scale)
            total = total + jnp.sum(weights, axis=0, keepdims=True)
            low = weights.astype(jnp.bfloat16)
            e_s[keys, :] = low
            attn_t = attn_t + product(jnp.transpose(kv_s[j, :, vcols]), low)
        inverse = 1.0 / total
        attn_low = (attn_t * inverse).astype(jnp.bfloat16)
        attn_s[0, cols, :] = attn_low[:, :rows]
        attn_s[1, cols, :] = attn_low[:, rows:]
        if head == head_count - 1:
            stores.append(begin(attn_s.at[0], attn_mine, out_sem.at[0]))
            stores.append(begin(attn_s.at[1], attn_theirs, out_sem.at[1]))
        g_t = jnp.concatenate([g_s[cols, :], recv_s[0, cols, :]], axis=1).astype(jnp.float32)
        row_dot = jnp.sum(g_t * attn_low.astype(jnp.float32), axis=0, keepdims=True) * inverse
        g_t = (g_t * inverse).astype(jnp.bfloat16)
        grad = jnp.transpose(g_t)
        query = jnp.concatenate([q_s[:, cols], jnp.transpose(query_recv)], axis=0)
        dq_t = jnp.zeros((HD, 2 * rows), jnp.float32)
        for j in range(block_count):
            keys = slice(j * rows, (j + 1) * rows)
            low = e_s[keys, :]
            dprobs = product(kv_s[j, :, vcols], g_t)
            dscore = (low.astype(jnp.float32) * (dprobs - row_dot)).astype(jnp.bfloat16)
            dq_t = dq_t + product(jnp.transpose(kv_s[j, :, cols]), dscore)
            part_s[j, :, cols] = (score_scale * product(dscore, query)).astype(jnp.bfloat16)
            part_s[j, :, vcols] = product(low, grad).astype(jnp.bfloat16)
            if head == head_count - 1:
                target = part_outs[j // INNER].at[j % INNER]
                stores.append(begin(part_s.at[j], target, part_sem.at[j]))
        dquery = (score_scale * jnp.transpose(dq_t)).astype(jnp.bfloat16)
        dq_s[0, :, cols] = dquery[:rows]
        dq_s[1, :, cols] = dquery[rows:]
    stores.append(begin(dq_s.at[0], dq_mine, out_sem.at[2]))
    stores.append(begin(dq_s.at[1], dq_theirs, out_sem.at[3]))
    for store in stores:
        store.wait()


def attention(at, queries, recv, g_mine, key_mask, row_mask, kv_blocks):
    block_count = len(kv_blocks)
    feats, rows = g_mine.shape
    heads = feats // HD
    keys = block_count * rows
    outer = block_count // INNER
    out = call(
        functools.partial(attention_kernel, block_count, heads),
        [bf16(feats, rows)] * 2 + [bf16(rows, feats)] * 2 + [bf16(INNER, rows, 2 * feats)] * outer,
        [SMEM] + [ANY] * (5 + block_count),
        [ANY] * (4 + outer),
        [
            pltpu.VMEM((rows, feats), jnp.bfloat16),
            pltpu.VMEM((2, feats, rows), jnp.bfloat16),
            pltpu.VMEM((feats, rows), jnp.bfloat16),
            pltpu.VMEM((keys, HD), jnp.bfloat16),
            pltpu.VMEM((8, 2 * rows), jnp.float32),
            pltpu.VMEM((block_count, rows, 2 * feats), jnp.bfloat16),
            pltpu.VMEM((keys, 2 * rows), jnp.bfloat16),
            pltpu.VMEM((keys, 2 * rows), jnp.float32),
            pltpu.VMEM((2, feats, rows), jnp.bfloat16),
            pltpu.VMEM((2, rows, feats), jnp.bfloat16),
            pltpu.VMEM((block_count, rows, 2 * feats), jnp.bfloat16),
            pltpu.SemaphoreType.DMA((5,)),
            pltpu.SemaphoreType.DMA((block_count,)),
            pltpu.SemaphoreType.DMA((4,)),
            pltpu.SemaphoreType.DMA((block_count,)),
        ],
        20,
        "attention",
    )(at, queries, recv, g_mine, key_mask, row_mask, *kv_blocks)
    return *out[:4], out[4:]


def grad_heads_kernel(part_count, place, at_ref, first_ref, q_ref, weight_ref, *refs):
    grads, refs = refs[: part_count - 1], refs[part_count - 1 :]
    mine, theirs = refs[:2]
    first_s, q_s, grad_s, weight_s, out_s, sem, weight_sem, grad_sem, out_sem = refs[2:]
    half = out_s.shape[1]
    width = grads[0].shape[1]
    first_load = begin(first_ref, first_s, sem.at[0])
    cols = pl.ds(pl.multiple_of((1 - at_ref[0]) * half, half), half)
    q_load = begin(q_ref.at[:, cols], q_s, sem.at[1])
    loads = []
    for k in range(part_count - 1):
        start = pl.multiple_of(at_ref[place + k] * width, width)
        columns = weight_ref.at[:, pl.ds(start, width)]
        loads.append(begin(grads[k], grad_s.at[k], grad_sem.at[k]))
        loads.append(begin(columns, weight_s.at[k], weight_sem.at[k]))
    q_load.wait()
    out_s[2] = jnp.transpose(q_s[...])
    copies = [begin(out_s.at[2], theirs.at[1], out_sem.at[2])]
    first_load.wait()
    summed = first_s[...]
    for k in range(part_count - 1):
        loads[2 * k].wait()
        loads[2 * k + 1].wait()
        summed = summed + against(weight_s[k], grad_s[k])
    first_s[...] = summed
    for side, target in enumerate((mine, theirs.at[0])):
        at = (1 - at_ref[0]) if side else at_ref[0]
        kept = first_s[pl.ds(pl.multiple_of(at * half, half), half), :]
        out_s[side] = kept.astype(jnp.bfloat16)
        copies.append(begin(out_s.at[side], target, out_sem.at[side]))
    for copy in copies:
        copy.wait()


def grad_heads(at, place, first, queries, out_weight, grads):
    feats, rows = first.shape
    half = feats // INNER
    count = len(grads)
    width = grads[0].shape[1]
    return call(
        functools.partial(grad_heads_kernel, count, place),
        [bf16(half, rows), bf16(2, half, rows)],
        [SMEM] + [ANY] * (2 + count),
        [ANY] * 2,
        [
            pltpu.VMEM((feats, rows), jnp.float32),
            pltpu.VMEM((rows, half), jnp.bfloat16),
            pltpu.VMEM((count - 1, rows, width), jnp.bfloat16),
            pltpu.VMEM((count - 1, feats, width), jnp.bfloat16),
            pltpu.VMEM((3, half, rows), jnp.bfloat16),
            pltpu.SemaphoreType.DMA((2,)),
            pltpu.SemaphoreType.DMA((count - 1,)),
            pltpu.SemaphoreType.DMA((count - 1,)),
            pltpu.SemaphoreType.DMA((3,)),
        ],
        3,
        "grad_heads",
    )(at, first, queries, out_weight, *grads[1:])


def pick_kernel(part_count, picked, places, at_ref, *refs):
    grads, refs = refs[:part_count], refs[part_count:]
    outs, (held_s, sem, out_sem) = refs[: len(places)], refs[len(places) :]
    _, outer, _, block = outs[0].shape
    pieces = grads[0].shape[1] // block
    loads = [begin(grads[k], held_s.at[k], sem.at[k]) for k in range(part_count)]
    for load in loads:
        load.wait()
    stores = []
    for index, steps_at in enumerate(places):
        for side in range(INNER):
            here = (1 - at_ref[0]) if side else at_ref[0]
            for k in range(outer):
                place = lax.rem(at_ref[1] + k, outer) * INNER + here
                cols = pl.ds(pl.multiple_of(lax.rem(place, pieces) * block, block), block)
                source = held_s.at[at_ref[steps_at + place // pieces], :, cols]
                order = (index * INNER + side) * outer + k
                stores.append(begin(source, outs[index].at[side, k], out_sem.at[order]))
    for store in stores:
        store.wait()


def pick_columns(at, places, grads, outer, picked, after):
    rows, width = grads[0].shape
    block = picked * width // (outer * INNER)
    return call(
        functools.partial(pick_kernel, len(grads), picked, places),
        [bf16(INNER, outer, rows, block)] * len(places),
        [SMEM] + [ANY] * len(grads),
        [ANY] * len(places),
        [
            pltpu.VMEM((len(grads), rows, width), jnp.bfloat16),
            pltpu.SemaphoreType.DMA((len(grads),)),
            pltpu.SemaphoreType.DMA((len(places) * INNER * outer,)),
        ],
        3,
        "pick_columns",
        after,
    )(at, *grads)


def weight_kernel(doc_count, side, steps, at_ref, *refs):
    attn, refs = refs[: INNER * doc_count], refs[INNER * doc_count :]
    grads, refs = refs[:doc_count], refs[doc_count:]
    out, attn_s, grad_s, out_s, attn_sem, grad_sem, out_sem = refs
    half = out.shape[1] // INNER
    attn_loads, grad_loads = [], []
    for doc in range(doc_count):
        for group in range(INNER):
            at = (1 - at_ref[0]) if group else at_ref[0]
            index = doc * INNER + group
            target = attn_s.at[doc, pl.ds(pl.multiple_of(at * half, half), half)]
            attn_loads.append(begin(attn[index], target, attn_sem.at[index]))
    for index, step in enumerate(steps):
        for doc in range(doc_count):
            sem = grad_sem.at[doc * len(steps) + index]
            grad_loads.append(begin(grads[doc].at[side, step], grad_s.at[doc, index], sem))
    for load in attn_loads:
        load.wait()
    stores = []
    for index in range(len(steps)):
        term = 0.0
        for doc in range(doc_count):
            grad_loads[index * doc_count + doc].wait()
            term = term + product(attn_s[doc], grad_s[doc, index])
        out_s[index] = term.astype(out_s.dtype)
        stores.append(begin(out_s.at[index], out.at[index], out_sem.at[index]))
    for store in stores:
        store.wait()


def weight_terms(at, attn, grads, side, steps, name, after=()):
    half, rows = attn[0].shape
    feats = half * INNER
    doc_count, count = len(grads), len(steps)
    width = grads[0].shape[3]
    return call(
        functools.partial(weight_kernel, doc_count, side, steps),
        bf16(count, feats, width),
        [SMEM] + [ANY] * (len(attn) + doc_count),
        ANY,
        [
            pltpu.VMEM((doc_count, feats, rows), jnp.bfloat16),
            pltpu.VMEM((doc_count, count, rows, width), jnp.bfloat16),
            pltpu.VMEM((count, feats, width), jnp.bfloat16),
            pltpu.SemaphoreType.DMA((len(attn),)),
            pltpu.SemaphoreType.DMA((doc_count * count,)),
            pltpu.SemaphoreType.DMA((count,)),
        ],
        4,
        name,
        after,
    )(at, *attn, *grads)


def weight_add_kernel(first, keep, recv, *refs):
    count = recv.shape[0]
    outs, (held_s, out_s, sem, out_sem) = refs[:count], refs[count:]
    loads = []
    for index in range(count):
        loads.append(begin(keep.at[first + index], held_s.at[0, index], sem.at[2 * index]))
        loads.append(begin(recv.at[index], held_s.at[1, index], sem.at[2 * index + 1]))
    stores = []
    for index in range(count):
        loads[2 * index].wait()
        loads[2 * index + 1].wait()
        summed = held_s[0, index].astype(jnp.float32) + held_s[1, index].astype(jnp.float32)
        out_s[index] = summed.astype(jnp.bfloat16)
        stores.append(begin(out_s.at[index], outs[index], out_sem.at[index]))
    for store in stores:
        store.wait()


def weight_add(first, keep, recv, after):
    count, feats, width = recv.shape
    return call(
        functools.partial(weight_add_kernel, first),
        [bf16(feats, width)] * count,
        [ANY] * 2,
        [ANY] * count,
        [
            pltpu.VMEM((2, count, feats, width), jnp.bfloat16),
            pltpu.VMEM((count, feats, width), jnp.bfloat16),
            pltpu.SemaphoreType.DMA((2 * count,)),
            pltpu.SemaphoreType.DMA((count,)),
        ],
        2,
        "weight_add",
        after,
    )(keep, recv)


def add_kernel(count, dq_theirs, *refs):
    terms, mine, theirs, scratch = refs[:count], refs[count], refs[count + 1], refs[count + 2 :]
    terms_s, mine_s, theirs_s, dq_s, term_sem, out_sem, dq_sem = scratch
    both = mine.shape[1]
    dq_load = begin(dq_theirs, dq_s, dq_sem)
    loads = {
        (side, c): begin(terms[c].at[side], terms_s.at[c, side], term_sem.at[c * INNER + side])
        for side in (1, 0)
        for c in range(count)
    }
    stores = []
    for side, (held_s, out) in ((1, (theirs_s, theirs)), (0, (mine_s, mine))):
        summed = 0.0
        for c in range(count):
            loads[side, c].wait()
            summed = summed + terms_s[c, side].astype(jnp.float32)
        held_s[:, :both] = summed.astype(jnp.bfloat16)
        if side:
            dq_load.wait()
            held_s[:, both:] = dq_s[...]
        stores.append(begin(held_s, out, out_sem.at[side]))
    for store in stores:
        store.wait()


def add_terms(dq_theirs, terms, after):
    _, rows, both = terms[0].shape
    half = both // 2
    count = len(terms)
    return call(
        functools.partial(add_kernel, count),
        [bf16(rows, both), bf16(rows, both + half)],
        [ANY] * (1 + count),
        [ANY] * 2,
        [
            pltpu.VMEM((count, INNER, rows, both), jnp.bfloat16),
            pltpu.VMEM((rows, both), jnp.bfloat16),
            pltpu.VMEM((rows, both + half), jnp.bfloat16),
            pltpu.VMEM((rows, half), jnp.bfloat16),
            pltpu.SemaphoreType.DMA((count * INNER,)),
            pltpu.SemaphoreType.DMA((INNER,)),
            pltpu.SemaphoreType.DMA,
        ],
        2,
        "add_terms",
        after,
    )(dq_theirs, *terms)


def join_kernel(at_ref, dq_mine, mine, recv, *refs):
    outs, (dq_s, mine_s, recv_s, out_s, sem, out_sem) = refs[:3], refs[3:]
    half = dq_mine.shape[1]
    loads = [
        begin(dq_mine, dq_s, sem.at[0]),
        begin(mine, mine_s, sem.at[1]),
        begin(recv, recv_s, sem.at[2]),
    ]
    here = pl.ds(pl.multiple_of(at_ref[0] * half, half), half)
    there = pl.ds(pl.multiple_of((1 - at_ref[0]) * half, half), half)
    for load in loads:
        load.wait()
    out_s[0, :, here] = dq_s[...]
    out_s[0, :, there] = recv_s[:, 2 * half :]
    for kind in range(2):
        cols = slice(kind * half, (kind + 1) * half)
        out_s[1 + kind, :, here] = mine_s[:, cols]
        out_s[1 + kind, :, there] = recv_s[:, cols]
    stores = [begin(out_s.at[index], out, out_sem.at[index]) for index, out in enumerate(outs)]
    for store in stores:
        store.wait()


def join_heads(at, dq_mine, mine, recv):
    rows, half = dq_mine.shape
    return call(
        join_kernel,
        [bf16(rows, INNER * half)] * 3,
        [SMEM] + [ANY] * 3,
        [ANY] * 3,
        [
            pltpu.VMEM(dq_mine.shape, jnp.bfloat16),
            pltpu.VMEM(mine.shape, jnp.bfloat16),
            pltpu.VMEM(recv.shape, jnp.bfloat16),
            pltpu.VMEM((3, rows, INNER * half), jnp.bfloat16),
            pltpu.SemaphoreType.DMA((3,)),
            pltpu.SemaphoreType.DMA((3,)),
        ],
        2,
        "join_heads",
    )(at, dq_mine, mine, recv)


def per_device(
    queries, key_heads, value_heads, grad_output, out_weight, block_pattern, global_offsets
):
    dp_count, ctx_count, tp_count = (lax.axis_size(name) for name in ("dp", "ctx", "tp"))
    dp_at, ctx_at, tp_at = (lax.axis_index(name) for name in ("dp", "ctx", "tp"))
    outer = ctx_count // INNER
    outer_at, inner_at = ctx_at // INNER, ctx_at % INNER
    picked = tp_count // dp_count

    def ctx_pairs(step, side, dp_step=0):
        moved = [(c + step * INNER) % ctx_count ^ side for c in range(ctx_count)]
        if not dp_step:
            return list(enumerate(moved))
        return [
            (d * ctx_count + c, (d + dp_step) % dp_count * ctx_count + moved[c])
            for d in range(dp_count)
            for c in range(ctx_count)
        ]

    def shift_pairs(count, step):
        return [(i, (i + step) % count) for i in range(count)]

    def dp_steps(which):
        return [(which * picked + i - tp_at) % tp_count for i in range(picked)]

    routes = [(step, side) for step in range(outer) for side in range(INNER)]
    sources = [
        ((outer_at - step) % outer) * INNER + (inner_at + side) % INNER for step, side in routes
    ]
    scalars = [inner_at, outer_at, tp_at] + sources
    columns_at = len(scalars)
    scalars = scalars + [(tp_at + step) % tp_count for step in range(1, tp_count)]
    groups_at = []
    for step in range(dp_count):
        groups_at.append(len(scalars))
        scalars = scalars + dp_steps((dp_at + step) % dp_count)
    at = jnp.stack(scalars)

    grad_own = grad_output[0]
    grads = [grad_own] + [
        lax.ppermute(grad_own, "tp", shift_pairs(tp_count, -step)) for step in range(1, tp_count)
    ]
    kv_mine, kv_theirs = part_heads(at, key_heads[0], value_heads[0])
    kv_recv = lax.ppermute(kv_theirs, "ctx", ctx_pairs(0, 1))
    kv_blocks = [
        lax.ppermute(kv_recv if side else kv_mine, "ctx", ctx_pairs(step, 0))
        if step
        else (kv_recv if side else kv_mine)
        for step, side in routes
    ]
    first, key_mask, row_mask = prelude(
        at, block_pattern, global_offsets, grad_own, out_weight, (kv_recv, kv_blocks[INNER], kv_blocks[-INNER])
    )
    g_mine, theirs = grad_heads(at, columns_at, first, queries[0], out_weight, grads)
    recv = lax.ppermute(theirs, "ctx", ctx_pairs(0, 1))
    kept, *sends = pick_columns(at, tuple(groups_at), grads, outer, picked, (g_mine,))
    grad_blocks = [kept] + [
        lax.ppermute(send, "dp", shift_pairs(dp_count, step + 1)) for step, send in enumerate(sends)
    ]

    attn_mine, attn_theirs, dq_mine, dq_theirs, parts = attention(
        at, queries[0], recv, g_mine, key_mask, row_mask, kv_blocks
    )
    attn_mine, attn_theirs, grad_blocks = lax.optimization_barrier(
        (attn_mine, attn_theirs, grad_blocks)
    )
    attn = []
    for step in range(dp_count):
        for held, side in ((attn_mine, 0), (attn_theirs, 1)):
            pairs = ctx_pairs(0, side, step)
            axes = ("dp", "ctx") if step else "ctx"
            attn.append(lax.ppermute(held, axes, pairs) if step or side else held)

    far_first = sorted(range(1, outer), key=lambda step: -min(step, outer - step))
    terms = [lax.ppermute(parts[step], "ctx", ctx_pairs(-step, 0)) for step in far_first]
    terms = [parts[0], *terms]

    order = [*far_first, 0]
    send = weight_terms(at, attn, grad_blocks, 1, order[:-1], "weight_sent")
    weight_recv = lax.ppermute(send, "ctx", ctx_pairs(0, 1))
    own_send = weight_terms(at, attn, grad_blocks, 1, order[-1:], "weight_own", (send,))
    own_recv = lax.ppermute(own_send, "ctx", ctx_pairs(0, 1))
    keep = weight_terms(at, attn, grad_blocks, 0, order, "weight_kept", (own_send,))
    weight_sums = weight_add(0, keep, weight_recv, ())
    weight_parts = [
        lax.ppermute(held, "ctx", ctx_pairs(step, 0)) for step, held in zip(order, weight_sums)
    ]
    terms_mine, terms_theirs = add_terms(dq_theirs, terms, weight_sums[-1:])
    terms_recv = lax.ppermute(terms_theirs, "ctx", ctx_pairs(0, 1))
    grad_q, grad_k, grad_v = join_heads(at, dq_mine, terms_mine, terms_recv)
    grad_weight = keep[-1].astype(jnp.float32) + own_recv[0].astype(jnp.float32)
    for part in weight_parts:
        grad_weight = grad_weight + part.astype(jnp.float32)
    grad_weight = grad_weight.astype(jnp.bfloat16)
    return grad_q[None], grad_k[None], grad_v[None], grad_weight.astype(jnp.bfloat16)


def solution(mesh):
    in_specs = (
        P("dp", "ctx", "tp"),
        P("dp", "ctx", "tp"),
        P("dp", "ctx", "tp"),
        P("dp", "ctx", "tp"),
        P("tp", None),
        P(),
        P(),
    )
    out_specs = (
        P("dp", "ctx", "tp"),
        P("dp", "ctx", "tp"),
        P("dp", "ctx", "tp"),
        P("tp", ("dp", "ctx")),
    )
    return jax.shard_map(
        per_device, mesh=mesh, in_specs=in_specs, out_specs=out_specs, check_vma=False
    )
```
